128 devices in a mesh: fsdp: 16 (over y, x), expert: 8 (over z, core).
Axes of the slice: x: 4, y: 4, z: 4, core: 2. Of those that a mesh axis runs over, the one named last changes fastest.
Arguments:
- hidden_in: bfloat16 [8, 2048, 2048], P('expert', 'fsdp'), may hold values from -6 to 6
- cotangent: bfloat16 [8, 2048, 2048], P('expert', 'fsdp'), may hold values from -6 to 6
- segments: int32 [8, 2048], P('expert'), may hold values from 0 to 128, as said below
- routes: int32 [8, 2048, 2], P('expert', 'fsdp'), may hold values from 0 to 7, all different within a row; in each aligned block of 128 rows (0 to 127, 128 to 255, ..., all dimensions but the last counted through in order) at most 42 rows name the same one
- attn_gain: bfloat16 [2048], P('fsdp'), may hold values from 0.099609375 to 1.8984375
- w_query: bfloat16 [2048, 2048], P('fsdp'), may hold values from -0.125 to 0.125
- w_key: bfloat16 [2048, 512], P('fsdp'), may hold values from -0.125 to 0.125
- w_value: bfloat16 [2048, 512], P('fsdp'), may hold values from -0.125 to 0.125
- w_out: bfloat16 [2048, 2048], P('fsdp'), may hold values from -0.5 to 0.5
- ffn_gain: bfloat16 [2048], P('fsdp'), may hold values from 0.099609375 to 1.8984375
- w_router: bfloat16 [2048, 8], P('fsdp'), may hold values from -0.0625 to 0.0625
- shared_gate: bfloat16 [2048, 2816], P('fsdp'), may hold values from -0.125 to 0.125
- shared_up: bfloat16 [2048, 2816], P('fsdp'), may hold values from -0.125 to 0.125
- shared_down: bfloat16 [2816, 2048], P('fsdp'), may hold values from -0.109375 to 0.109375
- expert_gate: bfloat16 [2048, 8, 1408], P('fsdp', 'expert'), may hold values from -0.125 to 0.125
- expert_up: bfloat16 [2048, 8, 1408], P('fsdp', 'expert'), may hold values from -0.125 to 0.125
- expert_down: bfloat16 [1408, 8, 2048], P('fsdp', 'expert'), may hold values from -0.15625 to 0.15625
Outputs:
- layer_out: bfloat16 [8, 2048, 2048], P('expert', 'fsdp')
- grad_input: bfloat16 [8, 2048, 2048], P('expert', 'fsdp')
- grad_attn_gain: float32 [2048], P('fsdp')
- grad_w_query: float32 [2048, 2048], P('fsdp')
- grad_w_key: float32 [2048, 512], P('fsdp')
- grad_w_value: float32 [2048, 512], P('fsdp')
- grad_w_out: float32 [2048, 2048], P('fsdp')
- grad_ffn_gain: float32 [2048], P('fsdp')
- grad_w_router: float32 [2048, 8], P('fsdp')
- grad_shared_gate: float32 [2048, 2816], P('fsdp')
- grad_shared_up: float32 [2048, 2816], P('fsdp')
- grad_shared_down: float32 [2816, 2048], P('fsdp')
- grad_expert_gate: float32 [2048, 8, 1408], P('fsdp', 'expert')
- grad_expert_up: float32 [2048, 8, 1408], P('fsdp', 'expert')
- grad_expert_down: float32 [1408, 8, 2048], P('fsdp', 'expert')
The draws below stay inside these ranges and needn't reach their ends.
Inputs may be any that keep to these rules, and one draw needn't show every extreme that they name: `segments`: in each sequence the document numbers start at 0 and rise by 0 or 1 from one token to the next; the last token's number is 128. `routes`: each token names 2 different experts; the tokens of one device name no expert more than 42 times.
All inputs are finite; a program needn't handle non-finite values.
Results may differ from the reference program's by a relative error of at most 0.025.
Values may be sent and summed in bfloat16 or wider, within the bound.
No kernel may reach another device: no remote copies, remote signals or barrier semaphores. Data moves between devices by JAX's collectives and lax.ppermute only.
A program may use at most 320 MiB of HBM per device.

```python
import math
import jax
import jax.numpy as jnp
import numpy as np
from jax import lax

D = 2048
H = 16
KV = 4
HD = 128
FF = 1408
SH = 2816
TOPK = 2
TOK_DEV = 128
LENGTH = 2048
SEQS = 8
EXPERTS = 8
CAP = 42


def draw_segments(key, part):
    key = jax.random.fold_in(key, 11)
    doc_start = jax.random.randint(key, (SEQS, 1), 1, TOK_DEV)
    doc_end = doc_start + LENGTH - TOK_DEV
    position = jnp.arange(LENGTH, dtype=jnp.int32)[None, :]
    inside = (position > doc_start) & (position < doc_end)
    boundary = ~inside & (position > 0)
    return jnp.cumsum(boundary.astype(jnp.int32), axis=1).astype(jnp.int32)


def block_levels(own_key, dims, pieces, low, top_value):
    factor_of = 1.0
    for dim, parts in pieces:
        heights = jax.random.uniform(jax.random.fold_in(jax.random.fold_in(own_key, 6), dim), (parts,), jnp.float32, low / len(pieces), top_value / len(pieces))
        factor_of = factor_of * jnp.repeat(jnp.exp(heights), dims[dim] // parts).reshape((-1,) + (1,) * (len(dims) - 1 - dim))
    return factor_of


def deal_out(key, own, number, rows, count, top, bound, slope):
    sequence = jax.random.permutation(key, count)
    crowded, ordinary = portions_of(count, rows * top, bound, slope, True), portions_of(count, rows * top, bound, slope, False)
    places = jnp.arange(count)

    def named(sizes, offset_by):
        used = int((sizes > 0).sum())
        fixed = max(1, used // 4)
        passed = fixed + (places - fixed + offset_by * (used - fixed)) % max(1, count - fixed)
        return jnp.zeros((count,), jnp.int32).at[sequence[jnp.where(places < fixed, places, passed)]].set(jnp.asarray(sizes, jnp.int32))

    sizes = jnp.where(number % 4 == 0, named(crowded, number // 4), named(ordinary, number - number // 4 - 1))
    mixed = jax.random.permutation(jax.random.fold_in(own, 3), count)
    source_of, taker = mixed[0:count // 2 * 2:2], mixed[1:count // 2 * 2:2]
    margin = jnp.minimum(sizes[source_of] - 1, bound - sizes[taker]) // 2
    margin = jnp.where((source_of == sequence[0]) | (taker == sequence[0]) | (sizes[taker] == 0), 0, jnp.maximum(margin, 0))
    passed = jax.random.randint(jax.random.fold_in(own, 4), (count // 2,), 0, 1 << 20) % (margin + 1)
    sizes = sizes.at[source_of].add(-passed).at[taker].add(passed)
    items = jnp.searchsorted(jnp.cumsum(sizes), jnp.arange(rows * top), side="right").astype(jnp.int32)
    grid = items.reshape(top, rows).T
    grid = grid[jax.random.permutation(jax.random.fold_in(own, 1), rows)]
    offset_by = jax.random.randint(jax.random.fold_in(own, 2), (rows, 1), 0, top)
    return jnp.take_along_axis(grid, (jnp.arange(top)[None, :] + offset_by) % top, axis=1)


def portions_of(count, total, most, slope, full):
    portions = [(1 << 20) // math.isqrt(standing ** slope) + 1 for standing in range(1, count + 1)]
    largest = most if full else min(most, max(-(-total // count), total * portions[0] // sum(portions)))
    least = 1 if total - largest >= count - 1 else 0
    counts, surplus = [largest] + [least] * (count - 1), total - largest - least * (count - 1)
    while surplus > 0:
        candidates = [i for i in range(1, count) if counts[i] < largest] or [i for i in range(1, count) if counts[i] < most]
        mass, left = sum([portions[i] for i in candidates]), surplus
        for i in candidates:
            addition = min(most - counts[i], max(1, left * portions[i] // mass), surplus)
            counts[i] = counts[i] + addition
            surplus = surplus - addition
    return np.array(counts)


def centred(own_key, dims, spread, most, pieces=(), held_as=jnp.bfloat16):
    array = jax.random.normal(own_key, dims, jnp.float32) * spread
    if len(pieces) > 0:
        array = block_levels(own_key, dims, pieces, -0.22, 0.18) * array
    return jnp.clip(array, min=-most, max=most).astype(held_as)


def setup_inputs(seed: int = 0) -> dict:
    key_of = jax.random.split(jax.random.key(seed), 18)
    hidden_in = centred(key_of[0], (SEQS, LENGTH, D), 1.0, 6.0, ((0, 8), (1, 16)))
    cotangent = centred(key_of[1], (SEQS, LENGTH, D), 1.0, 6.0, ((0, 8), (1, 16)))
    segments = draw_segments(jax.random.fold_in(key_of[17], 71), 0)
    routes_keys = jax.random.split(jax.random.fold_in(key_of[3], 1), SEQS * LENGTH // TOK_DEV)
    routes_turns = jax.random.permutation(jax.random.fold_in(key_of[3], 3), SEQS * LENGTH // TOK_DEV)
    routes = jax.vmap(lambda own, number: deal_out(jax.random.fold_in(key_of[3], 2), own, number, TOK_DEV, EXPERTS, TOPK, CAP, 2))(routes_keys, routes_turns).reshape((SEQS, LENGTH, TOPK))
    attn_gain = jnp.clip(1.0 + 0.18 * jax.random.normal(key_of[4], (D,), jnp.float32), 0.099609375, 1.8984375).astype(jnp.bfloat16)
    w_query = centred(key_of[5], (D, H * HD), D ** -0.5, 0.125, ((0, 16),))
    w_key = centred(key_of[6], (D, KV * HD), D ** -0.5, 0.125, ((0, 16),))
    w_value = centred(key_of[7], (D, KV * HD), D ** -0.5, 0.125, ((0, 16),))
    w_out = centred(key_of[8], (H * HD, D), (H * HD // 16) ** -0.5, 0.5, ((0, 16),))
    ffn_gain = jnp.clip(1.0 + 0.18 * jax.random.normal(key_of[9], (D,), jnp.float32), 0.099609375, 1.8984375).astype(jnp.bfloat16)
    w_router = centred(key_of[10], (D, EXPERTS), (4 * D) ** -0.5, 0.0625, ((0, 16),))
    shared_gate = centred(key_of[11], (D, SH), D ** -0.5, 0.125, ((0, 16),))
    shared_up = centred(key_of[12], (D, SH), D ** -0.5, 0.125, ((0, 16),))
    shared_down = centred(key_of[13], (SH, D), SH ** -0.5, 0.109375, ((0, 16),))
    expert_gate = centred(key_of[14], (D, EXPERTS, FF), D ** -0.5, 0.125, ((0, 16), (1, 8)))
    expert_up = centred(key_of[15], (D, EXPERTS, FF), D ** -0.5, 0.125, ((0, 16), (1, 8)))
    expert_down = centred(key_of[16], (FF, EXPERTS, D), FF ** -0.5, 0.15625, ((0, 16), (1, 8)))
    return {"hidden_in": hidden_in, "cotangent": cotangent, "segments": segments, "routes": routes, "attn_gain": attn_gain, "w_query": w_query, "w_key": w_key, "w_value": w_value, "w_out": w_out, "ffn_gain": ffn_gain, "w_router": w_router, "shared_gate": shared_gate, "shared_up": shared_up, "shared_down": shared_down, "expert_gate": expert_gate, "expert_up": expert_up, "expert_down": expert_down}


@jax.custom_vjp
def low(v):
    return lax.optimization_barrier(v.astype(jnp.bfloat16)).astype(jnp.float32)

@jax.custom_vjp
def low_back(v):
    return v

def low_keep(v):
    return (low(v), None)

def low_pass(kept, grad):
    return (grad,)

def back_keep(v):
    return (v, None)

def back_low(kept, grad):
    return (low(grad),)
low.defvjp(low_keep, low_pass)
low_back.defvjp(back_keep, back_low)
eps_norm = 1e-06
rope_base = 600000.0
masked_fill = -1e+30

def matmul_hi(left, right):
    return jnp.dot(left, right, precision=lax.Precision.HIGHEST, preferred_element_type=jnp.float32)

def rms_scale(values, gain_vec):
    factor = lax.rsqrt(lax.optimization_barrier(jnp.mean(values * values, axis=-1, keepdims=True)) + eps_norm)
    return values * factor * gain_vec

def rotary_tables(offset, span_count):
    inverse_freq = rope_base ** (-jnp.arange(HD // 2, dtype=jnp.float32) * 2.0 / HD)
    angles = (offset + jnp.arange(span_count)).astype(jnp.float32)[:, None] * inverse_freq[None, :]
    return (jnp.cos(angles)[:, None, :], jnp.sin(angles)[:, None, :])

def rotate(values, cosine, sine_part, turn_sign):
    half_width = values.shape[-1] // 2
    first_half = values[..., :half_width]
    second_half = values[..., half_width:]
    return jnp.concatenate([first_half * cosine - turn_sign * second_half * sine_part, second_half * cosine + turn_sign * first_half * sine_part], axis=-1)

def attend_one(packed):
    queries, keys, values, segment_ids = packed
    grouped = queries.reshape(LENGTH, KV, H // KV, HD)
    raw_scores = jnp.einsum('tkgd,skd->kgts', grouped, keys, precision=lax.Precision.HIGHEST) * HD ** (-0.5)
    scores = low_back(raw_scores)
    position = jnp.arange(LENGTH)
    allowed = (position[:, None] >= position[None, :]) & (segment_ids[:, None] == segment_ids[None, :])
    masked = jnp.where(allowed[None, None], scores, masked_fill)
    probs_low = low(jax.nn.softmax(masked, axis=-1))
    mixed = jnp.einsum('kgts,skd->tkgd', probs_low, values, precision=lax.Precision.HIGHEST)
    return mixed.reshape(LENGTH, H * HD)

def dispatch_table(routes):
    blocks = SEQS * LENGTH // TOK_DEV
    per_block = TOK_DEV * TOPK
    flat_routes = routes.reshape(blocks, per_block).astype(jnp.int32)
    expert_hot = (flat_routes[:, :, None] == jnp.arange(EXPERTS, dtype=jnp.int32)[None, None, :]).astype(jnp.int32)
    ranking = lax.optimization_barrier(jnp.sum((jnp.cumsum(expert_hot, axis=1) - 1) * expert_hot, axis=2)).astype(jnp.int32)
    block_ids = jnp.arange(blocks, dtype=jnp.int32)[:, None]
    slot_ids = (flat_routes * blocks + block_ids) * CAP + ranking
    pair_ids = jnp.arange(blocks * per_block, dtype=jnp.int32).reshape(blocks, per_block)
    slot_table = jnp.full((EXPERTS * blocks * CAP,), blocks * per_block, jnp.int32)
    slot_table = slot_table.at[slot_ids.reshape(-1)].set(pair_ids.reshape(-1))
    return slot_table.reshape(EXPERTS, blocks * CAP)

def expert_apply(packed):
    rows_in, gate_weight, up_weight, down_weight = packed
    gate_value = low_back(matmul_hi(rows_in, gate_weight))
    up_value = low_back(matmul_hi(rows_in, up_weight))
    hidden_value = low(jax.nn.silu(gate_value) * up_value)
    return matmul_hi(hidden_value, down_weight)

def forward(hidden_in, attn_gain, w_query, w_key, w_value, w_out, ffn_gain, w_router, shared_gate, shared_up, shared_down, expert_gate, expert_up, expert_down, segments, routes):
    token_total = SEQS * LENGTH
    flat_in = hidden_in.reshape(token_total, D)
    normed_one = low(rms_scale(flat_in, attn_gain))
    query_raw = low_back(matmul_hi(normed_one, w_query)).reshape(SEQS, LENGTH, H, HD)
    key_raw = low_back(matmul_hi(normed_one, w_key)).reshape(SEQS, LENGTH, KV, HD)
    values = low(low_back(matmul_hi(normed_one, w_value))).reshape(SEQS, LENGTH, KV, HD)
    cosine, sine_part = rotary_tables(0, LENGTH)
    queries = low(rotate(query_raw, cosine, sine_part, 1.0))
    keys = low(rotate(key_raw, cosine, sine_part, 1.0))
    mixed = lax.map(jax.checkpoint(attend_one), (queries, keys, values, segments))
    mixed = low(low_back(mixed.reshape(token_total, H * HD)))
    middle = flat_in + low_back(matmul_hi(mixed, w_out))
    normed_two = low(rms_scale(middle, ffn_gain))
    logits = matmul_hi(normed_two, w_router)
    route_flat = routes.reshape(token_total, TOPK).astype(jnp.int32)
    chosen = jnp.take_along_axis(logits, route_flat, axis=1)
    gates = jax.nn.softmax(chosen, axis=-1)
    gate_shared = low_back(matmul_hi(normed_two, shared_gate))
    up_shared = low_back(matmul_hi(normed_two, shared_up))
    hidden_shared = low(jax.nn.silu(gate_shared) * up_shared)
    shared_result = matmul_hi(hidden_shared, shared_down)
    pair_rows = low_back(jnp.repeat(normed_two, TOPK, axis=0))
    padded = jnp.concatenate([pair_rows, jnp.zeros((1, D), jnp.float32)], axis=0)
    slot_table = dispatch_table(routes)
    expert_in = padded[slot_table]
    expert_result = lax.map(jax.checkpoint(expert_apply), (expert_in, jnp.transpose(expert_gate, (1, 0, 2)), jnp.transpose(expert_up, (1, 0, 2)), jnp.transpose(expert_down, (1, 0, 2))))
    expert_rows = low(low_back(expert_result))
    returned = jnp.zeros((token_total * TOPK + 1, D), jnp.float32).at[slot_table.reshape(-1)].add(expert_rows.reshape(-1, D))
    per_pair = returned[:token_total * TOPK].reshape(token_total, TOPK, D)
    moe_result = lax.optimization_barrier(jnp.sum(gates[:, :, None] * per_pair, axis=1))
    return (middle + shared_result + moe_result).reshape(SEQS, LENGTH, D)

def reference(hidden_in, cotangent, segments, routes, attn_gain, w_query, w_key, w_value, w_out, ffn_gain, w_router, shared_gate, shared_up, shared_down, expert_gate, expert_up, expert_down):
    params = tuple((array_in.astype(jnp.float32) for array_in in (hidden_in, attn_gain, w_query, w_key, w_value, w_out, ffn_gain, w_router, shared_gate, shared_up, shared_down, expert_gate, expert_up, expert_down)))

    def run_layer(*floats):
        return forward(*floats, segments, routes)
    layer_out, pullback = jax.vjp(run_layer, *params)
    gradients = pullback(cotangent.astype(jnp.float32))
    return (layer_out.astype(jnp.bfloat16), gradients[0].astype(jnp.bfloat16), gradients[1], gradients[2], gradients[3], gradients[4], gradients[5], gradients[6], gradients[7], gradients[8], gradients[9], gradients[10], gradients[11], gradients[12], gradients[13])
```

```python
import jax
import jax.numpy as jnp
from jax import lax
from jax.experimental import pallas as pl
from jax.experimental.pallas import tpu as pltpu
from jax.sharding import PartitionSpec as P

D = 2048
H = 16
KV = 4
HD = 128
FF = 1408
SH = 2816
TOPK = 2
TOK = 128
LENGTH = 2048
SEQS = 8
EXPERTS = 8
FSDP = 16
ALL = SEQS * TOK
CAP = 42
SLOTS = SEQS * CAP
SH_ROWS = SH // FSDP
SH_PART = SH_ROWS // EXPERTS
SH_PAD = 24
SH_OWN = FSDP * SH_PAD
QBLOCK = 256

eps_norm = 1e-06
rope_base = 600000.0
masked_fill = -1e30
highest = lax.Precision.HIGHEST
low = jnp.bfloat16
wide = jnp.float32


def shift_pairs(step):
    return [(z * 2 + c, ((z + step) % 4) * 2 + c) for z in range(4) for c in range(2)]


core_pairs = [(z * 2 + c, z * 2 + 1 - c) for z in range(4) for c in range(2)]


def move_z(block, step):
    return lax.ppermute(block, "expert", shift_pairs(step))


def swap_core(block):
    return lax.ppermute(block, "expert", core_pairs)


def gather_rows(block):
    split = block.shape[0] // 32 * 16
    below = move_z(block, 1)
    above = move_z(block, -1)
    opposite = jnp.concatenate([move_z(below[:split], 1), move_z(above[split:], -1)], axis=0)
    mine = jnp.stack([block, above, opposite, below])
    return jnp.concatenate([mine, swap_core(mine)], axis=0)


def scatter_rows(parts):
    half = parts.shape[1] // 32 * 16
    chip = parts[:4].astype(wide) + swap_core(parts[4:]).astype(wide)
    from_below = move_z(chip[2, :half].astype(low), 1)
    from_above = move_z(chip[2, half:].astype(low), -1)
    to_above = jnp.concatenate([chip[1, :half] + from_below.astype(wide), chip[1, half:]], axis=0)
    to_below = jnp.concatenate([chip[3, :half], chip[3, half:] + from_above.astype(wide)], axis=0)
    first = move_z(to_above.astype(low), 1)
    second = move_z(to_below.astype(low), -1)
    return chip[0] + first.astype(wide) + second.astype(wide)


def exchange(blocks, expert):
    chip = jnp.stack([blocks[:4], swap_core(blocks[4:])], axis=1)
    got = jnp.stack([chip[0]] + [move_z(chip[step], step) for step in (1, 2, 3)])
    got = got.reshape((EXPERTS,) + blocks.shape[1:])
    z, core = expert // 2, expert % 2
    parts = []
    for source in range(EXPERTS):
        place = ((z - source // 2) % 4) * 2 + (core ^ (source % 2))
        parts.append(lax.dynamic_index_in_dim(got, place, 0, keepdims=False))
    return jnp.stack(parts)


def relative_owner(expert, block):
    return ((expert // 2 + block % 4) % 4) * 2 + ((expert % 2) ^ (block // 4))


def pack_tiles(block):
    rows, columns = block.shape[0] // 8, block.shape[1] // 128
    tiles = block.reshape(rows, 8, columns, 128).transpose(2, 1, 0, 3)
    return tiles.reshape(columns * 8, rows * 128)


def unpack_tiles(block, count):
    rows, columns = block.shape[1] // 128, block.shape[0] // (8 * count)
    tiles = block.reshape(count, columns, 8, rows, 128).transpose(0, 3, 2, 1, 4)
    return tiles.reshape(count * rows * 8, columns * 128)


def pack_all(block, count):
    rows, columns = block.shape[0] // (8 * count), block.shape[1] // 128
    tiles = block.reshape(count, rows, 8, columns, 128).transpose(0, 3, 2, 1, 4)
    return tiles.reshape(count * columns * 8, rows * 128)


def product(left, right, contract):
    return lax.dot_general(left, right, (contract, ((), ())), preferred_element_type=wide)


def mm(left, right):
    return product(left, right, ((1,), (0,)))


def mm_t(left, right):
    return product(left, right, ((1,), (1,)))


def t_mm(left, right):
    return product(left, right, ((0,), (0,)))


def block_scores(qkv_ref, seg_row_ref, seg_col_ref, start, reach):
    query = qkv_ref[pl.ds(start, QBLOCK), 0:HD]
    key = qkv_ref[pl.ds(0, reach), HD : 2 * HD]
    scores = mm_t(query, key) * HD ** (-0.5)
    query_pos = start + lax.broadcasted_iota(jnp.int32, (QBLOCK, reach), 0)
    key_pos = lax.broadcasted_iota(jnp.int32, (QBLOCK, reach), 1)
    same = seg_col_ref[pl.ds(start, QBLOCK), :] == seg_row_ref[:, pl.ds(0, reach)]
    return jnp.where(same & (query_pos >= key_pos), scores, masked_fill)


def attend_kernel(qkv_ref, seg_row_ref, seg_col_ref, mixed_ref, total_ref):
    for block in range(LENGTH // QBLOCK):
        start, reach = block * QBLOCK, (block + 1) * QBLOCK
        scores = block_scores(qkv_ref, seg_row_ref, seg_col_ref, start, reach)
        largest = jnp.max(scores, axis=-1, keepdims=True)
        exponent = jnp.exp(scores - largest)
        totals = jnp.sum(exponent, axis=-1, keepdims=True)
        probs_low = (exponent * (1.0 / totals)).astype(low)
        value = qkv_ref[pl.ds(0, reach), 2 * HD : 3 * HD]
        mixed_ref[pl.ds(start, QBLOCK), :] = mm(probs_low, value).astype(low)
        total_ref[pl.ds(start, QBLOCK), :] = largest + jnp.log(totals)


def attend_back_kernel(
    qkv_ref, grad_ref, total_ref, seg_row_ref, seg_col_ref, cos_ref, sin_ref, out_ref, key_acc, value_acc
):
    key_acc[...] = jnp.zeros_like(key_acc)
    value_acc[...] = jnp.zeros_like(value_acc)

    def turn_back(value, rows):
        return value * cos_ref[rows, :] + pltpu.roll(value, HD // 2, 1) * sin_ref[rows, :]

    for block in range(LENGTH // QBLOCK):
        start, reach = block * QBLOCK, (block + 1) * QBLOCK
        rows, span = pl.ds(start, QBLOCK), pl.ds(0, reach)
        scores = block_scores(qkv_ref, seg_row_ref, seg_col_ref, start, reach)
        probs = jnp.exp(scores - total_ref[rows, :])
        grad = grad_ref[rows, :]
        grad_probs = mm_t(grad, qkv_ref[span, 2 * HD : 3 * HD])
        inner = jnp.sum(probs * grad_probs, axis=-1, keepdims=True)
        grad_scores = (probs * (grad_probs - inner)).astype(low)
        scale = HD ** (-0.5)
        grad_query = mm(grad_scores, qkv_ref[span, HD : 2 * HD]) * scale
        out_ref[rows, 0:HD] = turn_back(grad_query, rows).astype(low)
        key_acc[span, :] += t_mm(grad_scores, qkv_ref[rows, 0:HD]) * scale
        value_acc[span, :] += t_mm(probs.astype(low), grad)
    for block in range(LENGTH // QBLOCK):
        rows = pl.ds(block * QBLOCK, QBLOCK)
        out_ref[rows, HD : 2 * HD] = turn_back(key_acc[rows, :], rows).astype(low)
        out_ref[rows, 2 * HD : 3 * HD] = value_acc[rows, :].astype(low)


vmem = pl.BlockSpec(memory_space=pltpu.VMEM)
smem = pl.BlockSpec(memory_space=pltpu.SMEM)
anywhere = pl.BlockSpec(memory_space=pl.ANY)
kernel_params = pltpu.CompilerParams(vmem_limit_bytes=48 * 1024 * 1024)


def attend(qkv, seg_row, seg_col):
    return pl.pallas_call(
        attend_kernel,
        out_shape=(
            jax.ShapeDtypeStruct((LENGTH, HD), low),
            jax.ShapeDtypeStruct((LENGTH, 1), wide),
        ),
        in_specs=[vmem] * 3,
        out_specs=(vmem, vmem),
        compiler_params=kernel_params,
        cost_estimate=pl.CostEstimate(
            flops=2 * LENGTH * LENGTH * HD, bytes_accessed=4 * LENGTH * HD * 2, transcendentals=LENGTH * LENGTH // 2
        ),
        name="attend",
    )(qkv, seg_row, seg_col)


def attend_back(qkv, grad, total, seg_row, seg_col, cos_all, sin_all):
    return pl.pallas_call(
        attend_back_kernel,
        out_shape=jax.ShapeDtypeStruct((LENGTH, 3 * HD), low),
        in_specs=[vmem] * 7,
        out_specs=vmem,
        scratch_shapes=[pltpu.VMEM((LENGTH, HD), wide), pltpu.VMEM((LENGTH, HD), wide)],
        compiler_params=kernel_params,
        cost_estimate=pl.CostEstimate(
            flops=5 * LENGTH * LENGTH * HD, bytes_accessed=8 * LENGTH * HD * 2, transcendentals=LENGTH * LENGTH // 2
        ),
        name="attend_back",
    )(qkv, grad, total, seg_row, seg_col, cos_all, sin_all)


ROWS = 256
FF_TILES = [(start, min(256, FF - start)) for start in range(0, FF, 256)]


def halves(value):
    upper = value.astype(low)
    return upper, (value - upper.astype(wide)).astype(low)


def silu_parts(gate_value):
    sig = 1.0 / (1.0 + jnp.exp(-gate_value))
    return sig, gate_value * sig


def swiglu_back(sig, act, up_value, grad):
    return (grad * up_value * (sig + act * (1.0 - sig))).astype(low), (grad * act).astype(low)


def ffn_kernel(
    expert_ref,
    normed_ref,
    cot_ref,
    slots_ref,
    slots_t_ref,
    routes_ref,
    router_ref,
    pack_ref,
    shared_down_ref,
    down_ref,
    grad_ref,
    gates_ref,
    hidden_s_ref,
    grad_gate_s_ref,
    grad_up_s_ref,
    incoming_ref,
    hidden_e_ref,
    gated_ref,
    grad_rows_ref,
    grad_gate_e_ref,
    grad_up_e_ref,
    w_gate_s,
    w_up_s,
    w_down_s,
    w_gate,
    w_up,
    w_down,
    gate_value,
    up_value,
    gate_parts,
    grad_in,
    sems,
):
    base = 3 * SH_OWN
    copies = [
        pltpu.make_async_copy(pack_ref.at[:, pl.ds(0, SH_OWN)], w_gate_s, sems.at[0]),
        pltpu.make_async_copy(pack_ref.at[:, pl.ds(SH_OWN, SH_OWN)], w_up_s, sems.at[1]),
        pltpu.make_async_copy(shared_down_ref, w_down_s, sems.at[2]),
        pltpu.make_async_copy(pack_ref.at[:, pl.ds(base, FF)], w_gate, sems.at[3]),
        pltpu.make_async_copy(pack_ref.at[:, pl.ds(base + FF, FF)], w_up, sems.at[4]),
        pltpu.make_async_copy(down_ref, w_down, sems.at[5]),
    ]
    for copy in copies:
        copy.start()
    expert = expert_ref[0]
    lane = lax.broadcasted_iota(jnp.int32, (ROWS, 128), 1)

    @pl.loop(0, ALL // ROWS)
    def route(step):
        rows = pl.ds(step * ROWS, ROWS)
        logits = mm(normed_ref[rows, :], router_ref[...])
        first, second = routes_ref[rows, 0:1], routes_ref[rows, 1:2]
        chosen_first = jnp.sum(jnp.where(lane == first, logits, 0.0), axis=1, keepdims=True)
        chosen_second = jnp.sum(jnp.where(lane == second, logits, 0.0), axis=1, keepdims=True)
        gate_first = 1.0 / (1.0 + jnp.exp(chosen_second - chosen_first))
        gate_second = 1.0 / (1.0 + jnp.exp(chosen_first - chosen_second))
        here = jnp.where(first == expert, gate_first, 0.0) + jnp.where(second == expert, gate_second, 0.0)
        upper, lower = halves(here)
        parts = jnp.where(lane == 0, upper.astype(wide), 0.0) + jnp.where(lane == 1, lower.astype(wide), 0.0)
        gate_parts[rows, :] = parts.astype(low)
        gates_ref[rows, :] = jnp.where(lane == 0, gate_first, 0.0) + jnp.where(lane == 1, gate_second, 0.0)

    @pl.loop(0, D // ROWS)
    def pick(step):
        columns = pl.ds(pl.multiple_of(step * ROWS, ROWS), ROWS)
        incoming_ref[:, columns] = mm(slots_ref[...], normed_ref[:, columns]).astype(low)
        grad_rows_ref[:, columns] = mm(slots_ref[...], cot_ref[:, columns]).astype(low)

    slot_parts = mm(slots_ref[...], gate_parts[...])
    slot_gate = slot_parts[:, 0:1] + slot_parts[:, 1:2]
    for copy in copies[:3]:
        copy.wait()

    @pl.loop(0, ALL // ROWS)
    def shared(step):
        rows = pl.ds(step * ROWS, ROWS)
        sig, act = silu_parts(mm(normed_ref[rows, :], w_gate_s[...]))
        up = mm(normed_ref[rows, :], w_up_s[...])
        hidden_s_ref[rows, :] = (act * up).astype(low)
        grad_hidden = mm_t(cot_ref[rows, :], w_down_s[...])
        grad_gate, grad_up = swiglu_back(sig, act, up, grad_hidden)
        grad_gate_s_ref[rows, :] = grad_gate
        grad_up_s_ref[rows, :] = grad_up

    for copy in copies[3:5]:
        copy.wait()
    for start, width in FF_TILES:
        columns = pl.ds(start, width)
        gate = mm(incoming_ref[...], w_gate[:, columns])
        up = mm(incoming_ref[...], w_up[:, columns])
        gate_value[:, columns] = gate
        up_value[:, columns] = up
        hidden_e_ref[:, columns] = (silu_parts(gate)[1] * up).astype(low)
    copies[5].wait()

    def forward(step, total):
        columns = pl.ds(pl.multiple_of(step * ROWS, ROWS), ROWS)
        rows = mm(hidden_e_ref[...], w_down[:, columns]).astype(low).astype(wide)
        cot = grad_rows_ref[:, columns].astype(wide)
        gated_ref[:, columns] = (rows * slot_gate).astype(low)
        grad_rows_ref[:, columns] = (cot * slot_gate).astype(low)
        return total + jnp.sum(rows * cot, axis=1, keepdims=True)

    slot_grad = lax.fori_loop(0, D // ROWS, forward, jnp.zeros((SLOTS, 1), wide))
    for start, width in FF_TILES:
        columns = pl.ds(start, width)
        grad_hidden = mm_t(grad_rows_ref[...], w_down[pl.ds(start, width), :])
        sig, act = silu_parts(gate_value[:, columns])
        grad_gate, grad_up = swiglu_back(sig, act, up_value[:, columns], grad_hidden)
        grad_gate_e_ref[:, columns] = grad_gate
        grad_up_e_ref[:, columns] = grad_up

    @pl.loop(0, D // ROWS)
    def back(step):
        columns = pl.ds(pl.multiple_of(step * ROWS, ROWS), ROWS)
        grad_in[:, columns] = (
            mm_t(grad_gate_e_ref[...], w_gate[columns, :]) + mm_t(grad_up_e_ref[...], w_up[columns, :])
        ).astype(low)

    upper, lower = halves(slot_grad)
    slot_lane = lax.broadcasted_iota(jnp.int32, (SLOTS, 128), 1)
    slot_parts = (
        jnp.where(slot_lane == expert, upper.astype(wide), 0.0)
        + jnp.where(slot_lane == expert + 8, lower.astype(wide), 0.0)
    ).astype(low)

    @pl.loop(0, ALL // ROWS)
    def total(step):
        rows = pl.ds(step * ROWS, ROWS)
        for tile in range(D // 512):
            columns = pl.ds(tile * 512, 512)
            grad_ref[rows, columns] = (
                mm_t(grad_gate_s_ref[rows, :], w_gate_s[columns, :])
                + mm_t(grad_up_s_ref[rows, :], w_up_s[columns, :])
                + mm(slots_t_ref[rows, :], grad_in[:, columns])
            ).astype(low)
        grad_ref[rows, D : D + 128] = mm(slots_t_ref[rows, :], slot_parts).astype(low)


def ffn(expert, normed, cot, slots, slots_t, routes, router, pack, shared_down, down):
    shapes = [
        ((ALL, D + 128), low),
        ((ALL, 128), wide),
        ((ALL, SH_OWN), low),
        ((ALL, SH_OWN), low),
        ((ALL, SH_OWN), low),
        ((SLOTS, D), low),
        ((SLOTS, FF), low),
        ((SLOTS, D), low),
        ((SLOTS, D), low),
        ((SLOTS, FF), low),
        ((SLOTS, FF), low),
    ]
    return pl.pallas_call(
        ffn_kernel,
        out_shape=tuple(jax.ShapeDtypeStruct(shape, kind) for shape, kind in shapes),
        in_specs=[smem] + [vmem] * 6 + [anywhere] * 3,
        out_specs=tuple([vmem] * len(shapes)),
        scratch_shapes=[
            pltpu.VMEM((D, SH_OWN), low),
            pltpu.VMEM((D, SH_OWN), low),
            pltpu.VMEM((SH_OWN, D), low),
            pltpu.VMEM((D, FF), low),
            pltpu.VMEM((D, FF), low),
            pltpu.VMEM((FF, D), low),
            pltpu.VMEM((SLOTS, FF), wide),
            pltpu.VMEM((SLOTS, FF), wide),
            pltpu.VMEM((ALL, 128), low),
            pltpu.VMEM((SLOTS, D), low),
            pltpu.SemaphoreType.DMA((6,)),
        ],
        compiler_params=pltpu.CompilerParams(vmem_limit_bytes=60 * 1024 * 1024),
        cost_estimate=pl.CostEstimate(flops=27 * 10**9, bytes_accessed=50 * 10**6, transcendentals=10**6),
        name="ffn",
    )(expert, normed, cot, slots, slots_t, routes, router, pack, shared_down, down)


def pack_rows(block):
    count, width = block.shape[0] // 8, block.shape[1] // 128
    return jnp.concatenate(
        [
            jnp.concatenate(
                [block[8 * i : 8 * i + 8, 128 * j : 128 * j + 128] for i in range(count)], axis=1
            )
            for j in range(width)
        ],
        axis=0,
    )


def ffn_weights_kernel(
    normed_ref,
    cot_ref,
    hidden_s_ref,
    grad_gate_s_ref,
    grad_up_s_ref,
    incoming_ref,
    hidden_e_ref,
    grad_rows_ref,
    grad_gate_e_ref,
    grad_up_e_ref,
    out_ref,
    down_s,
    down_e,
):
    step = pl.program_id(0)
    base = 3 * SH_OWN
    columns = pl.ds(pl.multiple_of(step * ROWS, ROWS), ROWS)

    @pl.when(step == 0)
    def _():
        @pl.loop(0, D // ROWS)
        def down(tile):
            part = pl.ds(pl.multiple_of(tile * ROWS, ROWS), ROWS)
            down_s[:, part] = t_mm(hidden_s_ref[...], cot_ref[:, part])
            down_e[:, part] = t_mm(hidden_e_ref[...], grad_rows_ref[:, part])

    normed = normed_ref[:, columns]
    out_ref[:, 0:SH_OWN] = t_mm(normed, grad_gate_s_ref[...]).astype(low)
    out_ref[:, SH_OWN : 2 * SH_OWN] = t_mm(normed, grad_up_s_ref[...]).astype(low)
    incoming = incoming_ref[:, columns]
    out_ref[:, base : base + FF] = t_mm(incoming, grad_gate_e_ref[...]).astype(low)
    out_ref[:, base + FF : base + 2 * FF] = t_mm(incoming, grad_up_e_ref[...]).astype(low)
    for part in range(ROWS // 128):
        place = step * (ROWS // 128) + part
        rows = slice(part * 128, part * 128 + 128)
        shared = down_s[pl.ds(pl.multiple_of(place * (SH_OWN // FSDP), 8), SH_OWN // FSDP), :]
        out_ref[rows, 2 * SH_OWN : base] = pack_rows(shared).astype(low)
        routed = down_e[pl.ds(pl.multiple_of(place * (FF // FSDP), 8), FF // FSDP), :]
        out_ref[rows, base + 2 * FF : base + 3 * FF] = pack_rows(routed).astype(low)


def ffn_weights(*operands):
    width = 3 * SH_OWN + 3 * FF
    return pl.pallas_call(
        ffn_weights_kernel,
        grid=(D // ROWS,),
        out_shape=jax.ShapeDtypeStruct((D, width), low),
        in_specs=[vmem] * 10,
        out_specs=pl.BlockSpec((ROWS, width), lambda step: (step, 0)),
        scratch_shapes=[pltpu.VMEM((SH_OWN, D), wide), pltpu.VMEM((FF, D), wide)],
        compiler_params=pltpu.CompilerParams(vmem_limit_bytes=56 * 1024 * 1024),
        cost_estimate=pl.CostEstimate(flops=11 * 10**9, bytes_accessed=40 * 10**6, transcendentals=0),
        name="ffn_weights",
    )(*operands)


def norm_factor(values):
    return lax.rsqrt(jnp.mean(values * values, axis=-1, keepdims=True) + eps_norm)


def norm_back(values, factor, gain, grad):
    scaled = grad * gain
    inner = jnp.mean(scaled * values, axis=-1, keepdims=True)
    return factor * scaled - values * (factor * factor * factor * inner)


def per_device(
    hidden_in,
    cotangent,
    segments,
    routes,
    attn_gain,
    w_query,
    w_key,
    w_value,
    w_out,
    ffn_gain,
    w_router,
    shared_gate,
    shared_up,
    shared_down,
    expert_gate,
    expert_up,
    expert_down,
):
    expert = lax.axis_index("expert")
    z, core = expert // 2, expert % 2
    place = lax.axis_index("fsdp")

    misc = jnp.concatenate(
        [attn_gain[:, None], ffn_gain[:, None], w_router, jnp.zeros((TOK, 118), low)], axis=1
    )
    attn_pack = jnp.concatenate(
        [
            lax.dynamic_slice_in_dim(w_query, 256 * expert, 256, 1),
            lax.dynamic_slice_in_dim(w_key, HD * z, HD, 1),
            lax.dynamic_slice_in_dim(w_value, HD * z, HD, 1),
            lax.dynamic_slice_in_dim(w_out, 256 * expert, 256, 1),
            misc,
        ],
        axis=1,
    )
    attn_all = lax.all_gather(attn_pack, "fsdp", axis=0, tiled=True)
    half_in, half_out = SH // 2, SH_OWN // 2
    sel_column = jnp.arange(half_out)
    picked = SH_ROWS * (sel_column // SH_PAD) + SH_PART * expert + sel_column % SH_PAD
    picked = jnp.where(sel_column % SH_PAD < SH_PART, picked, -1)
    select = (jnp.arange(half_in)[:, None] == picked[None, :]).astype(low)
    own_shared = mm(
        jnp.concatenate(
            [shared_gate[:, :half_in], shared_gate[:, half_in:], shared_up[:, :half_in], shared_up[:, half_in:]],
            axis=0,
        ),
        select,
    ).astype(low)
    own_down = jnp.pad(
        lax.dynamic_slice_in_dim(shared_down, SH_PART * expert, SH_PART, 0),
        ((0, SH_PAD - SH_PART), (0, 0)),
    )
    ffn_pack = jnp.concatenate(
        [
            own_shared[:TOK],
            own_shared[TOK : 2 * TOK],
            own_shared[2 * TOK : 3 * TOK],
            own_shared[3 * TOK :],
            pack_tiles(own_down),
            expert_gate[:, 0],
            expert_up[:, 0],
            pack_tiles(expert_down[:, 0]),
        ],
        axis=1,
    )
    ffn_all = lax.all_gather(ffn_pack, "fsdp", axis=0, tiled=True)

    ids = jnp.concatenate(
        [
            segments.astype(low),
            jnp.pad(routes[0].reshape(1, TOK * TOPK), ((0, 0), (0, LENGTH - TOK * TOPK))).astype(low),
            jnp.zeros((14, LENGTH), low),
        ],
        axis=0,
    )
    rows_in = gather_rows(jnp.concatenate([hidden_in[0], ids], axis=0))
    hidden = rows_in[:, :TOK].reshape(ALL, D)
    segment_all = rows_in[:, TOK].astype(jnp.int32)
    route_all = rows_in[:, TOK + 1, : TOK * TOPK].astype(jnp.int32).reshape(ALL, TOPK)
    cot_all = gather_rows(cotangent[0]).reshape(ALL, D)

    gain_one = attn_all[:, 768].astype(wide)
    gain_two = attn_all[:, 769].astype(wide)
    router = attn_all[:, 770:778]
    hidden_wide = hidden.astype(wide)
    factor_one = norm_factor(hidden_wide)
    normed_one = (hidden_wide * factor_one * gain_one).astype(low)
    qkv_raw = mm(normed_one, attn_all[:, :512]).reshape(SEQS, TOK, 4, HD)
    inverse_freq = rope_base ** (-jnp.arange(HD // 2, dtype=wide) * 2.0 / HD)
    angles = jnp.arange(LENGTH).astype(wide)[:, None] * inverse_freq[None, :]
    cosine, sine = jnp.cos(angles), jnp.sin(angles)
    cos_all = jnp.concatenate([cosine, cosine], axis=1)
    sin_back = jnp.concatenate([sine, -sine], axis=1)
    cos_own = lax.dynamic_slice_in_dim(cosine, place * TOK, TOK, 0)[:, None, :]
    sin_own = lax.dynamic_slice_in_dim(sine, place * TOK, TOK, 0)[:, None, :]
    first, second = qkv_raw[:, :, :3, : HD // 2], qkv_raw[:, :, :3, HD // 2 :]
    turned = jnp.concatenate(
        [first * cos_own - second * sin_own, second * cos_own + first * sin_own], axis=-1
    ).astype(low)
    key_value = jnp.concatenate([turned[:, :, 2], qkv_raw[:, :, 3].astype(low)], axis=-1)
    sent = jnp.stack(
        [
            jnp.concatenate([turned[:, :, 0], key_value], axis=-1),
            jnp.concatenate([turned[:, :, 1], key_value], axis=-1),
        ],
        axis=1,
    ).reshape(LENGTH, 3 * HD)
    qkv = lax.all_to_all(sent, "fsdp", split_axis=0, concat_axis=0, tiled=True)
    seg_row = lax.dynamic_slice_in_dim(segment_all, place // 2, 1, 0)
    seg_col = seg_row.reshape(LENGTH, 1)
    mixed_head, log_total = attend(qkv, seg_row, seg_col)
    mixed = (
        lax.all_to_all(mixed_head, "fsdp", split_axis=0, concat_axis=0, tiled=True)
        .reshape(SEQS, 2, TOK, HD)
        .transpose(0, 2, 1, 3)
        .reshape(ALL, 2 * HD)
    )
    out_columns = attn_all[:, 512:768].reshape(EXPERTS, 256, 256)
    owners = [relative_owner(expert, block) for block in range(EXPERTS)]
    w_out_own = exchange(
        jnp.stack([lax.dynamic_index_in_dim(out_columns, owner, 0, keepdims=False) for owner in owners]), expert
    )
    w_out_own = w_out_own.transpose(1, 0, 2).reshape(256, D)
    own_hidden = hidden_in[0].astype(wide)
    middle = own_hidden + scatter_rows(mm(mixed, w_out_own).astype(low).reshape(SEQS, TOK, D))
    factor_two = norm_factor(middle)
    normed_two = gather_rows((middle * factor_two * gain_two).astype(low)).reshape(ALL, D)

    hit = jnp.any(route_all == expert, axis=1).astype(wide)
    order = jnp.arange(ALL)
    rank = mm(hit.astype(low)[None, :], (order[:, None] < order[None, :]).astype(low))
    slot_bool = (rank.astype(jnp.int32) == jnp.arange(SLOTS)[:, None]) & (hit > 0.5)[None, :]
    slots = slot_bool.astype(low)
    slots_t = slot_bool.T.astype(low)

    base = 3 * SH_OWN
    shared_down_w = unpack_tiles(ffn_all[:, 2 * SH_OWN : base], FSDP)
    down_w = unpack_tiles(ffn_all[:, base + 2 * FF :], FSDP)
    (
        grad_normed,
        gates,
        hidden_shared,
        grad_gate_shared,
        grad_up_shared,
        incoming,
        hidden_expert,
        gated_rows,
        grad_rows,
        grad_gate_expert,
        grad_up_expert,
    ) = ffn(
        expert[None],
        normed_two,
        cot_all,
        slots,
        slots_t,
        route_all,
        jnp.pad(router, ((0, 0), (0, 120))),
        ffn_all,
        shared_down_w,
        down_w,
    )
    own_grad = scatter_rows(grad_normed.reshape(SEQS, TOK, D + 128))
    ffn_grads = ffn_weights(
        normed_two,
        cot_all,
        hidden_shared,
        grad_gate_shared,
        grad_up_shared,
        incoming,
        hidden_expert,
        grad_rows,
        grad_gate_expert,
        grad_up_expert,
    )
    route_grads = own_grad[:, D : D + 8] + own_grad[:, D + 8 : D + 16]
    own_hot = (route_all[:TOK, :, None] == jnp.arange(EXPERTS)[None, None, :]).astype(wide)
    own_gates = gates[:TOK, :TOPK]
    grad_gates = jnp.sum(own_hot * route_grads[:, None, :], axis=-1)
    grad_chosen = own_gates * (grad_gates - jnp.sum(own_gates * grad_gates, axis=-1, keepdims=True))
    grad_logits = jnp.sum(own_hot * grad_chosen[:, :, None], axis=1)
    grad_two = own_grad[:, :D] + product_wide(grad_logits, router)
    grad_gain_two = jnp.sum(grad_two * middle * factor_two, axis=0)
    cot_own = cotangent[0].astype(wide)
    grad_middle = cot_own + norm_back(middle, factor_two, gain_two, grad_two)
    gain_rows = jnp.stack(halves(grad_gain_two))
    logit_upper, logit_lower = halves(grad_logits.T.reshape(1, TOK * EXPERTS))
    back_rows = gather_rows(
        jnp.concatenate(
            [
                grad_middle.astype(low),
                gain_rows,
                jnp.concatenate([logit_upper, logit_lower], axis=1),
                jnp.zeros((13, D), low),
            ],
            axis=0,
        )
    )
    back_rows, ffn_grads = lax.optimization_barrier((back_rows, ffn_grads))
    ffn_sums = lax.psum_scatter(ffn_grads, "fsdp", scatter_dimension=0, tiled=True)
    grad_expert_gate = ffn_sums[:, base : base + FF].astype(wide)[:, None]
    grad_expert_up = ffn_sums[:, base + FF : base + 2 * FF].astype(wide)[:, None]
    grad_expert_down = unpack_tiles(ffn_sums[:, base + 2 * FF :], 1).astype(wide)[:, None]

    grad_attn = back_rows[:, :TOK].reshape(ALL, D)
    gain_two_sum = jnp.sum(back_rows[:, TOK : TOK + 2].astype(wide), axis=(0, 1))
    logit_parts = back_rows[:, TOK + 2].reshape(SEQS, 2, EXPERTS, TOK)

    hidden_shared, gated_rows, _ = lax.optimization_barrier((hidden_shared, gated_rows, back_rows))
    result = mm(hidden_shared, shared_down_w) + t_mm(slots, gated_rows)
    own_result = scatter_rows(result.astype(low).reshape(SEQS, TOK, D))
    layer_out = (middle + own_result).astype(low)

    grad_mixed = mm_t(grad_attn, w_out_own).astype(low)
    sent_back = grad_mixed.reshape(SEQS, TOK, 2, HD).transpose(0, 2, 1, 3).reshape(LENGTH, HD)
    grad_head = lax.all_to_all(sent_back, "fsdp", split_axis=0, concat_axis=0, tiled=True)
    grads_head = attend_back(qkv, grad_head, log_total, seg_row, seg_col, cos_all, sin_back)
    grads_qkv = lax.all_to_all(grads_head, "fsdp", split_axis=0, concat_axis=0, tiled=True)

    grad_out = t_mm(mixed, grad_attn).astype(low).reshape(256, EXPERTS, 256).transpose(1, 0, 2)
    grad_out = exchange(
        jnp.stack([lax.dynamic_index_in_dim(grad_out, owner, 0, keepdims=False) for owner in owners]), expert
    ).reshape(FSDP, TOK, 256)
    logit_rows = logit_parts.transpose(1, 2, 0, 3).reshape(2 * EXPERTS, ALL)
    grad_router = mm(logit_rows, normed_two)
    small_rows = jnp.concatenate(
        [grad_router[:EXPERTS] + grad_router[EXPERTS:], gain_two_sum[None], jnp.zeros((7, D), wide)], axis=0
    )
    small_rows = jnp.pad(small_rows.reshape(16, FSDP, TOK).transpose(1, 0, 2).astype(low), ((0, 0), (0, 0), (0, 128)))
    out_pack = jnp.concatenate([grad_out, small_rows], axis=1).reshape(FSDP * (TOK + 16), 256)
    out_pack, grads_qkv = lax.optimization_barrier((out_pack, grads_qkv))
    out_sums = sum_blocks(out_pack, TOK + 16)

    grads_qkv = grads_qkv.reshape(SEQS, 2, TOK, 3 * HD)
    grad_query = grads_qkv[..., :HD].transpose(0, 2, 1, 3).reshape(ALL, 2 * HD)
    grad_kv = jnp.sum(grads_qkv[..., HD:].astype(wide), axis=1).reshape(ALL, 2, 2, HD // 2)
    is_first = core == 0
    kv_mine = jnp.where(is_first, grad_kv[:, :, 0], grad_kv[:, :, 1]).reshape(ALL, HD)
    kv_other = jnp.where(is_first, grad_kv[:, :, 1], grad_kv[:, :, 0]).reshape(ALL, HD).astype(low)
    kv_other = jnp.concatenate([kv_other[ALL // 2 :], kv_other[: ALL // 2]], axis=0)
    grad_kv_own = (kv_mine + swap_core(kv_other).astype(wide)).astype(low)
    grad_qkv = jnp.concatenate([grad_query, grad_kv_own], axis=1)
    qkv_grads = t_mm(normed_one, grad_qkv).astype(low)
    qkv_sums = sum_blocks(qkv_grads, TOK)

    kv_weight = attn_all[:, 256:512].reshape(D, 2, 2, HD // 2)
    kv_weight = jnp.where(is_first, kv_weight[:, :, 0], kv_weight[:, :, 1]).reshape(D, HD)
    qkv_weight = jnp.concatenate([attn_all[:, :256], kv_weight], axis=1)
    qkv_grads, grad_qkv = lax.optimization_barrier((qkv_grads, grad_qkv))
    grad_normed_one = mm_t(grad_qkv, qkv_weight)
    own_grad_one = scatter_rows(grad_normed_one.astype(low).reshape(SEQS, TOK, D))
    grad_input = grad_middle + norm_back(own_hidden, factor_one[:TOK], gain_one, own_grad_one)

    shared_shards = lax.all_gather(
        jnp.concatenate([ffn_sums[:, :base], out_sums[:TOK].astype(low)], axis=1), "expert", axis=0
    )
    half_rows = SH_PAD * EXPERTS * FSDP // 2
    put_row = jnp.arange(half_rows)
    source, within = put_row // half_out, put_row % half_out
    target = SH_ROWS * (within // SH_PAD) + SH_PART * source + within % SH_PAD
    target = jnp.where(within % SH_PAD < SH_PART, target, -1)
    spread = (target[:, None] == jnp.arange(half_in)[None, :]).astype(low)

    def dense_columns(part):
        return part.transpose(1, 0, 2).reshape(TOK, -1)

    gate_up = shared_shards[:, :, : 2 * SH_OWN].reshape(EXPERTS, TOK, 4, half_out)
    gate_up = mm(gate_up.transpose(2, 1, 0, 3).reshape(4 * TOK, EXPERTS * half_out), spread)
    grad_shared_gate = jnp.concatenate([gate_up[:TOK], gate_up[TOK : 2 * TOK]], axis=1)
    grad_shared_up = jnp.concatenate([gate_up[2 * TOK : 3 * TOK], gate_up[3 * TOK :]], axis=1)
    down_parts = unpack_tiles(shared_shards[:, :, 2 * SH_OWN : base].reshape(EXPERTS * TOK, SH_OWN), EXPERTS)
    grad_shared_down = (
        down_parts.reshape(EXPERTS, SH_PAD, D)[:, :SH_PART].reshape(SH_ROWS, D).astype(wide)
    )
    grad_w_out = dense_columns(shared_shards[:, :, base:].astype(wide))

    own_weight = lax.dynamic_slice_in_dim(qkv_weight, place * TOK, TOK, 0)
    gain_part = jnp.sum(qkv_sums * own_weight.astype(wide), axis=1, keepdims=True)
    gain_upper, gain_lower = halves(gain_part / attn_gain.astype(wide)[:, None])
    qkv_shards = lax.all_gather(
        jnp.concatenate([qkv_sums.astype(low), gain_upper, gain_lower, jnp.zeros((TOK, 126), low)], axis=1),
        "expert",
        axis=0,
    ).astype(wide)
    return (
        layer_out[None],
        grad_input.astype(low)[None],
        jnp.sum(qkv_shards[:, :, 384:386], axis=(0, 2)),
        dense_columns(qkv_shards[:, :, :256]),
        dense_columns(qkv_shards[:, :, 256:320]),
        dense_columns(qkv_shards[:, :, 320:384]),
        grad_w_out,
        out_sums[TOK + EXPERTS, :TOK],
        out_sums[TOK : TOK + EXPERTS, :TOK].T,
        grad_shared_gate,
        grad_shared_up,
        grad_shared_down,
        grad_expert_gate,
        grad_expert_up,
        grad_expert_down,
    )


def sum_blocks(block, rows):
    parts = lax.all_to_all(block, "fsdp", split_axis=0, concat_axis=0, tiled=True)
    return jnp.sum(parts.reshape(FSDP, rows, block.shape[1]).astype(wide), axis=0)


def product_wide(left, router):
    return lax.dot_general(
        left, router.astype(wide), (((1,), (1,)), ((), ())), precision=highest, preferred_element_type=wide
    )


def solution(mesh):
    in_specs = (
        P("expert", "fsdp", None),
        P("expert", "fsdp", None),
        P("expert", None),
        P("expert", "fsdp", None),
        P("fsdp"),
        P("fsdp", None),
        P("fsdp", None),
        P("fsdp", None),
        P("fsdp", None),
        P("fsdp"),
        P("fsdp", None),
        P("fsdp", None),
        P("fsdp", None),
        P("fsdp", None),
        P("fsdp", "expert", None),
        P("fsdp", "expert", None),
        P("fsdp", "expert", None),
    )
    out_specs = (
        P("expert", "fsdp", None),
        P("expert", "fsdp", None),
        P("fsdp"),
        P("fsdp", None),
        P("fsdp", None),
        P("fsdp", None),
        P("fsdp", None),
        P("fsdp"),
        P("fsdp", None),
        P("fsdp", None),
        P("fsdp", None),
        P("fsdp", None),
        P("fsdp", "expert", None),
        P("fsdp", "expert", None),
        P("fsdp", "expert", None),
    )
    return jax.shard_map(
        per_device, mesh=mesh, in_specs=in_specs, out_specs=out_specs, check_vma=False
    )
```

```python
import jax
import jax.numpy as jnp
from jax import lax
from jax.experimental import pallas as pl
from jax.experimental.pallas import tpu as pltpu
from jax.sharding import PartitionSpec as P

D = 2048
H = 16
KV = 4
HD = 128
FF = 1408
SH = 2816
TOPK = 2
TOK = 128
LENGTH = 2048
SEQS = 8
EXPERTS = 8
FSDP = 16
ALL = SEQS * TOK
CAP = 42
SLOTS = SEQS * CAP
SH_ROWS = SH // FSDP
SH_PART = SH_ROWS // EXPERTS
SH_PAD = 24
SH_OWN = FSDP * SH_PAD
QBLOCK = 256

eps_norm = 1e-06
rope_base = 600000.0
masked_fill = -1e30
highest = lax.Precision.HIGHEST
low = jnp.bfloat16
wide = jnp.float32


def shift_pairs(step):
    return [(z * 2 + c, ((z + step) % 4) * 2 + c) for z in range(4) for c in range(2)]


core_pairs = [(z * 2 + c, z * 2 + 1 - c) for z in range(4) for c in range(2)]


def move_z(block, step):
    return lax.ppermute(block, "expert", shift_pairs(step))


def swap_core(block):
    return lax.ppermute(block, "expert", core_pairs)


def together(*values):
    return lax.optimization_barrier(values)


TOP = TOK // 2


def first_pieces(block):
    return move_z(block, 1), move_z(block, -1)


def other_pieces(block, below, above):
    upper, lower = move_z(below[:TOP], 1), move_z(above[TOP:], -1)
    mine = [block, above, upper, lower, below]
    return mine + [swap_core(piece) for piece in mine]


def gather_pieces(block):
    return other_pieces(block, *first_pieces(block))


PIECES = [(4 * side + block, start) for side in (0, 1) for block, start in ((0, 0), (1, 0), (2, 0), (2, TOP), (3, 0))]


def place_pieces(pieces):
    whole = [pieces[0], pieces[1], jnp.concatenate(pieces[2:4], axis=0), pieces[4]]
    whole += [pieces[5], pieces[6], jnp.concatenate(pieces[7:9], axis=0), pieces[9]]
    return jnp.concatenate(whole, axis=0)


def load_pieces(refs, rows_ref, extra_ref, sems):
    copies = []
    for index, (ref, (block, start)) in enumerate(zip(refs, PIECES)):
        count = min(ref.shape[0], TOK - start)
        copies.append(
            pltpu.make_async_copy(
                ref.at[pl.ds(0, count), :], rows_ref.at[pl.ds(block * TOK + start, count), :], sems.at[2 * index]
            )
        )
        if extra_ref is not None and ref.shape[0] > count:
            copies.append(
                pltpu.make_async_copy(
                    ref.at[pl.ds(count, 16), :], extra_ref.at[pl.ds(block * 16, 16), :], sems.at[2 * index + 1]
                )
            )
    for copy in copies:
        copy.start()
    return copies


def scatter_start(mine, received):
    chip = mine.reshape(4, TOK, -1).astype(wide) + received.reshape(4, TOK, -1).astype(wide)
    from_below = move_z(chip[2, :TOP].astype(low), 1)
    from_above = move_z(chip[2, TOP:].astype(low), -1)
    to_above = jnp.concatenate([chip[1, :TOP] + from_below.astype(wide), chip[1, TOP:]], axis=0)
    to_below = jnp.concatenate([chip[3, :TOP], chip[3, TOP:] + from_above.astype(wide)], axis=0)
    return chip[0], to_above.astype(low), to_below.astype(low)


def scatter_end(own, first, second):
    return own + first.astype(wide) + second.astype(wide)


def scatter_rows(mine, other):
    own, to_above, to_below = scatter_start(mine, swap_core(other))
    return scatter_end(own, move_z(to_above, 1), move_z(to_below, -1))


def exchange(blocks, expert):
    chip = jnp.stack([blocks[:4], swap_core(blocks[4:])], axis=1)
    got = jnp.stack([chip[0]] + [move_z(chip[step], step) for step in (1, 2, 3)])
    got = got.reshape((EXPERTS,) + blocks.shape[1:])
    z, core = expert // 2, expert % 2
    parts = []
    for source in range(EXPERTS):
        place = ((z - source // 2) % 4) * 2 + (core ^ (source % 2))
        parts.append(lax.dynamic_index_in_dim(got, place, 0, keepdims=False))
    return jnp.stack(parts)


def relative_owner(expert, block):
    return ((expert // 2 + block % 4) % 4) * 2 + ((expert % 2) ^ (block // 4))


def pack_tiles(block):
    rows, columns = block.shape[0] // 8, block.shape[1] // 128
    tiles = block.reshape(rows, 8, columns, 128).transpose(2, 1, 0, 3)
    return tiles.reshape(columns * 8, rows * 128)


def unpack_tiles(block, count):
    rows, columns = block.shape[1] // 128, block.shape[0] // (8 * count)
    tiles = block.reshape(count, columns, 8, rows, 128).transpose(0, 3, 2, 1, 4)
    return tiles.reshape(count * rows * 8, columns * 128)


def product(left, right, contract):
    return lax.dot_general(left, right, (contract, ((), ())), preferred_element_type=wide)


def mm(left, right):
    return product(left, right, ((1,), (0,)))


def mm_t(left, right):
    return product(left, right, ((1,), (1,)))


def t_mm(left, right):
    return product(left, right, ((0,), (0,)))


def block_scores(qkv_ref, seg_row_ref, seg_col_ref, start, reach):
    query = qkv_ref[pl.ds(start, QBLOCK), 0:HD]
    key = qkv_ref[pl.ds(0, reach), HD : 2 * HD]
    scores = mm_t(query, key) * HD ** (-0.5)
    query_pos = start + lax.broadcasted_iota(jnp.int32, (QBLOCK, reach), 0)
    key_pos = lax.broadcasted_iota(jnp.int32, (QBLOCK, reach), 1)
    same = seg_col_ref[pl.ds(start, QBLOCK), :] == seg_row_ref[:, pl.ds(0, reach)]
    return jnp.where(same & (query_pos >= key_pos), scores, masked_fill)


def attend_kernel(qkv_ref, seg_row_ref, seg_col_ref, mixed_ref, total_ref):
    for block in range(LENGTH // QBLOCK):
        start, reach = block * QBLOCK, (block + 1) * QBLOCK
        scores = block_scores(qkv_ref, seg_row_ref, seg_col_ref, start, reach)
        largest = jnp.max(scores, axis=-1, keepdims=True)
        exponent = jnp.exp(scores - largest)
        totals = jnp.sum(exponent, axis=-1, keepdims=True)
        probs_low = (exponent * (1.0 / totals)).astype(low)
        value = qkv_ref[pl.ds(0, reach), 2 * HD : 3 * HD]
        mixed_ref[pl.ds(start, QBLOCK), :] = mm(probs_low, value).astype(low)
        total_ref[pl.ds(start, QBLOCK), :] = largest + jnp.log(totals)


def attend_back_kernel(
    qkv_ref, grad_ref, total_ref, seg_row_ref, seg_col_ref, cos_ref, sin_ref, out_ref, key_acc, value_acc
):
    key_acc[...] = jnp.zeros_like(key_acc)
    value_acc[...] = jnp.zeros_like(value_acc)

    def turn_back(value, rows):
        return value * cos_ref[rows, :] + pltpu.roll(value, HD // 2, 1) * sin_ref[rows, :]

    for block in range(LENGTH // QBLOCK):
        start, reach = block * QBLOCK, (block + 1) * QBLOCK
        rows, span = pl.ds(start, QBLOCK), pl.ds(0, reach)
        scores = block_scores(qkv_ref, seg_row_ref, seg_col_ref, start, reach)
        probs = jnp.exp(scores - total_ref[rows, :])
        grad = grad_ref[rows, :]
        grad_probs = mm_t(grad, qkv_ref[span, 2 * HD : 3 * HD])
        inner = jnp.sum(probs * grad_probs, axis=-1, keepdims=True)
        grad_scores = (probs * (grad_probs - inner)).astype(low)
        scale = HD ** (-0.5)
        grad_query = mm(grad_scores, qkv_ref[span, HD : 2 * HD]) * scale
        out_ref[rows, 0:HD] = turn_back(grad_query, rows).astype(low)
        key_acc[span, :] += t_mm(grad_scores, qkv_ref[rows, 0:HD]) * scale
        value_acc[span, :] += t_mm(probs.astype(low), grad)
    for block in range(LENGTH // QBLOCK):
        rows = pl.ds(block * QBLOCK, QBLOCK)
        out_ref[rows, HD : 2 * HD] = turn_back(key_acc[rows, :], rows).astype(low)
        out_ref[rows, 2 * HD : 3 * HD] = value_acc[rows, :].astype(low)


vmem = pl.BlockSpec(memory_space=pltpu.VMEM)
smem = pl.BlockSpec(memory_space=pltpu.SMEM)
anywhere = pl.BlockSpec(memory_space=pl.ANY)
kernel_params = pltpu.CompilerParams(vmem_limit_bytes=48 * 1024 * 1024)


def attend(qkv, seg_row, seg_col):
    return pl.pallas_call(
        attend_kernel,
        out_shape=(
            jax.ShapeDtypeStruct((LENGTH, HD), low),
            jax.ShapeDtypeStruct((LENGTH, 1), wide),
        ),
        in_specs=[vmem] * 3,
        out_specs=(vmem, vmem),
        compiler_params=kernel_params,
        cost_estimate=pl.CostEstimate(
            flops=2 * LENGTH * LENGTH * HD, bytes_accessed=4 * LENGTH * HD * 2, transcendentals=LENGTH * LENGTH // 2
        ),
        name="attend",
    )(qkv, seg_row, seg_col)


def attend_back(qkv, grad, total, seg_row, seg_col, cos_all, sin_all):
    return pl.pallas_call(
        attend_back_kernel,
        out_shape=jax.ShapeDtypeStruct((LENGTH, 3 * HD), low),
        in_specs=[vmem] * 7,
        out_specs=vmem,
        scratch_shapes=[pltpu.VMEM((LENGTH, HD), wide), pltpu.VMEM((LENGTH, HD), wide)],
        compiler_params=kernel_params,
        cost_estimate=pl.CostEstimate(
            flops=5 * LENGTH * LENGTH * HD, bytes_accessed=8 * LENGTH * HD * 2, transcendentals=LENGTH * LENGTH // 2
        ),
        name="attend_back",
    )(qkv, grad, total, seg_row, seg_col, cos_all, sin_all)


ROWS = 256
FF_TILES = [(start, min(256, FF - start)) for start in range(0, FF, 256)]
PACK = 3 * SH_OWN + 3 * FF


def params(mebibytes):
    return pltpu.CompilerParams(vmem_limit_bytes=mebibytes * 1024 * 1024)


def cost(flops, moved, special=0):
    return pl.CostEstimate(flops=int(flops), bytes_accessed=int(moved), transcendentals=int(special))


def project_kernel(*refs):
    pieces, (attn_ref, cos_ref, sin_ref) = refs[:10], refs[10:13]
    normed_ref, sent_ref, factor_ref, gains_ref, ids_ref, hidden, sems = refs[13:]
    copies = load_pieces(pieces, hidden, ids_ref, sems)
    pick = lax.broadcasted_iota(jnp.int32, (16, TOK), 0) == lax.broadcasted_iota(jnp.int32, (16, TOK), 1)
    gains_ref[...] = mm_t(pick.astype(wide).astype(low), attn_ref[:, 768:896])
    for copy in copies:
        copy.wait()
    gain = gains_ref[0:1, :]

    @pl.loop(0, ALL // ROWS)
    def step(index):
        rows = pl.ds(index * ROWS, ROWS)
        values = hidden[rows, :].astype(wide)
        factor = lax.rsqrt(jnp.mean(values * values, axis=-1, keepdims=True) + eps_norm)
        factor_ref[rows, :] = factor
        normed = (values * factor * gain).astype(low)
        normed_ref[rows, :] = normed
        raw = mm(normed, attn_ref[:, 0:512])

        def turn(value):
            return (value * cos_ref[...] + pltpu.roll(value, HD // 2, 1) * sin_ref[...]).astype(low)

        key = turn(raw[:, 2 * HD : 3 * HD])
        value = raw[:, 3 * HD :].astype(low)
        for head in range(2):
            query = turn(raw[:, head * HD : (head + 1) * HD])
            for part in range(2):
                place = pl.ds(index * 4 * TOK + (2 * part + head) * TOK, TOK)
                within = slice(part * TOK, (part + 1) * TOK)
                sent_ref[place, 0:HD] = query[within]
                sent_ref[place, HD : 2 * HD] = key[within]
                sent_ref[place, 2 * HD : 3 * HD] = value[within]


def project(pieces, attn_all, cos_two, sin_two):
    return pl.pallas_call(
        project_kernel,
        out_shape=(
            jax.ShapeDtypeStruct((ALL, D), low),
            jax.ShapeDtypeStruct((LENGTH, 3 * HD), low),
            jax.ShapeDtypeStruct((ALL, 1), wide),
            jax.ShapeDtypeStruct((16, D), wide),
            jax.ShapeDtypeStruct((SEQS * 16, D), low),
        ),
        in_specs=[anywhere] * 10 + [vmem] * 3,
        out_specs=tuple([vmem] * 5),
        scratch_shapes=[pltpu.VMEM((ALL, D), low), pltpu.SemaphoreType.DMA((20,))],
        compiler_params=params(40),
        cost_estimate=cost(2.2e9, 16e6),
        name="project",
    )(*pieces, attn_all, cos_two, sin_two)


def mix_back_kernel(*refs):
    pieces, weight_ref = refs[:10], refs[10]
    grad_ref, extra_ref, sent_ref, sems = refs[11:]
    for copy in load_pieces(pieces, grad_ref, extra_ref, sems):
        copy.wait()

    @pl.loop(0, ALL // ROWS)
    def step(index):
        grad = mm_t(grad_ref[pl.ds(index * ROWS, ROWS), :], weight_ref[...]).astype(low)
        for part in range(2):
            for head in range(2):
                place = pl.ds(index * 4 * TOK + (2 * part + head) * TOK, TOK)
                sent_ref[place, :] = grad[part * TOK : (part + 1) * TOK, head * HD : (head + 1) * HD]


def mix_back(pieces, weight):
    return pl.pallas_call(
        mix_back_kernel,
        out_shape=(
            jax.ShapeDtypeStruct((ALL, D), low),
            jax.ShapeDtypeStruct((SEQS * 16, D), low),
            jax.ShapeDtypeStruct((LENGTH, HD), low),
        ),
        in_specs=[anywhere] * 10 + [vmem],
        out_specs=(vmem, vmem, vmem),
        scratch_shapes=[pltpu.SemaphoreType.DMA((20,))],
        compiler_params=params(40),
        cost_estimate=cost(1.1e9, 10e6),
        name="mix_back",
    )(*pieces, weight)


def collect_kernel(core_ref, grads_ref, query_ref, mine_ref, other_ref):
    first = core_ref[0] == 0

    @pl.loop(0, SEQS)
    def step(index):
        rows = pl.ds(index * TOK, TOK)
        swapped = pl.ds(((index + SEQS // 2) % SEQS) * TOK, TOK)
        one = grads_ref[pl.ds(index * 2 * TOK, TOK), :]
        two = grads_ref[pl.ds(index * 2 * TOK + TOK, TOK), :]
        query_ref[rows, 0:HD] = one[:, :HD]
        query_ref[rows, HD : 2 * HD] = two[:, :HD]
        total = one[:, HD:].astype(wide) + two[:, HD:].astype(wide)
        lower = jnp.concatenate([total[:, : HD // 2], total[:, HD : HD + HD // 2]], axis=1)
        upper = jnp.concatenate([total[:, HD // 2 : HD], total[:, HD + HD // 2 :]], axis=1)
        mine_ref[rows, :] = jnp.where(first, lower, upper)
        other_ref[swapped, :] = jnp.where(first, upper, lower).astype(low)


def collect(core, grads):
    return pl.pallas_call(
        collect_kernel,
        out_shape=(
            jax.ShapeDtypeStruct((ALL, 2 * HD), low),
            jax.ShapeDtypeStruct((ALL, HD), wide),
            jax.ShapeDtypeStruct((ALL, HD), low),
        ),
        in_specs=[smem, vmem],
        out_specs=(vmem, vmem, vmem),
        compiler_params=params(32),
        cost_estimate=cost(1e6, 4e6),
        name="collect",
    )(core, grads)


def qkv_weights_kernel(normed_ref, query_ref, mine_ref, got_ref, out_ref, grad_ref):
    grad_ref[:, 0 : 2 * HD] = query_ref[...]
    grad_ref[:, 2 * HD : 3 * HD] = (mine_ref[...] + got_ref[...].astype(wide)).astype(low)

    @pl.loop(0, D // ROWS)
    def step(index):
        columns = pl.ds(pl.multiple_of(index * ROWS, ROWS), ROWS)
        out_ref[pl.ds(index * ROWS, ROWS), :] = t_mm(normed_ref[:, columns], grad_ref[...]).astype(low)


def qkv_weights(normed, query, mine, got):
    return pl.pallas_call(
        qkv_weights_kernel,
        out_shape=(jax.ShapeDtypeStruct((D, 3 * HD), low), jax.ShapeDtypeStruct((ALL, 3 * HD), low)),
        in_specs=[vmem] * 4,
        out_specs=(vmem, vmem),
        compiler_params=params(32),
        cost_estimate=cost(1.6e9, 8e6),
        name="qkv_weights",
    )(normed, query, mine, got)


def finish_kernel(shards_ref, query_ref, key_ref, value_ref, out_ref, gain_ref):
    gain = jnp.zeros((TOK, TOK), wide)
    for source in range(EXPERTS):
        query_ref[:, source * 256 : (source + 1) * 256] = shards_ref[source, :, 0:256].astype(wide)
        out_ref[:, source * 256 : (source + 1) * 256] = shards_ref[source, :, 384:640].astype(wide)
        gain = gain + shards_ref[source, :, 640:768].astype(wide)
    for pair in range(KV):
        one = shards_ref[2 * pair, :, 256:384].astype(wide)
        two = shards_ref[2 * pair + 1, :, 256:384].astype(wide)
        columns = slice(pair * HD, (pair + 1) * HD)
        key_ref[:, columns] = jnp.concatenate([one[:, : HD // 2], two[:, : HD // 2]], axis=1)
        value_ref[:, columns] = jnp.concatenate([one[:, HD // 2 :], two[:, HD // 2 :]], axis=1)
    gain_ref[...] = jnp.sum(gain, axis=1, keepdims=True)


def finish(shards):
    widths = (H * HD, KV * HD, KV * HD, H * HD, 1)
    return pl.pallas_call(
        finish_kernel,
        out_shape=tuple(jax.ShapeDtypeStruct((TOK, width), wide) for width in widths),
        in_specs=[vmem],
        out_specs=tuple([vmem] * 5),
        compiler_params=params(32),
        cost_estimate=cost(1e6, 4e6),
        name="finish",
    )(shards)


def halves(value):
    upper = value.astype(low)
    return upper, (value - upper.astype(wide)).astype(low)


def silu_parts(gate_value):
    sig = 1.0 / (1.0 + jnp.exp(-gate_value))
    return sig, gate_value * sig


def swiglu_back(sig, act, up_value, grad):
    return (grad * up_value * (sig + act * (1.0 - sig))).astype(low), (grad * act).astype(low)


def ffn_kernel(*refs):
    expert_ref, slots_ref, slots_t_ref, routes_ref, router_ref = refs[:5]
    pieces, (cot_hbm, pack_ref, shared_down_ref, down_ref) = refs[5:15], refs[15:19]
    grad_mine, grad_other, gates_ref = refs[19:22]
    outs = refs[22:31]
    normed_ref, cot_ref, grad_ref = refs[31:34]
    (
        hidden_s_ref,
        grad_gate_s_ref,
        grad_up_s_ref,
        incoming_ref,
        hidden_e_ref,
        gated_ref,
        grad_rows_ref,
        grad_gate_e_ref,
        grad_up_e_ref,
    ) = refs[34:43]
    w_gate_s, w_up_s, w_down_s, w_gate, w_up, w_down = refs[43:49]
    gate_value, up_value, gate_parts, grad_in, piece_sems, sems, out_sems = refs[49:]
    base = 3 * SH_OWN
    piece_copies = load_pieces(pieces, normed_ref, None, piece_sems)
    cot_copy = pltpu.make_async_copy(cot_hbm, cot_ref, sems.at[6])
    cot_copy.start()
    copies = [
        pltpu.make_async_copy(pack_ref.at[:, pl.ds(0, SH_OWN)], w_gate_s, sems.at[0]),
        pltpu.make_async_copy(pack_ref.at[:, pl.ds(SH_OWN, SH_OWN)], w_up_s, sems.at[1]),
        pltpu.make_async_copy(shared_down_ref, w_down_s, sems.at[2]),
        pltpu.make_async_copy(pack_ref.at[:, pl.ds(base, FF)], w_gate, sems.at[3]),
        pltpu.make_async_copy(pack_ref.at[:, pl.ds(base + FF, FF)], w_up, sems.at[4]),
        pltpu.make_async_copy(down_ref, w_down, sems.at[5]),
    ]
    for copy in copies:
        copy.start()
    kept = refs[34:43]

    def send(index):
        copy = pltpu.make_async_copy(kept[index], outs[index], out_sems.at[index])
        copy.start()
        return copy

    expert = expert_ref[0]
    lane = lax.broadcasted_iota(jnp.int32, (ROWS, 128), 1)
    for copy in piece_copies:
        copy.wait()

    @pl.loop(0, ALL // ROWS)
    def route(step):
        rows = pl.ds(step * ROWS, ROWS)
        logits = mm(normed_ref[rows, :], router_ref[...])
        first, second = routes_ref[rows, 0:1], routes_ref[rows, 1:2]
        chosen_first = jnp.sum(jnp.where(lane == first + 2, logits, 0.0), axis=1, keepdims=True)
        chosen_second = jnp.sum(jnp.where(lane == second + 2, logits, 0.0), axis=1, keepdims=True)
        gate_first = 1.0 / (1.0 + jnp.exp(chosen_second - chosen_first))
        gate_second = 1.0 / (1.0 + jnp.exp(chosen_first - chosen_second))
        here = jnp.where(first == expert, gate_first, 0.0) + jnp.where(second == expert, gate_second, 0.0)
        upper, lower = halves(here)
        parts = jnp.where(lane == 0, upper.astype(wide), 0.0) + jnp.where(lane == 1, lower.astype(wide), 0.0)
        gate_parts[rows, :] = parts.astype(low)

        @pl.when(step == 0)
        def _():
            both = jnp.where(lane == 0, gate_first, 0.0) + jnp.where(lane == 1, gate_second, 0.0)
            gates_ref[...] = both[:TOK]

    cot_copy.wait()

    @pl.loop(0, D // ROWS)
    def pick(step):
        columns = pl.ds(pl.multiple_of(step * ROWS, ROWS), ROWS)
        incoming_ref[:, columns] = mm(slots_ref[...], normed_ref[:, columns]).astype(low)
        grad_rows_ref[:, columns] = mm(slots_ref[...], cot_ref[:, columns]).astype(low)

    slot_parts = mm(slots_ref[...], gate_parts[...])
    slot_gate = slot_parts[:, 0:1] + slot_parts[:, 1:2]
    sent = [send(3)]
    for copy in copies[:3]:
        copy.wait()

    @pl.loop(0, ALL // ROWS)
    def shared(step):
        rows = pl.ds(step * ROWS, ROWS)
        sig, act = silu_parts(mm(normed_ref[rows, :], w_gate_s[...]))
        up = mm(normed_ref[rows, :], w_up_s[...])
        hidden_s_ref[rows, :] = (act * up).astype(low)
        grad_hidden = mm_t(cot_ref[rows, :], w_down_s[...])
        grad_gate, grad_up = swiglu_back(sig, act, up, grad_hidden)
        grad_gate_s_ref[rows, :] = grad_gate
        grad_up_s_ref[rows, :] = grad_up

    sent += [send(0), send(1), send(2)]
    for copy in copies[3:5]:
        copy.wait()
    for start, width in FF_TILES:
        columns = pl.ds(start, width)
        gate = mm(incoming_ref[...], w_gate[:, columns])
        up = mm(incoming_ref[...], w_up[:, columns])
        gate_value[:, columns] = gate
        up_value[:, columns] = up
        hidden_e_ref[:, columns] = (silu_parts(gate)[1] * up).astype(low)
    sent.append(send(4))
    copies[5].wait()

    def forward(step, total):
        columns = pl.ds(pl.multiple_of(step * ROWS, ROWS), ROWS)
        rows = mm(hidden_e_ref[...], w_down[:, columns]).astype(low).astype(wide)
        cot = grad_rows_ref[:, columns].astype(wide)
        gated_ref[:, columns] = (rows * slot_gate).astype(low)
        grad_rows_ref[:, columns] = (cot * slot_gate).astype(low)
        return total + jnp.sum(rows * cot, axis=1, keepdims=True)

    slot_grad = lax.fori_loop(0, D // ROWS, forward, jnp.zeros((SLOTS, 1), wide))
    sent += [send(5), send(6)]
    for start, width in FF_TILES:
        columns = pl.ds(start, width)
        grad_hidden = mm_t(grad_rows_ref[...], w_down[pl.ds(start, width), :])
        sig, act = silu_parts(gate_value[:, columns])
        grad_gate, grad_up = swiglu_back(sig, act, up_value[:, columns], grad_hidden)
        grad_gate_e_ref[:, columns] = grad_gate
        grad_up_e_ref[:, columns] = grad_up
    sent += [send(7), send(8)]

    @pl.loop(0, D // ROWS)
    def back(step):
        columns = pl.ds(pl.multiple_of(step * ROWS, ROWS), ROWS)
        grad_in[:, columns] = (
            mm_t(grad_gate_e_ref[...], w_gate[columns, :]) + mm_t(grad_up_e_ref[...], w_up[columns, :])
        ).astype(low)

    upper, lower = halves(slot_grad)
    slot_lane = lax.broadcasted_iota(jnp.int32, (SLOTS, 128), 1)
    slot_parts = (
        jnp.where(slot_lane == expert, upper.astype(wide), 0.0)
        + jnp.where(slot_lane == expert + 8, lower.astype(wide), 0.0)
    ).astype(low)

    def total(start):
        @pl.loop(0, ALL // (2 * ROWS))
        def _(step):
            rows = pl.ds(start + step * ROWS, ROWS)
            for tile in range(D // 512):
                columns = pl.ds(tile * 512, 512)
                grad_ref[rows, columns] = (
                    mm_t(grad_gate_s_ref[rows, :], w_gate_s[columns, :])
                    + mm_t(grad_up_s_ref[rows, :], w_up_s[columns, :])
                    + mm(slots_t_ref[rows, :], grad_in[:, columns])
                ).astype(low)
            grad_ref[rows, D : D + 128] = mm(slots_t_ref[rows, :], slot_parts).astype(low)

    total(ALL // 2)
    other = pltpu.make_async_copy(grad_ref.at[pl.ds(ALL // 2, ALL // 2), :], grad_other, sems.at[7])
    other.start()
    total(0)
    mine = pltpu.make_async_copy(grad_ref.at[pl.ds(0, ALL // 2), :], grad_mine, sems.at[8])
    mine.start()
    for copy in sent + [other, mine]:
        copy.wait()


def ffn(expert, slots, slots_t, routes, router, pieces, cot, pack, shared_down, down):
    kept = [(ALL, SH_OWN)] * 3 + [(SLOTS, D), (SLOTS, FF), (SLOTS, D), (SLOTS, D), (SLOTS, FF), (SLOTS, FF)]
    grads = [(ALL // 2, D + 128)] * 2
    return pl.pallas_call(
        ffn_kernel,
        out_shape=tuple(
            [jax.ShapeDtypeStruct(shape, low) for shape in grads]
            + [jax.ShapeDtypeStruct((TOK, 128), wide)]
            + [jax.ShapeDtypeStruct(shape, low) for shape in kept]
        ),
        in_specs=[smem] + [vmem] * 4 + [anywhere] * 14,
        out_specs=tuple([anywhere] * 2 + [vmem] + [anywhere] * 9),
        scratch_shapes=[pltpu.VMEM((ALL, D), low), pltpu.VMEM((ALL, D), low), pltpu.VMEM((ALL, D + 128), low)]
        + [pltpu.VMEM(shape, low) for shape in kept]
        + [
            pltpu.VMEM((D, SH_OWN), low),
            pltpu.VMEM((D, SH_OWN), low),
            pltpu.VMEM((SH_OWN, D), low),
            pltpu.VMEM((D, FF), low),
            pltpu.VMEM((D, FF), low),
            pltpu.VMEM((FF, D), low),
            pltpu.VMEM((SLOTS, FF), wide),
            pltpu.VMEM((SLOTS, FF), wide),
            pltpu.VMEM((ALL, 128), low),
            pltpu.VMEM((SLOTS, D), low),
            pltpu.SemaphoreType.DMA((20,)),
            pltpu.SemaphoreType.DMA((9,)),
            pltpu.SemaphoreType.DMA((9,)),
        ],
        compiler_params=params(60),
        cost_estimate=cost(27e9, 50e6, 1e6),
        name="ffn",
    )(expert, slots, slots_t, routes, router, *pieces, cot, pack, shared_down, down)


def pack_rows(block):
    count, width = block.shape[0] // 8, block.shape[1] // 128
    return jnp.concatenate(
        [
            jnp.concatenate(
                [block[8 * i : 8 * i + 8, 128 * j : 128 * j + 128] for i in range(count)], axis=1
            )
            for j in range(width)
        ],
        axis=0,
    )


def expert_weights_kernel(
    incoming_ref, hidden_ref, grad_rows_ref, grad_gate_ref, grad_up_ref, out_ref, buffer, down, sems
):
    base = 3 * SH_OWN

    @pl.loop(0, D // ROWS)
    def first(tile):
        part = pl.ds(pl.multiple_of(tile * ROWS, ROWS), ROWS)
        down[:, part] = t_mm(hidden_ref[...], grad_rows_ref[:, part])

    def slab(slot, step):
        rows = pl.ds(pl.multiple_of(step * ROWS, ROWS), ROWS)
        return pltpu.make_async_copy(buffer.at[slot], out_ref.at[rows, pl.ds(base, 3 * FF)], sems.at[slot])

    @pl.loop(0, D // ROWS)
    def each(step):
        slot = lax.rem(step, 2)

        @pl.when(step >= 2)
        def _():
            slab(slot, step - 2).wait()

        incoming = incoming_ref[:, pl.ds(pl.multiple_of(step * ROWS, ROWS), ROWS)]
        buffer[slot, :, 0:FF] = t_mm(incoming, grad_gate_ref[...]).astype(low)
        buffer[slot, :, FF : 2 * FF] = t_mm(incoming, grad_up_ref[...]).astype(low)
        for part in range(ROWS // TOK):
            place = step * (ROWS // TOK) + part
            count = FF // FSDP
            routed = down[pl.ds(pl.multiple_of(place * count, 8), count), :]
            buffer[slot, part * TOK : (part + 1) * TOK, 2 * FF : 3 * FF] = pack_rows(routed).astype(low)
        slab(slot, step).start()

    slab(0, D // ROWS - 2).wait()
    slab(1, D // ROWS - 1).wait()


def expert_weights(*operands):
    return pl.pallas_call(
        expert_weights_kernel,
        out_shape=jax.ShapeDtypeStruct((D, PACK), low),
        in_specs=[vmem] * 5,
        out_specs=anywhere,
        scratch_shapes=[
            pltpu.VMEM((2, ROWS, 3 * FF), low),
            pltpu.VMEM((FF, D), wide),
            pltpu.SemaphoreType.DMA((2,)),
        ],
        compiler_params=params(48),
        cost_estimate=cost(6e9, 24e6),
        name="expert_weights",
    )(*operands)


def shared_weights_kernel(*refs):
    pieces = refs[1:11]
    cot_ref, hidden_ref, grad_gate_ref, grad_up_ref = refs[11:15]
    out_ref, normed_ref, buffer, down, piece_sems, sems = refs[15:]
    copies = load_pieces(pieces, normed_ref, None, piece_sems)

    @pl.loop(0, D // ROWS)
    def first(tile):
        part = pl.ds(pl.multiple_of(tile * ROWS, ROWS), ROWS)
        down[:, part] = t_mm(hidden_ref[...], cot_ref[:, part])

    for copy in copies:
        copy.wait()

    def slab(slot, step):
        rows = pl.ds(pl.multiple_of(step * ROWS, ROWS), ROWS)
        return pltpu.make_async_copy(buffer.at[slot], out_ref.at[rows, pl.ds(0, 3 * SH_OWN)], sems.at[slot])

    @pl.loop(0, D // ROWS)
    def each(step):
        slot = lax.rem(step, 2)

        @pl.when(step >= 2)
        def _():
            slab(slot, step - 2).wait()

        normed = normed_ref[:, pl.ds(pl.multiple_of(step * ROWS, ROWS), ROWS)]
        buffer[slot, :, 0:SH_OWN] = t_mm(normed, grad_gate_ref[...]).astype(low)
        buffer[slot, :, SH_OWN : 2 * SH_OWN] = t_mm(normed, grad_up_ref[...]).astype(low)
        for part in range(ROWS // TOK):
            place = step * (ROWS // TOK) + part
            shared = down[pl.ds(pl.multiple_of(place * SH_PAD, 8), SH_PAD), :]
            buffer[slot, part * TOK : (part + 1) * TOK, 2 * SH_OWN :] = pack_rows(shared).astype(low)
        slab(slot, step).start()

    slab(0, D // ROWS - 2).wait()
    slab(1, D // ROWS - 1).wait()


def shared_weights(pack, pieces, cot, hidden, grad_gate, grad_up):
    return pl.pallas_call(
        shared_weights_kernel,
        out_shape=jax.ShapeDtypeStruct((D, PACK), low),
        in_specs=[anywhere] * 11 + [vmem] * 4,
        out_specs=anywhere,
        scratch_shapes=[
            pltpu.VMEM((ALL, D), low),
            pltpu.VMEM((2, ROWS, 3 * SH_OWN), low),
            pltpu.VMEM((SH_OWN, D), wide),
            pltpu.SemaphoreType.DMA((20,)),
            pltpu.SemaphoreType.DMA((2,)),
        ],
        input_output_aliases={0: 0},
        compiler_params=params(48),
        cost_estimate=cost(5e9, 18e6),
        name="shared_weights",
    )(pack, *pieces, cot, hidden, grad_gate, grad_up)


def norm_factor(values):
    return lax.rsqrt(jnp.mean(values * values, axis=-1, keepdims=True) + eps_norm)


def norm_back(values, factor, gain, grad):
    scaled = grad * gain
    inner = jnp.mean(scaled * values, axis=-1, keepdims=True)
    return factor * scaled - values * (factor * factor * factor * inner)


def per_device(
    hidden_in,
    cotangent,
    segments,
    routes,
    attn_gain,
    w_query,
    w_key,
    w_value,
    w_out,
    ffn_gain,
    w_router,
    shared_gate,
    shared_up,
    shared_down,
    expert_gate,
    expert_up,
    expert_down,
):
    expert = lax.axis_index("expert")
    z, core = expert // 2, expert % 2
    place = lax.axis_index("fsdp")

    misc = jnp.concatenate(
        [attn_gain[:, None], ffn_gain[:, None], w_router, jnp.zeros((TOK, 118), low)], axis=1
    )
    attn_pack = jnp.concatenate(
        [
            lax.dynamic_slice_in_dim(w_query, 256 * expert, 256, 1),
            lax.dynamic_slice_in_dim(w_key, HD * z, HD, 1),
            lax.dynamic_slice_in_dim(w_value, HD * z, HD, 1),
            lax.dynamic_slice_in_dim(w_out, 256 * expert, 256, 1),
            misc,
        ],
        axis=1,
    )
    attn_all = lax.all_gather(attn_pack, "fsdp", axis=0, tiled=True)
    half_in, half_out = SH // 2, SH_OWN // 2
    sel_column = jnp.arange(half_out)
    picked = SH_ROWS * (sel_column // SH_PAD) + SH_PART * expert + sel_column % SH_PAD
    picked = jnp.where(sel_column % SH_PAD < SH_PART, picked, -1)
    select = (jnp.arange(half_in)[:, None] == picked[None, :]).astype(low)
    own_shared = mm(
        jnp.concatenate(
            [shared_gate[:, :half_in], shared_gate[:, half_in:], shared_up[:, :half_in], shared_up[:, half_in:]],
            axis=0,
        ),
        select,
    ).astype(low)
    own_down = jnp.pad(
        lax.dynamic_slice_in_dim(shared_down, SH_PART * expert, SH_PART, 0),
        ((0, SH_PAD - SH_PART), (0, 0)),
    )
    ffn_pack = jnp.concatenate(
        [
            own_shared[:TOK],
            own_shared[TOK : 2 * TOK],
            own_shared[2 * TOK : 3 * TOK],
            own_shared[3 * TOK :],
            pack_tiles(own_down),
            expert_gate[:, 0],
            expert_up[:, 0],
            pack_tiles(expert_down[:, 0]),
        ],
        axis=1,
    )
    ffn_all = lax.all_gather(ffn_pack, "fsdp", axis=0, tiled=True)

    ids = jnp.concatenate(
        [
            segments.astype(low),
            jnp.pad(routes[0].reshape(1, TOK * TOPK), ((0, 0), (0, LENGTH - TOK * TOPK))).astype(low),
            jnp.zeros((14, LENGTH), low),
        ],
        axis=0,
    )
    hidden_pieces = gather_pieces(jnp.concatenate([hidden_in[0], ids], axis=0))
    cot_block, *hidden_pieces = together(cotangent[0], *hidden_pieces)
    cot_pieces = gather_pieces(cot_block)

    inverse_freq = rope_base ** (-jnp.arange(HD // 2, dtype=wide) * 2.0 / HD)
    angles = jnp.arange(LENGTH).astype(wide)[:, None] * inverse_freq[None, :]
    cosine, sine = jnp.cos(angles), jnp.sin(angles)
    cos_all = jnp.concatenate([cosine, cosine], axis=1)
    sin_back = jnp.concatenate([sine, -sine], axis=1)
    cos_own = lax.dynamic_slice_in_dim(cos_all, place * TOK, TOK, 0)
    sin_own = -lax.dynamic_slice_in_dim(sin_back, place * TOK, TOK, 0)
    cos_two, sin_two = jnp.concatenate([cos_own, cos_own]), jnp.concatenate([sin_own, sin_own])
    attn_all, cos_two, sin_two, cos_all, sin_back = together(attn_all, cos_two, sin_two, cos_all, sin_back)
    normed_one, sent, factor_one, gains, ids_all = project(hidden_pieces, attn_all, cos_two, sin_two)
    qkv = lax.all_to_all(sent, "fsdp", split_axis=0, concat_axis=0, tiled=True)

    ids_all = ids_all.reshape(SEQS, 16, D)
    seg_row = lax.dynamic_slice_in_dim(ids_all[:, 0].astype(jnp.int32), place // 2, 1, 0)
    seg_col = seg_row.reshape(LENGTH, 1)
    route_all = ids_all[:, 1, : TOK * TOPK].astype(jnp.int32).reshape(ALL, TOPK)
    hit = jnp.any(route_all == expert, axis=1).astype(wide)
    order = jnp.arange(ALL)
    rank = mm(hit.astype(low)[None, :], (order[:, None] < order[None, :]).astype(low))
    slot_bool = (rank.astype(jnp.int32) == jnp.arange(SLOTS)[:, None]) & (hit > 0.5)[None, :]
    slots = slot_bool.astype(low)
    slots_t = slot_bool.T.astype(low)
    cot_all = place_pieces(cot_pieces)
    out_columns = attn_all[:, 512:768].reshape(EXPERTS, 256, 256)
    owners = [relative_owner(expert, block) for block in range(EXPERTS)]
    w_out_own = exchange(
        jnp.stack([lax.dynamic_index_in_dim(out_columns, owner, 0, keepdims=False) for owner in owners]), expert
    )
    w_out_own = w_out_own.transpose(1, 0, 2).reshape(256, D)
    router = attn_all[:, 768:896]
    qkv, seg_row, seg_col, route_all, slots, slots_t, cot_all, w_out_own, router = together(
        qkv, seg_row, seg_col, route_all, slots, slots_t, cot_all, w_out_own, router
    )
    mixed_head, log_total = attend(qkv, seg_row, seg_col)
    mixed = (
        lax.all_to_all(mixed_head, "fsdp", split_axis=0, concat_axis=0, tiled=True)
        .reshape(SEQS, 2, TOK, HD)
        .transpose(0, 2, 1, 3)
        .reshape(ALL, 2 * HD)
    )
    own_hidden = hidden_in[0].astype(wide)
    half = ALL // 2
    middle = own_hidden + scatter_rows(
        mm(mixed[:half], w_out_own).astype(low), mm(mixed[half:], w_out_own).astype(low)
    )
    factor_two = norm_factor(middle)
    gain_one, gain_two = gains[0:1], gains[1:2]
    normed_pieces = gather_pieces((middle * factor_two * gain_two).astype(low))

    base = 3 * SH_OWN
    shared_down_w = unpack_tiles(ffn_all[:, 2 * SH_OWN : base], FSDP)
    down_w = unpack_tiles(ffn_all[:, base + 2 * FF :], FSDP)
    (
        grad_mine,
        grad_other,
        gates,
        hidden_shared,
        grad_gate_shared,
        grad_up_shared,
        incoming,
        hidden_expert,
        gated_rows,
        grad_rows,
        grad_gate_expert,
        grad_up_expert,
    ) = ffn(
        expert[None], slots, slots_t, route_all, router, normed_pieces, cot_all, ffn_all, shared_down_w, down_w
    )
    own_grad, to_above, to_below = scatter_start(grad_mine, swap_core(grad_other))
    to_above, to_below, incoming, hidden_expert, grad_rows = together(
        to_above, to_below, incoming, hidden_expert, grad_rows
    )
    from_below, from_above = move_z(to_above, 1), move_z(to_below, -1)
    ffn_grads = expert_weights(incoming, hidden_expert, grad_rows, grad_gate_expert, grad_up_expert)
    from_below, from_above, ffn_grads = together(from_below, from_above, ffn_grads)
    own_grad = scatter_end(own_grad, from_below, from_above)
    route_grads = own_grad[:, D : D + 8] + own_grad[:, D + 8 : D + 16]
    own_hot = (route_all[:TOK, :, None] == jnp.arange(EXPERTS)[None, None, :]).astype(wide)
    own_gates = gates[:TOK, :TOPK]
    grad_gates = jnp.sum(own_hot * route_grads[:, None, :], axis=-1)
    grad_chosen = own_gates * (grad_gates - jnp.sum(own_gates * grad_gates, axis=-1, keepdims=True))
    grad_logits = jnp.sum(own_hot * grad_chosen[:, :, None], axis=1)
    grad_two = own_grad[:, :D] + product_wide(grad_logits, gains[2:10])
    grad_gain_two = jnp.sum(grad_two * middle * factor_two, axis=0)
    grad_middle = cotangent[0].astype(wide) + norm_back(middle, factor_two, gain_two, grad_two)
    logit_upper, logit_lower = halves(grad_logits.T.reshape(1, TOK * EXPERTS))
    back_block = jnp.concatenate(
        [
            grad_middle.astype(low),
            jnp.stack(halves(grad_gain_two)),
            jnp.concatenate([logit_upper, logit_lower], axis=1),
            jnp.zeros((13, D), low),
        ],
        axis=0,
    )
    back_block, ffn_grads = together(back_block, ffn_grads)
    below, above = first_pieces(back_block)
    ffn_grads = shared_weights(ffn_grads, normed_pieces, cot_all, hidden_shared, grad_gate_shared, grad_up_shared)
    below, above, ffn_grads = together(below, above, ffn_grads)
    back_pieces = other_pieces(back_block, below, above)
    ffn_sums = lax.psum_scatter(ffn_grads, "fsdp", scatter_dimension=0, tiled=True)

    grad_attn, extra, sent_back = mix_back(back_pieces, w_out_own)
    grad_head = lax.all_to_all(sent_back, "fsdp", split_axis=0, concat_axis=0, tiled=True)
    grads_head = attend_back(qkv, grad_head, log_total, seg_row, seg_col, cos_all, sin_back)
    grads_qkv = lax.all_to_all(grads_head, "fsdp", split_axis=0, concat_axis=0, tiled=True)

    hidden_shared, gated_rows, slots_t, _ = together(hidden_shared, gated_rows, slots_t, sent_back)
    result_mine = mm(hidden_shared[:half], shared_down_w) + mm(slots_t[:half], gated_rows)
    result_other = mm(hidden_shared[half:], shared_down_w) + mm(slots_t[half:], gated_rows)
    layer_out = (middle + scatter_rows(result_mine.astype(low), result_other.astype(low))).astype(low)

    grad_out = t_mm(mixed, grad_attn).astype(low).reshape(256, EXPERTS, 256).transpose(1, 0, 2)
    grad_out = exchange(
        jnp.stack([lax.dynamic_index_in_dim(grad_out, owner, 0, keepdims=False) for owner in owners]), expert
    ).reshape(FSDP, TOK, 256)
    extra = extra.reshape(SEQS, 16, D)
    gain_two_sum = jnp.sum(extra[:, :2].astype(wide), axis=(0, 1))
    logit_rows = extra[:, 2].reshape(SEQS, 2, EXPERTS, TOK).transpose(1, 2, 0, 3).reshape(2 * EXPERTS, ALL)
    grad_router = mm(logit_rows, place_pieces(normed_pieces))
    small_rows = jnp.concatenate(
        [grad_router[:EXPERTS] + grad_router[EXPERTS:], gain_two_sum[None], jnp.zeros((7, D), wide)], axis=0
    )
    small_rows = jnp.pad(small_rows.reshape(16, FSDP, TOK).transpose(1, 0, 2).astype(low), ((0, 0), (0, 0), (0, 128)))
    out_pack = jnp.concatenate([grad_out, small_rows], axis=1).reshape(FSDP * (TOK + 16), 256)
    out_pack, grads_qkv, layer_out = together(out_pack, grads_qkv, layer_out)
    out_sums = sum_blocks(out_pack, TOK + 16)

    grad_query, kv_mine, kv_other = collect(core[None], grads_qkv)
    qkv_grads, grad_qkv = qkv_weights(normed_one, grad_query, kv_mine, swap_core(kv_other))
    qkv_sums = sum_blocks(qkv_grads, TOK)
    is_first = core == 0
    kv_weight = attn_all[:, 256:512].reshape(D, 2, 2, HD // 2)
    kv_weight = jnp.where(is_first, kv_weight[:, :, 0], kv_weight[:, :, 1]).reshape(D, HD)
    qkv_weight = jnp.concatenate([attn_all[:, :256], kv_weight], axis=1)
    grad_normed_mine = mm_t(grad_qkv[:half], qkv_weight).astype(low)
    grad_normed_other = mm_t(grad_qkv[half:], qkv_weight).astype(low)
    own_grad_one = scatter_rows(grad_normed_mine, grad_normed_other)
    grad_input = grad_middle + norm_back(own_hidden, factor_one[:TOK], gain_one, own_grad_one)

    shared_shards = lax.all_gather(ffn_sums[:, :base], "expert", axis=0)
    half_rows = SH_PAD * EXPERTS * FSDP // 2
    put_row = jnp.arange(half_rows)
    source, within = put_row // half_out, put_row % half_out
    target = SH_ROWS * (within // SH_PAD) + SH_PART * source + within % SH_PAD
    target = jnp.where(within % SH_PAD < SH_PART, target, -1)
    spread = (target[:, None] == jnp.arange(half_in)[None, :]).astype(low)
    gate_up = shared_shards[:, :, : 2 * SH_OWN].reshape(EXPERTS, TOK, 4, half_out)
    gate_up = mm(gate_up.transpose(2, 1, 0, 3).reshape(4 * TOK, EXPERTS * half_out), spread)
    grad_shared_gate = jnp.concatenate([gate_up[:TOK], gate_up[TOK : 2 * TOK]], axis=1)
    grad_shared_up = jnp.concatenate([gate_up[2 * TOK : 3 * TOK], gate_up[3 * TOK :]], axis=1)
    down_parts = unpack_tiles(shared_shards[:, :, 2 * SH_OWN : base].reshape(EXPERTS * TOK, SH_OWN), EXPERTS)
    grad_shared_down = (
        down_parts.reshape(EXPERTS, SH_PAD, D)[:, :SH_PART].reshape(SH_ROWS, D).astype(wide)
    )
    grad_expert_gate = ffn_sums[:, base : base + FF].astype(wide)[:, None]
    grad_expert_up = ffn_sums[:, base + FF : base + 2 * FF].astype(wide)[:, None]
    grad_expert_down = unpack_tiles(ffn_sums[:, base + 2 * FF :], 1).astype(wide)[:, None]

    own_weight = lax.dynamic_slice_in_dim(qkv_weight, place * TOK, TOK, 0)
    gain_part = jnp.sum(qkv_sums * own_weight.astype(wide), axis=1, keepdims=True)
    gain_upper, gain_lower = halves(gain_part / attn_gain.astype(wide)[:, None])
    shards = jnp.concatenate(
        [qkv_sums.astype(low), out_sums[:TOK].astype(low), gain_upper, gain_lower, jnp.zeros((TOK, 126), low)], axis=1
    )
    (
        shards,
        grad_shared_gate,
        grad_shared_up,
        grad_shared_down,
        grad_expert_gate,
        grad_expert_up,
        grad_expert_down,
    ) = together(
        shards,
        grad_shared_gate,
        grad_shared_up,
        grad_shared_down,
        grad_expert_gate,
        grad_expert_up,
        grad_expert_down,
    )
    grad_w_query, grad_w_key, grad_w_value, grad_w_out, grad_attn_gain = finish(
        lax.all_gather(shards, "expert", axis=0)
    )
    return (
        layer_out[None],
        grad_input.astype(low)[None],
        grad_attn_gain[:, 0],
        grad_w_query,
        grad_w_key,
        grad_w_value,
        grad_w_out,
        out_sums[TOK + EXPERTS, :TOK],
        out_sums[TOK : TOK + EXPERTS, :TOK].T,
        grad_shared_gate,
        grad_shared_up,
        grad_shared_down,
        grad_expert_gate,
        grad_expert_up,
        grad_expert_down,
    )


def sum_blocks(block, rows):
    parts = lax.all_to_all(block, "fsdp", split_axis=0, concat_axis=0, tiled=True)
    return jnp.sum(parts.reshape(FSDP, rows, block.shape[1]).astype(wide), axis=0)


def product_wide(left, right):
    return lax.dot_general(
        left, right, (((1,), (0,)), ((), ())), precision=highest, preferred_element_type=wide
    )


def solution(mesh):
    in_specs = (
        P("expert", "fsdp", None),
        P("expert", "fsdp", None),
        P("expert", None),
        P("expert", "fsdp", None),
        P("fsdp"),
        P("fsdp", None),
        P("fsdp", None),
        P("fsdp", None),
        P("fsdp", None),
        P("fsdp"),
        P("fsdp", None),
        P("fsdp", None),
        P("fsdp", None),
        P("fsdp", None),
        P("fsdp", "expert", None),
        P("fsdp", "expert", None),
        P("fsdp", "expert", None),
    )
    out_specs = (
        P("expert", "fsdp", None),
        P("expert", "fsdp", None),
        P("fsdp"),
        P("fsdp", None),
        P("fsdp", None),
        P("fsdp", None),
        P("fsdp", None),
        P("fsdp"),
        P("fsdp", None),
        P("fsdp", None),
        P("fsdp", None),
        P("fsdp", None),
        P("fsdp", "expert", None),
        P("fsdp", "expert", None),
        P("fsdp", "expert", None),
    )
    return jax.shard_map(
        per_device, mesh=mesh, in_specs=in_specs, out_specs=out_specs, check_vma=False
    )
```

```python
import jax
import jax.numpy as jnp
from jax import lax
from jax.experimental import pallas as pl
from jax.experimental.pallas import tpu as pltpu
from jax.sharding import PartitionSpec as P

D = 2048
H = 16
KV = 4
HD = 128
FF = 1408
SH = 2816
TOPK = 2
TOK = 128
LENGTH = 2048
SEQS = 8
EXPERTS = 8
FSDP = 16
ALL = SEQS * TOK
CAP = 42
SLOTS = SEQS * CAP
SH_ROWS = SH // FSDP
SH_PART = SH_ROWS // EXPERTS
SH_PAD = 24
SH_OWN = FSDP * SH_PAD
QBLOCK = 256

eps_norm = 1e-06
rope_base = 600000.0
masked_fill = -1e30
highest = lax.Precision.HIGHEST
low = jnp.bfloat16
wide = jnp.float32


def shift_pairs(step):
    return [(z * 2 + c, ((z + step) % 4) * 2 + c) for z in range(4) for c in range(2)]


core_pairs = [(z * 2 + c, z * 2 + 1 - c) for z in range(4) for c in range(2)]


def move_z(block, step):
    return lax.ppermute(block, "expert", shift_pairs(step))


def swap_core(block):
    return lax.ppermute(block, "expert", core_pairs)


def together(*values):
    return lax.optimization_barrier(values)


TOP = TOK // 2


def first_pieces(block):
    return move_z(block, 1), move_z(block, -1)


def other_pieces(block, below, above):
    upper, lower = move_z(below[:TOP], 1), move_z(above[TOP:], -1)
    mine = [block, above, upper, lower, below]
    return mine + [swap_core(piece) for piece in mine]


def gather_pieces(block):
    return other_pieces(block, *first_pieces(block))


PIECES = [(4 * side + block, start) for side in (0, 1) for block, start in ((0, 0), (1, 0), (2, 0), (2, TOP), (3, 0))]


def place_pieces(pieces):
    whole = [pieces[0], pieces[1], jnp.concatenate(pieces[2:4], axis=0), pieces[4]]
    whole += [pieces[5], pieces[6], jnp.concatenate(pieces[7:9], axis=0), pieces[9]]
    return jnp.concatenate(whole, axis=0)


def load_pieces(refs, rows_ref, extra_ref, sems):
    copies = []
    for index, (ref, (block, start)) in enumerate(zip(refs, PIECES)):
        count = min(ref.shape[0], TOK - start)
        copies.append(
            pltpu.make_async_copy(
                ref.at[pl.ds(0, count), :], rows_ref.at[pl.ds(block * TOK + start, count), :], sems.at[2 * index]
            )
        )
        if extra_ref is not None and ref.shape[0] > count:
            copies.append(
                pltpu.make_async_copy(
                    ref.at[pl.ds(count, 16), :], extra_ref.at[pl.ds(block * 16, 16), :], sems.at[2 * index + 1]
                )
            )
    for copy in copies:
        copy.start()
    return copies


def scatter_start(mine, received):
    chip = mine.reshape(4, TOK, -1).astype(wide) + received.reshape(4, TOK, -1).astype(wide)
    from_below = move_z(chip[2, :TOP].astype(low), 1)
    from_above = move_z(chip[2, TOP:].astype(low), -1)
    to_above = jnp.concatenate([chip[1, :TOP] + from_below.astype(wide), chip[1, TOP:]], axis=0)
    to_below = jnp.concatenate([chip[3, :TOP], chip[3, TOP:] + from_above.astype(wide)], axis=0)
    return chip[0], to_above.astype(low), to_below.astype(low)


def scatter_end(own, first, second):
    return own + first.astype(wide) + second.astype(wide)


def scatter_rows(mine, other):
    own, to_above, to_below = scatter_start(mine, swap_core(other))
    return scatter_end(own, move_z(to_above, 1), move_z(to_below, -1))


def exchange(mine, other):
    got = swap_core(other)
    chip = jnp.stack([mine[1:], got[1:]], axis=1)
    return mine[0], got[0], *[move_z(chip[step - 1], step) for step in (1, 2, 3)]


def source_owners(expert):
    return jnp.stack([((expert // 2 - index // 2) % 4) * 2 + ((expert % 2) ^ (index % 2)) for index in range(EXPERTS)])


def relative_owner(expert, block):
    return ((expert // 2 + block % 4) % 4) * 2 + ((expert % 2) ^ (block // 4))


def pack_tiles(block):
    rows, columns = block.shape[0] // 8, block.shape[1] // 128
    tiles = block.reshape(rows, 8, columns, 128).transpose(2, 1, 0, 3)
    return tiles.reshape(columns * 8, rows * 128)


def unpack_tiles(block, count):
    rows, columns = block.shape[1] // 128, block.shape[0] // (8 * count)
    tiles = block.reshape(count, columns, 8, rows, 128).transpose(0, 3, 2, 1, 4)
    return tiles.reshape(count * rows * 8, columns * 128)


def product(left, right, contract):
    return lax.dot_general(left, right, (contract, ((), ())), preferred_element_type=wide)


def mm(left, right):
    return product(left, right, ((1,), (0,)))


def mm_t(left, right):
    return product(left, right, ((1,), (1,)))


def t_mm(left, right):
    return product(left, right, ((0,), (0,)))


def segment_columns(seg_blocks_ref):
    return seg_blocks_ref[...].T


def block_scores(qkv_ref, seg_row_ref, columns, start, reach):
    query = qkv_ref[pl.ds(start, QBLOCK), 0:HD]
    key = qkv_ref[pl.ds(0, reach), HD : 2 * HD]
    scores = mm_t(query, key) * HD ** (-0.5)
    query_pos = start + lax.broadcasted_iota(jnp.int32, (QBLOCK, reach), 0)
    key_pos = lax.broadcasted_iota(jnp.int32, (QBLOCK, reach), 1)
    block = start // TOK
    column = jnp.concatenate([columns[:, block : block + 1], columns[:, block + 1 : block + 2]], axis=0)
    same = column == seg_row_ref[:, pl.ds(0, reach)]
    return jnp.where(same & (query_pos >= key_pos), scores, masked_fill)


def attend_kernel(qkv_ref, seg_row_ref, seg_blocks_ref, mixed_ref, total_ref):
    columns = segment_columns(seg_blocks_ref)
    for block in range(LENGTH // QBLOCK):
        start, reach = block * QBLOCK, (block + 1) * QBLOCK
        scores = block_scores(qkv_ref, seg_row_ref, columns, start, reach)
        largest = jnp.max(scores, axis=-1, keepdims=True)
        exponent = jnp.exp(scores - largest)
        totals = jnp.sum(exponent, axis=-1, keepdims=True)
        probs_low = (exponent * (1.0 / totals)).astype(low)
        value = qkv_ref[pl.ds(0, reach), 2 * HD : 3 * HD]
        mixed_ref[pl.ds(start, QBLOCK), :] = mm(probs_low, value).astype(low)
        total_ref[pl.ds(start, QBLOCK), :] = largest + jnp.log(totals)


def attend_back_kernel(
    qkv_ref, grad_ref, total_ref, seg_row_ref, seg_blocks_ref, cos_ref, sin_ref, out_ref, key_acc, value_acc
):
    columns = segment_columns(seg_blocks_ref)
    key_acc[...] = jnp.zeros_like(key_acc)
    value_acc[...] = jnp.zeros_like(value_acc)

    def turn_back(value, rows):
        return value * cos_ref[rows, :] + pltpu.roll(value, HD // 2, 1) * sin_ref[rows, :]

    for block in range(LENGTH // QBLOCK):
        start, reach = block * QBLOCK, (block + 1) * QBLOCK
        rows, span = pl.ds(start, QBLOCK), pl.ds(0, reach)
        scores = block_scores(qkv_ref, seg_row_ref, columns, start, reach)
        probs = jnp.exp(scores - total_ref[rows, :])
        grad = grad_ref[rows, :]
        grad_probs = mm_t(grad, qkv_ref[span, 2 * HD : 3 * HD])
        inner = jnp.sum(probs * grad_probs, axis=-1, keepdims=True)
        grad_scores = (probs * (grad_probs - inner)).astype(low)
        scale = HD ** (-0.5)
        grad_query = mm(grad_scores, qkv_ref[span, HD : 2 * HD]) * scale
        out_ref[rows, 0:HD] = turn_back(grad_query, rows).astype(low)
        key_acc[span, :] += t_mm(grad_scores, qkv_ref[rows, 0:HD]) * scale
        value_acc[span, :] += t_mm(probs.astype(low), grad)
    for block in range(LENGTH // QBLOCK):
        rows = pl.ds(block * QBLOCK, QBLOCK)
        out_ref[rows, HD : 2 * HD] = turn_back(key_acc[rows, :], rows).astype(low)
        out_ref[rows, 2 * HD : 3 * HD] = value_acc[rows, :].astype(low)


vmem = pl.BlockSpec(memory_space=pltpu.VMEM)
smem = pl.BlockSpec(memory_space=pltpu.SMEM)
anywhere = pl.BlockSpec(memory_space=pl.ANY)
kernel_params = pltpu.CompilerParams(vmem_limit_bytes=48 * 1024 * 1024)


def attend(qkv, seg_row, seg_blocks):
    return pl.pallas_call(
        attend_kernel,
        out_shape=(
            jax.ShapeDtypeStruct((LENGTH, HD), low),
            jax.ShapeDtypeStruct((LENGTH, 1), wide),
        ),
        in_specs=[vmem] * 3,
        out_specs=(vmem, vmem),
        compiler_params=kernel_params,
        cost_estimate=pl.CostEstimate(
            flops=2 * LENGTH * LENGTH * HD, bytes_accessed=4 * LENGTH * HD * 2, transcendentals=LENGTH * LENGTH // 2
        ),
        name="attend",
    )(qkv, seg_row, seg_blocks)


def attend_back(qkv, grad, total, seg_row, seg_blocks, cos_all, sin_all):
    return pl.pallas_call(
        attend_back_kernel,
        out_shape=jax.ShapeDtypeStruct((LENGTH, 3 * HD), low),
        in_specs=[vmem] * 7,
        out_specs=vmem,
        scratch_shapes=[pltpu.VMEM((LENGTH, HD), wide), pltpu.VMEM((LENGTH, HD), wide)],
        compiler_params=kernel_params,
        cost_estimate=pl.CostEstimate(
            flops=5 * LENGTH * LENGTH * HD, bytes_accessed=8 * LENGTH * HD * 2, transcendentals=LENGTH * LENGTH // 2
        ),
        name="attend_back",
    )(qkv, grad, total, seg_row, seg_blocks, cos_all, sin_all)


ROWS = 256
FF_TILES = [(start, min(256, FF - start)) for start in range(0, FF, 256)]
PACK = 3 * SH_OWN + 3 * FF


def params(mebibytes):
    return pltpu.CompilerParams(vmem_limit_bytes=mebibytes * 1024 * 1024)


def cost(flops, moved, special=0):
    return pl.CostEstimate(flops=int(flops), bytes_accessed=int(moved), transcendentals=int(special))


def project_kernel(*refs):
    pieces, (attn_ref, cos_ref, sin_ref) = refs[:10], refs[10:13]
    normed_ref, sent_ref, factor_ref, gains_ref, ids_ref, hidden, sems = refs[13:]
    copies = load_pieces(pieces, hidden, ids_ref, sems)
    pick = lax.broadcasted_iota(jnp.int32, (16, TOK), 0) == lax.broadcasted_iota(jnp.int32, (16, TOK), 1)
    gains_ref[...] = mm_t(pick.astype(wide).astype(low), attn_ref[:, 768:896])
    for copy in copies:
        copy.wait()
    gain = gains_ref[0:1, :]

    @pl.loop(0, ALL // ROWS)
    def step(index):
        rows = pl.ds(index * ROWS, ROWS)
        values = hidden[rows, :].astype(wide)
        factor = lax.rsqrt(jnp.mean(values * values, axis=-1, keepdims=True) + eps_norm)
        factor_ref[rows, :] = factor
        normed = (values * factor * gain).astype(low)
        normed_ref[rows, :] = normed
        raw = mm(normed, attn_ref[:, 0:512])

        def turn(value):
            return (value * cos_ref[...] + pltpu.roll(value, HD // 2, 1) * sin_ref[...]).astype(low)

        key = turn(raw[:, 2 * HD : 3 * HD])
        value = raw[:, 3 * HD :].astype(low)
        for head in range(2):
            query = turn(raw[:, head * HD : (head + 1) * HD])
            for part in range(2):
                place = pl.ds(index * 4 * TOK + (2 * part + head) * TOK, TOK)
                within = slice(part * TOK, (part + 1) * TOK)
                sent_ref[place, 0:HD] = query[within]
                sent_ref[place, HD : 2 * HD] = key[within]
                sent_ref[place, 2 * HD : 3 * HD] = value[within]


def project(pieces, attn_all, cos_two, sin_two):
    return pl.pallas_call(
        project_kernel,
        out_shape=(
            jax.ShapeDtypeStruct((ALL, D), low),
            jax.ShapeDtypeStruct((LENGTH, 3 * HD), low),
            jax.ShapeDtypeStruct((ALL, 1), wide),
            jax.ShapeDtypeStruct((16, D), wide),
            jax.ShapeDtypeStruct((SEQS * 16, D), low),
        ),
        in_specs=[anywhere] * 10 + [vmem] * 3,
        out_specs=tuple([vmem] * 5),
        scratch_shapes=[pltpu.VMEM((ALL, D), low), pltpu.SemaphoreType.DMA((20,))],
        compiler_params=params(40),
        cost_estimate=cost(2.2e9, 16e6),
        name="project",
    )(*pieces, attn_all, cos_two, sin_two)


def mix_back_kernel(*refs):
    pieces, weight_ref = refs[:10], refs[10]
    grad_ref, extra_ref, sent_ref, sems = refs[11:]
    for copy in load_pieces(pieces, grad_ref, extra_ref, sems):
        copy.wait()

    @pl.loop(0, ALL // ROWS)
    def step(index):
        grad = mm_t(grad_ref[pl.ds(index * ROWS, ROWS), :], weight_ref[...]).astype(low)
        for part in range(2):
            for head in range(2):
                place = pl.ds(index * 4 * TOK + (2 * part + head) * TOK, TOK)
                sent_ref[place, :] = grad[part * TOK : (part + 1) * TOK, head * HD : (head + 1) * HD]


def mix_back(pieces, weight):
    return pl.pallas_call(
        mix_back_kernel,
        out_shape=(
            jax.ShapeDtypeStruct((ALL, D), low),
            jax.ShapeDtypeStruct((SEQS * 16, D), low),
            jax.ShapeDtypeStruct((LENGTH, HD), low),
        ),
        in_specs=[anywhere] * 10 + [vmem],
        out_specs=(vmem, vmem, vmem),
        scratch_shapes=[pltpu.SemaphoreType.DMA((20,))],
        compiler_params=params(40),
        cost_estimate=cost(1.1e9, 10e6),
        name="mix_back",
    )(*pieces, weight)


def collect_kernel(core_ref, grads_ref, query_ref, mine_ref, other_ref):
    first = core_ref[0] == 0

    @pl.loop(0, SEQS)
    def step(index):
        rows = pl.ds(index * TOK, TOK)
        swapped = pl.ds(((index + SEQS // 2) % SEQS) * TOK, TOK)
        one = grads_ref[pl.ds(index * 2 * TOK, TOK), :]
        two = grads_ref[pl.ds(index * 2 * TOK + TOK, TOK), :]
        query_ref[rows, 0:HD] = one[:, :HD]
        query_ref[rows, HD : 2 * HD] = two[:, :HD]
        total = one[:, HD:].astype(wide) + two[:, HD:].astype(wide)
        lower = jnp.concatenate([total[:, : HD // 2], total[:, HD : HD + HD // 2]], axis=1)
        upper = jnp.concatenate([total[:, HD // 2 : HD], total[:, HD + HD // 2 :]], axis=1)
        mine_ref[rows, :] = jnp.where(first, lower, upper)
        other_ref[swapped, :] = jnp.where(first, upper, lower).astype(low)


def collect(core, grads):
    return pl.pallas_call(
        collect_kernel,
        out_shape=(
            jax.ShapeDtypeStruct((ALL, 2 * HD), low),
            jax.ShapeDtypeStruct((ALL, HD), wide),
            jax.ShapeDtypeStruct((ALL, HD), low),
        ),
        in_specs=[smem, vmem],
        out_specs=(vmem, vmem, vmem),
        compiler_params=params(32),
        cost_estimate=cost(1e6, 4e6),
        name="collect",
    )(core, grads)


def qkv_weights_kernel(normed_ref, query_ref, mine_ref, got_ref, out_ref, grad_ref):
    grad_ref[:, 0 : 2 * HD] = query_ref[...]
    grad_ref[:, 2 * HD : 3 * HD] = (mine_ref[...] + got_ref[...].astype(wide)).astype(low)

    @pl.loop(0, D // ROWS)
    def step(index):
        columns = pl.ds(pl.multiple_of(index * ROWS, ROWS), ROWS)
        out_ref[pl.ds(index * ROWS, ROWS), :] = t_mm(normed_ref[:, columns], grad_ref[...]).astype(low)


def qkv_weights(normed, query, mine, got):
    return pl.pallas_call(
        qkv_weights_kernel,
        out_shape=(jax.ShapeDtypeStruct((D, 3 * HD), low), jax.ShapeDtypeStruct((ALL, 3 * HD), low)),
        in_specs=[vmem] * 4,
        out_specs=(vmem, vmem),
        compiler_params=params(32),
        cost_estimate=cost(1.6e9, 8e6),
        name="qkv_weights",
    )(normed, query, mine, got)


def finish_kernel(shards_ref, query_ref, key_ref, value_ref, out_ref, gain_ref):
    gain = jnp.zeros((TOK, TOK), wide)
    for source in range(EXPERTS):
        query_ref[:, source * 256 : (source + 1) * 256] = shards_ref[source, :, 0:256].astype(wide)
        out_ref[:, source * 256 : (source + 1) * 256] = shards_ref[source, :, 384:640].astype(wide)
        gain = gain + shards_ref[source, :, 640:768].astype(wide)
    for pair in range(KV):
        one = shards_ref[2 * pair, :, 256:384].astype(wide)
        two = shards_ref[2 * pair + 1, :, 256:384].astype(wide)
        columns = slice(pair * HD, (pair + 1) * HD)
        key_ref[:, columns] = jnp.concatenate([one[:, : HD // 2], two[:, : HD // 2]], axis=1)
        value_ref[:, columns] = jnp.concatenate([one[:, HD // 2 :], two[:, HD // 2 :]], axis=1)
    gain_ref[...] = jnp.sum(gain, axis=1, keepdims=True)


def finish(shards):
    widths = (H * HD, KV * HD, KV * HD, H * HD, 1)
    return pl.pallas_call(
        finish_kernel,
        out_shape=tuple(jax.ShapeDtypeStruct((TOK, width), wide) for width in widths),
        in_specs=[vmem],
        out_specs=tuple([vmem] * 5),
        compiler_params=params(32),
        cost_estimate=cost(1e6, 4e6),
        name="finish",
    )(shards)


def halves(value):
    upper = value.astype(low)
    return upper, (value - upper.astype(wide)).astype(low)


def silu_parts(gate_value):
    sig = 1.0 / (1.0 + jnp.exp(-gate_value))
    return sig, gate_value * sig


def swiglu_back(sig, act, up_value, grad):
    return (grad * up_value * (sig + act * (1.0 - sig))).astype(low), (grad * act).astype(low)


def ffn_kernel(*refs):
    expert_ref, slots_hbm, slots_t_hbm, routes_ref, router_hbm = refs[:5]
    pieces, (cot_hbm, pack_ref, shared_down_ref, down_ref) = refs[5:15], refs[15:19]
    grad_mine, grad_other, gates_ref = refs[19:22]
    outs = refs[22:29]
    normed_ref, cot_ref, grad_ref = refs[29:32]
    kept = refs[32:39]
    hidden_s, grad_s, incoming, hidden_e, gated, grad_rows, grad_e = kept
    w_in_s, w_down_s, w_in, w_down, slots_ref, slots_t_ref = refs[39:45]
    raw, gate_parts, grad_in, piece_sems, sems, out_sems = refs[45:]
    base = 3 * SH_OWN
    piece_copies = load_pieces(pieces, normed_ref, None, piece_sems)
    copies = [
        pltpu.make_async_copy(pack_ref.at[:, pl.ds(0, 2 * SH_OWN)], w_in_s.at[:, pl.ds(0, 2 * SH_OWN)], sems.at[0]),
        pltpu.make_async_copy(router_hbm, w_in_s.at[:, pl.ds(2 * SH_OWN, 128)], sems.at[1]),
        pltpu.make_async_copy(cot_hbm, cot_ref, sems.at[2]),
        pltpu.make_async_copy(shared_down_ref, w_down_s, sems.at[3]),
        pltpu.make_async_copy(slots_hbm, slots_ref, sems.at[4]),
        pltpu.make_async_copy(pack_ref.at[:, pl.ds(base, 2 * FF)], w_in, sems.at[5]),
        pltpu.make_async_copy(down_ref, w_down, sems.at[6]),
        pltpu.make_async_copy(slots_t_hbm, slots_t_ref, sems.at[7]),
    ]
    for copy in copies:
        copy.start()

    def send(index):
        copy = pltpu.make_async_copy(kept[index], outs[index], out_sems.at[index])
        copy.start()
        return copy

    expert = expert_ref[0]
    lane = lax.broadcasted_iota(jnp.int32, (ROWS, 128), 1)
    for copy in piece_copies + copies[:4]:
        copy.wait()
    for step in range(ALL // ROWS):
        rows = pl.ds(step * ROWS, ROWS)
        both = mm(normed_ref[rows, :], w_in_s[...])
        sig, act = silu_parts(both[:, :SH_OWN])
        up = both[:, SH_OWN : 2 * SH_OWN]
        hidden_s[rows, :] = (act * up).astype(low)
        grad_hidden = mm_t(cot_ref[rows, :], w_down_s[...])
        grad_gate, grad_up = swiglu_back(sig, act, up, grad_hidden)
        grad_s[rows, 0:SH_OWN] = grad_gate
        grad_s[rows, SH_OWN : 2 * SH_OWN] = grad_up
        logits = both[:, 2 * SH_OWN :]
        first, second = routes_ref[rows, 0:1], routes_ref[rows, 1:2]
        chosen_first = jnp.sum(jnp.where(lane == first + 2, logits, 0.0), axis=1, keepdims=True)
        chosen_second = jnp.sum(jnp.where(lane == second + 2, logits, 0.0), axis=1, keepdims=True)
        gate_first = 1.0 / (1.0 + jnp.exp(chosen_second - chosen_first))
        gate_second = 1.0 / (1.0 + jnp.exp(chosen_first - chosen_second))
        here = jnp.where(first == expert, gate_first, 0.0) + jnp.where(second == expert, gate_second, 0.0)
        upper, lower = halves(here)
        parts = jnp.where(lane == 0, upper.astype(wide), 0.0) + jnp.where(lane == 1, lower.astype(wide), 0.0)
        gate_parts[rows, :] = parts.astype(low)
        if step == 0:
            both_gates = jnp.where(lane == 0, gate_first, 0.0) + jnp.where(lane == 1, gate_second, 0.0)
            gates_ref[...] = both_gates[:TOK]
    sent = [send(0), send(1)]
    copies[4].wait()
    for step in range(D // ROWS):
        columns = pl.ds(step * ROWS, ROWS)
        incoming[:, columns] = mm(slots_ref[...], normed_ref[:, columns]).astype(low)
        grad_rows[:, columns] = mm(slots_ref[...], cot_ref[:, columns]).astype(low)
    slot_parts = mm(slots_ref[...], gate_parts[...])
    slot_gate = slot_parts[:, 0:1] + slot_parts[:, 1:2]
    sent.append(send(2))
    copies[5].wait()
    for step in range(2 * FF // ROWS):
        columns = pl.ds(step * ROWS, ROWS)
        raw[:, columns] = mm(incoming[...], w_in[:, columns])
    for start, width in FF_TILES:
        gate, up = raw[:, start : start + width], raw[:, FF + start : FF + start + width]
        hidden_e[:, start : start + width] = (silu_parts(gate)[1] * up).astype(low)
    sent.append(send(3))
    copies[6].wait()
    slot_grad = jnp.zeros((SLOTS, 1), wide)
    for step in range(D // ROWS):
        columns = pl.ds(step * ROWS, ROWS)
        rows = mm(hidden_e[...], w_down[:, columns]).astype(low).astype(wide)
        cot = grad_rows[:, columns].astype(wide)
        gated[:, columns] = (rows * slot_gate).astype(low)
        grad_rows[:, columns] = (cot * slot_gate).astype(low)
        slot_grad = slot_grad + jnp.sum(rows * cot, axis=1, keepdims=True)
    sent += [send(4), send(5)]
    for start, width in FF_TILES:
        grad_hidden = mm_t(grad_rows[...], w_down[pl.ds(start, width), :])
        sig, act = silu_parts(raw[:, start : start + width])
        grad_gate, grad_up = swiglu_back(sig, act, raw[:, FF + start : FF + start + width], grad_hidden)
        grad_e[:, start : start + width] = grad_gate
        grad_e[:, FF + start : FF + start + width] = grad_up
    sent.append(send(6))
    for step in range(D // ROWS):
        columns = pl.ds(step * ROWS, ROWS)
        grad_in[:, columns] = mm_t(grad_e[...], w_in[columns, :]).astype(low)
    upper, lower = halves(slot_grad)
    slot_lane = lax.broadcasted_iota(jnp.int32, (SLOTS, 128), 1)
    slot_parts = (
        jnp.where(slot_lane == expert, upper.astype(wide), 0.0)
        + jnp.where(slot_lane == expert + 8, lower.astype(wide), 0.0)
    ).astype(low)
    copies[7].wait()
    half = ALL // 2
    for side, target in ((1, grad_other), (0, grad_mine)):
        for step in range(half // ROWS):
            rows = pl.ds(side * half + step * ROWS, ROWS)
            for tile in range(D // 512):
                columns = pl.ds(tile * 512, 512)
                grad_ref[rows, columns] = (
                    mm_t(grad_s[rows, :], w_in_s[columns, 0 : 2 * SH_OWN])
                    + mm(slots_t_ref[rows, :], grad_in[:, columns])
                ).astype(low)
            grad_ref[rows, D : D + 128] = mm(slots_t_ref[rows, :], slot_parts).astype(low)
        copy = pltpu.make_async_copy(grad_ref.at[pl.ds(side * half, half), :], target, sems.at[8 + side])
        copy.start()
        sent.append(copy)
    for copy in sent:
        copy.wait()


def ffn(expert, slots, slots_t, routes, router, pieces, cot, pack, shared_down, down):
    kept = [(ALL, SH_OWN), (ALL, 2 * SH_OWN), (SLOTS, D), (SLOTS, FF), (SLOTS, D), (SLOTS, D), (SLOTS, 2 * FF)]
    grads = [(ALL // 2, D + 128)] * 2
    return pl.pallas_call(
        ffn_kernel,
        out_shape=tuple(
            [jax.ShapeDtypeStruct(shape, low) for shape in grads]
            + [jax.ShapeDtypeStruct((TOK, 128), wide)]
            + [jax.ShapeDtypeStruct(shape, low) for shape in kept]
        ),
        in_specs=[smem, anywhere, anywhere, vmem] + [anywhere] * 15,
        out_specs=tuple([anywhere] * 2 + [vmem] + [anywhere] * 7),
        scratch_shapes=[pltpu.VMEM((ALL, D), low), pltpu.VMEM((ALL, D), low), pltpu.VMEM((ALL, D + 128), low)]
        + [pltpu.VMEM(shape, low) for shape in kept]
        + [
            pltpu.VMEM((D, 2 * SH_OWN + 128), low),
            pltpu.VMEM((SH_OWN, D), low),
            pltpu.VMEM((D, 2 * FF), low),
            pltpu.VMEM((FF, D), low),
            pltpu.VMEM((SLOTS, ALL), low),
            pltpu.VMEM((ALL, SLOTS), low),
            pltpu.VMEM((SLOTS, 2 * FF), wide),
            pltpu.VMEM((ALL, 128), low),
            pltpu.VMEM((SLOTS, D), low),
            pltpu.SemaphoreType.DMA((20,)),
            pltpu.SemaphoreType.DMA((10,)),
            pltpu.SemaphoreType.DMA((7,)),
        ],
        compiler_params=params(60),
        cost_estimate=cost(27e9, 50e6, 1e6),
        name="ffn",
    )(expert, slots, slots_t, routes, router, *pieces, cot, pack, shared_down, down)


def pack_rows(block):
    count, width = block.shape[0] // 8, block.shape[1] // 128
    return jnp.concatenate(
        [
            jnp.concatenate(
                [block[8 * i : 8 * i + 8, 128 * j : 128 * j + 128] for i in range(count)], axis=1
            )
            for j in range(width)
        ],
        axis=0,
    )


def slab(buffer, out_ref, sems, step, start):
    return pltpu.make_async_copy(
        buffer.at[step % 2],
        out_ref.at[pl.ds(step * ROWS, ROWS), pl.ds(start, buffer.shape[2])],
        sems.at[step % 2],
    )


def weight_slabs(tokens_ref, grad_ref, down, out_ref, buffer, sems, start):
    width = grad_ref.shape[1]
    count = width // 2 // FSDP
    for step in range(D // ROWS):
        slot = step % 2
        if step >= 2:
            slab(buffer, out_ref, sems, step - 2, start).wait()
        buffer[slot, :, 0:width] = t_mm(tokens_ref[:, pl.ds(step * ROWS, ROWS)], grad_ref[...]).astype(low)
        for part in range(ROWS // TOK):
            place = step * (ROWS // TOK) + part
            packed = pack_rows(down[pl.ds(place * count, count), :]).astype(low)
            buffer[slot, part * TOK : (part + 1) * TOK, width:] = packed
        slab(buffer, out_ref, sems, step, start).start()
    for step in (D // ROWS - 2, D // ROWS - 1):
        slab(buffer, out_ref, sems, step, start).wait()


def expert_weights_kernel(incoming_ref, hidden_ref, grad_rows_ref, grad_ref, out_ref, buffer, down, sems):
    for tile in range(D // ROWS):
        part = pl.ds(tile * ROWS, ROWS)
        down[:, part] = t_mm(hidden_ref[...], grad_rows_ref[:, part])
    weight_slabs(incoming_ref, grad_ref, down, out_ref, buffer, sems, 3 * SH_OWN)


def expert_weights(*operands):
    return pl.pallas_call(
        expert_weights_kernel,
        out_shape=jax.ShapeDtypeStruct((D, PACK), low),
        in_specs=[vmem] * 4,
        out_specs=anywhere,
        scratch_shapes=[
            pltpu.VMEM((2, ROWS, 3 * FF), low),
            pltpu.VMEM((FF, D), wide),
            pltpu.SemaphoreType.DMA((2,)),
        ],
        compiler_params=params(48),
        cost_estimate=cost(6e9, 24e6),
        name="expert_weights",
    )(*operands)


def shared_weights_kernel(*refs):
    pieces, cot_ref, hidden_ref, grad_ref = refs[1:11], refs[11], refs[12], refs[13]
    out_ref, normed_ref, buffer, down, piece_sems, sems = refs[14:]
    copies = load_pieces(pieces, normed_ref, None, piece_sems)
    for tile in range(D // ROWS):
        part = pl.ds(tile * ROWS, ROWS)
        down[:, part] = t_mm(hidden_ref[...], cot_ref[:, part])
    for copy in copies:
        copy.wait()
    weight_slabs(normed_ref, grad_ref, down, out_ref, buffer, sems, 0)


def shared_weights(pack, pieces, cot, hidden, grad):
    return pl.pallas_call(
        shared_weights_kernel,
        out_shape=(jax.ShapeDtypeStruct((D, PACK), low), jax.ShapeDtypeStruct((ALL, D), low)),
        in_specs=[anywhere] * 11 + [vmem] * 3,
        out_specs=(anywhere, vmem),
        scratch_shapes=[
            pltpu.VMEM((2, ROWS, 3 * SH_OWN), low),
            pltpu.VMEM((SH_OWN, D), wide),
            pltpu.SemaphoreType.DMA((20,)),
            pltpu.SemaphoreType.DMA((2,)),
        ],
        input_output_aliases={0: 0},
        compiler_params=params(48),
        cost_estimate=cost(5e9, 18e6),
        name="shared_weights",
    )(pack, *pieces, cot, hidden, grad)


def out_rows_kernel(place_ref, *refs):
    parts, out_ref, sems = refs[:5], refs[5], refs[6]
    copies = []
    for index in range(EXPERTS):
        step, side = index // 2, index % 2
        source = parts[step + 1].at[side] if step else parts[side]
        columns = pl.ds(pl.multiple_of(place_ref[index] * 256, 256), 256)
        copies.append(pltpu.make_async_copy(source, out_ref.at[:, columns], sems.at[index]))
    for copy in copies:
        copy.start()
    for copy in copies:
        copy.wait()


def out_rows(places, parts):
    return pl.pallas_call(
        out_rows_kernel,
        out_shape=jax.ShapeDtypeStruct((256, D), low),
        in_specs=[smem] + [anywhere] * 5,
        out_specs=anywhere,
        scratch_shapes=[pltpu.SemaphoreType.DMA((EXPERTS,))],
        cost_estimate=cost(0, 2e6),
        name="out_rows",
    )(places, *parts)


def out_weights_kernel(place_ref, mixed_ref, grad_ref, normed_ref, logits_ref, mine_ref, other_ref, router_ref):
    for index in range(EXPERTS):
        columns = pl.ds(pl.multiple_of(place_ref[index] * 256, 256), 256)
        target = mine_ref if index < 4 else other_ref
        target[index % 4] = t_mm(mixed_ref[...], grad_ref[:, columns]).astype(low)
    router_ref[...] = mm(logits_ref[...], normed_ref[...])


def out_weights(owners, mixed, grad, normed, logits):
    blocks = jax.ShapeDtypeStruct((4, 256, 256), low)
    return pl.pallas_call(
        out_weights_kernel,
        out_shape=(blocks, blocks, jax.ShapeDtypeStruct((2 * EXPERTS, D), wide)),
        in_specs=[smem] + [vmem] * 4,
        out_specs=(vmem, vmem, vmem),
        compiler_params=params(32),
        cost_estimate=cost(1.2e9, 10e6),
        name="out_weights",
    )(owners, mixed, grad, normed, logits)


def back_two_kernel(
    own_ref, first_ref, second_ref, middle_ref, cot_ref, gains_ref, gates_ref, routes_ref, block_ref, grad_ref
):
    total = own_ref[...] + first_ref[...].astype(wide) + second_ref[...].astype(wide)
    lane = lax.broadcasted_iota(jnp.int32, (TOK, 128), 1)
    extra = total[:, D:]
    first, second = routes_ref[:, 0:1], routes_ref[:, 1:2]

    def taken(route):
        return jnp.sum(jnp.where((lane == route) | (lane == route + 8), extra, 0.0), axis=1, keepdims=True)

    gate_first, gate_second = gates_ref[:, 0:1], gates_ref[:, 1:2]
    taken_first, taken_second = taken(first), taken(second)
    inner = gate_first * taken_first + gate_second * taken_second
    chosen_first, chosen_second = gate_first * (taken_first - inner), gate_second * (taken_second - inner)
    logits = jnp.where(lane == first, chosen_first, 0.0) + jnp.where(lane == second, chosen_second, 0.0)
    grad = total[:, :D]
    for index in range(EXPERTS):
        grad = grad + logits[:, index : index + 1] * gains_ref[2 + index : 3 + index, :]
    middle = middle_ref[...]
    factor = lax.rsqrt(jnp.mean(middle * middle, axis=-1, keepdims=True) + eps_norm)
    scaled = grad * gains_ref[1:2, :]
    mean = jnp.mean(scaled * middle, axis=-1, keepdims=True)
    result = cot_ref[...].astype(wide) + factor * scaled - middle * (factor * factor * factor * mean)
    grad_ref[...] = result
    block_ref[0:TOK, :] = result.astype(low)
    gain_upper, gain_lower = halves(jnp.sum(grad * middle * factor, axis=0, keepdims=True))
    upper, lower = halves(logits.T[0:EXPERTS, :])
    rows = [gain_upper, gain_lower]
    upper, lower = upper.astype(wide), lower.astype(wide)
    flat = [upper[index : index + 1, :] for index in range(EXPERTS)] + [
        lower[index : index + 1, :] for index in range(EXPERTS)
    ]
    rows.append(jnp.concatenate(flat, axis=1))
    rows = [row.astype(wide) for row in rows] + [jnp.zeros((13, D), wide)]
    block_ref[TOK : TOK + 16, :] = jnp.concatenate(rows, axis=0).astype(low)


def back_two(*operands):
    return pl.pallas_call(
        back_two_kernel,
        out_shape=(jax.ShapeDtypeStruct((TOK + 16, D), low), jax.ShapeDtypeStruct((TOK, D), wide)),
        in_specs=[vmem] * 8,
        out_specs=(vmem, vmem),
        compiler_params=params(32),
        cost_estimate=cost(1e7, 6e6),
        name="back_two",
    )(*operands)


def norm_factor(values):
    return lax.rsqrt(jnp.mean(values * values, axis=-1, keepdims=True) + eps_norm)


def norm_back(values, factor, gain, grad):
    scaled = grad * gain
    inner = jnp.mean(scaled * values, axis=-1, keepdims=True)
    return factor * scaled - values * (factor * factor * factor * inner)


def per_device(
    hidden_in,
    cotangent,
    segments,
    routes,
    attn_gain,
    w_query,
    w_key,
    w_value,
    w_out,
    ffn_gain,
    w_router,
    shared_gate,
    shared_up,
    shared_down,
    expert_gate,
    expert_up,
    expert_down,
):
    expert = lax.axis_index("expert")
    z, core = expert // 2, expert % 2
    place = lax.axis_index("fsdp")

    misc = jnp.concatenate(
        [attn_gain[:, None], ffn_gain[:, None], w_router, jnp.zeros((TOK, 118), low)], axis=1
    )
    attn_pack = jnp.concatenate(
        [
            lax.dynamic_slice_in_dim(w_query, 256 * expert, 256, 1),
            lax.dynamic_slice_in_dim(w_key, HD * z, HD, 1),
            lax.dynamic_slice_in_dim(w_value, HD * z, HD, 1),
            lax.dynamic_slice_in_dim(w_out, 256 * expert, 256, 1),
            misc,
        ],
        axis=1,
    )
    attn_all = lax.all_gather(attn_pack, "fsdp", axis=0, tiled=True)
    half_in, half_out = SH // 2, SH_OWN // 2
    sel_column = jnp.arange(half_out)
    picked = SH_ROWS * (sel_column // SH_PAD) + SH_PART * expert + sel_column % SH_PAD
    picked = jnp.where(sel_column % SH_PAD < SH_PART, picked, -1)
    select = (jnp.arange(half_in)[:, None] == picked[None, :]).astype(low)
    own_shared = mm(
        jnp.concatenate(
            [shared_gate[:, :half_in], shared_gate[:, half_in:], shared_up[:, :half_in], shared_up[:, half_in:]],
            axis=0,
        ),
        select,
    ).astype(low)
    own_down = jnp.pad(
        lax.dynamic_slice_in_dim(shared_down, SH_PART * expert, SH_PART, 0),
        ((0, SH_PAD - SH_PART), (0, 0)),
    )
    ffn_pack = jnp.concatenate(
        [
            own_shared[:TOK],
            own_shared[TOK : 2 * TOK],
            own_shared[2 * TOK : 3 * TOK],
            own_shared[3 * TOK :],
            pack_tiles(own_down),
            expert_gate[:, 0],
            expert_up[:, 0],
            pack_tiles(expert_down[:, 0]),
        ],
        axis=1,
    )
    ffn_all = lax.all_gather(ffn_pack, "fsdp", axis=0, tiled=True)

    ids = jnp.concatenate(
        [
            segments.astype(low),
            jnp.pad(routes[0].reshape(1, TOK * TOPK), ((0, 0), (0, LENGTH - TOK * TOPK))).astype(low),
            jnp.zeros((14, LENGTH), low),
        ],
        axis=0,
    )
    hidden_pieces = gather_pieces(jnp.concatenate([hidden_in[0], ids], axis=0))

    inverse_freq = rope_base ** (-jnp.arange(HD // 2, dtype=wide) * 2.0 / HD)
    angles = jnp.arange(LENGTH).astype(wide)[:, None] * inverse_freq[None, :]
    cosine, sine = jnp.cos(angles), jnp.sin(angles)
    cos_all = jnp.concatenate([cosine, cosine], axis=1)
    sin_back = jnp.concatenate([sine, -sine], axis=1)
    cos_own = lax.dynamic_slice_in_dim(cos_all, place * TOK, TOK, 0)
    sin_own = -lax.dynamic_slice_in_dim(sin_back, place * TOK, TOK, 0)
    cos_two, sin_two = jnp.concatenate([cos_own, cos_own]), jnp.concatenate([sin_own, sin_own])
    attn_all, cos_two, sin_two, cos_all, sin_back = together(attn_all, cos_two, sin_two, cos_all, sin_back)
    normed_one, sent, factor_one, gains, ids_all = project(hidden_pieces, attn_all, cos_two, sin_two)
    qkv = lax.all_to_all(sent, "fsdp", split_axis=0, concat_axis=0, tiled=True)

    ids_all = ids_all.reshape(SEQS, 16, D)
    seg_row = lax.dynamic_slice_in_dim(ids_all[:, 0].astype(wide), place // 2, 1, 0)
    seg_blocks = jnp.pad(seg_row.reshape(FSDP, TOK), ((0, TOK - FSDP), (0, 0)))
    route_all = ids_all[:, 1, : TOK * TOPK].astype(jnp.int32).reshape(ALL, TOPK)
    hit = jnp.any(route_all == expert, axis=1).astype(wide)
    order = jnp.arange(ALL)
    rank = mm(hit.astype(low)[None, :], (order[:, None] < order[None, :]).astype(low))
    slot_bool = (rank.astype(jnp.int32) == jnp.arange(SLOTS)[:, None]) & (hit > 0.5)[None, :]
    slots = slot_bool.astype(low)
    slots_t = slot_bool.T.astype(low)
    out_columns = attn_all[:, 512:768].reshape(EXPERTS, 256, 256)
    owners = jnp.stack([relative_owner(expert, block) for block in range(EXPERTS)])
    out_blocks = [lax.dynamic_index_in_dim(out_columns, owners[block], 0) for block in range(EXPERTS)]
    out_mine, out_other = jnp.concatenate(out_blocks[:4]), jnp.concatenate(out_blocks[4:])
    out_mine, out_other, _ = together(out_mine, out_other, sent)
    w_out_own = out_rows(source_owners(expert), exchange(out_mine, out_other))
    cot_block, _ = together(cotangent[0], w_out_own)
    cot_pieces = gather_pieces(cot_block)
    router = attn_all[:, 768:896]
    qkv, seg_row, seg_blocks, route_all, slots, slots_t, w_out_own, router = together(
        qkv, seg_row, seg_blocks, route_all, slots, slots_t, w_out_own, router
    )
    mixed_head, log_total = attend(qkv, seg_row, seg_blocks)
    mixed = (
        lax.all_to_all(mixed_head, "fsdp", split_axis=0, concat_axis=0, tiled=True)
        .reshape(SEQS, 2, TOK, HD)
        .transpose(0, 2, 1, 3)
        .reshape(ALL, 2 * HD)
    )
    mixed, *cot_pieces = together(mixed, *cot_pieces)
    cot_all = place_pieces(cot_pieces)
    own_hidden = hidden_in[0].astype(wide)
    half = ALL // 2
    middle = own_hidden + scatter_rows(
        mm(mixed[:half], w_out_own).astype(low), mm(mixed[half:], w_out_own).astype(low)
    )
    factor_two = norm_factor(middle)
    gain_one, gain_two = gains[0:1], gains[1:2]
    normed_block = (middle * factor_two * gain_two).astype(low)

    base = 3 * SH_OWN
    shared_down_w = unpack_tiles(ffn_all[:, 2 * SH_OWN : base], FSDP)
    down_w = unpack_tiles(ffn_all[:, base + 2 * FF :], FSDP)
    below, above = first_pieces(normed_block)
    below, above, shared_down_w, down_w, cot_all = together(below, above, shared_down_w, down_w, cot_all)
    normed_pieces = other_pieces(normed_block, below, above)
    (
        grad_mine,
        grad_other,
        gates,
        hidden_shared,
        grad_shared,
        incoming,
        hidden_expert,
        gated_rows,
        grad_rows,
        grad_expert,
    ) = ffn(
        expert[None], slots, slots_t, route_all, router, normed_pieces, cot_all, ffn_all, shared_down_w, down_w
    )
    own_grad, to_above, to_below = scatter_start(grad_mine, swap_core(grad_other))
    to_above, to_below, incoming, hidden_expert, grad_rows = together(
        to_above, to_below, incoming, hidden_expert, grad_rows
    )
    from_below, from_above = move_z(to_above, 1), move_z(to_below, -1)
    ffn_grads = expert_weights(incoming, hidden_expert, grad_rows, grad_expert)
    from_below, from_above, ffn_grads = together(from_below, from_above, ffn_grads)
    back_block, grad_middle = back_two(
        own_grad, from_below, from_above, middle, cotangent[0], gains, gates, route_all[:TOK]
    )
    back_block, ffn_grads = together(back_block, ffn_grads)
    below, above = first_pieces(back_block)
    ffn_grads, normed_two = shared_weights(ffn_grads, normed_pieces, cot_all, hidden_shared, grad_shared)
    below, above, ffn_grads = together(below, above, ffn_grads)
    back_pieces = other_pieces(back_block, below, above)
    ffn_sums = lax.psum_scatter(ffn_grads, "fsdp", scatter_dimension=0, tiled=True)

    grad_attn, extra, sent_back = mix_back(back_pieces, w_out_own)
    grad_head = lax.all_to_all(sent_back, "fsdp", split_axis=0, concat_axis=0, tiled=True)
    grads_head = attend_back(qkv, grad_head, log_total, seg_row, seg_blocks, cos_all, sin_back)
    grads_qkv = lax.all_to_all(grads_head, "fsdp", split_axis=0, concat_axis=0, tiled=True)

    hidden_shared, gated_rows, slots_t, _ = together(hidden_shared, gated_rows, slots_t, sent_back)
    result_mine = mm(hidden_shared[:half], shared_down_w) + mm(slots_t[:half], gated_rows)
    result_other = mm(hidden_shared[half:], shared_down_w) + mm(slots_t[half:], gated_rows)
    layer_out = (middle + scatter_rows(result_mine.astype(low), result_other.astype(low))).astype(low)

    extra = extra.reshape(SEQS, 16, D)
    gain_two_sum = jnp.sum(extra[:, :2].astype(wide), axis=(0, 1))
    logit_rows = extra[:, 2].reshape(SEQS, 2, EXPERTS, TOK).transpose(1, 2, 0, 3).reshape(2 * EXPERTS, ALL)
    out_mine, out_other, grad_router = out_weights(owners, mixed, grad_attn, normed_two, logit_rows)
    out_parts = exchange(out_mine, out_other)
    out_parts = jnp.concatenate([jnp.stack(out_parts[:2])[None], jnp.stack(out_parts[2:])]).reshape(EXPERTS, 256, 256)
    places = [((z - source // 2) % 4) * 2 + (core ^ (source % 2)) for source in range(EXPERTS)]
    grad_out = jnp.stack([lax.dynamic_index_in_dim(out_parts, where, 0, keepdims=False) for where in places])
    grad_out = grad_out.reshape(FSDP, TOK, 256)
    small_rows = jnp.concatenate(
        [grad_router[:EXPERTS] + grad_router[EXPERTS:], gain_two_sum[None], jnp.zeros((7, D), wide)], axis=0
    )
    small_rows = jnp.pad(small_rows.reshape(16, FSDP, TOK).transpose(1, 0, 2).astype(low), ((0, 0), (0, 0), (0, 128)))
    out_pack = jnp.concatenate([grad_out, small_rows], axis=1).reshape(FSDP * (TOK + 16), 256)
    out_pack, grads_qkv, layer_out = together(out_pack, grads_qkv, layer_out)
    out_sums = sum_blocks(out_pack, TOK + 16)

    grad_query, kv_mine, kv_other = collect(core[None], grads_qkv)
    qkv_grads, grad_qkv = qkv_weights(normed_one, grad_query, kv_mine, swap_core(kv_other))
    qkv_sums = sum_blocks(qkv_grads, TOK)
    ffn_sums, _ = together(ffn_sums, qkv_grads)
    is_first = core == 0
    kv_weight = attn_all[:, 256:512].reshape(D, 2, 2, HD // 2)
    kv_weight = jnp.where(is_first, kv_weight[:, :, 0], kv_weight[:, :, 1]).reshape(D, HD)
    qkv_weight = jnp.concatenate([attn_all[:, :256], kv_weight], axis=1)
    grad_normed_mine = mm_t(grad_qkv[:half], qkv_weight).astype(low)
    grad_normed_other = mm_t(grad_qkv[half:], qkv_weight).astype(low)
    own_grad_one = scatter_rows(grad_normed_mine, grad_normed_other)
    grad_input = grad_middle + norm_back(own_hidden, factor_one[:TOK], gain_one, own_grad_one)

    shared_shards = lax.all_gather(ffn_sums[:, :base], "expert", axis=0)
    half_rows = SH_PAD * EXPERTS * FSDP // 2
    put_row = jnp.arange(half_rows)
    source, within = put_row // half_out, put_row % half_out
    target = SH_ROWS * (within // SH_PAD) + SH_PART * source + within % SH_PAD
    target = jnp.where(within % SH_PAD < SH_PART, target, -1)
    spread = (target[:, None] == jnp.arange(half_in)[None, :]).astype(low)
    gate_up = shared_shards[:, :, : 2 * SH_OWN].reshape(EXPERTS, TOK, 4, half_out)
    gate_up = mm(gate_up.transpose(2, 1, 0, 3).reshape(4 * TOK, EXPERTS * half_out), spread)
    grad_shared_gate = jnp.concatenate([gate_up[:TOK], gate_up[TOK : 2 * TOK]], axis=1)
    grad_shared_up = jnp.concatenate([gate_up[2 * TOK : 3 * TOK], gate_up[3 * TOK :]], axis=1)
    down_parts = unpack_tiles(shared_shards[:, :, 2 * SH_OWN : base].reshape(EXPERTS * TOK, SH_OWN), EXPERTS)
    grad_shared_down = (
        down_parts.reshape(EXPERTS, SH_PAD, D)[:, :SH_PART].reshape(SH_ROWS, D).astype(wide)
    )
    grad_expert_gate = ffn_sums[:, base : base + FF].astype(wide)[:, None]
    grad_expert_up = ffn_sums[:, base + FF : base + 2 * FF].astype(wide)[:, None]
    grad_expert_down = unpack_tiles(ffn_sums[:, base + 2 * FF :], 1).astype(wide)[:, None]

    own_weight = lax.dynamic_slice_in_dim(qkv_weight, place * TOK, TOK, 0)
    gain_part = jnp.sum(qkv_sums * own_weight.astype(wide), axis=1, keepdims=True)
    gain_upper, gain_lower = halves(gain_part / attn_gain.astype(wide)[:, None])
    shards = jnp.concatenate(
        [qkv_sums.astype(low), out_sums[:TOK].astype(low), gain_upper, gain_lower, jnp.zeros((TOK, 126), low)], axis=1
    )
    grad_w_query, grad_w_key, grad_w_value, grad_w_out, grad_attn_gain = finish(
        lax.all_gather(shards, "expert", axis=0)
    )
    return (
        layer_out[None],
        grad_input.astype(low)[None],
        grad_attn_gain[:, 0],
        grad_w_query,
        grad_w_key,
        grad_w_value,
        grad_w_out,
        out_sums[TOK + EXPERTS, :TOK],
        out_sums[TOK : TOK + EXPERTS, :TOK].T,
        grad_shared_gate,
        grad_shared_up,
        grad_shared_down,
        grad_expert_gate,
        grad_expert_up,
        grad_expert_down,
    )


def sum_blocks(block, rows):
    parts = lax.all_to_all(block, "fsdp", split_axis=0, concat_axis=0, tiled=True)
    return jnp.sum(parts.reshape(FSDP, rows, block.shape[1]).astype(wide), axis=0)


def product_wide(left, right):
    return lax.dot_general(
        left, right, (((1,), (0,)), ((), ())), precision=highest, preferred_element_type=wide
    )


def solution(mesh):
    in_specs = (
        P("expert", "fsdp", None),
        P("expert", "fsdp", None),
        P("expert", None),
        P("expert", "fsdp", None),
        P("fsdp"),
        P("fsdp", None),
        P("fsdp", None),
        P("fsdp", None),
        P("fsdp", None),
        P("fsdp"),
        P("fsdp", None),
        P("fsdp", None),
        P("fsdp", None),
        P("fsdp", None),
        P("fsdp", "expert", None),
        P("fsdp", "expert", None),
        P("fsdp", "expert", None),
    )
    out_specs = (
        P("expert", "fsdp", None),
        P("expert", "fsdp", None),
        P("fsdp"),
        P("fsdp", None),
        P("fsdp", None),
        P("fsdp", None),
        P("fsdp", None),
        P("fsdp"),
        P("fsdp", None),
        P("fsdp", None),
        P("fsdp", None),
        P("fsdp", None),
        P("fsdp", "expert", None),
        P("fsdp", "expert", None),
        P("fsdp", "expert", None),
    )
    return jax.shard_map(
        per_device, mesh=mesh, in_specs=in_specs, out_specs=out_specs, check_vma=False
    )
```

```python
import jax
import jax.numpy as jnp
from jax import lax
from jax.experimental import pallas as pl
from jax.experimental.pallas import tpu as pltpu
from jax.sharding import PartitionSpec as P

D = 2048
H = 16
KV = 4
HD = 128
FF = 1408
SH = 2816
TOPK = 2
TOK = 128
LENGTH = 2048
SEQS = 8
EXPERTS = 8
FSDP = 16
ALL = SEQS * TOK
CAP = 42
SLOTS = SEQS * CAP
SH_ROWS = SH // FSDP
SH_PART = SH_ROWS // EXPERTS
SH_PAD = 24
SH_OWN = FSDP * SH_PAD
QBLOCK = 256

eps_norm = 1e-06
rope_base = 600000.0
masked_fill = -1e30
low = jnp.bfloat16
wide = jnp.float32


def shift_pairs(step):
    return [(z * 2 + c, ((z + step) % 4) * 2 + c) for z in range(4) for c in range(2)]


core_pairs = [(z * 2 + c, z * 2 + 1 - c) for z in range(4) for c in range(2)]


def move_z(block, step):
    return lax.ppermute(block, "expert", shift_pairs(step))


def swap_core(block):
    return lax.ppermute(block, "expert", core_pairs)


def together(*values):
    return lax.optimization_barrier(values)


TOP = TOK // 2


def first_pieces(block):
    return move_z(block, 1), move_z(block, -1)


def other_pieces(block, below, above):
    upper, lower = move_z(below[:TOP], 1), move_z(above[TOP:], -1)
    mine = [block, above, upper, lower, below]
    return mine + [swap_core(piece) for piece in mine]


def gather_pieces(block):
    return other_pieces(block, *first_pieces(block))


PIECES = [(4 * side + block, start) for side in (0, 1) for block, start in ((0, 0), (1, 0), (2, 0), (2, TOP), (3, 0))]


def load_pieces(refs, rows_ref, extra_ref, sems):
    copies = []
    for index, (ref, (block, start)) in enumerate(zip(refs, PIECES)):
        count = min(ref.shape[0], TOK - start)
        copies.append(
            pltpu.make_async_copy(
                ref.at[pl.ds(0, count), :], rows_ref.at[pl.ds(block * TOK + start, count), :], sems.at[2 * index]
            )
        )
        if extra_ref is not None and ref.shape[0] > count:
            copies.append(
                pltpu.make_async_copy(
                    ref.at[pl.ds(count, 16), :], extra_ref.at[pl.ds(block * 16, 16), :], sems.at[2 * index + 1]
                )
            )
    for copy in copies:
        copy.start()
    return copies


def scatter_start(mine, received):
    chip = mine.reshape(4, TOK, -1).astype(wide) + received.reshape(4, TOK, -1).astype(wide)
    from_below = move_z(chip[2, :TOP].astype(low), 1)
    from_above = move_z(chip[2, TOP:].astype(low), -1)
    to_above = jnp.concatenate([chip[1, :TOP] + from_below.astype(wide), chip[1, TOP:]], axis=0)
    to_below = jnp.concatenate([chip[3, :TOP], chip[3, TOP:] + from_above.astype(wide)], axis=0)
    return chip[0], to_above.astype(low), to_below.astype(low)


def scatter_end(own, first, second):
    return own + first.astype(wide) + second.astype(wide)


def scatter_rows(mine, other):
    own, to_above, to_below = scatter_start(mine, swap_core(other))
    return scatter_end(own, move_z(to_above, 1), move_z(to_below, -1))


def exchange(mine, other):
    got = swap_core(other)
    chip = jnp.stack([mine[1:], got[1:]], axis=1)
    return mine[0], got[0], *[move_z(chip[step - 1], step) for step in (1, 2, 3)]


def source_owners(expert):
    return jnp.stack([((expert // 2 - index // 2) % 4) * 2 + ((expert % 2) ^ (index % 2)) for index in range(EXPERTS)])


def relative_owner(expert, block):
    return ((expert // 2 + block % 4) % 4) * 2 + ((expert % 2) ^ (block // 4))


def pack_tiles(block):
    rows, columns = block.shape[0] // 8, block.shape[1] // 128
    tiles = block.reshape(rows, 8, columns, 128).transpose(2, 1, 0, 3)
    return tiles.reshape(columns * 8, rows * 128)


def unpack_tiles(block, count):
    rows, columns = block.shape[1] // 128, block.shape[0] // (8 * count)
    tiles = block.reshape(count, columns, 8, rows, 128).transpose(0, 3, 2, 1, 4)
    return tiles.reshape(count * rows * 8, columns * 128)


def product(left, right, contract):
    return lax.dot_general(left, right, (contract, ((), ())), preferred_element_type=wide)


def mm(left, right):
    return product(left, right, ((1,), (0,)))


def mm_t(left, right):
    return product(left, right, ((1,), (1,)))


def t_mm(left, right):
    return product(left, right, ((0,), (0,)))


def segment_columns(seg_blocks_ref):
    return seg_blocks_ref[...].T


def block_scores(qkv_ref, seg_row_ref, columns, start, reach):
    query = qkv_ref[pl.ds(start, QBLOCK), 0:HD]
    key = qkv_ref[pl.ds(0, reach), HD : 2 * HD]
    scores = mm_t(query, key) * HD ** (-0.5)
    query_pos = start + lax.broadcasted_iota(jnp.int32, (QBLOCK, reach), 0)
    key_pos = lax.broadcasted_iota(jnp.int32, (QBLOCK, reach), 1)
    block = start // TOK
    column = jnp.concatenate([columns[:, block : block + 1], columns[:, block + 1 : block + 2]], axis=0)
    same = column == seg_row_ref[:, pl.ds(0, reach)]
    return jnp.where(same & (query_pos >= key_pos), scores, masked_fill)


def attend_kernel(qkv_ref, seg_row_ref, seg_blocks_ref, mixed_ref, total_ref):
    columns = segment_columns(seg_blocks_ref)
    for block in range(LENGTH // QBLOCK):
        start, reach = block * QBLOCK, (block + 1) * QBLOCK
        scores = block_scores(qkv_ref, seg_row_ref, columns, start, reach)
        largest = jnp.max(scores, axis=-1, keepdims=True)
        exponent = jnp.exp(scores - largest)
        totals = jnp.sum(exponent, axis=-1, keepdims=True)
        probs_low = (exponent * (1.0 / totals)).astype(low)
        value = qkv_ref[pl.ds(0, reach), 2 * HD : 3 * HD]
        mixed_ref[pl.ds(start, QBLOCK), :] = mm(probs_low, value).astype(low)
        total_ref[pl.ds(start, QBLOCK), :] = largest + jnp.log(totals)


def attend_back_kernel(
    qkv_ref, grad_ref, total_ref, seg_row_ref, seg_blocks_ref, cos_ref, sin_ref, out_ref, key_acc, value_acc
):
    columns = segment_columns(seg_blocks_ref)
    key_acc[...] = jnp.zeros_like(key_acc)
    value_acc[...] = jnp.zeros_like(value_acc)

    def turn_back(value, rows):
        return value * cos_ref[rows, :] + pltpu.roll(value, HD // 2, 1) * sin_ref[rows, :]

    for block in range(LENGTH // QBLOCK):
        start, reach = block * QBLOCK, (block + 1) * QBLOCK
        rows, span = pl.ds(start, QBLOCK), pl.ds(0, reach)
        scores = block_scores(qkv_ref, seg_row_ref, columns, start, reach)
        probs = jnp.exp(scores - total_ref[rows, :])
        grad = grad_ref[rows, :]
        grad_probs = mm_t(grad, qkv_ref[span, 2 * HD : 3 * HD])
        inner = jnp.sum(probs * grad_probs, axis=-1, keepdims=True)
        grad_scores = (probs * (grad_probs - inner)).astype(low)
        scale = HD ** (-0.5)
        grad_query = mm(grad_scores, qkv_ref[span, HD : 2 * HD]) * scale
        out_ref[rows, 0:HD] = turn_back(grad_query, rows).astype(low)
        key_acc[span, :] += t_mm(grad_scores, qkv_ref[rows, 0:HD]) * scale
        value_acc[span, :] += t_mm(probs.astype(low), grad)
    for block in range(LENGTH // QBLOCK):
        rows = pl.ds(block * QBLOCK, QBLOCK)
        out_ref[rows, HD : 2 * HD] = turn_back(key_acc[rows, :], rows).astype(low)
        out_ref[rows, 2 * HD : 3 * HD] = value_acc[rows, :].astype(low)


vmem = pl.BlockSpec(memory_space=pltpu.VMEM)
smem = pl.BlockSpec(memory_space=pltpu.SMEM)
anywhere = pl.BlockSpec(memory_space=pl.ANY)
kernel_params = pltpu.CompilerParams(vmem_limit_bytes=48 * 1024 * 1024)


def attend(qkv, seg_row, seg_blocks):
    return pl.pallas_call(
        attend_kernel,
        out_shape=(
            jax.ShapeDtypeStruct((LENGTH, HD), low),
            jax.ShapeDtypeStruct((LENGTH, 1), wide),
        ),
        in_specs=[vmem] * 3,
        out_specs=(vmem, vmem),
        compiler_params=kernel_params,
        cost_estimate=pl.CostEstimate(
            flops=2 * LENGTH * LENGTH * HD, bytes_accessed=4 * LENGTH * HD * 2, transcendentals=LENGTH * LENGTH // 2
        ),
        name="attend",
    )(qkv, seg_row, seg_blocks)


def attend_back(qkv, grad, total, seg_row, seg_blocks, cos_all, sin_all):
    return pl.pallas_call(
        attend_back_kernel,
        out_shape=jax.ShapeDtypeStruct((LENGTH, 3 * HD), low),
        in_specs=[vmem] * 7,
        out_specs=vmem,
        scratch_shapes=[pltpu.VMEM((LENGTH, HD), wide), pltpu.VMEM((LENGTH, HD), wide)],
        compiler_params=kernel_params,
        cost_estimate=pl.CostEstimate(
            flops=5 * LENGTH * LENGTH * HD, bytes_accessed=8 * LENGTH * HD * 2, transcendentals=LENGTH * LENGTH // 2
        ),
        name="attend_back",
    )(qkv, grad, total, seg_row, seg_blocks, cos_all, sin_all)


ROWS = 256
FF_TILES = [(start, min(256, FF - start)) for start in range(0, FF, 256)]
PACK = 3 * SH_OWN + 3 * FF


def params(mebibytes):
    return pltpu.CompilerParams(vmem_limit_bytes=mebibytes * 1024 * 1024)


def cost(flops, moved, special=0):
    return pl.CostEstimate(flops=int(flops), bytes_accessed=int(moved), transcendentals=int(special))


def project_kernel(*refs):
    pieces, (attn_ref, cos_ref, sin_ref) = refs[:10], refs[10:13]
    normed_ref, sent_ref, factor_ref, gains_ref, ids_ref, hidden, sems = refs[13:]
    copies = load_pieces(pieces, hidden, ids_ref, sems)
    pick = lax.broadcasted_iota(jnp.int32, (16, TOK), 0) == lax.broadcasted_iota(jnp.int32, (16, TOK), 1)
    gains_ref[...] = mm_t(pick.astype(wide).astype(low), attn_ref[:, 768:896])
    for copy in copies:
        copy.wait()
    gain = gains_ref[0:1, :]

    @pl.loop(0, ALL // ROWS)
    def step(index):
        rows = pl.ds(index * ROWS, ROWS)
        values = hidden[rows, :].astype(wide)
        factor = lax.rsqrt(jnp.mean(values * values, axis=-1, keepdims=True) + eps_norm)
        factor_ref[rows, :] = factor
        normed = (values * factor * gain).astype(low)
        normed_ref[rows, :] = normed
        raw = mm(normed, attn_ref[:, 0:512])

        def turn(value):
            return (value * cos_ref[...] + pltpu.roll(value, HD // 2, 1) * sin_ref[...]).astype(low)

        key = turn(raw[:, 2 * HD : 3 * HD])
        value = raw[:, 3 * HD :].astype(low)
        for head in range(2):
            query = turn(raw[:, head * HD : (head + 1) * HD])
            for part in range(2):
                place = pl.ds(index * 4 * TOK + (2 * part + head) * TOK, TOK)
                within = slice(part * TOK, (part + 1) * TOK)
                sent_ref[place, 0:HD] = query[within]
                sent_ref[place, HD : 2 * HD] = key[within]
                sent_ref[place, 2 * HD : 3 * HD] = value[within]


def project(pieces, attn_all, cos_two, sin_two):
    return pl.pallas_call(
        project_kernel,
        out_shape=(
            jax.ShapeDtypeStruct((ALL, D), low),
            jax.ShapeDtypeStruct((LENGTH, 3 * HD), low),
            jax.ShapeDtypeStruct((ALL, 1), wide),
            jax.ShapeDtypeStruct((16, D), wide),
            jax.ShapeDtypeStruct((SEQS * 16, D), low),
        ),
        in_specs=[anywhere] * 10 + [vmem] * 3,
        out_specs=tuple([vmem] * 5),
        scratch_shapes=[pltpu.VMEM((ALL, D), low), pltpu.SemaphoreType.DMA((20,))],
        compiler_params=params(40),
        cost_estimate=cost(2.2e9, 16e6),
        name="project",
    )(*pieces, attn_all, cos_two, sin_two)


def mix_back_kernel(*refs):
    pieces, weight_ref = refs[:10], refs[10]
    grad_ref, extra_ref, sent_ref, sems = refs[11:]
    for copy in load_pieces(pieces, grad_ref, extra_ref, sems):
        copy.wait()

    @pl.loop(0, ALL // ROWS)
    def step(index):
        grad = mm_t(grad_ref[pl.ds(index * ROWS, ROWS), :], weight_ref[...]).astype(low)
        for part in range(2):
            for head in range(2):
                place = pl.ds(index * 4 * TOK + (2 * part + head) * TOK, TOK)
                sent_ref[place, :] = grad[part * TOK : (part + 1) * TOK, head * HD : (head + 1) * HD]


def mix_back(pieces, weight):
    return pl.pallas_call(
        mix_back_kernel,
        out_shape=(
            jax.ShapeDtypeStruct((ALL, D), low),
            jax.ShapeDtypeStruct((SEQS * 16, D), low),
            jax.ShapeDtypeStruct((LENGTH, HD), low),
        ),
        in_specs=[anywhere] * 10 + [vmem],
        out_specs=(vmem, vmem, vmem),
        scratch_shapes=[pltpu.SemaphoreType.DMA((20,))],
        compiler_params=params(40),
        cost_estimate=cost(1.1e9, 10e6),
        name="mix_back",
    )(*pieces, weight)


def collect_kernel(core_ref, grads_ref, query_ref, mine_ref, other_ref):
    first = core_ref[0] == 0

    @pl.loop(0, SEQS)
    def step(index):
        rows = pl.ds(index * TOK, TOK)
        swapped = pl.ds(((index + SEQS // 2) % SEQS) * TOK, TOK)
        one = grads_ref[pl.ds(index * 2 * TOK, TOK), :]
        two = grads_ref[pl.ds(index * 2 * TOK + TOK, TOK), :]
        query_ref[rows, 0:HD] = one[:, :HD]
        query_ref[rows, HD : 2 * HD] = two[:, :HD]
        total = one[:, HD:].astype(wide) + two[:, HD:].astype(wide)
        lower = jnp.concatenate([total[:, : HD // 2], total[:, HD : HD + HD // 2]], axis=1)
        upper = jnp.concatenate([total[:, HD // 2 : HD], total[:, HD + HD // 2 :]], axis=1)
        mine_ref[rows, :] = jnp.where(first, lower, upper)
        other_ref[swapped, :] = jnp.where(first, upper, lower).astype(low)


def collect(core, grads):
    return pl.pallas_call(
        collect_kernel,
        out_shape=(
            jax.ShapeDtypeStruct((ALL, 2 * HD), low),
            jax.ShapeDtypeStruct((ALL, HD), wide),
            jax.ShapeDtypeStruct((ALL, HD), low),
        ),
        in_specs=[smem, vmem],
        out_specs=(vmem, vmem, vmem),
        compiler_params=params(32),
        cost_estimate=cost(1e6, 4e6),
        name="collect",
    )(core, grads)


def qkv_weights_kernel(normed_ref, query_ref, mine_ref, got_ref, out_ref, grad_ref):
    grad_ref[:, 0 : 2 * HD] = query_ref[...]
    grad_ref[:, 2 * HD : 3 * HD] = (mine_ref[...] + got_ref[...].astype(wide)).astype(low)

    @pl.loop(0, D // ROWS)
    def step(index):
        columns = pl.ds(pl.multiple_of(index * ROWS, ROWS), ROWS)
        out_ref[pl.ds(index * ROWS, ROWS), :] = t_mm(normed_ref[:, columns], grad_ref[...]).astype(low)


def qkv_weights(normed, query, mine, got):
    return pl.pallas_call(
        qkv_weights_kernel,
        out_shape=(jax.ShapeDtypeStruct((D, 3 * HD), low), jax.ShapeDtypeStruct((ALL, 3 * HD), low)),
        in_specs=[vmem] * 4,
        out_specs=(vmem, vmem),
        compiler_params=params(32),
        cost_estimate=cost(1.6e9, 8e6),
        name="qkv_weights",
    )(normed, query, mine, got)


def finish_kernel(place_ref, *refs):
    pieces, (query_ref, key_ref, value_ref, out_ref, gain_ref, shards, sems) = refs[:10], refs[10:]
    for copy in load_pieces(pieces, shards, None, sems):
        copy.wait()
    gain = jnp.zeros((TOK, TOK), wide)
    for block in range(EXPERTS):
        rows = pl.ds(block * TOK, TOK)
        columns = pl.ds(pl.multiple_of(place_ref[block] * 256, 256), 256)
        query_ref[:, columns] = shards[rows, 0:256].astype(wide)
        out_ref[:, columns] = shards[rows, 384:640].astype(wide)
        gain = gain + shards[rows, 640:768].astype(wide)
    gain_ref[...] = jnp.sum(gain, axis=1, keepdims=True)
    for step in range(KV):
        one = shards[pl.ds(step * TOK, TOK), 256:384].astype(wide)
        two = shards[pl.ds((step + KV) * TOK, TOK), 256:384].astype(wide)
        first = lax.rem(place_ref[step], 2) == 0
        lower, upper = jnp.where(first, one, two), jnp.where(first, two, one)
        columns = pl.ds(pl.multiple_of(lax.div(place_ref[step], 2) * HD, HD), HD)
        key_ref[:, columns] = jnp.concatenate([lower[:, : HD // 2], upper[:, : HD // 2]], axis=1)
        value_ref[:, columns] = jnp.concatenate([lower[:, HD // 2 :], upper[:, HD // 2 :]], axis=1)


def finish(owners, pieces):
    widths = (H * HD, KV * HD, KV * HD, H * HD, 1)
    return pl.pallas_call(
        finish_kernel,
        out_shape=tuple(jax.ShapeDtypeStruct((TOK, width), wide) for width in widths),
        in_specs=[smem] + [anywhere] * 10,
        out_specs=tuple([vmem] * 5),
        scratch_shapes=[pltpu.VMEM((ALL, 768), low), pltpu.SemaphoreType.DMA((20,))],
        compiler_params=params(32),
        cost_estimate=cost(1e6, 4e6),
        name="finish",
    )(owners, *pieces)


def finish_shared_kernel(*refs):
    pieces, spread_ref, spread_rows_ref = refs[:10], refs[10], refs[11]
    gate_ref, up_ref, down_ref, shards, left, rows_in, sems = refs[12:]
    for copy in load_pieces(pieces, shards, None, sems):
        copy.wait()
    width = SH_OWN // 2
    for block in range(EXPERTS):
        rows = pl.ds(block * TOK, TOK)
        for part in range(4):
            left[part * TOK : (part + 1) * TOK, block * width : (block + 1) * width] = shards[
                rows, part * width : (part + 1) * width
            ]
        packed = shards[rows, 2 * SH_OWN : 3 * SH_OWN].astype(wide)
        rows_in[block * SH_PAD : (block + 1) * SH_PAD, :] = jnp.concatenate(
            [
                jnp.concatenate(
                    [packed[8 * j : 8 * j + 8, 128 * i : 128 * i + 128] for j in range(D // 128)], axis=1
                )
                for i in range(SH_PAD // 8)
            ],
            axis=0,
        )
    for start in range(0, SH // 2, 256):
        count = min(256, SH // 2 - start)
        both = mm(left[...], spread_ref[:, start : start + count])
        for part in range(4):
            target = gate_ref if part < 2 else up_ref
            begin = (part % 2) * (SH // 2) + start
            target[:, begin : begin + count] = both[part * TOK : (part + 1) * TOK]
    down_ref[...] = mm(spread_rows_ref[...], rows_in[...].astype(low))


def finish_shared(pieces, spread, spread_rows):
    return pl.pallas_call(
        finish_shared_kernel,
        out_shape=(
            jax.ShapeDtypeStruct((TOK, SH), wide),
            jax.ShapeDtypeStruct((TOK, SH), wide),
            jax.ShapeDtypeStruct((SH_ROWS, D), wide),
        ),
        in_specs=[anywhere] * 10 + [vmem] * 2,
        out_specs=(vmem, vmem, vmem),
        scratch_shapes=[
            pltpu.VMEM((ALL, 3 * SH_OWN), low),
            pltpu.VMEM((4 * TOK, EXPERTS * SH_OWN // 2), low),
            pltpu.VMEM((EXPERTS * SH_PAD, D), wide),
            pltpu.SemaphoreType.DMA((20,)),
        ],
        compiler_params=params(40),
        cost_estimate=cost(2.2e9, 12e6),
        name="finish_shared",
    )(*pieces, spread, spread_rows)


def halves(value):
    upper = value.astype(low)
    return upper, (value - upper.astype(wide)).astype(low)


def silu_parts(gate_value):
    sig = 1.0 / (1.0 + jnp.exp(-gate_value))
    return sig, gate_value * sig


def swiglu_back(sig, act, up_value, grad):
    return (grad * up_value * (sig + act * (1.0 - sig))).astype(low), (grad * act).astype(low)


def ffn_kernel(*refs):
    expert_ref, slots_hbm, slots_t_hbm, routes_ref, router_hbm = refs[:5]
    pieces, cot_pieces, (pack_ref, shared_down_ref, down_ref) = refs[5:15], refs[15:25], refs[25:28]
    grad_mine, grad_other, gates_ref = refs[28:31]
    outs = refs[31:38]
    normed_ref, cot_ref, grad_ref = refs[38:41]
    kept = refs[41:48]
    hidden_s, grad_s, incoming, hidden_e, gated, grad_rows, grad_e = kept
    w_in_s, w_down_s, w_in, w_down, slots_ref, slots_t_ref = refs[48:54]
    raw, gate_parts, grad_in, piece_sems, cot_sems, sems, out_sems = refs[54:]
    base = 3 * SH_OWN
    piece_copies = load_pieces(pieces, normed_ref, None, piece_sems)
    cot_copies = load_pieces(cot_pieces, cot_ref, None, cot_sems)
    copies = [
        pltpu.make_async_copy(pack_ref.at[:, pl.ds(0, 2 * SH_OWN)], w_in_s.at[:, pl.ds(0, 2 * SH_OWN)], sems.at[0]),
        pltpu.make_async_copy(router_hbm, w_in_s.at[:, pl.ds(2 * SH_OWN, 128)], sems.at[1]),
        pltpu.make_async_copy(shared_down_ref, w_down_s, sems.at[3]),
        pltpu.make_async_copy(slots_hbm, slots_ref, sems.at[4]),
        pltpu.make_async_copy(pack_ref.at[:, pl.ds(base, 2 * FF)], w_in, sems.at[5]),
        pltpu.make_async_copy(down_ref, w_down, sems.at[6]),
        pltpu.make_async_copy(slots_t_hbm, slots_t_ref, sems.at[7]),
    ]
    for copy in copies:
        copy.start()

    def send(index):
        copy = pltpu.make_async_copy(kept[index], outs[index], out_sems.at[index])
        copy.start()
        return copy

    expert = expert_ref[0]
    lane = lax.broadcasted_iota(jnp.int32, (ROWS, 128), 1)
    for copy in piece_copies + cot_copies + copies[:3]:
        copy.wait()
    for step in range(ALL // ROWS):
        rows = pl.ds(step * ROWS, ROWS)
        both = mm(normed_ref[rows, :], w_in_s[...])
        sig, act = silu_parts(both[:, :SH_OWN])
        up = both[:, SH_OWN : 2 * SH_OWN]
        hidden_s[rows, :] = (act * up).astype(low)
        grad_hidden = mm_t(cot_ref[rows, :], w_down_s[...])
        grad_gate, grad_up = swiglu_back(sig, act, up, grad_hidden)
        grad_s[rows, 0:SH_OWN] = grad_gate
        grad_s[rows, SH_OWN : 2 * SH_OWN] = grad_up
        logits = both[:, 2 * SH_OWN :]
        first, second = routes_ref[rows, 0:1], routes_ref[rows, 1:2]
        chosen_first = jnp.sum(jnp.where(lane == first + 2, logits, 0.0), axis=1, keepdims=True)
        chosen_second = jnp.sum(jnp.where(lane == second + 2, logits, 0.0), axis=1, keepdims=True)
        gate_first = 1.0 / (1.0 + jnp.exp(chosen_second - chosen_first))
        gate_second = 1.0 / (1.0 + jnp.exp(chosen_first - chosen_second))
        here = jnp.where(first == expert, gate_first, 0.0) + jnp.where(second == expert, gate_second, 0.0)
        upper, lower = halves(here)
        parts = jnp.where(lane == 0, upper.astype(wide), 0.0) + jnp.where(lane == 1, lower.astype(wide), 0.0)
        gate_parts[rows, :] = parts.astype(low)
        if step == 0:
            both_gates = jnp.where(lane == 0, gate_first, 0.0) + jnp.where(lane == 1, gate_second, 0.0)
            gates_ref[...] = both_gates[:TOK]
    sent = [send(0), send(1)]
    copies[3].wait()
    for step in range(D // ROWS):
        columns = pl.ds(step * ROWS, ROWS)
        incoming[:, columns] = mm(slots_ref[...], normed_ref[:, columns]).astype(low)
        grad_rows[:, columns] = mm(slots_ref[...], cot_ref[:, columns]).astype(low)
    slot_parts = mm(slots_ref[...], gate_parts[...])
    slot_gate = slot_parts[:, 0:1] + slot_parts[:, 1:2]
    sent.append(send(2))
    copies[4].wait()
    for step in range(2 * FF // ROWS):
        columns = pl.ds(step * ROWS, ROWS)
        raw[:, columns] = mm(incoming[...], w_in[:, columns])
    for start, width in FF_TILES:
        gate, up = raw[:, start : start + width], raw[:, FF + start : FF + start + width]
        hidden_e[:, start : start + width] = (silu_parts(gate)[1] * up).astype(low)
    sent.append(send(3))
    copies[5].wait()
    slot_grad = jnp.zeros((SLOTS, 1), wide)
    for step in range(D // ROWS):
        columns = pl.ds(step * ROWS, ROWS)
        rows = mm(hidden_e[...], w_down[:, columns]).astype(low).astype(wide)
        cot = grad_rows[:, columns].astype(wide)
        gated[:, columns] = (rows * slot_gate).astype(low)
        grad_rows[:, columns] = (cot * slot_gate).astype(low)
        slot_grad = slot_grad + jnp.sum(rows * cot, axis=1, keepdims=True)
    sent += [send(4), send(5)]
    for start, width in FF_TILES:
        grad_hidden = mm_t(grad_rows[...], w_down[pl.ds(start, width), :])
        sig, act = silu_parts(raw[:, start : start + width])
        grad_gate, grad_up = swiglu_back(sig, act, raw[:, FF + start : FF + start + width], grad_hidden)
        grad_e[:, start : start + width] = grad_gate
        grad_e[:, FF + start : FF + start + width] = grad_up
    sent.append(send(6))
    for step in range(D // ROWS):
        columns = pl.ds(step * ROWS, ROWS)
        grad_in[:, columns] = mm_t(grad_e[...], w_in[columns, :]).astype(low)
    upper, lower = halves(slot_grad)
    slot_lane = lax.broadcasted_iota(jnp.int32, (SLOTS, 128), 1)
    slot_parts = (
        jnp.where(slot_lane == expert, upper.astype(wide), 0.0)
        + jnp.where(slot_lane == expert + 8, lower.astype(wide), 0.0)
    ).astype(low)
    copies[6].wait()
    half = ALL // 2
    for side, target in ((1, grad_other), (0, grad_mine)):
        for step in range(half // ROWS):
            rows = pl.ds(side * half + step * ROWS, ROWS)
            for tile in range(D // 512):
                columns = pl.ds(tile * 512, 512)
                grad_ref[rows, columns] = (
                    mm_t(grad_s[rows, :], w_in_s[columns, 0 : 2 * SH_OWN])
                    + mm(slots_t_ref[rows, :], grad_in[:, columns])
                ).astype(low)
            grad_ref[rows, D : D + 128] = mm(slots_t_ref[rows, :], slot_parts).astype(low)
        copy = pltpu.make_async_copy(grad_ref.at[pl.ds(side * half, half), :], target, sems.at[8 + side])
        copy.start()
        sent.append(copy)
    for copy in sent:
        copy.wait()


def ffn(expert, slots, slots_t, routes, router, pieces, cot_pieces, pack, shared_down, down):
    kept = [(ALL, SH_OWN), (ALL, 2 * SH_OWN), (SLOTS, D), (SLOTS, FF), (SLOTS, D), (SLOTS, D), (SLOTS, 2 * FF)]
    grads = [(ALL // 2, D + 128)] * 2
    return pl.pallas_call(
        ffn_kernel,
        out_shape=tuple(
            [jax.ShapeDtypeStruct(shape, low) for shape in grads]
            + [jax.ShapeDtypeStruct((TOK, 128), wide)]
            + [jax.ShapeDtypeStruct(shape, low) for shape in kept]
        ),
        in_specs=[smem, anywhere, anywhere, vmem] + [anywhere] * 24,
        out_specs=tuple([anywhere] * 2 + [vmem] + [anywhere] * 7),
        scratch_shapes=[pltpu.VMEM((ALL, D), low), pltpu.VMEM((ALL, D), low), pltpu.VMEM((ALL, D + 128), low)]
        + [pltpu.VMEM(shape, low) for shape in kept]
        + [
            pltpu.VMEM((D, 2 * SH_OWN + 128), low),
            pltpu.VMEM((SH_OWN, D), low),
            pltpu.VMEM((D, 2 * FF), low),
            pltpu.VMEM((FF, D), low),
            pltpu.VMEM((SLOTS, ALL), low),
            pltpu.VMEM((ALL, SLOTS), low),
            pltpu.VMEM((SLOTS, 2 * FF), wide),
            pltpu.VMEM((ALL, 128), low),
            pltpu.VMEM((SLOTS, D), low),
            pltpu.SemaphoreType.DMA((20,)),
            pltpu.SemaphoreType.DMA((20,)),
            pltpu.SemaphoreType.DMA((10,)),
            pltpu.SemaphoreType.DMA((7,)),
        ],
        compiler_params=params(60),
        cost_estimate=cost(27e9, 50e6, 1e6),
        name="ffn",
    )(expert, slots, slots_t, routes, router, *pieces, *cot_pieces, pack, shared_down, down)


def pack_rows(block):
    count, width = block.shape[0] // 8, block.shape[1] // 128
    return jnp.concatenate(
        [
            jnp.concatenate(
                [block[8 * i : 8 * i + 8, 128 * j : 128 * j + 128] for i in range(count)], axis=1
            )
            for j in range(width)
        ],
        axis=0,
    )


def slab(buffer, out_ref, sems, step, start):
    return pltpu.make_async_copy(
        buffer.at[step % 2],
        out_ref.at[pl.ds(step * ROWS, ROWS), pl.ds(start, buffer.shape[2])],
        sems.at[step % 2],
    )


def weight_slabs(tokens_ref, grad_ref, down, out_ref, buffer, sems, start):
    width = grad_ref.shape[1]
    count = width // 2 // FSDP
    for step in range(D // ROWS):
        slot = step % 2
        if step >= 2:
            slab(buffer, out_ref, sems, step - 2, start).wait()
        buffer[slot, :, 0:width] = t_mm(tokens_ref[:, pl.ds(step * ROWS, ROWS)], grad_ref[...]).astype(low)
        for part in range(ROWS // TOK):
            place = step * (ROWS // TOK) + part
            packed = pack_rows(down[pl.ds(place * count, count), :]).astype(low)
            buffer[slot, part * TOK : (part + 1) * TOK, width:] = packed
        slab(buffer, out_ref, sems, step, start).start()
    for step in (D // ROWS - 2, D // ROWS - 1):
        slab(buffer, out_ref, sems, step, start).wait()


def shared_weights_kernel(*refs):
    pieces, cot_pieces, hidden_ref, grad_ref = refs[:10], refs[10:20], refs[20], refs[21]
    out_ref, normed_ref, cot_ref, buffer, down, piece_sems, cot_sems, sems = refs[22:]
    cot_copies = load_pieces(cot_pieces, cot_ref, None, cot_sems)
    copies = load_pieces(pieces, normed_ref, None, piece_sems)
    for copy in cot_copies:
        copy.wait()
    for tile in range(D // ROWS):
        part = pl.ds(tile * ROWS, ROWS)
        down[:, part] = t_mm(hidden_ref[...], cot_ref[:, part])
    for copy in copies:
        copy.wait()
    weight_slabs(normed_ref, grad_ref, down, out_ref, buffer, sems, 0)


def shared_weights(pieces, cot_pieces, hidden, grad):
    return pl.pallas_call(
        shared_weights_kernel,
        out_shape=(jax.ShapeDtypeStruct((D, PACK), low), jax.ShapeDtypeStruct((ALL, D), low)),
        in_specs=[anywhere] * 20 + [vmem] * 2,
        out_specs=(anywhere, vmem),
        scratch_shapes=[
            pltpu.VMEM((ALL, D), low),
            pltpu.VMEM((2, ROWS, 3 * SH_OWN), low),
            pltpu.VMEM((SH_OWN, D), wide),
            pltpu.SemaphoreType.DMA((20,)),
            pltpu.SemaphoreType.DMA((20,)),
            pltpu.SemaphoreType.DMA((2,)),
        ],
        compiler_params=params(48),
        cost_estimate=cost(5e9, 18e6),
        name="shared_weights",
    )(*pieces, *cot_pieces, hidden, grad)


def expert_weights_kernel(_, incoming_ref, hidden_ref, grad_rows_ref, grad_ref, out_ref, buffer, down, sems):
    for tile in range(D // ROWS):
        part = pl.ds(tile * ROWS, ROWS)
        down[:, part] = t_mm(hidden_ref[...], grad_rows_ref[:, part])
    weight_slabs(incoming_ref, grad_ref, down, out_ref, buffer, sems, 3 * SH_OWN)


def expert_weights(*operands):
    return pl.pallas_call(
        expert_weights_kernel,
        out_shape=jax.ShapeDtypeStruct((D, PACK), low),
        in_specs=[anywhere] + [vmem] * 4,
        out_specs=anywhere,
        scratch_shapes=[
            pltpu.VMEM((2, ROWS, 3 * FF), low),
            pltpu.VMEM((FF, D), wide),
            pltpu.SemaphoreType.DMA((2,)),
        ],
        input_output_aliases={0: 0},
        compiler_params=params(48),
        cost_estimate=cost(6e9, 24e6),
        name="expert_weights",
    )(*operands)


def out_rows_kernel(place_ref, *refs):
    parts, out_ref = refs[:5], refs[5]
    for index in range(EXPERTS):
        step, side = index // 2, index % 2
        columns = pl.ds(pl.multiple_of(place_ref[index] * 256, 256), 256)
        out_ref[:, columns] = parts[step + 1][side] if step else parts[side][...]


def out_rows(places, parts):
    return pl.pallas_call(
        out_rows_kernel,
        out_shape=jax.ShapeDtypeStruct((256, D), low),
        in_specs=[smem] + [vmem] * 5,
        out_specs=vmem,
        compiler_params=params(32),
        cost_estimate=cost(0, 2e6),
        name="out_rows",
    )(places, *parts)


def out_weights_kernel(place_ref, mixed_ref, grad_ref, normed_ref, logits_ref, mine_ref, other_ref, router_ref):
    for index in range(EXPERTS):
        columns = pl.ds(pl.multiple_of(place_ref[index] * 256, 256), 256)
        target = mine_ref if index < 4 else other_ref
        target[index % 4] = t_mm(mixed_ref[...], grad_ref[:, columns]).astype(low)
    router_ref[...] = mm(logits_ref[...], normed_ref[...])


def out_weights(owners, mixed, grad, normed, logits):
    blocks = jax.ShapeDtypeStruct((4, 256, 256), low)
    return pl.pallas_call(
        out_weights_kernel,
        out_shape=(blocks, blocks, jax.ShapeDtypeStruct((2 * EXPERTS, D), wide)),
        in_specs=[smem] + [vmem] * 4,
        out_specs=(vmem, vmem, vmem),
        compiler_params=params(32),
        cost_estimate=cost(1.2e9, 10e6),
        name="out_weights",
    )(owners, mixed, grad, normed, logits)


def back_two_kernel(
    own_ref, first_ref, second_ref, middle_ref, cot_ref, gains_ref, gates_ref, routes_ref, block_ref, grad_ref
):
    total = own_ref[...] + first_ref[...].astype(wide) + second_ref[...].astype(wide)
    lane = lax.broadcasted_iota(jnp.int32, (TOK, 128), 1)
    extra = total[:, D:]
    first, second = routes_ref[:, 0:1], routes_ref[:, 1:2]

    def taken(route):
        return jnp.sum(jnp.where((lane == route) | (lane == route + 8), extra, 0.0), axis=1, keepdims=True)

    gate_first, gate_second = gates_ref[:, 0:1], gates_ref[:, 1:2]
    taken_first, taken_second = taken(first), taken(second)
    inner = gate_first * taken_first + gate_second * taken_second
    chosen_first, chosen_second = gate_first * (taken_first - inner), gate_second * (taken_second - inner)
    logits = jnp.where(lane == first, chosen_first, 0.0) + jnp.where(lane == second, chosen_second, 0.0)
    grad = total[:, :D]
    for index in range(EXPERTS):
        grad = grad + logits[:, index : index + 1] * gains_ref[2 + index : 3 + index, :]
    middle = middle_ref[...]
    factor = lax.rsqrt(jnp.mean(middle * middle, axis=-1, keepdims=True) + eps_norm)
    scaled = grad * gains_ref[1:2, :]
    mean = jnp.mean(scaled * middle, axis=-1, keepdims=True)
    result = cot_ref[...].astype(wide) + factor * scaled - middle * (factor * factor * factor * mean)
    grad_ref[...] = result
    block_ref[0:TOK, :] = result.astype(low)
    gain_upper, gain_lower = halves(jnp.sum(grad * middle * factor, axis=0, keepdims=True))
    upper, lower = halves(logits.T[0:EXPERTS, :])
    rows = [gain_upper, gain_lower]
    upper, lower = upper.astype(wide), lower.astype(wide)
    flat = [upper[index : index + 1, :] for index in range(EXPERTS)] + [
        lower[index : index + 1, :] for index in range(EXPERTS)
    ]
    rows.append(jnp.concatenate(flat, axis=1))
    rows = [row.astype(wide) for row in rows] + [jnp.zeros((13, D), wide)]
    block_ref[TOK : TOK + 16, :] = jnp.concatenate(rows, axis=0).astype(low)


def back_two(*operands):
    return pl.pallas_call(
        back_two_kernel,
        out_shape=(jax.ShapeDtypeStruct((TOK + 16, D), low), jax.ShapeDtypeStruct((TOK, D), wide)),
        in_specs=[vmem] * 8,
        out_specs=(vmem, vmem),
        compiler_params=params(32),
        cost_estimate=cost(1e7, 6e6),
        name="back_two",
    )(*operands)


def norm_factor(values):
    return lax.rsqrt(jnp.mean(values * values, axis=-1, keepdims=True) + eps_norm)


def norm_back(values, factor, gain, grad):
    scaled = grad * gain
    inner = jnp.mean(scaled * values, axis=-1, keepdims=True)
    return factor * scaled - values * (factor * factor * factor * inner)


def per_device(
    hidden_in,
    cotangent,
    segments,
    routes,
    attn_gain,
    w_query,
    w_key,
    w_value,
    w_out,
    ffn_gain,
    w_router,
    shared_gate,
    shared_up,
    shared_down,
    expert_gate,
    expert_up,
    expert_down,
):
    expert = lax.axis_index("expert")
    z, core = expert // 2, expert % 2
    place = lax.axis_index("fsdp")

    misc = jnp.concatenate(
        [attn_gain[:, None], ffn_gain[:, None], w_router, jnp.zeros((TOK, 118), low)], axis=1
    )
    attn_pack = jnp.concatenate(
        [
            lax.dynamic_slice_in_dim(w_query, 256 * expert, 256, 1),
            lax.dynamic_slice_in_dim(w_key, HD * z, HD, 1),
            lax.dynamic_slice_in_dim(w_value, HD * z, HD, 1),
            lax.dynamic_slice_in_dim(w_out, 256 * expert, 256, 1),
            misc,
        ],
        axis=1,
    )
    attn_all = lax.all_gather(attn_pack, "fsdp", axis=0, tiled=True)
    half_in, half_out = SH // 2, SH_OWN // 2
    sel_column = jnp.arange(half_out)
    picked = SH_ROWS * (sel_column // SH_PAD) + SH_PART * expert + sel_column % SH_PAD
    picked = jnp.where(sel_column % SH_PAD < SH_PART, picked, -1)
    select = (jnp.arange(half_in)[:, None] == picked[None, :]).astype(low)
    own_shared = mm(
        jnp.concatenate(
            [shared_gate[:, :half_in], shared_gate[:, half_in:], shared_up[:, :half_in], shared_up[:, half_in:]],
            axis=0,
        ),
        select,
    ).astype(low)
    own_down = jnp.pad(
        lax.dynamic_slice_in_dim(shared_down, SH_PART * expert, SH_PART, 0),
        ((0, SH_PAD - SH_PART), (0, 0)),
    )
    ffn_pack = jnp.concatenate(
        [
            own_shared[:TOK],
            own_shared[TOK : 2 * TOK],
            own_shared[2 * TOK : 3 * TOK],
            own_shared[3 * TOK :],
            pack_tiles(own_down),
            expert_gate[:, 0],
            expert_up[:, 0],
            pack_tiles(expert_down[:, 0]),
        ],
        axis=1,
    )
    ffn_all = lax.all_gather(ffn_pack, "fsdp", axis=0, tiled=True)

    ids = jnp.concatenate(
        [
            segments.astype(low),
            jnp.pad(routes[0].reshape(1, TOK * TOPK), ((0, 0), (0, LENGTH - TOK * TOPK))).astype(low),
            jnp.zeros((14, LENGTH), low),
        ],
        axis=0,
    )
    hidden_pieces = gather_pieces(jnp.concatenate([hidden_in[0], ids], axis=0))
    cot_block, *hidden_pieces = together(cotangent[0], *hidden_pieces)
    cot_pieces = gather_pieces(cot_block)

    inverse_freq = rope_base ** (-jnp.arange(HD // 2, dtype=wide) * 2.0 / HD)
    angles = jnp.arange(LENGTH).astype(wide)[:, None] * inverse_freq[None, :]
    cosine, sine = jnp.cos(angles), jnp.sin(angles)
    cos_all = jnp.concatenate([cosine, cosine], axis=1)
    sin_back = jnp.concatenate([sine, -sine], axis=1)
    cos_own = lax.dynamic_slice_in_dim(cos_all, place * TOK, TOK, 0)
    sin_own = -lax.dynamic_slice_in_dim(sin_back, place * TOK, TOK, 0)
    cos_two, sin_two = jnp.concatenate([cos_own, cos_own]), jnp.concatenate([sin_own, sin_own])
    attn_all, cos_two, sin_two, cos_all, sin_back = together(attn_all, cos_two, sin_two, cos_all, sin_back)
    normed_one, sent, factor_one, gains, ids_all = project(hidden_pieces, attn_all, cos_two, sin_two)
    qkv = lax.all_to_all(sent, "fsdp", split_axis=0, concat_axis=0, tiled=True)

    ids_all = ids_all.reshape(SEQS, 16, D)
    seg_row = lax.dynamic_slice_in_dim(ids_all[:, 0].astype(wide), place // 2, 1, 0)
    seg_blocks = jnp.pad(seg_row.reshape(FSDP, TOK), ((0, TOK - FSDP), (0, 0)))
    route_all = ids_all[:, 1, : TOK * TOPK].astype(jnp.int32).reshape(ALL, TOPK)
    hit = jnp.any(route_all == expert, axis=1).astype(wide)
    order = jnp.arange(ALL)
    rank = mm(hit.astype(low)[None, :], (order[:, None] < order[None, :]).astype(low))
    slot_bool = (rank.astype(jnp.int32) == jnp.arange(SLOTS)[:, None]) & (hit > 0.5)[None, :]
    slots = slot_bool.astype(low)
    slots_t = slot_bool.T.astype(low)
    out_columns = attn_all[:, 512:768].reshape(EXPERTS, 256, 256)
    owners = jnp.stack([relative_owner(expert, block) for block in range(EXPERTS)])
    out_blocks = [lax.dynamic_index_in_dim(out_columns, owners[block], 0) for block in range(EXPERTS)]
    out_mine, out_other = jnp.concatenate(out_blocks[:4]), jnp.concatenate(out_blocks[4:])
    out_mine, out_other, _ = together(out_mine, out_other, sent)
    w_out_own = out_rows(source_owners(expert), exchange(out_mine, out_other))
    router = attn_all[:, 768:896]
    qkv, seg_row, seg_blocks, route_all, slots, slots_t, w_out_own, router = together(
        qkv, seg_row, seg_blocks, route_all, slots, slots_t, w_out_own, router
    )
    mixed_head, log_total = attend(qkv, seg_row, seg_blocks)
    mixed = (
        lax.all_to_all(mixed_head, "fsdp", split_axis=0, concat_axis=0, tiled=True)
        .reshape(SEQS, 2, TOK, HD)
        .transpose(0, 2, 1, 3)
        .reshape(ALL, 2 * HD)
    )
    own_hidden = hidden_in[0].astype(wide)
    half = ALL // 2
    middle = own_hidden + scatter_rows(
        mm(mixed[:half], w_out_own).astype(low), mm(mixed[half:], w_out_own).astype(low)
    )
    factor_two = norm_factor(middle)
    gain_one, gain_two = gains[0:1], gains[1:2]
    normed_block = (middle * factor_two * gain_two).astype(low)

    base = 3 * SH_OWN
    shared_down_w = unpack_tiles(ffn_all[:, 2 * SH_OWN : base], FSDP)
    down_w = unpack_tiles(ffn_all[:, base + 2 * FF :], FSDP)
    below, above = first_pieces(normed_block)
    below, above, shared_down_w, down_w = together(below, above, shared_down_w, down_w)
    normed_pieces = other_pieces(normed_block, below, above)
    (
        grad_mine,
        grad_other,
        gates,
        hidden_shared,
        grad_shared,
        incoming,
        hidden_expert,
        gated_rows,
        grad_rows,
        grad_expert,
    ) = ffn(
        expert[None], slots, slots_t, route_all, router, normed_pieces, cot_pieces, ffn_all, shared_down_w, down_w
    )
    received = swap_core(grad_other)
    ffn_grads, normed_two = shared_weights(normed_pieces, cot_pieces, hidden_shared, grad_shared)
    received, ffn_grads = together(received, ffn_grads)
    own_grad, to_above, to_below = scatter_start(grad_mine, received)
    to_above, to_below, ffn_grads = together(to_above, to_below, ffn_grads)
    from_below, from_above = move_z(to_above, 1), move_z(to_below, -1)
    ffn_grads = expert_weights(ffn_grads, incoming, hidden_expert, grad_rows, grad_expert)
    from_below, from_above, ffn_grads = together(from_below, from_above, ffn_grads)
    ffn_sums = lax.psum_scatter(ffn_grads, "fsdp", scatter_dimension=0, tiled=True)
    back_block, grad_middle = back_two(
        own_grad, from_below, from_above, middle, cotangent[0], gains, gates, route_all[:TOK]
    )
    back_pieces = gather_pieces(back_block)

    grad_attn, extra, sent_back = mix_back(back_pieces, w_out_own)
    grad_head = lax.all_to_all(sent_back, "fsdp", split_axis=0, concat_axis=0, tiled=True)
    grads_head = attend_back(qkv, grad_head, log_total, seg_row, seg_blocks, cos_all, sin_back)
    grads_qkv = lax.all_to_all(grads_head, "fsdp", split_axis=0, concat_axis=0, tiled=True)

    hidden_shared, gated_rows, slots_t, _ = together(hidden_shared, gated_rows, slots_t, sent_back)
    result_mine = mm(hidden_shared[:half], shared_down_w) + mm(slots_t[:half], gated_rows)
    result_other = mm(hidden_shared[half:], shared_down_w) + mm(slots_t[half:], gated_rows)
    layer_out = (middle + scatter_rows(result_mine.astype(low), result_other.astype(low))).astype(low)

    extra = extra.reshape(SEQS, 16, D)
    gain_two_sum = jnp.sum(extra[:, :2].astype(wide), axis=(0, 1))
    logit_rows = extra[:, 2].reshape(SEQS, 2, EXPERTS, TOK).transpose(1, 2, 0, 3).reshape(2 * EXPERTS, ALL)
    out_mine, out_other, grad_router = out_weights(owners, mixed, grad_attn, normed_two, logit_rows)
    out_parts = exchange(out_mine, out_other)
    out_parts = jnp.concatenate([jnp.stack(out_parts[:2])[None], jnp.stack(out_parts[2:])]).reshape(EXPERTS, 256, 256)
    places = [((z - source // 2) % 4) * 2 + (core ^ (source % 2)) for source in range(EXPERTS)]
    grad_out = jnp.stack([lax.dynamic_index_in_dim(out_parts, where, 0, keepdims=False) for where in places])
    grad_out = grad_out.reshape(FSDP, TOK, 256)
    small_rows = jnp.concatenate(
        [grad_router[:EXPERTS] + grad_router[EXPERTS:], gain_two_sum[None], jnp.zeros((7, D), wide)], axis=0
    )
    small_rows = small_rows.reshape(16, FSDP, TOK).transpose(1, 0, 2).astype(low)
    small_rows = jnp.pad(small_rows, ((0, 0), (0, 0), (0, 512)))
    small_rows, grad_out, grads_qkv, layer_out = together(small_rows, grad_out, grads_qkv, layer_out)

    grad_query, kv_mine, kv_other = collect(core[None], grads_qkv)
    qkv_grads, grad_qkv = qkv_weights(normed_one, grad_query, kv_mine, swap_core(kv_other))
    attn_grads = jnp.concatenate([qkv_grads.reshape(FSDP, TOK, 3 * HD), grad_out], axis=2)
    attn_grads = jnp.concatenate([attn_grads, small_rows], axis=1).reshape(FSDP * (TOK + 16), 640)
    attn_parts = lax.all_to_all(attn_grads, "fsdp", split_axis=0, concat_axis=0, tiled=True)

    is_first = core == 0
    kv_weight = attn_all[:, 256:512].reshape(D, 2, 2, HD // 2)
    kv_weight = jnp.where(is_first, kv_weight[:, :, 0], kv_weight[:, :, 1]).reshape(D, HD)
    qkv_weight = jnp.concatenate([attn_all[:, :256], kv_weight], axis=1)
    grad_qkv, _ = together(grad_qkv, attn_grads)
    grad_normed_other = mm_t(grad_qkv[half:], qkv_weight).astype(low)
    grad_normed_mine = mm_t(grad_qkv[:half], qkv_weight).astype(low)
    own_grad_one = scatter_rows(grad_normed_mine, grad_normed_other)
    grad_input = (grad_middle + norm_back(own_hidden, factor_one[:TOK], gain_one, own_grad_one)).astype(low)
    attn_parts, grad_input = together(attn_parts, grad_input)
    attn_sums = jnp.sum(attn_parts.reshape(FSDP, TOK + 16, 640).astype(wide), axis=0)

    own_weight = lax.dynamic_slice_in_dim(qkv_weight, place * TOK, TOK, 0)
    gain_part = jnp.sum(attn_sums[:TOK, :384] * own_weight.astype(wide), axis=1, keepdims=True)
    gain_upper, gain_lower = halves(gain_part / attn_gain.astype(wide)[:, None])
    shards = jnp.concatenate(
        [attn_sums[:TOK].astype(low), gain_upper, gain_lower, jnp.zeros((TOK, 126), low)], axis=1
    )
    grad_w_query, grad_w_key, grad_w_value, grad_w_out, grad_attn_gain = finish(owners, gather_pieces(shards))

    ffn_sums, _ = together(ffn_sums, attn_grads)
    put_row = jnp.arange(SH_PAD * EXPERTS * FSDP // 2)
    source, within = owners[put_row // half_out], put_row % half_out
    target = SH_ROWS * (within // SH_PAD) + SH_PART * source + within % SH_PAD
    target = jnp.where(within % SH_PAD < SH_PART, target, -1)
    spread = (target[:, None] == jnp.arange(half_in)[None, :]).astype(low)
    put_row = jnp.arange(EXPERTS * SH_PAD)
    target = SH_PART * owners[put_row // SH_PAD] + put_row % SH_PAD
    target = jnp.where(put_row % SH_PAD < SH_PART, target, -1)
    spread_rows = (jnp.arange(SH_ROWS)[:, None] == target[None, :]).astype(low)
    spread, spread_rows, _ = together(spread, spread_rows, sent)
    grad_shared_gate, grad_shared_up, grad_shared_down = finish_shared(
        gather_pieces(ffn_sums[:, :base]), spread, spread_rows
    )
    grad_expert_gate = ffn_sums[:, base : base + FF].astype(wide)[:, None]
    grad_expert_up = ffn_sums[:, base + FF : base + 2 * FF].astype(wide)[:, None]
    grad_expert_down = unpack_tiles(ffn_sums[:, base + 2 * FF :], 1).astype(wide)[:, None]
    return (
        layer_out[None],
        grad_input[None],
        grad_attn_gain[:, 0],
        grad_w_query,
        grad_w_key,
        grad_w_value,
        grad_w_out,
        attn_sums[TOK + EXPERTS, :TOK],
        attn_sums[TOK : TOK + EXPERTS, :TOK].T,
        grad_shared_gate,
        grad_shared_up,
        grad_shared_down,
        grad_expert_gate,
        grad_expert_up,
        grad_expert_down,
    )


def solution(mesh):
    in_specs = (
        P("expert", "fsdp", None),
        P("expert", "fsdp", None),
        P("expert", None),
        P("expert", "fsdp", None),
        P("fsdp"),
        P("fsdp", None),
        P("fsdp", None),
        P("fsdp", None),
        P("fsdp", None),
        P("fsdp"),
        P("fsdp", None),
        P("fsdp", None),
        P("fsdp", None),
        P("fsdp", None),
        P("fsdp", "expert", None),
        P("fsdp", "expert", None),
        P("fsdp", "expert", None),
    )
    out_specs = (
        P("expert", "fsdp", None),
        P("expert", "fsdp", None),
        P("fsdp"),
        P("fsdp", None),
        P("fsdp", None),
        P("fsdp", None),
        P("fsdp", None),
        P("fsdp"),
        P("fsdp", None),
        P("fsdp", None),
        P("fsdp", None),
        P("fsdp", None),
        P("fsdp", "expert", None),
        P("fsdp", "expert", None),
        P("fsdp", "expert", None),
    )
    return jax.shard_map(
        per_device, mesh=mesh, in_specs=in_specs, out_specs=out_specs, check_vma=False
    )
```

```python
import jax
import jax.numpy as jnp
from jax import lax
from jax.experimental import pallas as pl
from jax.experimental.pallas import tpu as pltpu
from jax.sharding import PartitionSpec as P

D = 2048
H = 16
KV = 4
HD = 128
FF = 1408
SH = 2816
TOPK = 2
TOK = 128
LENGTH = 2048
SEQS = 8
EXPERTS = 8
FSDP = 16
ALL = SEQS * TOK
CAP = 42
SLOTS = SEQS * CAP
SH_ROWS = SH // FSDP
SH_PART = SH_ROWS // EXPERTS
SH_PAD = 24
SH_OWN = FSDP * SH_PAD
QBLOCK = 256

eps_norm = 1e-06
rope_base = 600000.0
masked_fill = -1e30
low = jnp.bfloat16
wide = jnp.float32


def shift_pairs(step):
    return [(z * 2 + c, ((z + step) % 4) * 2 + c) for z in range(4) for c in range(2)]


core_pairs = [(z * 2 + c, z * 2 + 1 - c) for z in range(4) for c in range(2)]


def move_z(block, step):
    return lax.ppermute(block, "expert", shift_pairs(step))


def swap_core(block):
    return lax.ppermute(block, "expert", core_pairs)


def together(*values):
    return lax.optimization_barrier(values)


TOP = TOK // 2


def first_pieces(block):
    return move_z(block, 1), move_z(block, -1)


def other_pieces(block, below, above):
    upper, lower = move_z(below[:TOP], 1), move_z(above[TOP:], -1)
    mine = [block, above, upper, lower, below]
    return mine + [swap_core(piece) for piece in mine]


def gather_pieces(block):
    return other_pieces(block, *first_pieces(block))


PIECES = [(4 * side + block, start) for side in (0, 1) for block, start in ((0, 0), (1, 0), (2, 0), (2, TOP), (3, 0))]


def load_pieces(refs, rows_ref, extra_ref, sems):
    copies = []
    for index, (ref, (block, start)) in enumerate(zip(refs, PIECES)):
        count = min(ref.shape[0], TOK - start)
        copies.append(
            pltpu.make_async_copy(
                ref.at[pl.ds(0, count), :], rows_ref.at[pl.ds(block * TOK + start, count), :], sems.at[2 * index]
            )
        )
        if extra_ref is not None and ref.shape[0] > count:
            copies.append(
                pltpu.make_async_copy(
                    ref.at[pl.ds(count, 16), :], extra_ref.at[pl.ds(block * 16, 16), :], sems.at[2 * index + 1]
                )
            )
    for copy in copies:
        copy.start()
    return copies


def scatter_start(mine, received):
    chip = mine.reshape(4, TOK, -1).astype(wide) + received.reshape(4, TOK, -1).astype(wide)
    from_below = move_z(chip[2, :TOP].astype(low), 1)
    from_above = move_z(chip[2, TOP:].astype(low), -1)
    to_above = jnp.concatenate([chip[1, :TOP] + from_below.astype(wide), chip[1, TOP:]], axis=0)
    to_below = jnp.concatenate([chip[3, :TOP], chip[3, TOP:] + from_above.astype(wide)], axis=0)
    return chip[0], to_above.astype(low), to_below.astype(low)


def scatter_end(own, first, second):
    return own + first.astype(wide) + second.astype(wide)


def scatter_rows(mine, other):
    own, to_above, to_below = scatter_start(mine, swap_core(other))
    return scatter_end(own, move_z(to_above, 1), move_z(to_below, -1))


def exchange(mine, other):
    got = swap_core(other)
    chip = jnp.stack([mine[1:], got[1:]], axis=1)
    return mine[0], got[0], *[move_z(chip[step - 1], step) for step in (1, 2, 3)]


def source_owners(expert):
    return jnp.stack([((expert // 2 - index // 2) % 4) * 2 + ((expert % 2) ^ (index % 2)) for index in range(EXPERTS)])


def relative_owner(expert, block):
    return ((expert // 2 + block % 4) % 4) * 2 + ((expert % 2) ^ (block // 4))


def pack_tiles(block):
    rows, columns = block.shape[0] // 8, block.shape[1] // 128
    tiles = block.reshape(rows, 8, columns, 128).transpose(2, 1, 0, 3)
    return tiles.reshape(columns * 8, rows * 128)


def unpack_tiles(block, count):
    rows, columns = block.shape[1] // 128, block.shape[0] // (8 * count)
    tiles = block.reshape(count, columns, 8, rows, 128).transpose(0, 3, 2, 1, 4)
    return tiles.reshape(count * rows * 8, columns * 128)


def product(left, right, contract):
    return lax.dot_general(left, right, (contract, ((), ())), preferred_element_type=wide)


def mm(left, right):
    return product(left, right, ((1,), (0,)))


def mm_t(left, right):
    return product(left, right, ((1,), (1,)))


def t_mm(left, right):
    return product(left, right, ((0,), (0,)))


def segment_columns(seg_blocks_ref):
    return seg_blocks_ref[...].T


def block_scores(qkv_ref, seg_row_ref, columns, start, reach):
    query = qkv_ref[pl.ds(start, QBLOCK), 0:HD]
    key = qkv_ref[pl.ds(0, reach), HD : 2 * HD]
    scores = mm_t(query, key) * HD ** (-0.5)
    query_pos = start + lax.broadcasted_iota(jnp.int32, (QBLOCK, reach), 0)
    key_pos = lax.broadcasted_iota(jnp.int32, (QBLOCK, reach), 1)
    block = start // TOK
    column = jnp.concatenate([columns[:, block : block + 1], columns[:, block + 1 : block + 2]], axis=0)
    same = column == seg_row_ref[:, pl.ds(0, reach)]
    return jnp.where(same & (query_pos >= key_pos), scores, masked_fill)


def attend_kernel(qkv_ref, seg_row_ref, seg_blocks_ref, mixed_ref, total_ref):
    columns = segment_columns(seg_blocks_ref)
    for block in range(LENGTH // QBLOCK):
        start, reach = block * QBLOCK, (block + 1) * QBLOCK
        scores = block_scores(qkv_ref, seg_row_ref, columns, start, reach)
        largest = jnp.max(scores, axis=-1, keepdims=True)
        exponent = jnp.exp(scores - largest)
        totals = jnp.sum(exponent, axis=-1, keepdims=True)
        probs_low = (exponent * (1.0 / totals)).astype(low)
        value = qkv_ref[pl.ds(0, reach), 2 * HD : 3 * HD]
        mixed_ref[pl.ds(start, QBLOCK), :] = mm(probs_low, value).astype(low)
        total_ref[pl.ds(start, QBLOCK), :] = largest + jnp.log(totals)


def attend_back_kernel(
    qkv_ref, grad_ref, total_ref, seg_row_ref, seg_blocks_ref, cos_ref, sin_ref, out_ref, key_acc, value_acc
):
    columns = segment_columns(seg_blocks_ref)
    key_acc[...] = jnp.zeros_like(key_acc)
    value_acc[...] = jnp.zeros_like(value_acc)

    def turn_back(value, rows):
        return value * cos_ref[rows, :] + pltpu.roll(value, HD // 2, 1) * sin_ref[rows, :]

    for block in range(LENGTH // QBLOCK):
        start, reach = block * QBLOCK, (block + 1) * QBLOCK
        rows, span = pl.ds(start, QBLOCK), pl.ds(0, reach)
        scores = block_scores(qkv_ref, seg_row_ref, columns, start, reach)
        probs = jnp.exp(scores - total_ref[rows, :])
        grad = grad_ref[rows, :]
        grad_probs = mm_t(grad, qkv_ref[span, 2 * HD : 3 * HD])
        inner = jnp.sum(probs * grad_probs, axis=-1, keepdims=True)
        grad_scores = (probs * (grad_probs - inner)).astype(low)
        scale = HD ** (-0.5)
        grad_query = mm(grad_scores, qkv_ref[span, HD : 2 * HD]) * scale
        out_ref[rows, 0:HD] = turn_back(grad_query, rows).astype(low)
        key_acc[span, :] += t_mm(grad_scores, qkv_ref[rows, 0:HD]) * scale
        value_acc[span, :] += t_mm(probs.astype(low), grad)
    for block in range(LENGTH // QBLOCK):
        rows = pl.ds(block * QBLOCK, QBLOCK)
        out_ref[rows, HD : 2 * HD] = turn_back(key_acc[rows, :], rows).astype(low)
        out_ref[rows, 2 * HD : 3 * HD] = value_acc[rows, :].astype(low)


vmem = pl.BlockSpec(memory_space=pltpu.VMEM)
smem = pl.BlockSpec(memory_space=pltpu.SMEM)
anywhere = pl.BlockSpec(memory_space=pl.ANY)
kernel_params = pltpu.CompilerParams(vmem_limit_bytes=48 * 1024 * 1024)


def attend(qkv, seg_row, seg_blocks):
    return pl.pallas_call(
        attend_kernel,
        out_shape=(
            jax.ShapeDtypeStruct((LENGTH, HD), low),
            jax.ShapeDtypeStruct((LENGTH, 1), wide),
        ),
        in_specs=[vmem] * 3,
        out_specs=(vmem, vmem),
        compiler_params=kernel_params,
        cost_estimate=pl.CostEstimate(
            flops=2 * LENGTH * LENGTH * HD, bytes_accessed=4 * LENGTH * HD * 2, transcendentals=LENGTH * LENGTH // 2
        ),
        name="attend",
    )(qkv, seg_row, seg_blocks)


def attend_back(qkv, grad, total, seg_row, seg_blocks, cos_all, sin_all):
    return pl.pallas_call(
        attend_back_kernel,
        out_shape=jax.ShapeDtypeStruct((LENGTH, 3 * HD), low),
        in_specs=[vmem] * 7,
        out_specs=vmem,
        scratch_shapes=[pltpu.VMEM((LENGTH, HD), wide), pltpu.VMEM((LENGTH, HD), wide)],
        compiler_params=kernel_params,
        cost_estimate=pl.CostEstimate(
            flops=5 * LENGTH * LENGTH * HD, bytes_accessed=8 * LENGTH * HD * 2, transcendentals=LENGTH * LENGTH // 2
        ),
        name="attend_back",
    )(qkv, grad, total, seg_row, seg_blocks, cos_all, sin_all)


ROWS = 256
FF_TILES = [(start, min(256, FF - start)) for start in range(0, FF, 256)]
PACK = 3 * SH_OWN + 3 * FF


def params(mebibytes):
    return pltpu.CompilerParams(vmem_limit_bytes=mebibytes * 1024 * 1024)


def cost(flops, moved, special=0):
    return pl.CostEstimate(flops=int(flops), bytes_accessed=int(moved), transcendentals=int(special))


def project_kernel(*refs):
    pieces, (attn_ref, cos_ref, sin_ref) = refs[:10], refs[10:13]
    normed_ref, sent_ref, factor_ref, gains_ref, ids_ref, hidden, sems = refs[13:]
    copies = load_pieces(pieces, hidden, ids_ref, sems)
    pick = lax.broadcasted_iota(jnp.int32, (16, TOK), 0) == lax.broadcasted_iota(jnp.int32, (16, TOK), 1)
    gains_ref[...] = mm_t(pick.astype(wide).astype(low), attn_ref[:, 768:896])
    for copy in copies:
        copy.wait()
    gain = gains_ref[0:1, :]

    @pl.loop(0, ALL // ROWS)
    def step(index):
        rows = pl.ds(index * ROWS, ROWS)
        values = hidden[rows, :].astype(wide)
        factor = lax.rsqrt(jnp.mean(values * values, axis=-1, keepdims=True) + eps_norm)
        factor_ref[rows, :] = factor
        normed = (values * factor * gain).astype(low)
        normed_ref[rows, :] = normed
        raw = mm(normed, attn_ref[:, 0:512])

        def turn(value):
            return (value * cos_ref[...] + pltpu.roll(value, HD // 2, 1) * sin_ref[...]).astype(low)

        key = turn(raw[:, 2 * HD : 3 * HD])
        value = raw[:, 3 * HD :].astype(low)
        for head in range(2):
            query = turn(raw[:, head * HD : (head + 1) * HD])
            for part in range(2):
                place = pl.ds(index * 4 * TOK + (2 * part + head) * TOK, TOK)
                within = slice(part * TOK, (part + 1) * TOK)
                sent_ref[place, 0:HD] = query[within]
                sent_ref[place, HD : 2 * HD] = key[within]
                sent_ref[place, 2 * HD : 3 * HD] = value[within]


def project(pieces, attn_all, cos_two, sin_two):
    return pl.pallas_call(
        project_kernel,
        out_shape=(
            jax.ShapeDtypeStruct((ALL, D), low),
            jax.ShapeDtypeStruct((LENGTH, 3 * HD), low),
            jax.ShapeDtypeStruct((ALL, 1), wide),
            jax.ShapeDtypeStruct((16, D), wide),
            jax.ShapeDtypeStruct((SEQS * 16, D), low),
        ),
        in_specs=[anywhere] * 10 + [vmem] * 3,
        out_specs=tuple([vmem] * 5),
        scratch_shapes=[pltpu.VMEM((ALL, D), low), pltpu.SemaphoreType.DMA((20,))],
        compiler_params=params(40),
        cost_estimate=cost(2.2e9, 16e6),
        name="project",
    )(*pieces, attn_all, cos_two, sin_two)


def mix_back_kernel(*refs):
    pieces, weight_ref = refs[:10], refs[10]
    grad_ref, extra_ref, sent_ref, sems = refs[11:]
    for copy in load_pieces(pieces, grad_ref, extra_ref, sems):
        copy.wait()

    @pl.loop(0, ALL // ROWS)
    def step(index):
        grad = mm_t(grad_ref[pl.ds(index * ROWS, ROWS), :], weight_ref[...]).astype(low)
        for part in range(2):
            for head in range(2):
                place = pl.ds(index * 4 * TOK + (2 * part + head) * TOK, TOK)
                sent_ref[place, :] = grad[part * TOK : (part + 1) * TOK, head * HD : (head + 1) * HD]


def mix_back(pieces, weight):
    return pl.pallas_call(
        mix_back_kernel,
        out_shape=(
            jax.ShapeDtypeStruct((ALL, D), low),
            jax.ShapeDtypeStruct((SEQS * 16, D), low),
            jax.ShapeDtypeStruct((LENGTH, HD), low),
        ),
        in_specs=[anywhere] * 10 + [vmem],
        out_specs=(vmem, vmem, vmem),
        scratch_shapes=[pltpu.SemaphoreType.DMA((20,))],
        compiler_params=params(40),
        cost_estimate=cost(1.1e9, 10e6),
        name="mix_back",
    )(*pieces, weight)


def collect_kernel(core_ref, grads_ref, query_ref, mine_ref, other_ref):
    first = core_ref[0] == 0

    @pl.loop(0, SEQS)
    def step(index):
        rows = pl.ds(index * TOK, TOK)
        swapped = pl.ds(((index + SEQS // 2) % SEQS) * TOK, TOK)
        one = grads_ref[pl.ds(index * 2 * TOK, TOK), :]
        two = grads_ref[pl.ds(index * 2 * TOK + TOK, TOK), :]
        query_ref[rows, 0:HD] = one[:, :HD]
        query_ref[rows, HD : 2 * HD] = two[:, :HD]
        total = one[:, HD:].astype(wide) + two[:, HD:].astype(wide)
        lower = jnp.concatenate([total[:, : HD // 2], total[:, HD : HD + HD // 2]], axis=1)
        upper = jnp.concatenate([total[:, HD // 2 : HD], total[:, HD + HD // 2 :]], axis=1)
        mine_ref[rows, :] = jnp.where(first, lower, upper)
        other_ref[swapped, :] = jnp.where(first, upper, lower).astype(low)


def collect(core, grads):
    return pl.pallas_call(
        collect_kernel,
        out_shape=(
            jax.ShapeDtypeStruct((ALL, 2 * HD), low),
            jax.ShapeDtypeStruct((ALL, HD), wide),
            jax.ShapeDtypeStruct((ALL, HD), low),
        ),
        in_specs=[smem, vmem],
        out_specs=(vmem, vmem, vmem),
        compiler_params=params(32),
        cost_estimate=cost(1e6, 4e6),
        name="collect",
    )(core, grads)


def qkv_weights_kernel(normed_ref, query_ref, mine_ref, got_ref, out_ref, grad_ref):
    grad_ref[:, 0 : 2 * HD] = query_ref[...]
    grad_ref[:, 2 * HD : 3 * HD] = (mine_ref[...] + got_ref[...].astype(wide)).astype(low)

    @pl.loop(0, D // ROWS)
    def step(index):
        columns = pl.ds(pl.multiple_of(index * ROWS, ROWS), ROWS)
        out_ref[pl.ds(index * ROWS, ROWS), :] = t_mm(normed_ref[:, columns], grad_ref[...]).astype(low)


def qkv_weights(normed, query, mine, got):
    return pl.pallas_call(
        qkv_weights_kernel,
        out_shape=(jax.ShapeDtypeStruct((D, 3 * HD), low), jax.ShapeDtypeStruct((ALL, 3 * HD), low)),
        in_specs=[vmem] * 4,
        out_specs=(vmem, vmem),
        compiler_params=params(32),
        cost_estimate=cost(1.6e9, 8e6),
        name="qkv_weights",
    )(normed, query, mine, got)


def finish_kernel(shards_ref, query_ref, key_ref, value_ref, out_ref, gain_ref):
    gain = jnp.zeros((TOK, TOK), wide)
    for source in range(EXPERTS):
        query_ref[:, source * 256 : (source + 1) * 256] = shards_ref[source, :, 0:256].astype(wide)
        out_ref[:, source * 256 : (source + 1) * 256] = shards_ref[source, :, 384:640].astype(wide)
        gain = gain + shards_ref[source, :, 640:768].astype(wide)
    for pair in range(KV):
        one = shards_ref[2 * pair, :, 256:384].astype(wide)
        two = shards_ref[2 * pair + 1, :, 256:384].astype(wide)
        columns = slice(pair * HD, (pair + 1) * HD)
        key_ref[:, columns] = jnp.concatenate([one[:, : HD // 2], two[:, : HD // 2]], axis=1)
        value_ref[:, columns] = jnp.concatenate([one[:, HD // 2 :], two[:, HD // 2 :]], axis=1)
    gain_ref[...] = jnp.sum(gain, axis=1, keepdims=True)


def finish(shards):
    widths = (H * HD, KV * HD, KV * HD, H * HD, 1)
    return pl.pallas_call(
        finish_kernel,
        out_shape=tuple(jax.ShapeDtypeStruct((TOK, width), wide) for width in widths),
        in_specs=[vmem],
        out_specs=tuple([vmem] * 5),
        compiler_params=params(32),
        cost_estimate=cost(1e6, 4e6),
        name="finish",
    )(shards)


def finish_shared_kernel(*refs):
    shards, spread_ref, spread_rows_ref = refs[:3]
    gate_ref, up_ref, down_ref, left, rows_in = refs[3:]
    width = SH_OWN // 2
    for block in range(EXPERTS):
        rows = pl.ds(block * TOK, TOK)
        for part in range(4):
            left[part * TOK : (part + 1) * TOK, block * width : (block + 1) * width] = shards[
                rows, part * width : (part + 1) * width
            ]
        packed = shards[rows, 2 * SH_OWN : 3 * SH_OWN].astype(wide)
        rows_in[block * SH_PAD : (block + 1) * SH_PAD, :] = jnp.concatenate(
            [
                jnp.concatenate(
                    [packed[8 * j : 8 * j + 8, 128 * i : 128 * i + 128] for j in range(D // 128)], axis=1
                )
                for i in range(SH_PAD // 8)
            ],
            axis=0,
        )
    for start in range(0, SH // 2, 256):
        count = min(256, SH // 2 - start)
        both = mm(left[...], spread_ref[:, start : start + count])
        for part in range(4):
            target = gate_ref if part < 2 else up_ref
            begin = (part % 2) * (SH // 2) + start
            target[:, begin : begin + count] = both[part * TOK : (part + 1) * TOK]
    down_ref[...] = mm(spread_rows_ref[...], rows_in[...].astype(low))


def finish_shared(shards, spread, spread_rows):
    return pl.pallas_call(
        finish_shared_kernel,
        out_shape=(
            jax.ShapeDtypeStruct((TOK, SH), wide),
            jax.ShapeDtypeStruct((TOK, SH), wide),
            jax.ShapeDtypeStruct((SH_ROWS, D), wide),
        ),
        in_specs=[vmem] * 3,
        out_specs=(vmem, vmem, vmem),
        scratch_shapes=[
            pltpu.VMEM((4 * TOK, EXPERTS * SH_OWN // 2), low),
            pltpu.VMEM((EXPERTS * SH_PAD, D), wide),
        ],
        compiler_params=params(40),
        cost_estimate=cost(2.2e9, 12e6),
        name="finish_shared",
    )(shards, spread, spread_rows)


def halves(value):
    upper = value.astype(low)
    return upper, (value - upper.astype(wide)).astype(low)


def silu_parts(gate_value):
    sig = 1.0 / (1.0 + jnp.exp(-gate_value))
    return sig, gate_value * sig


def swiglu_back(sig, act, up_value, grad):
    return (grad * up_value * (sig + act * (1.0 - sig))).astype(low), (grad * act).astype(low)


def pack_rows(block):
    count, width = block.shape[0] // 8, block.shape[1] // 128
    return jnp.concatenate(
        [
            jnp.concatenate(
                [block[8 * i : 8 * i + 8, 128 * j : 128 * j + 128] for i in range(count)], axis=1
            )
            for j in range(width)
        ],
        axis=0,
    )


def ffn_kernel(*refs):
    expert_ref, slots_hbm, slots_t_hbm, routes_ref, router_hbm = refs[:5]
    pieces, cot_pieces, pack_ref = refs[5:15], refs[15:25], refs[25]
    grad_mine, grad_other, gates_ref = refs[26:29]
    outs = refs[29:37]
    normed_ref, cot_ref, grad_ref = refs[37:40]
    kept = refs[40:48]
    hidden_s, grad_s, incoming, hidden_e, gated, grad_rows, grad_e, w_down_s = kept
    w_in_s, w_in, w_down, slots_ref, slots_t_ref = refs[48:53]
    raw, gate_parts, grad_in, piece_sems, cot_sems, sems, out_sems = refs[53:]
    base = 3 * SH_OWN
    half_d = D // 2

    def stage_shared(part):
        return pltpu.make_async_copy(
            pack_ref.at[pl.ds(part * half_d, half_d), pl.ds(2 * SH_OWN, SH_OWN)],
            grad_ref.at[:, pl.ds(FF + part * SH_OWN, SH_OWN)],
            sems.at[part],
        )

    def stage_down(part):
        return pltpu.make_async_copy(
            pack_ref.at[pl.ds(part * half_d, half_d), pl.ds(base + 2 * FF, FF)],
            grad_ref.at[:, pl.ds(0, FF)],
            sems.at[2 + part],
        )

    def unpack(target, pair, row, start, width):
        count = 2 * width // FSDP
        both = [
            pack_rows(grad_ref[row + part * TOK : row + (part + 1) * TOK, start : start + width].astype(wide))
            for part in range(2)
        ]
        target[pair * count : (pair + 1) * count, :] = jnp.concatenate(both, axis=0).astype(low)

    copies = [
        pltpu.make_async_copy(router_hbm, w_in_s.at[:, pl.ds(2 * SH_OWN, 128)], sems.at[4]),
        pltpu.make_async_copy(pack_ref.at[:, pl.ds(0, 2 * SH_OWN)], w_in_s.at[:, pl.ds(0, 2 * SH_OWN)], sems.at[5]),
        pltpu.make_async_copy(slots_hbm, slots_ref, sems.at[6]),
        pltpu.make_async_copy(pack_ref.at[:, pl.ds(base, 2 * FF)], w_in, sems.at[7]),
        pltpu.make_async_copy(slots_t_hbm, slots_t_ref, sems.at[8]),
    ]
    stage_shared(0).start()
    stage_shared(1).start()
    copies[0].start()
    copies[1].start()
    piece_copies = load_pieces(pieces, normed_ref, None, piece_sems)
    cot_copies = load_pieces(cot_pieces, cot_ref, None, cot_sems)
    stage_down(0).start()
    for copy in copies[2:]:
        copy.start()

    def send(index):
        copy = pltpu.make_async_copy(kept[index], outs[index], out_sems.at[index])
        copy.start()
        return copy

    expert = expert_ref[0]
    lane = lax.broadcasted_iota(jnp.int32, (ROWS, 128), 1)
    for part in range(2):
        stage_shared(part).wait()
        for pair in range(4):
            unpack(w_down_s, part * 4 + pair, pair * 2 * TOK, FF + part * SH_OWN, SH_OWN)
    for copy in piece_copies + cot_copies + copies[:2]:
        copy.wait()
    stage_down(0).wait()
    for step in range(ALL // ROWS):
        unpack(w_down, step, step * 2 * TOK, 0, FF)
        rows = pl.ds(step * ROWS, ROWS)
        both = mm(normed_ref[rows, :], w_in_s[...])
        sig, act = silu_parts(both[:, :SH_OWN])
        up = both[:, SH_OWN : 2 * SH_OWN]
        hidden_s[rows, :] = (act * up).astype(low)
        grad_hidden = mm_t(cot_ref[rows, :], w_down_s[...])
        grad_gate, grad_up = swiglu_back(sig, act, up, grad_hidden)
        grad_s[rows, 0:SH_OWN] = grad_gate
        grad_s[rows, SH_OWN : 2 * SH_OWN] = grad_up
        logits = both[:, 2 * SH_OWN :]
        first, second = routes_ref[rows, 0:1], routes_ref[rows, 1:2]
        chosen_first = jnp.sum(jnp.where(lane == first + 2, logits, 0.0), axis=1, keepdims=True)
        chosen_second = jnp.sum(jnp.where(lane == second + 2, logits, 0.0), axis=1, keepdims=True)
        gate_first = 1.0 / (1.0 + jnp.exp(chosen_second - chosen_first))
        gate_second = 1.0 / (1.0 + jnp.exp(chosen_first - chosen_second))
        here = jnp.where(first == expert, gate_first, 0.0) + jnp.where(second == expert, gate_second, 0.0)
        upper, lower = halves(here)
        parts = jnp.where(lane == 0, upper.astype(wide), 0.0) + jnp.where(lane == 1, lower.astype(wide), 0.0)
        gate_parts[rows, :] = parts.astype(low)
        if step == 0:
            both_gates = jnp.where(lane == 0, gate_first, 0.0) + jnp.where(lane == 1, gate_second, 0.0)
            gates_ref[...] = both_gates[:TOK]
    stage_down(1).start()
    sent = [send(0), send(1), send(7)]
    copies[2].wait()
    for step in range(D // ROWS):
        columns = pl.ds(step * ROWS, ROWS)
        incoming[:, columns] = mm(slots_ref[...], normed_ref[:, columns]).astype(low)
        grad_rows[:, columns] = mm(slots_ref[...], cot_ref[:, columns]).astype(low)
    slot_parts = mm(slots_ref[...], gate_parts[...])
    slot_gate = slot_parts[:, 0:1] + slot_parts[:, 1:2]
    sent.append(send(2))
    copies[3].wait()
    stage_down(1).wait()
    for step in range(4):
        unpack(w_down, 4 + step, step * 2 * TOK, 0, FF)
    for step in range(2 * FF // ROWS):
        columns = pl.ds(step * ROWS, ROWS)
        raw[:, columns] = mm(incoming[...], w_in[:, columns])
    for start, width in FF_TILES:
        gate, up = raw[:, start : start + width], raw[:, FF + start : FF + start + width]
        hidden_e[:, start : start + width] = (silu_parts(gate)[1] * up).astype(low)
    sent.append(send(3))
    slot_grad = jnp.zeros((SLOTS, 1), wide)
    for step in range(D // ROWS):
        columns = pl.ds(step * ROWS, ROWS)
        rows = mm(hidden_e[...], w_down[:, columns]).astype(low).astype(wide)
        cot = grad_rows[:, columns].astype(wide)
        gated[:, columns] = (rows * slot_gate).astype(low)
        grad_rows[:, columns] = (cot * slot_gate).astype(low)
        slot_grad = slot_grad + jnp.sum(rows * cot, axis=1, keepdims=True)
    sent += [send(4), send(5)]
    for start, width in FF_TILES:
        grad_hidden = mm_t(grad_rows[...], w_down[pl.ds(start, width), :])
        sig, act = silu_parts(raw[:, start : start + width])
        grad_gate, grad_up = swiglu_back(sig, act, raw[:, FF + start : FF + start + width], grad_hidden)
        grad_e[:, start : start + width] = grad_gate
        grad_e[:, FF + start : FF + start + width] = grad_up
    sent.append(send(6))
    for step in range(D // ROWS):
        columns = pl.ds(step * ROWS, ROWS)
        grad_in[:, columns] = mm_t(grad_e[...], w_in[columns, :]).astype(low)
    upper, lower = halves(slot_grad)
    slot_lane = lax.broadcasted_iota(jnp.int32, (SLOTS, 128), 1)
    slot_parts = (
        jnp.where(slot_lane == expert, upper.astype(wide), 0.0)
        + jnp.where(slot_lane == expert + 8, lower.astype(wide), 0.0)
    ).astype(low)
    copies[4].wait()
    half = ALL // 2
    for side, target in ((1, grad_other), (0, grad_mine)):
        for step in range(half // ROWS):
            rows = pl.ds(side * half + step * ROWS, ROWS)
            for tile in range(D // 512):
                columns = pl.ds(tile * 512, 512)
                grad_ref[rows, columns] = (
                    mm_t(grad_s[rows, :], w_in_s[columns, 0 : 2 * SH_OWN])
                    + mm(slots_t_ref[rows, :], grad_in[:, columns])
                ).astype(low)
            grad_ref[rows, D : D + 128] = mm(slots_t_ref[rows, :], slot_parts).astype(low)
        copy = pltpu.make_async_copy(grad_ref.at[pl.ds(side * half, half), :], target, sems.at[9 + side])
        copy.start()
        sent.append(copy)
    for copy in sent:
        copy.wait()


def ffn(expert, slots, slots_t, routes, router, pieces, cot_pieces, pack):
    kept = [(ALL, SH_OWN), (ALL, 2 * SH_OWN), (SLOTS, D), (SLOTS, FF), (SLOTS, D), (SLOTS, D), (SLOTS, 2 * FF)]
    kept.append((SH_OWN, D))
    grads = [(ALL // 2, D + 128)] * 2
    return pl.pallas_call(
        ffn_kernel,
        out_shape=tuple(
            [jax.ShapeDtypeStruct(shape, low) for shape in grads]
            + [jax.ShapeDtypeStruct((TOK, 128), wide)]
            + [jax.ShapeDtypeStruct(shape, low) for shape in kept]
        ),
        in_specs=[smem, anywhere, anywhere, vmem] + [anywhere] * 22,
        out_specs=tuple([anywhere] * 2 + [vmem] + [anywhere] * 8),
        scratch_shapes=[pltpu.VMEM((ALL, D), low), pltpu.VMEM((ALL, D), low), pltpu.VMEM((ALL, D + 128), low)]
        + [pltpu.VMEM(shape, low) for shape in kept]
        + [
            pltpu.VMEM((D, 2 * SH_OWN + 128), low),
            pltpu.VMEM((D, 2 * FF), low),
            pltpu.VMEM((FF, D), low),
            pltpu.VMEM((SLOTS, ALL), low),
            pltpu.VMEM((ALL, SLOTS), low),
            pltpu.VMEM((SLOTS, 2 * FF), wide),
            pltpu.VMEM((ALL, 128), low),
            pltpu.VMEM((SLOTS, D), low),
            pltpu.SemaphoreType.DMA((20,)),
            pltpu.SemaphoreType.DMA((20,)),
            pltpu.SemaphoreType.DMA((11,)),
            pltpu.SemaphoreType.DMA((8,)),
        ],
        compiler_params=params(60),
        cost_estimate=cost(27e9, 50e6, 1e6),
        name="ffn",
    )(expert, slots, slots_t, routes, router, *pieces, *cot_pieces, pack)


def slab(buffer, out_ref, sems, step, start):
    return pltpu.make_async_copy(
        buffer.at[step % 2],
        out_ref.at[pl.ds(step * ROWS, ROWS), pl.ds(start, buffer.shape[2])],
        sems.at[step % 2],
    )


def weight_slabs(tokens_ref, grad_ref, down, out_ref, buffer, sems, start):
    width = grad_ref.shape[1]
    count = width // 2 // FSDP
    for step in range(D // ROWS):
        slot = step % 2
        if step >= 2:
            slab(buffer, out_ref, sems, step - 2, start).wait()
        buffer[slot, :, 0:width] = t_mm(tokens_ref[:, pl.ds(step * ROWS, ROWS)], grad_ref[...]).astype(low)
        for part in range(ROWS // TOK):
            place = step * (ROWS // TOK) + part
            packed = pack_rows(down[pl.ds(place * count, count), :]).astype(low)
            buffer[slot, part * TOK : (part + 1) * TOK, width:] = packed
        slab(buffer, out_ref, sems, step, start).start()
    for step in (D // ROWS - 2, D // ROWS - 1):
        slab(buffer, out_ref, sems, step, start).wait()


def shared_weights_kernel(*refs):
    pieces, cot_pieces, hidden_ref, grad_ref = refs[:10], refs[10:20], refs[20], refs[21]
    out_ref, normed_ref, cot_ref, buffer, down, piece_sems, cot_sems, sems = refs[22:]
    cot_copies = load_pieces(cot_pieces, cot_ref, None, cot_sems)
    copies = load_pieces(pieces, normed_ref, None, piece_sems)
    for copy in cot_copies:
        copy.wait()
    for tile in range(D // ROWS):
        part = pl.ds(tile * ROWS, ROWS)
        down[:, part] = t_mm(hidden_ref[...], cot_ref[:, part])
    for copy in copies:
        copy.wait()
    weight_slabs(normed_ref, grad_ref, down, out_ref, buffer, sems, 0)


def shared_weights(pieces, cot_pieces, hidden, grad):
    return pl.pallas_call(
        shared_weights_kernel,
        out_shape=(jax.ShapeDtypeStruct((D, PACK), low), jax.ShapeDtypeStruct((ALL, D), low)),
        in_specs=[anywhere] * 20 + [vmem] * 2,
        out_specs=(anywhere, vmem),
        scratch_shapes=[
            pltpu.VMEM((ALL, D), low),
            pltpu.VMEM((2, ROWS, 3 * SH_OWN), low),
            pltpu.VMEM((SH_OWN, D), wide),
            pltpu.SemaphoreType.DMA((20,)),
            pltpu.SemaphoreType.DMA((20,)),
            pltpu.SemaphoreType.DMA((2,)),
        ],
        compiler_params=params(60),
        cost_estimate=cost(5e9, 18e6),
        name="shared_weights",
    )(*pieces, *cot_pieces, hidden, grad)


def expert_weights_kernel(_, incoming_ref, hidden_ref, grad_rows_ref, grad_ref, out_ref, buffer, down, sems):
    for tile in range(D // ROWS):
        part = pl.ds(tile * ROWS, ROWS)
        down[:, part] = t_mm(hidden_ref[...], grad_rows_ref[:, part])
    weight_slabs(incoming_ref, grad_ref, down, out_ref, buffer, sems, 3 * SH_OWN)


def expert_weights(*operands):
    return pl.pallas_call(
        expert_weights_kernel,
        out_shape=jax.ShapeDtypeStruct((D, PACK), low),
        in_specs=[anywhere] + [vmem] * 4,
        out_specs=anywhere,
        scratch_shapes=[
            pltpu.VMEM((2, ROWS, 3 * FF), low),
            pltpu.VMEM((FF, D), wide),
            pltpu.SemaphoreType.DMA((2,)),
        ],
        input_output_aliases={0: 0},
        compiler_params=params(48),
        cost_estimate=cost(6e9, 24e6),
        name="expert_weights",
    )(*operands)


def out_rows_kernel(place_ref, *refs):
    parts, out_ref = refs[:5], refs[5]
    for index in range(EXPERTS):
        step, side = index // 2, index % 2
        columns = pl.ds(pl.multiple_of(place_ref[index] * 256, 256), 256)
        out_ref[:, columns] = parts[step + 1][side] if step else parts[side][...]


def out_rows(places, parts):
    return pl.pallas_call(
        out_rows_kernel,
        out_shape=jax.ShapeDtypeStruct((256, D), low),
        in_specs=[smem] + [vmem] * 5,
        out_specs=vmem,
        compiler_params=params(32),
        cost_estimate=cost(0, 2e6),
        name="out_rows",
    )(places, *parts)


def out_weights_kernel(place_ref, mixed_ref, grad_ref, normed_ref, logits_ref, mine_ref, other_ref, router_ref):
    for index in range(EXPERTS):
        columns = pl.ds(pl.multiple_of(place_ref[index] * 256, 256), 256)
        target = mine_ref if index < 4 else other_ref
        target[index % 4] = t_mm(mixed_ref[...], grad_ref[:, columns]).astype(low)
    router_ref[...] = mm(logits_ref[...], normed_ref[...])


def out_weights(owners, mixed, grad, normed, logits):
    blocks = jax.ShapeDtypeStruct((4, 256, 256), low)
    return pl.pallas_call(
        out_weights_kernel,
        out_shape=(blocks, blocks, jax.ShapeDtypeStruct((2 * EXPERTS, D), wide)),
        in_specs=[smem] + [vmem] * 4,
        out_specs=(vmem, vmem, vmem),
        compiler_params=params(32),
        cost_estimate=cost(1.2e9, 10e6),
        name="out_weights",
    )(owners, mixed, grad, normed, logits)


def back_two_kernel(
    own_ref, first_ref, second_ref, middle_ref, cot_ref, gains_ref, gates_ref, routes_ref, block_ref, grad_ref
):
    total = own_ref[...] + first_ref[...].astype(wide) + second_ref[...].astype(wide)
    lane = lax.broadcasted_iota(jnp.int32, (TOK, 128), 1)
    extra = total[:, D:]
    first, second = routes_ref[:, 0:1], routes_ref[:, 1:2]

    def taken(route):
        return jnp.sum(jnp.where((lane == route) | (lane == route + 8), extra, 0.0), axis=1, keepdims=True)

    gate_first, gate_second = gates_ref[:, 0:1], gates_ref[:, 1:2]
    taken_first, taken_second = taken(first), taken(second)
    inner = gate_first * taken_first + gate_second * taken_second
    chosen_first, chosen_second = gate_first * (taken_first - inner), gate_second * (taken_second - inner)
    logits = jnp.where(lane == first, chosen_first, 0.0) + jnp.where(lane == second, chosen_second, 0.0)
    grad = total[:, :D]
    for index in range(EXPERTS):
        grad = grad + logits[:, index : index + 1] * gains_ref[2 + index : 3 + index, :]
    middle = middle_ref[...]
    factor = lax.rsqrt(jnp.mean(middle * middle, axis=-1, keepdims=True) + eps_norm)
    scaled = grad * gains_ref[1:2, :]
    mean = jnp.mean(scaled * middle, axis=-1, keepdims=True)
    result = cot_ref[...].astype(wide) + factor * scaled - middle * (factor * factor * factor * mean)
    grad_ref[...] = result
    block_ref[0:TOK, :] = result.astype(low)
    gain_upper, gain_lower = halves(jnp.sum(grad * middle * factor, axis=0, keepdims=True))
    upper, lower = halves(logits.T[0:EXPERTS, :])
    rows = [gain_upper, gain_lower]
    upper, lower = upper.astype(wide), lower.astype(wide)
    flat = [upper[index : index + 1, :] for index in range(EXPERTS)] + [
        lower[index : index + 1, :] for index in range(EXPERTS)
    ]
    rows.append(jnp.concatenate(flat, axis=1))
    rows = [row.astype(wide) for row in rows] + [jnp.zeros((13, D), wide)]
    block_ref[TOK : TOK + 16, :] = jnp.concatenate(rows, axis=0).astype(low)


def back_two(*operands):
    return pl.pallas_call(
        back_two_kernel,
        out_shape=(jax.ShapeDtypeStruct((TOK + 16, D), low), jax.ShapeDtypeStruct((TOK, D), wide)),
        in_specs=[vmem] * 8,
        out_specs=(vmem, vmem),
        compiler_params=params(32),
        cost_estimate=cost(1e7, 6e6),
        name="back_two",
    )(*operands)


def norm_factor(values):
    return lax.rsqrt(jnp.mean(values * values, axis=-1, keepdims=True) + eps_norm)


def norm_back(values, factor, gain, grad):
    scaled = grad * gain
    inner = jnp.mean(scaled * values, axis=-1, keepdims=True)
    return factor * scaled - values * (factor * factor * factor * inner)


def per_device(
    hidden_in,
    cotangent,
    segments,
    routes,
    attn_gain,
    w_query,
    w_key,
    w_value,
    w_out,
    ffn_gain,
    w_router,
    shared_gate,
    shared_up,
    shared_down,
    expert_gate,
    expert_up,
    expert_down,
):
    expert = lax.axis_index("expert")
    z, core = expert // 2, expert % 2
    place = lax.axis_index("fsdp")

    misc = jnp.concatenate(
        [attn_gain[:, None], ffn_gain[:, None], w_router, jnp.zeros((TOK, 118), low)], axis=1
    )
    attn_pack = jnp.concatenate(
        [
            lax.dynamic_slice_in_dim(w_query, 256 * expert, 256, 1),
            lax.dynamic_slice_in_dim(w_key, HD * z, HD, 1),
            lax.dynamic_slice_in_dim(w_value, HD * z, HD, 1),
            lax.dynamic_slice_in_dim(w_out, 256 * expert, 256, 1),
            misc,
        ],
        axis=1,
    )
    attn_all = lax.all_gather(attn_pack, "fsdp", axis=0, tiled=True)
    half_in, half_out = SH // 2, SH_OWN // 2
    sel_column = jnp.arange(half_out)
    picked = SH_ROWS * (sel_column // SH_PAD) + SH_PART * expert + sel_column % SH_PAD
    picked = jnp.where(sel_column % SH_PAD < SH_PART, picked, -1)
    select = (jnp.arange(half_in)[:, None] == picked[None, :]).astype(low)
    own_shared = mm(
        jnp.concatenate(
            [shared_gate[:, :half_in], shared_gate[:, half_in:], shared_up[:, :half_in], shared_up[:, half_in:]],
            axis=0,
        ),
        select,
    ).astype(low)
    own_down = jnp.pad(
        lax.dynamic_slice_in_dim(shared_down, SH_PART * expert, SH_PART, 0),
        ((0, SH_PAD - SH_PART), (0, 0)),
    )
    ffn_pack = jnp.concatenate(
        [
            own_shared[:TOK],
            own_shared[TOK : 2 * TOK],
            own_shared[2 * TOK : 3 * TOK],
            own_shared[3 * TOK :],
            pack_tiles(own_down),
            expert_gate[:, 0],
            expert_up[:, 0],
            pack_tiles(expert_down[:, 0]),
        ],
        axis=1,
    )
    ffn_all = lax.all_gather(ffn_pack, "fsdp", axis=0, tiled=True)

    ids = jnp.concatenate(
        [
            segments.astype(low),
            jnp.pad(routes[0].reshape(1, TOK * TOPK), ((0, 0), (0, LENGTH - TOK * TOPK))).astype(low),
            jnp.zeros((14, LENGTH), low),
        ],
        axis=0,
    )
    hidden_pieces = gather_pieces(jnp.concatenate([hidden_in[0], ids], axis=0))
    cot_block, *hidden_pieces = together(cotangent[0], *hidden_pieces)
    cot_pieces = gather_pieces(cot_block)

    inverse_freq = rope_base ** (-jnp.arange(HD // 2, dtype=wide) * 2.0 / HD)
    angles = jnp.arange(LENGTH).astype(wide)[:, None] * inverse_freq[None, :]
    cosine, sine = jnp.cos(angles), jnp.sin(angles)
    cos_all = jnp.concatenate([cosine, cosine], axis=1)
    sin_back = jnp.concatenate([sine, -sine], axis=1)
    cos_own = lax.dynamic_slice_in_dim(cos_all, place * TOK, TOK, 0)
    sin_own = -lax.dynamic_slice_in_dim(sin_back, place * TOK, TOK, 0)
    cos_two, sin_two = jnp.concatenate([cos_own, cos_own]), jnp.concatenate([sin_own, sin_own])
    attn_all, cos_two, sin_two, cos_all, sin_back = together(attn_all, cos_two, sin_two, cos_all, sin_back)
    normed_one, sent, factor_one, gains, ids_all = project(hidden_pieces, attn_all, cos_two, sin_two)
    qkv = lax.all_to_all(sent, "fsdp", split_axis=0, concat_axis=0, tiled=True)

    ids_all = ids_all.reshape(SEQS, 16, D)
    seg_row = lax.dynamic_slice_in_dim(ids_all[:, 0].astype(wide), place // 2, 1, 0)
    seg_blocks = jnp.pad(seg_row.reshape(FSDP, TOK), ((0, TOK - FSDP), (0, 0)))
    route_all = ids_all[:, 1, : TOK * TOPK].astype(jnp.int32).reshape(ALL, TOPK)
    hit = jnp.any(route_all == expert, axis=1).astype(wide)
    order = jnp.arange(ALL)
    rank = mm(hit.astype(low)[None, :], (order[:, None] < order[None, :]).astype(low))
    slot_bool = (rank.astype(jnp.int32) == jnp.arange(SLOTS)[:, None]) & (hit > 0.5)[None, :]
    slots = slot_bool.astype(low)
    slots_t = slot_bool.T.astype(low)
    out_columns = attn_all[:, 512:768].reshape(EXPERTS, 256, 256)
    owners = jnp.stack([relative_owner(expert, block) for block in range(EXPERTS)])
    out_blocks = [lax.dynamic_index_in_dim(out_columns, owners[block], 0) for block in range(EXPERTS)]
    out_mine, out_other = jnp.concatenate(out_blocks[:4]), jnp.concatenate(out_blocks[4:])
    out_mine, out_other, _ = together(out_mine, out_other, sent)
    w_out_own = out_rows(source_owners(expert), exchange(out_mine, out_other))
    router = attn_all[:, 768:896]
    is_first = core == 0
    kv_weight = attn_all[:, 256:512].reshape(D, 2, 2, HD // 2)
    kv_weight = jnp.where(is_first, kv_weight[:, :, 0], kv_weight[:, :, 1]).reshape(D, HD)
    qkv_weight = jnp.concatenate([attn_all[:, :256], kv_weight], axis=1)
    route_own = route_all[:TOK]
    qkv, seg_row, seg_blocks, route_all, slots, slots_t, w_out_own, router, qkv_weight, route_own, *cot_pieces = together(
        qkv, seg_row, seg_blocks, route_all, slots, slots_t, w_out_own, router, qkv_weight, route_own, *cot_pieces
    )
    mixed_head, log_total = attend(qkv, seg_row, seg_blocks)
    mixed = (
        lax.all_to_all(mixed_head, "fsdp", split_axis=0, concat_axis=0, tiled=True)
        .reshape(SEQS, 2, TOK, HD)
        .transpose(0, 2, 1, 3)
        .reshape(ALL, 2 * HD)
    )
    own_hidden = hidden_in[0].astype(wide)
    half = ALL // 2
    middle = own_hidden + scatter_rows(
        mm(mixed[:half], w_out_own).astype(low), mm(mixed[half:], w_out_own).astype(low)
    )
    factor_two = norm_factor(middle)
    gain_one, gain_two = gains[0:1], gains[1:2]
    normed_block = (middle * factor_two * gain_two).astype(low)

    base = 3 * SH_OWN
    normed_pieces = gather_pieces(normed_block)
    (
        grad_mine,
        grad_other,
        gates,
        hidden_shared,
        grad_shared,
        incoming,
        hidden_expert,
        gated_rows,
        grad_rows,
        grad_expert,
        shared_down_w,
    ) = ffn(expert[None], slots, slots_t, route_all, router, normed_pieces, cot_pieces, ffn_all)
    received = swap_core(grad_other)
    ffn_grads, normed_two = shared_weights(normed_pieces, cot_pieces, hidden_shared, grad_shared)
    received, ffn_grads = together(received, ffn_grads)
    own_grad, to_above, to_below = scatter_start(grad_mine, received)
    to_above, to_below, ffn_grads = together(to_above, to_below, ffn_grads)
    from_below, from_above = move_z(to_above, 1), move_z(to_below, -1)
    ffn_grads = expert_weights(ffn_grads, incoming, hidden_expert, grad_rows, grad_expert)
    from_below, from_above, ffn_grads = together(from_below, from_above, ffn_grads)
    ffn_sums = lax.psum_scatter(ffn_grads, "fsdp", scatter_dimension=0, tiled=True)
    back_block, grad_middle = back_two(
        own_grad, from_below, from_above, middle, cotangent[0], gains, gates, route_own
    )
    back_block, hidden_shared, gated_rows = together(back_block, hidden_shared, gated_rows)
    below, above = first_pieces(back_block)
    result_other = (mm(hidden_shared[half:], shared_down_w) + mm(slots_t[half:], gated_rows)).astype(low)
    result_mine = (mm(hidden_shared[:half], shared_down_w) + mm(slots_t[:half], gated_rows)).astype(low)
    below, above, result_other, result_mine = together(below, above, result_other, result_mine)
    back_pieces = other_pieces(back_block, below, above)

    grad_attn, extra, sent_back = mix_back(back_pieces, w_out_own)
    grad_head = lax.all_to_all(sent_back, "fsdp", split_axis=0, concat_axis=0, tiled=True)
    grads_head = attend_back(qkv, grad_head, log_total, seg_row, seg_blocks, cos_all, sin_back)
    grads_qkv = lax.all_to_all(grads_head, "fsdp", split_axis=0, concat_axis=0, tiled=True)
    result_other, result_mine, _ = together(result_other, result_mine, sent_back)
    layer_out = (middle + scatter_rows(result_mine, result_other)).astype(low)

    extra, grad_attn, _ = together(extra, grad_attn, grads_head)
    extra = extra.reshape(SEQS, 16, D)
    gain_two_sum = jnp.sum(extra[:, :2].astype(wide), axis=(0, 1))
    logit_rows = extra[:, 2].reshape(SEQS, 2, EXPERTS, TOK).transpose(1, 2, 0, 3).reshape(2 * EXPERTS, ALL)
    out_mine, out_other, grad_router = out_weights(owners, mixed, grad_attn, normed_two, logit_rows)
    out_parts = exchange(out_mine, out_other)
    out_parts = jnp.concatenate([jnp.stack(out_parts[:2])[None], jnp.stack(out_parts[2:])]).reshape(EXPERTS, 256, 256)
    places = [((z - source // 2) % 4) * 2 + (core ^ (source % 2)) for source in range(EXPERTS)]
    grad_out = jnp.stack([lax.dynamic_index_in_dim(out_parts, where, 0, keepdims=False) for where in places])
    grad_out = grad_out.reshape(FSDP, TOK, 256)
    small_rows = jnp.concatenate(
        [grad_router[:EXPERTS] + grad_router[EXPERTS:], gain_two_sum[None], jnp.zeros((7, D), wide)], axis=0
    )
    small_rows = small_rows.reshape(16, FSDP, TOK).transpose(1, 0, 2).astype(low)
    small_rows = jnp.pad(small_rows, ((0, 0), (0, 0), (0, 512)))
    small_rows, grad_out, grads_qkv, layer_out = together(small_rows, grad_out, grads_qkv, layer_out)

    grad_query, kv_mine, kv_other = collect(core[None], grads_qkv)
    qkv_grads, grad_qkv = qkv_weights(normed_one, grad_query, kv_mine, swap_core(kv_other))
    attn_grads = jnp.concatenate([qkv_grads.reshape(FSDP, TOK, 3 * HD), grad_out], axis=2)
    attn_grads = jnp.concatenate([attn_grads, small_rows], axis=1).reshape(FSDP * (TOK + 16), 640)
    attn_parts = lax.all_to_all(attn_grads, "fsdp", split_axis=0, concat_axis=0, tiled=True)

    grad_qkv, _ = together(grad_qkv, attn_grads)
    grad_normed_other = mm_t(grad_qkv[half:], qkv_weight).astype(low)
    grad_normed_mine = mm_t(grad_qkv[:half], qkv_weight).astype(low)
    own_grad_one, to_above, to_below = scatter_start(grad_normed_mine, swap_core(grad_normed_other))
    attn_parts, to_above, to_below = together(attn_parts, to_above, to_below)
    own_grad_one = scatter_end(own_grad_one, move_z(to_above, 1), move_z(to_below, -1))
    grad_input = (grad_middle + norm_back(own_hidden, factor_one[:TOK], gain_one, own_grad_one)).astype(low)
    attn_sums = jnp.sum(attn_parts.reshape(FSDP, TOK + 16, 640).astype(wide), axis=0)

    own_weight = lax.dynamic_slice_in_dim(qkv_weight, place * TOK, TOK, 0)
    gain_part = jnp.sum(attn_sums[:TOK, :384] * own_weight.astype(wide), axis=1, keepdims=True)
    gain_upper, gain_lower = halves(gain_part / attn_gain.astype(wide)[:, None])
    shards = jnp.concatenate(
        [attn_sums[:TOK].astype(low), gain_upper, gain_lower, jnp.zeros((TOK, 126), low)], axis=1
    )
    grad_w_query, grad_w_key, grad_w_value, grad_w_out, grad_attn_gain = finish(
        lax.all_gather(shards, "expert", axis=0)
    )

    ffn_sums, _ = together(ffn_sums, attn_grads)
    put_row = jnp.arange(SH_PAD * EXPERTS * FSDP // 2)
    source, within = put_row // half_out, put_row % half_out
    target = SH_ROWS * (within // SH_PAD) + SH_PART * source + within % SH_PAD
    target = jnp.where(within % SH_PAD < SH_PART, target, -1)
    spread = (target[:, None] == jnp.arange(half_in)[None, :]).astype(low)
    put_row = jnp.arange(EXPERTS * SH_PAD)
    target = SH_PART * (put_row // SH_PAD) + put_row % SH_PAD
    target = jnp.where(put_row % SH_PAD < SH_PART, target, -1)
    spread_rows = (jnp.arange(SH_ROWS)[:, None] == target[None, :]).astype(low)
    spread, spread_rows, _ = together(spread, spread_rows, sent)
    grad_shared_gate, grad_shared_up, grad_shared_down = finish_shared(
        lax.all_gather(ffn_sums[:, :base], "expert", axis=0, tiled=True), spread, spread_rows
    )
    grad_expert_gate = ffn_sums[:, base : base + FF].astype(wide)[:, None]
    grad_expert_up = ffn_sums[:, base + FF : base + 2 * FF].astype(wide)[:, None]
    grad_expert_down = unpack_tiles(ffn_sums[:, base + 2 * FF :], 1).astype(wide)[:, None]
    return (
        layer_out[None],
        grad_input[None],
        grad_attn_gain[:, 0],
        grad_w_query,
        grad_w_key,
        grad_w_value,
        grad_w_out,
        attn_sums[TOK + EXPERTS, :TOK],
        attn_sums[TOK : TOK + EXPERTS, :TOK].T,
        grad_shared_gate,
        grad_shared_up,
        grad_shared_down,
        grad_expert_gate,
        grad_expert_up,
        grad_expert_down,
    )


def solution(mesh):
    in_specs = (
        P("expert", "fsdp", None),
        P("expert", "fsdp", None),
        P("expert", None),
        P("expert", "fsdp", None),
        P("fsdp"),
        P("fsdp", None),
        P("fsdp", None),
        P("fsdp", None),
        P("fsdp", None),
        P("fsdp"),
        P("fsdp", None),
        P("fsdp", None),
        P("fsdp", None),
        P("fsdp", None),
        P("fsdp", "expert", None),
        P("fsdp", "expert", None),
        P("fsdp", "expert", None),
    )
    out_specs = (
        P("expert", "fsdp", None),
        P("expert", "fsdp", None),
        P("fsdp"),
        P("fsdp", None),
        P("fsdp", None),
        P("fsdp", None),
        P("fsdp", None),
        P("fsdp"),
        P("fsdp", None),
        P("fsdp", None),
        P("fsdp", None),
        P("fsdp", None),
        P("fsdp", "expert", None),
        P("fsdp", "expert", None),
        P("fsdp", "expert", None),
    )
    return jax.shard_map(
        per_device, mesh=mesh, in_specs=in_specs, out_specs=out_specs, check_vma=False
    )
```

```python
import jax
import jax.numpy as jnp
from jax import lax
from jax.experimental import pallas as pl
from jax.experimental.pallas import tpu as pltpu
from jax.sharding import PartitionSpec as P

D = 2048
H = 16
KV = 4
HD = 128
FF = 1408
SH = 2816
TOPK = 2
TOK = 128
LENGTH = 2048
SEQS = 8
EXPERTS = 8
FSDP = 16
ALL = SEQS * TOK
CAP = 42
SLOTS = SEQS * CAP
SH_ROWS = SH // FSDP
SH_PART = SH_ROWS // EXPERTS
SH_PAD = 24
SH_OWN = FSDP * SH_PAD
QBLOCK = 256

eps_norm = 1e-06
rope_base = 600000.0
masked_fill = -1e30
low = jnp.bfloat16
wide = jnp.float32


def shift_pairs(step):
    return [(z * 2 + c, ((z + step) % 4) * 2 + c) for z in range(4) for c in range(2)]


core_pairs = [(z * 2 + c, z * 2 + 1 - c) for z in range(4) for c in range(2)]


def move_z(block, step):
    return lax.ppermute(block, "expert", shift_pairs(step))


def swap_core(block):
    return lax.ppermute(block, "expert", core_pairs)


def together(*values):
    return lax.optimization_barrier(values)


TOP = TOK // 2


def first_pieces(block):
    return move_z(block, 1), move_z(block, -1)


def other_pieces(block, below, above):
    upper, lower = move_z(below[:TOP], 1), move_z(above[TOP:], -1)
    mine = [block, above, upper, lower, below]
    return mine + [swap_core(piece) for piece in mine]


def gather_pieces(block):
    return other_pieces(block, *first_pieces(block))


PIECES = [(4 * side + block, start) for side in (0, 1) for block, start in ((0, 0), (1, 0), (2, 0), (2, TOP), (3, 0))]


def load_pieces(refs, rows_ref, extra_ref, sems):
    copies = []
    for index, (ref, (block, start)) in enumerate(zip(refs, PIECES)):
        count = min(ref.shape[0], TOK - start)
        copies.append(
            pltpu.make_async_copy(
                ref.at[pl.ds(0, count), :], rows_ref.at[pl.ds(block * TOK + start, count), :], sems.at[2 * index]
            )
        )
        if extra_ref is not None and ref.shape[0] > count:
            copies.append(
                pltpu.make_async_copy(
                    ref.at[pl.ds(count, 16), :], extra_ref.at[pl.ds(block * 16, 16), :], sems.at[2 * index + 1]
                )
            )
    for copy in copies:
        copy.start()
    return copies


def scatter_start(mine, received):
    chip = mine.reshape(4, TOK, -1).astype(wide) + received.reshape(4, TOK, -1).astype(wide)
    from_below = move_z(chip[2, :TOP].astype(low), 1)
    from_above = move_z(chip[2, TOP:].astype(low), -1)
    to_above = jnp.concatenate([chip[1, :TOP] + from_below.astype(wide), chip[1, TOP:]], axis=0)
    to_below = jnp.concatenate([chip[3, :TOP], chip[3, TOP:] + from_above.astype(wide)], axis=0)
    return chip[0], to_above.astype(low), to_below.astype(low)


def scatter_end(own, first, second):
    return own + first.astype(wide) + second.astype(wide)


def scatter_rows(mine, other):
    own, to_above, to_below = scatter_start(mine, swap_core(other))
    return scatter_end(own, move_z(to_above, 1), move_z(to_below, -1))


def exchange(mine, other):
    got = swap_core(other)
    chip = jnp.stack([mine[1:], got[1:]], axis=1)
    return mine[0], got[0], *[move_z(chip[step - 1], step) for step in (1, 2, 3)]


def source_owners(expert):
    return jnp.stack([((expert // 2 - index // 2) % 4) * 2 + ((expert % 2) ^ (index % 2)) for index in range(EXPERTS)])


def relative_owner(expert, block):
    return ((expert // 2 + block % 4) % 4) * 2 + ((expert % 2) ^ (block // 4))


def pack_tiles(block):
    rows, columns = block.shape[0] // 8, block.shape[1] // 128
    tiles = block.reshape(rows, 8, columns, 128).transpose(2, 1, 0, 3)
    return tiles.reshape(columns * 8, rows * 128)


def unpack_tiles(block, count):
    rows, columns = block.shape[1] // 128, block.shape[0] // (8 * count)
    tiles = block.reshape(count, columns, 8, rows, 128).transpose(0, 3, 2, 1, 4)
    return tiles.reshape(count * rows * 8, columns * 128)


def product(left, right, contract):
    return lax.dot_general(left, right, (contract, ((), ())), preferred_element_type=wide)


def mm(left, right):
    return product(left, right, ((1,), (0,)))


def mm_t(left, right):
    return product(left, right, ((1,), (1,)))


def t_mm(left, right):
    return product(left, right, ((0,), (0,)))


def segment_columns(seg_blocks_ref):
    return seg_blocks_ref[...].T


def block_scores(qkv_ref, seg_row_ref, columns, start, reach):
    query = qkv_ref[pl.ds(start, QBLOCK), 0:HD]
    key = qkv_ref[pl.ds(0, reach), HD : 2 * HD]
    scores = mm_t(query, key) * HD ** (-0.5)
    query_pos = start + lax.broadcasted_iota(jnp.int32, (QBLOCK, reach), 0)
    key_pos = lax.broadcasted_iota(jnp.int32, (QBLOCK, reach), 1)
    block = start // TOK
    column = jnp.concatenate([columns[:, block : block + 1], columns[:, block + 1 : block + 2]], axis=0)
    same = column == seg_row_ref[:, pl.ds(0, reach)]
    return jnp.where(same & (query_pos >= key_pos), scores, masked_fill)


def attend_kernel(qkv_ref, seg_row_ref, seg_blocks_ref, mixed_ref, total_ref):
    columns = segment_columns(seg_blocks_ref)
    for block in range(LENGTH // QBLOCK):
        start, reach = block * QBLOCK, (block + 1) * QBLOCK
        scores = block_scores(qkv_ref, seg_row_ref, columns, start, reach)
        largest = jnp.max(scores, axis=-1, keepdims=True)
        exponent = jnp.exp(scores - largest)
        totals = jnp.sum(exponent, axis=-1, keepdims=True)
        probs_low = (exponent * (1.0 / totals)).astype(low)
        value = qkv_ref[pl.ds(0, reach), 2 * HD : 3 * HD]
        mixed_ref[pl.ds(start, QBLOCK), :] = mm(probs_low, value).astype(low)
        total_ref[pl.ds(start, QBLOCK), :] = largest + jnp.log(totals)


def attend_back_kernel(
    qkv_ref, grad_ref, total_ref, seg_row_ref, seg_blocks_ref, cos_ref, sin_ref, out_ref, key_acc, value_acc
):
    columns = segment_columns(seg_blocks_ref)
    key_acc[...] = jnp.zeros_like(key_acc)
    value_acc[...] = jnp.zeros_like(value_acc)

    def turn_back(value, rows):
        return value * cos_ref[rows, :] + pltpu.roll(value, HD // 2, 1) * sin_ref[rows, :]

    for block in range(LENGTH // QBLOCK):
        start, reach = block * QBLOCK, (block + 1) * QBLOCK
        rows, span = pl.ds(start, QBLOCK), pl.ds(0, reach)
        scores = block_scores(qkv_ref, seg_row_ref, columns, start, reach)
        probs = jnp.exp(scores - total_ref[rows, :])
        grad = grad_ref[rows, :]
        grad_probs = mm_t(grad, qkv_ref[span, 2 * HD : 3 * HD])
        inner = jnp.sum(probs * grad_probs, axis=-1, keepdims=True)
        grad_scores = (probs * (grad_probs - inner)).astype(low)
        scale = HD ** (-0.5)
        grad_query = mm(grad_scores, qkv_ref[span, HD : 2 * HD]) * scale
        out_ref[rows, 0:HD] = turn_back(grad_query, rows).astype(low)
        key_acc[span, :] += t_mm(grad_scores, qkv_ref[rows, 0:HD]) * scale
        value_acc[span, :] += t_mm(probs.astype(low), grad)
    for block in range(LENGTH // QBLOCK):
        rows = pl.ds(block * QBLOCK, QBLOCK)
        out_ref[rows, HD : 2 * HD] = turn_back(key_acc[rows, :], rows).astype(low)
        out_ref[rows, 2 * HD : 3 * HD] = value_acc[rows, :].astype(low)


vmem = pl.BlockSpec(memory_space=pltpu.VMEM)
smem = pl.BlockSpec(memory_space=pltpu.SMEM)
anywhere = pl.BlockSpec(memory_space=pl.ANY)
kernel_params = pltpu.CompilerParams(vmem_limit_bytes=48 * 1024 * 1024)


def attend(qkv, seg_row, seg_blocks):
    return pl.pallas_call(
        attend_kernel,
        out_shape=(
            jax.ShapeDtypeStruct((LENGTH, HD), low),
            jax.ShapeDtypeStruct((LENGTH, 1), wide),
        ),
        in_specs=[vmem] * 3,
        out_specs=(vmem, vmem),
        compiler_params=kernel_params,
        cost_estimate=pl.CostEstimate(
            flops=2 * LENGTH * LENGTH * HD, bytes_accessed=4 * LENGTH * HD * 2, transcendentals=LENGTH * LENGTH // 2
        ),
        name="attend",
    )(qkv, seg_row, seg_blocks)


def attend_back(qkv, grad, total, seg_row, seg_blocks, cos_all, sin_all):
    return pl.pallas_call(
        attend_back_kernel,
        out_shape=jax.ShapeDtypeStruct((LENGTH, 3 * HD), low),
        in_specs=[vmem] * 7,
        out_specs=vmem,
        scratch_shapes=[pltpu.VMEM((LENGTH, HD), wide), pltpu.VMEM((LENGTH, HD), wide)],
        compiler_params=kernel_params,
        cost_estimate=pl.CostEstimate(
            flops=5 * LENGTH * LENGTH * HD, bytes_accessed=8 * LENGTH * HD * 2, transcendentals=LENGTH * LENGTH // 2
        ),
        name="attend_back",
    )(qkv, grad, total, seg_row, seg_blocks, cos_all, sin_all)


ROWS = 256
FF_TILES = [(start, min(256, FF - start)) for start in range(0, FF, 256)]


def params(mebibytes):
    return pltpu.CompilerParams(vmem_limit_bytes=mebibytes * 1024 * 1024)


def cost(flops, moved, special=0):
    return pl.CostEstimate(flops=int(flops), bytes_accessed=int(moved), transcendentals=int(special))


def project_kernel(*refs):
    pieces, (attn_ref, cos_ref, sin_ref) = refs[:10], refs[10:13]
    normed_ref, sent_ref, factor_ref, gains_ref, ids_ref, hidden, sems = refs[13:]
    copies = load_pieces(pieces, hidden, ids_ref, sems)
    pick = lax.broadcasted_iota(jnp.int32, (16, TOK), 0) == lax.broadcasted_iota(jnp.int32, (16, TOK), 1)
    gains_ref[...] = mm_t(pick.astype(wide).astype(low), attn_ref[:, 768:896])
    for copy in copies:
        copy.wait()
    gain = gains_ref[0:1, :]

    @pl.loop(0, ALL // ROWS)
    def step(index):
        rows = pl.ds(index * ROWS, ROWS)
        values = hidden[rows, :].astype(wide)
        factor = lax.rsqrt(jnp.mean(values * values, axis=-1, keepdims=True) + eps_norm)
        factor_ref[rows, :] = factor
        normed = (values * factor * gain).astype(low)
        normed_ref[rows, :] = normed
        raw = mm(normed, attn_ref[:, 0:512])

        def turn(value):
            return (value * cos_ref[...] + pltpu.roll(value, HD // 2, 1) * sin_ref[...]).astype(low)

        key = turn(raw[:, 2 * HD : 3 * HD])
        value = raw[:, 3 * HD :].astype(low)
        for head in range(2):
            query = turn(raw[:, head * HD : (head + 1) * HD])
            for part in range(2):
                place = pl.ds(index * 4 * TOK + (2 * part + head) * TOK, TOK)
                within = slice(part * TOK, (part + 1) * TOK)
                sent_ref[place, 0:HD] = query[within]
                sent_ref[place, HD : 2 * HD] = key[within]
                sent_ref[place, 2 * HD : 3 * HD] = value[within]


def project(pieces, attn_all, cos_two, sin_two):
    return pl.pallas_call(
        project_kernel,
        out_shape=(
            jax.ShapeDtypeStruct((ALL, D), low),
            jax.ShapeDtypeStruct((LENGTH, 3 * HD), low),
            jax.ShapeDtypeStruct((ALL, 1), wide),
            jax.ShapeDtypeStruct((16, D), wide),
            jax.ShapeDtypeStruct((SEQS * 16, D), low),
        ),
        in_specs=[anywhere] * 10 + [vmem] * 3,
        out_specs=tuple([vmem] * 5),
        scratch_shapes=[pltpu.VMEM((ALL, D), low), pltpu.SemaphoreType.DMA((20,))],
        compiler_params=params(40),
        cost_estimate=cost(2.2e9, 16e6),
        name="project",
    )(*pieces, attn_all, cos_two, sin_two)


def mix_back_kernel(place_ref, *refs):
    pieces, weight_ref, mixed_ref = refs[:10], refs[10], refs[11]
    sent_ref, mine_ref, other_ref, small_ref, grad_ref, extra_ref, sems = refs[12:]
    for copy in load_pieces(pieces, grad_ref, extra_ref, sems):
        copy.wait()
    for index in range(ALL // ROWS):
        grad = mm_t(grad_ref[pl.ds(index * ROWS, ROWS), :], weight_ref[...]).astype(low)
        for part in range(2):
            for head in range(2):
                place = pl.ds(index * 4 * TOK + (2 * part + head) * TOK, TOK)
                sent_ref[place, :] = grad[part * TOK : (part + 1) * TOK, head * HD : (head + 1) * HD]
    for index in range(EXPERTS):
        columns = pl.ds(pl.multiple_of(place_ref[index] * 256, 256), 256)
        target = mine_ref if index < 4 else other_ref
        target[index % 4] = t_mm(mixed_ref[...], grad_ref[:, columns]).astype(low)
    small = extra_ref[0:16, :].astype(wide)
    for index in range(1, SEQS):
        small = small + extra_ref[index * 16 : (index + 1) * 16, :].astype(wide)
    small_ref[...] = small


def mix_back(owners, pieces, weight, mixed):
    blocks = jax.ShapeDtypeStruct((4, 256, 256), low)
    return pl.pallas_call(
        mix_back_kernel,
        out_shape=(jax.ShapeDtypeStruct((LENGTH, HD), low), blocks, blocks, jax.ShapeDtypeStruct((16, D), wide)),
        in_specs=[smem] + [anywhere] * 10 + [vmem] * 2,
        out_specs=(vmem, vmem, vmem, vmem),
        scratch_shapes=[
            pltpu.VMEM((ALL, D), low),
            pltpu.VMEM((SEQS * 16, D), low),
            pltpu.SemaphoreType.DMA((20,)),
        ],
        compiler_params=params(60),
        cost_estimate=cost(2.2e9, 10e6),
        name="mix_back",
    )(owners, *pieces, weight, mixed)


def collect_kernel(core_ref, grads_ref, query_ref, mine_ref, other_ref):
    first = core_ref[0] == 0

    @pl.loop(0, SEQS)
    def step(index):
        rows = pl.ds(index * TOK, TOK)
        swapped = pl.ds(((index + SEQS // 2) % SEQS) * TOK, TOK)
        one = grads_ref[pl.ds(index * 2 * TOK, TOK), :]
        two = grads_ref[pl.ds(index * 2 * TOK + TOK, TOK), :]
        query_ref[rows, 0:HD] = one[:, :HD]
        query_ref[rows, HD : 2 * HD] = two[:, :HD]
        total = one[:, HD:].astype(wide) + two[:, HD:].astype(wide)
        lower = jnp.concatenate([total[:, : HD // 2], total[:, HD : HD + HD // 2]], axis=1)
        upper = jnp.concatenate([total[:, HD // 2 : HD], total[:, HD + HD // 2 :]], axis=1)
        mine_ref[rows, :] = jnp.where(first, lower, upper)
        other_ref[swapped, :] = jnp.where(first, upper, lower).astype(low)


def collect(core, grads):
    return pl.pallas_call(
        collect_kernel,
        out_shape=(
            jax.ShapeDtypeStruct((ALL, 2 * HD), low),
            jax.ShapeDtypeStruct((ALL, HD), wide),
            jax.ShapeDtypeStruct((ALL, HD), low),
        ),
        in_specs=[smem, vmem],
        out_specs=(vmem, vmem, vmem),
        compiler_params=params(32),
        cost_estimate=cost(1e6, 4e6),
        name="collect",
    )(core, grads)


def qkv_weights_kernel(normed_ref, query_ref, mine_ref, got_ref, out_ref, grad_ref):
    grad_ref[:, 0 : 2 * HD] = query_ref[...]
    grad_ref[:, 2 * HD : 3 * HD] = (mine_ref[...] + got_ref[...].astype(wide)).astype(low)

    @pl.loop(0, D // ROWS)
    def step(index):
        columns = pl.ds(pl.multiple_of(index * ROWS, ROWS), ROWS)
        out_ref[pl.ds(index * ROWS, ROWS), :] = t_mm(normed_ref[:, columns], grad_ref[...]).astype(low)


def qkv_weights(normed, query, mine, got):
    return pl.pallas_call(
        qkv_weights_kernel,
        out_shape=(jax.ShapeDtypeStruct((D, 3 * HD), low), jax.ShapeDtypeStruct((ALL, 3 * HD), low)),
        in_specs=[vmem] * 4,
        out_specs=(vmem, vmem),
        compiler_params=params(32),
        cost_estimate=cost(1.6e9, 8e6),
        name="qkv_weights",
    )(normed, query, mine, got)


def finish_kernel(shards_ref, query_ref, key_ref, value_ref, gain_ref):
    gain = jnp.zeros((TOK, TOK), wide)
    for source in range(EXPERTS):
        query_ref[:, source * 256 : (source + 1) * 256] = shards_ref[source, :, 0:256].astype(wide)
        gain = gain + shards_ref[source, :, 384:512].astype(wide)
    for pair in range(KV):
        one = shards_ref[2 * pair, :, 256:384].astype(wide)
        two = shards_ref[2 * pair + 1, :, 256:384].astype(wide)
        columns = slice(pair * HD, (pair + 1) * HD)
        key_ref[:, columns] = jnp.concatenate([one[:, : HD // 2], two[:, : HD // 2]], axis=1)
        value_ref[:, columns] = jnp.concatenate([one[:, HD // 2 :], two[:, HD // 2 :]], axis=1)
    gain_ref[...] = jnp.sum(gain, axis=1, keepdims=True)


def finish(shards):
    widths = (H * HD, KV * HD, KV * HD, 1)
    return pl.pallas_call(
        finish_kernel,
        out_shape=tuple(jax.ShapeDtypeStruct((TOK, width), wide) for width in widths),
        in_specs=[vmem],
        out_specs=tuple([vmem] * 4),
        compiler_params=params(32),
        cost_estimate=cost(1e6, 4e6),
        name="finish",
    )(shards)


def finish_dense_kernel(shards_ref, spread_ref, spread_rows_ref, gate_ref, up_ref, down_ref, out_ref, left, rows_in):
    width = SH_OWN // 2
    for source in range(EXPERTS):
        for part in range(4):
            left[part * TOK : (part + 1) * TOK, source * width : (source + 1) * width] = shards_ref[
                source, :, part * width : (part + 1) * width
            ]
        packed = shards_ref[source, :, 2 * SH_OWN : 3 * SH_OWN].astype(wide)
        rows_in[source * SH_PAD : (source + 1) * SH_PAD, :] = pack_rows(packed)
        out_ref[:, source * 256 : (source + 1) * 256] = shards_ref[source, :, 3 * SH_OWN :].astype(wide)
    for start in range(0, SH // 2, 256):
        count = min(256, SH // 2 - start)
        both = mm(left[...], spread_ref[:, start : start + count])
        for part in range(4):
            target = gate_ref if part < 2 else up_ref
            begin = (part % 2) * (SH // 2) + start
            target[:, begin : begin + count] = both[part * TOK : (part + 1) * TOK]
    down_ref[...] = mm(spread_rows_ref[...], rows_in[...].astype(low))


def finish_dense(shards, spread, spread_rows):
    shapes = [(TOK, SH), (TOK, SH), (SH_ROWS, D), (TOK, D)]
    return pl.pallas_call(
        finish_dense_kernel,
        out_shape=tuple(jax.ShapeDtypeStruct(shape, wide) for shape in shapes),
        in_specs=[vmem] * 3,
        out_specs=tuple([vmem] * 4),
        scratch_shapes=[
            pltpu.VMEM((4 * TOK, EXPERTS * SH_OWN // 2), low),
            pltpu.VMEM((EXPERTS * SH_PAD, D), wide),
        ],
        compiler_params=params(40),
        cost_estimate=cost(2.2e9, 12e6),
        name="finish_dense",
    )(shards, spread, spread_rows)


def halves(value):
    upper = value.astype(low)
    return upper, (value - upper.astype(wide)).astype(low)


def silu_parts(gate_value):
    sig = 1.0 / (1.0 + jnp.exp(-gate_value))
    return sig, gate_value * sig


def swiglu_back(sig, act, up_value, grad):
    return (grad * up_value * (sig + act * (1.0 - sig))).astype(low), (grad * act).astype(low)


def pack_rows(block):
    count, width = block.shape[0] // 8, block.shape[1] // 128
    return jnp.concatenate(
        [
            jnp.concatenate(
                [block[8 * i : 8 * i + 8, 128 * j : 128 * j + 128] for i in range(count)], axis=1
            )
            for j in range(width)
        ],
        axis=0,
    )


def slab(buffer, out_ref, sems, step):
    return pltpu.make_async_copy(buffer.at[step % 2], out_ref.at[pl.ds(step * ROWS, ROWS), :], sems.at[step % 2])


def send_slabs(tokens_ref, grad_ref, down_rows, out_ref, buffer, sems):
    width = grad_ref.shape[1]
    count = width // 2 // FSDP
    for step in range(D // ROWS):
        slot = step % 2
        if step >= 2:
            slab(buffer, out_ref, sems, step - 2).wait()
        buffer[slot, :, 0:width] = t_mm(tokens_ref[:, pl.ds(step * ROWS, ROWS)], grad_ref[...]).astype(low)
        down = down_rows(step)
        for part in range(2):
            packed = pack_rows(down[part * count : (part + 1) * count]).astype(low)
            buffer[slot, part * TOK : (part + 1) * TOK, width:] = packed
        slab(buffer, out_ref, sems, step).start()
    for step in (D // ROWS - 2, D // ROWS - 1):
        slab(buffer, out_ref, sems, step).wait()


def unpack(target, pair, stage, row, start, width):
    count = 2 * width // FSDP
    both = [
        pack_rows(stage[row + part * TOK : row + (part + 1) * TOK, start : start + width].astype(wide))
        for part in range(2)
    ]
    target[pair * count : (pair + 1) * count, :] = jnp.concatenate(both, axis=0).astype(low)


def experts_kernel(*refs):
    expert_ref, slots_hbm, routes_ref, router_hbm = refs[:4]
    pieces, cot_pieces, pack_ref = refs[4:14], refs[14:24], refs[24]
    out_ref, gates_ref, parts_ref, gated_out, grad_in_out = refs[25:30]
    normed_ref, cot_ref, incoming, hidden, gated, grad_rows, grad_ref, grad_in = refs[30:38]
    router_ref, w_in, w_down, stage, slots_ref, raw, gate_parts, buffer = refs[38:46]
    piece_sems, cot_sems, sems, slab_sems = refs[46:]
    base = 3 * SH_OWN
    half_d = D // 2

    def stage_down(part):
        return pltpu.make_async_copy(
            pack_ref.at[pl.ds(part * half_d, half_d), pl.ds(base + 2 * FF, FF)], stage, sems.at[part]
        )

    copies = [
        pltpu.make_async_copy(router_hbm, router_ref, sems.at[2]),
        pltpu.make_async_copy(slots_hbm, slots_ref, sems.at[3]),
        pltpu.make_async_copy(pack_ref.at[:, pl.ds(base, 2 * FF)], w_in, sems.at[4]),
    ]
    copies[0].start()
    piece_copies = load_pieces(pieces, normed_ref, None, piece_sems)
    copies[1].start()
    stage_down(0).start()
    cot_copies = load_pieces(cot_pieces, cot_ref, None, cot_sems)
    copies[2].start()
    expert = expert_ref[0]
    lane = lax.broadcasted_iota(jnp.int32, (ROWS, 128), 1)
    for copy in piece_copies + copies[:1]:
        copy.wait()
    for step in range(ALL // ROWS):
        rows = pl.ds(step * ROWS, ROWS)
        logits = mm(normed_ref[rows, :], router_ref[...])
        first, second = routes_ref[rows, 0:1], routes_ref[rows, 1:2]
        chosen_first = jnp.sum(jnp.where(lane == first + 2, logits, 0.0), axis=1, keepdims=True)
        chosen_second = jnp.sum(jnp.where(lane == second + 2, logits, 0.0), axis=1, keepdims=True)
        gate_first = 1.0 / (1.0 + jnp.exp(chosen_second - chosen_first))
        gate_second = 1.0 / (1.0 + jnp.exp(chosen_first - chosen_second))
        here = jnp.where(first == expert, gate_first, 0.0) + jnp.where(second == expert, gate_second, 0.0)
        upper, lower = halves(here)
        parts = jnp.where(lane == 0, upper.astype(wide), 0.0) + jnp.where(lane == 1, lower.astype(wide), 0.0)
        gate_parts[rows, :] = parts.astype(low)
        if step == 0:
            both_gates = jnp.where(lane == 0, gate_first, 0.0) + jnp.where(lane == 1, gate_second, 0.0)
            gates_ref[...] = both_gates[:TOK]
    copies[1].wait()
    for step in range(D // ROWS):
        columns = pl.ds(step * ROWS, ROWS)
        incoming[:, columns] = mm(slots_ref[...], normed_ref[:, columns]).astype(low)
    stage_down(0).wait()
    for copy in cot_copies:
        copy.wait()
    for step in range(D // ROWS):
        columns = pl.ds(step * ROWS, ROWS)
        grad_rows[:, columns] = mm(slots_ref[...], cot_ref[:, columns]).astype(low)
        if step < 4:
            unpack(w_down, step, stage, step * 2 * TOK, 0, FF)
    stage_down(1).start()
    slot_parts = mm(slots_ref[...], gate_parts[...])
    slot_gate = slot_parts[:, 0:1] + slot_parts[:, 1:2]
    copies[2].wait()
    for step in range(2 * FF // ROWS):
        columns = pl.ds(step * ROWS, ROWS)
        raw[:, columns] = mm(incoming[...], w_in[:, columns])
    stage_down(1).wait()
    for step in range(4):
        unpack(w_down, 4 + step, stage, step * 2 * TOK, 0, FF)
    for start, width in FF_TILES:
        gate, up = raw[:, start : start + width], raw[:, FF + start : FF + start + width]
        hidden[:, start : start + width] = (silu_parts(gate)[1] * up).astype(low)
    slot_grad = jnp.zeros((SLOTS, 1), wide)
    for step in range(D // ROWS):
        columns = pl.ds(step * ROWS, ROWS)
        rows = mm(hidden[...], w_down[:, columns]).astype(low).astype(wide)
        cot = grad_rows[:, columns].astype(wide)
        gated[:, columns] = (rows * slot_gate).astype(low)
        grad_rows[:, columns] = (cot * slot_gate).astype(low)
        slot_grad = slot_grad + jnp.sum(rows * cot, axis=1, keepdims=True)
    gated_copy = pltpu.make_async_copy(gated, gated_out, sems.at[5])
    gated_copy.start()
    for start, width in FF_TILES:
        grad_hidden = mm_t(grad_rows[...], w_down[pl.ds(start, width), :])
        sig, act = silu_parts(raw[:, start : start + width])
        grad_gate, grad_up = swiglu_back(sig, act, raw[:, FF + start : FF + start + width], grad_hidden)
        grad_ref[:, start : start + width] = grad_gate
        grad_ref[:, FF + start : FF + start + width] = grad_up
    for step in range(D // ROWS):
        columns = pl.ds(step * ROWS, ROWS)
        grad_in[:, columns] = mm_t(grad_ref[...], w_in[columns, :]).astype(low)
    grad_copy = pltpu.make_async_copy(grad_in, grad_in_out, sems.at[6])
    grad_copy.start()
    upper, lower = halves(slot_grad)
    slot_lane = lax.broadcasted_iota(jnp.int32, (SLOTS, 128), 1)
    parts_ref[...] = (
        jnp.where(slot_lane == expert, upper.astype(wide), 0.0)
        + jnp.where(slot_lane == expert + 8, lower.astype(wide), 0.0)
    ).astype(low)

    def down_rows(step):
        count = 2 * FF // FSDP
        return t_mm(hidden[:, step * count : (step + 1) * count], grad_rows[...])

    send_slabs(incoming, grad_ref, down_rows, out_ref, buffer, slab_sems)
    gated_copy.wait()
    grad_copy.wait()


def experts(expert, slots, routes, router, pieces, cot_pieces, pack):
    rows = [(SLOTS, D), (SLOTS, FF), (SLOTS, D), (SLOTS, D), (SLOTS, 2 * FF), (SLOTS, D)]
    return pl.pallas_call(
        experts_kernel,
        out_shape=(
            jax.ShapeDtypeStruct((D, 3 * FF), low),
            jax.ShapeDtypeStruct((TOK, 128), wide),
            jax.ShapeDtypeStruct((SLOTS, 128), low),
            jax.ShapeDtypeStruct((SLOTS, D), low),
            jax.ShapeDtypeStruct((SLOTS, D), low),
        ),
        in_specs=[smem, anywhere, vmem] + [anywhere] * 22,
        out_specs=(anywhere, vmem, vmem, anywhere, anywhere),
        scratch_shapes=[pltpu.VMEM((ALL, D), low), pltpu.VMEM((ALL, D), low)]
        + [pltpu.VMEM(shape, low) for shape in rows]
        + [
            pltpu.VMEM((D, 128), low),
            pltpu.VMEM((D, 2 * FF), low),
            pltpu.VMEM((FF, D), low),
            pltpu.VMEM((D // 2, FF), low),
            pltpu.VMEM((SLOTS, ALL), low),
            pltpu.VMEM((SLOTS, 2 * FF), wide),
            pltpu.VMEM((ALL, 128), low),
            pltpu.VMEM((2, ROWS, 3 * FF), low),
            pltpu.SemaphoreType.DMA((20,)),
            pltpu.SemaphoreType.DMA((20,)),
            pltpu.SemaphoreType.DMA((7,)),
            pltpu.SemaphoreType.DMA((2,)),
        ],
        compiler_params=params(60),
        cost_estimate=cost(24e9, 60e6, 1e6),
        name="experts",
    )(expert, slots, routes, router, *pieces, *cot_pieces, pack)


def shared_kernel(*refs):
    slots_t_hbm, pieces, cot_pieces = refs[0], refs[1:11], refs[11:21]
    pack_ref, grad_in_hbm, parts_ref = refs[21:24]
    grad_mine, grad_other, hidden_out, grad_out, down_out = refs[24:29]
    normed_ref, cot_ref, grad_ref, hidden, grad_hidden_ref, w_in, w_down, stage, slots_t_ref, grad_in = refs[29:39]
    piece_sems, cot_sems, sems = refs[39:]
    half_d = D // 2

    def stage_shared(part):
        return pltpu.make_async_copy(
            pack_ref.at[pl.ds(part * half_d, half_d), pl.ds(2 * SH_OWN, SH_OWN)], stage.at[part], sems.at[part]
        )

    stage_shared(0).start()
    stage_shared(1).start()
    piece_copies = load_pieces(pieces, normed_ref, None, piece_sems)
    copies = [
        pltpu.make_async_copy(pack_ref.at[:, pl.ds(0, 2 * SH_OWN)], w_in, sems.at[2]),
        pltpu.make_async_copy(slots_t_hbm, slots_t_ref, sems.at[3]),
        pltpu.make_async_copy(grad_in_hbm, grad_in, sems.at[4]),
    ]
    copies[0].start()
    cot_copies = load_pieces(cot_pieces, cot_ref, None, cot_sems)
    copies[1].start()
    copies[2].start()
    for part in range(2):
        stage_shared(part).wait()
        for pair in range(4):
            unpack(w_down, part * 4 + pair, stage.at[part], pair * 2 * TOK, 0, SH_OWN)
    for copy in piece_copies + copies[:1] + cot_copies:
        copy.wait()
    for step in range(ALL // ROWS):
        rows = pl.ds(step * ROWS, ROWS)
        both = mm(normed_ref[rows, :], w_in[...])
        sig, act = silu_parts(both[:, :SH_OWN])
        up = both[:, SH_OWN:]
        hidden[rows, :] = (act * up).astype(low)
        grad_gate, grad_up = swiglu_back(sig, act, up, mm_t(cot_ref[rows, :], w_down[...]))
        grad_hidden_ref[rows, 0:SH_OWN] = grad_gate
        grad_hidden_ref[rows, SH_OWN : 2 * SH_OWN] = grad_up
    sent = [
        pltpu.make_async_copy(hidden, hidden_out, sems.at[5]),
        pltpu.make_async_copy(grad_hidden_ref, grad_out, sems.at[6]),
        pltpu.make_async_copy(w_down, down_out, sems.at[7]),
    ]
    for copy in sent:
        copy.start()
    for copy in copies[1:]:
        copy.wait()
    half = ALL // 2
    for side, target in ((1, grad_other), (0, grad_mine)):
        for step in range(half // ROWS):
            rows = pl.ds(side * half + step * ROWS, ROWS)
            for tile in range(D // 512):
                columns = pl.ds(tile * 512, 512)
                grad_ref[rows, columns] = (
                    mm_t(grad_hidden_ref[rows, :], w_in[columns, :]) + mm(slots_t_ref[rows, :], grad_in[:, columns])
                ).astype(low)
            grad_ref[rows, D : D + 128] = mm(slots_t_ref[rows, :], parts_ref[...]).astype(low)
        copy = pltpu.make_async_copy(grad_ref.at[pl.ds(side * half, half), :], target, sems.at[8 + side])
        copy.start()
        sent.append(copy)
    for copy in sent:
        copy.wait()


def shared(slots_t, pieces, cot_pieces, pack, grad_in, parts):
    outs = [(ALL // 2, D + 128)] * 2 + [(ALL, SH_OWN), (ALL, 2 * SH_OWN), (SH_OWN, D)]
    return pl.pallas_call(
        shared_kernel,
        out_shape=tuple(jax.ShapeDtypeStruct(shape, low) for shape in outs),
        in_specs=[anywhere] * 23 + [vmem],
        out_specs=tuple([anywhere] * 5),
        scratch_shapes=[
            pltpu.VMEM((ALL, D), low),
            pltpu.VMEM((ALL, D), low),
            pltpu.VMEM((ALL, D + 128), low),
            pltpu.VMEM((ALL, SH_OWN), low),
            pltpu.VMEM((ALL, 2 * SH_OWN), low),
            pltpu.VMEM((D, 2 * SH_OWN), low),
            pltpu.VMEM((SH_OWN, D), low),
            pltpu.VMEM((2, D // 2, SH_OWN), low),
            pltpu.VMEM((ALL, SLOTS), low),
            pltpu.VMEM((SLOTS, D), low),
            pltpu.SemaphoreType.DMA((20,)),
            pltpu.SemaphoreType.DMA((20,)),
            pltpu.SemaphoreType.DMA((10,)),
        ],
        compiler_params=params(60),
        cost_estimate=cost(9.5e9, 30e6, 1e6),
        name="shared",
    )(slots_t, *pieces, *cot_pieces, pack, grad_in, parts)


def shared_weights_kernel(*refs):
    pieces, cot_pieces, hidden_ref, grad_ref = refs[:10], refs[10:20], refs[20], refs[21]
    out_ref, normed_ref, cot_ref, buffer, down, piece_sems, cot_sems, sems = refs[22:]
    cot_copies = load_pieces(cot_pieces, cot_ref, None, cot_sems)
    copies = load_pieces(pieces, normed_ref, None, piece_sems)
    for copy in cot_copies:
        copy.wait()
    for tile in range(D // ROWS):
        part = pl.ds(tile * ROWS, ROWS)
        down[:, part] = t_mm(hidden_ref[...], cot_ref[:, part])
    for copy in copies:
        copy.wait()
    count = 2 * SH_PAD
    send_slabs(
        normed_ref, grad_ref, lambda step: down[step * count : (step + 1) * count, :], out_ref, buffer, sems
    )


def shared_weights(pieces, cot_pieces, hidden, grad):
    return pl.pallas_call(
        shared_weights_kernel,
        out_shape=jax.ShapeDtypeStruct((D, 3 * SH_OWN), low),
        in_specs=[anywhere] * 20 + [vmem] * 2,
        out_specs=anywhere,
        scratch_shapes=[
            pltpu.VMEM((ALL, D), low),
            pltpu.VMEM((ALL, D), low),
            pltpu.VMEM((2, ROWS, 3 * SH_OWN), low),
            pltpu.VMEM((SH_OWN, D), wide),
            pltpu.SemaphoreType.DMA((20,)),
            pltpu.SemaphoreType.DMA((20,)),
            pltpu.SemaphoreType.DMA((2,)),
        ],
        compiler_params=params(60),
        cost_estimate=cost(5e9, 18e6),
        name="shared_weights",
    )(*pieces, *cot_pieces, hidden, grad)


def out_rows_kernel(place_ref, *refs):
    parts, out_ref = refs[:5], refs[5]
    for index in range(EXPERTS):
        step, side = index // 2, index % 2
        columns = pl.ds(pl.multiple_of(place_ref[index] * 256, 256), 256)
        out_ref[:, columns] = parts[step + 1][side] if step else parts[side][...]


def out_rows(places, parts):
    return pl.pallas_call(
        out_rows_kernel,
        out_shape=jax.ShapeDtypeStruct((256, D), low),
        in_specs=[smem] + [vmem] * 5,
        out_specs=vmem,
        compiler_params=params(32),
        cost_estimate=cost(0, 2e6),
        name="out_rows",
    )(places, *parts)


def back_two_kernel(
    own_ref, first_ref, second_ref, middle_ref, cot_ref, gains_ref, gates_ref, routes_ref, block_ref, grad_ref
):
    total = own_ref[...] + first_ref[...].astype(wide) + second_ref[...].astype(wide)
    lane = lax.broadcasted_iota(jnp.int32, (TOK, 128), 1)
    extra = total[:, D:]
    first, second = routes_ref[:, 0:1], routes_ref[:, 1:2]

    def taken(route):
        return jnp.sum(jnp.where((lane == route) | (lane == route + 8), extra, 0.0), axis=1, keepdims=True)

    gate_first, gate_second = gates_ref[:, 0:1], gates_ref[:, 1:2]
    taken_first, taken_second = taken(first), taken(second)
    inner = gate_first * taken_first + gate_second * taken_second
    chosen_first, chosen_second = gate_first * (taken_first - inner), gate_second * (taken_second - inner)
    logits = jnp.where(lane == first, chosen_first, 0.0) + jnp.where(lane == second, chosen_second, 0.0)
    grad = total[:, :D]
    for index in range(EXPERTS):
        grad = grad + logits[:, index : index + 1] * gains_ref[2 + index : 3 + index, :]
    middle = middle_ref[...]
    factor = lax.rsqrt(jnp.mean(middle * middle, axis=-1, keepdims=True) + eps_norm)
    scaled = grad * gains_ref[1:2, :]
    mean = jnp.mean(scaled * middle, axis=-1, keepdims=True)
    result = cot_ref[...].astype(wide) + factor * scaled - middle * (factor * factor * factor * mean)
    grad_ref[...] = result
    block_ref[0:TOK, :] = result.astype(low)
    gain_upper, gain_lower = halves(jnp.sum(grad * middle * factor, axis=0, keepdims=True))
    normed = (middle * factor * gains_ref[1:2, :]).astype(low)
    logit_upper, logit_lower = halves(logits.T[0:EXPERTS, :])
    router = mm(logit_upper, normed) + mm(logit_lower, normed)
    rows = [gain_upper.astype(wide), gain_lower.astype(wide), router, jnp.zeros((6, D), wide)]
    block_ref[TOK : TOK + 16, :] = jnp.concatenate(rows, axis=0).astype(low)


def back_two(*operands):
    return pl.pallas_call(
        back_two_kernel,
        out_shape=(jax.ShapeDtypeStruct((TOK + 16, D), low), jax.ShapeDtypeStruct((TOK, D), wide)),
        in_specs=[vmem] * 8,
        out_specs=(vmem, vmem),
        compiler_params=params(32),
        cost_estimate=cost(1e7, 6e6),
        name="back_two",
    )(*operands)


def norm_factor(values):
    return lax.rsqrt(jnp.mean(values * values, axis=-1, keepdims=True) + eps_norm)


def norm_back(values, factor, gain, grad):
    scaled = grad * gain
    inner = jnp.mean(scaled * values, axis=-1, keepdims=True)
    return factor * scaled - values * (factor * factor * factor * inner)


def per_device(
    hidden_in,
    cotangent,
    segments,
    routes,
    attn_gain,
    w_query,
    w_key,
    w_value,
    w_out,
    ffn_gain,
    w_router,
    shared_gate,
    shared_up,
    shared_down,
    expert_gate,
    expert_up,
    expert_down,
):
    expert = lax.axis_index("expert")
    z, core = expert // 2, expert % 2
    place = lax.axis_index("fsdp")

    misc = jnp.concatenate(
        [attn_gain[:, None], ffn_gain[:, None], w_router, jnp.zeros((TOK, 118), low)], axis=1
    )
    attn_pack = jnp.concatenate(
        [
            lax.dynamic_slice_in_dim(w_query, 256 * expert, 256, 1),
            lax.dynamic_slice_in_dim(w_key, HD * z, HD, 1),
            lax.dynamic_slice_in_dim(w_value, HD * z, HD, 1),
            lax.dynamic_slice_in_dim(w_out, 256 * expert, 256, 1),
            misc,
        ],
        axis=1,
    )
    attn_all = lax.all_gather(attn_pack, "fsdp", axis=0, tiled=True)
    half_in, half_out = SH // 2, SH_OWN // 2
    sel_column = jnp.arange(half_out)
    picked = SH_ROWS * (sel_column // SH_PAD) + SH_PART * expert + sel_column % SH_PAD
    picked = jnp.where(sel_column % SH_PAD < SH_PART, picked, -1)
    select = (jnp.arange(half_in)[:, None] == picked[None, :]).astype(low)
    own_shared = mm(
        jnp.concatenate(
            [shared_gate[:, :half_in], shared_gate[:, half_in:], shared_up[:, :half_in], shared_up[:, half_in:]],
            axis=0,
        ),
        select,
    ).astype(low)
    own_down = jnp.pad(
        lax.dynamic_slice_in_dim(shared_down, SH_PART * expert, SH_PART, 0),
        ((0, SH_PAD - SH_PART), (0, 0)),
    )
    ffn_pack = jnp.concatenate(
        [
            own_shared[:TOK],
            own_shared[TOK : 2 * TOK],
            own_shared[2 * TOK : 3 * TOK],
            own_shared[3 * TOK :],
            pack_tiles(own_down),
            expert_gate[:, 0],
            expert_up[:, 0],
            pack_tiles(expert_down[:, 0]),
        ],
        axis=1,
    )
    ffn_all = lax.all_gather(ffn_pack, "fsdp", axis=0, tiled=True)

    ids = jnp.concatenate(
        [
            segments.astype(low),
            jnp.pad(routes[0].reshape(1, TOK * TOPK), ((0, 0), (0, LENGTH - TOK * TOPK))).astype(low),
            jnp.zeros((14, LENGTH), low),
        ],
        axis=0,
    )
    hidden_pieces = gather_pieces(jnp.concatenate([hidden_in[0], ids], axis=0))
    cot_block, *hidden_pieces = together(cotangent[0], *hidden_pieces)
    cot_pieces = gather_pieces(cot_block)

    inverse_freq = rope_base ** (-jnp.arange(HD // 2, dtype=wide) * 2.0 / HD)
    angles = jnp.arange(LENGTH).astype(wide)[:, None] * inverse_freq[None, :]
    cosine, sine = jnp.cos(angles), jnp.sin(angles)
    cos_all = jnp.concatenate([cosine, cosine], axis=1)
    sin_back = jnp.concatenate([sine, -sine], axis=1)
    cos_own = lax.dynamic_slice_in_dim(cos_all, place * TOK, TOK, 0)
    sin_own = -lax.dynamic_slice_in_dim(sin_back, place * TOK, TOK, 0)
    cos_two, sin_two = jnp.concatenate([cos_own, cos_own]), jnp.concatenate([sin_own, sin_own])
    attn_all, cos_two, sin_two, cos_all, sin_back = together(attn_all, cos_two, sin_two, cos_all, sin_back)
    normed_one, sent, factor_one, gains, ids_all = project(hidden_pieces, attn_all, cos_two, sin_two)
    qkv = lax.all_to_all(sent, "fsdp", split_axis=0, concat_axis=0, tiled=True)

    ids_all = ids_all.reshape(SEQS, 16, D)
    seg_row = lax.dynamic_slice_in_dim(ids_all[:, 0].astype(wide), place // 2, 1, 0)
    seg_blocks = jnp.pad(seg_row.reshape(FSDP, TOK), ((0, TOK - FSDP), (0, 0)))
    route_all = ids_all[:, 1, : TOK * TOPK].astype(jnp.int32).reshape(ALL, TOPK)
    hit = jnp.any(route_all == expert, axis=1).astype(wide)
    order = jnp.arange(ALL)
    rank = mm(hit.astype(low)[None, :], (order[:, None] < order[None, :]).astype(low))
    slot_bool = (rank.astype(jnp.int32) == jnp.arange(SLOTS)[:, None]) & (hit > 0.5)[None, :]
    slots = slot_bool.astype(low)
    slots_t = slot_bool.T.astype(low)
    out_columns = attn_all[:, 512:768].reshape(EXPERTS, 256, 256)
    owners = jnp.stack([relative_owner(expert, block) for block in range(EXPERTS)])
    out_blocks = [lax.dynamic_index_in_dim(out_columns, owners[block], 0) for block in range(EXPERTS)]
    out_mine, out_other = jnp.concatenate(out_blocks[:4]), jnp.concatenate(out_blocks[4:])
    out_mine, out_other, _ = together(out_mine, out_other, sent)
    w_out_own = out_rows(source_owners(expert), exchange(out_mine, out_other))
    router = attn_all[:, 768:896]
    is_first = core == 0
    kv_weight = attn_all[:, 256:512].reshape(D, 2, 2, HD // 2)
    kv_weight = jnp.where(is_first, kv_weight[:, :, 0], kv_weight[:, :, 1]).reshape(D, HD)
    qkv_weight = jnp.concatenate([attn_all[:, :256], kv_weight], axis=1)
    route_own = route_all[:TOK]
    qkv, seg_row, seg_blocks, route_all, slots, slots_t, w_out_own, router, qkv_weight, route_own, *cot_pieces = together(
        qkv, seg_row, seg_blocks, route_all, slots, slots_t, w_out_own, router, qkv_weight, route_own, *cot_pieces
    )
    mixed_head, log_total = attend(qkv, seg_row, seg_blocks)
    mixed = (
        lax.all_to_all(mixed_head, "fsdp", split_axis=0, concat_axis=0, tiled=True)
        .reshape(SEQS, 2, TOK, HD)
        .transpose(0, 2, 1, 3)
        .reshape(ALL, 2 * HD)
    )
    own_hidden = hidden_in[0].astype(wide)
    half = ALL // 2
    middle = own_hidden + scatter_rows(
        mm(mixed[:half], w_out_own).astype(low), mm(mixed[half:], w_out_own).astype(low)
    )
    factor_two = norm_factor(middle)
    gain_one, gain_two = gains[0:1], gains[1:2]
    normed_block = (middle * factor_two * gain_two).astype(low)

    base = 3 * SH_OWN
    normed_pieces = gather_pieces(normed_block)
    expert_grads, gates, slot_parts, gated_rows, grad_in = experts(
        expert[None], slots, route_all, router, normed_pieces, cot_pieces, ffn_all
    )
    expert_sums = lax.psum_scatter(expert_grads, "fsdp", scatter_dimension=0, tiled=True)
    grad_mine, grad_other, hidden_shared, grad_shared, shared_down_w = shared(
        slots_t, normed_pieces, cot_pieces, ffn_all, grad_in, slot_parts
    )
    own_grad, to_above, to_below = scatter_start(grad_mine, swap_core(grad_other))
    to_above, to_below, hidden_shared, grad_shared = together(to_above, to_below, hidden_shared, grad_shared)
    from_below, from_above = move_z(to_above, 1), move_z(to_below, -1)
    shared_grads = shared_weights(normed_pieces, cot_pieces, hidden_shared, grad_shared)
    from_below, from_above, shared_grads = together(from_below, from_above, shared_grads)
    back_block, grad_middle = back_two(
        own_grad, from_below, from_above, middle, cotangent[0], gains, gates, route_own
    )
    back_block, hidden_shared, gated_rows = together(back_block, hidden_shared, gated_rows)
    below, above = first_pieces(back_block)
    result_other = (mm(hidden_shared[half:], shared_down_w) + mm(slots_t[half:], gated_rows)).astype(low)
    result_mine = (mm(hidden_shared[:half], shared_down_w) + mm(slots_t[:half], gated_rows)).astype(low)
    below, above, result_other, result_mine = together(below, above, result_other, result_mine)
    back_pieces = other_pieces(back_block, below, above)

    sent_back, out_mine, out_other, small_rows = mix_back(owners, back_pieces, w_out_own, mixed)
    grad_head = lax.all_to_all(sent_back, "fsdp", split_axis=0, concat_axis=0, tiled=True)
    grads_head = attend_back(qkv, grad_head, log_total, seg_row, seg_blocks, cos_all, sin_back)
    grads_qkv = lax.all_to_all(grads_head, "fsdp", split_axis=0, concat_axis=0, tiled=True)
    result_other, result_mine, _ = together(result_other, result_mine, sent_back)
    layer_out = (middle + scatter_rows(result_mine, result_other)).astype(low)

    out_parts = exchange(out_mine, out_other)
    out_parts = jnp.concatenate([jnp.stack(out_parts[:2])[None], jnp.stack(out_parts[2:])]).reshape(EXPERTS, 256, 256)
    places = [((z - source // 2) % 4) * 2 + (core ^ (source % 2)) for source in range(EXPERTS)]
    grad_out = [lax.dynamic_index_in_dim(out_parts, where, 0, keepdims=False) for where in places]
    small_columns = jnp.pad(small_rows.T.astype(low), ((0, 0), (0, 112)))
    dense_grads = jnp.concatenate([shared_grads, jnp.concatenate(grad_out, axis=0), small_columns], axis=1)
    dense_sums = lax.psum_scatter(dense_grads, "fsdp", scatter_dimension=0, tiled=True)
    grads_qkv, layer_out, dense_grads = together(grads_qkv, layer_out, dense_grads)

    grad_query, kv_mine, kv_other = collect(core[None], grads_qkv)
    qkv_grads, grad_qkv = qkv_weights(normed_one, grad_query, kv_mine, swap_core(kv_other))
    attn_parts = lax.all_to_all(qkv_grads, "fsdp", split_axis=0, concat_axis=0, tiled=True)

    grad_normed_other = mm_t(grad_qkv[half:], qkv_weight).astype(low)
    grad_normed_mine = mm_t(grad_qkv[:half], qkv_weight).astype(low)
    own_grad_one, to_above, to_below = scatter_start(grad_normed_mine, swap_core(grad_normed_other))
    attn_parts, to_above, to_below = together(attn_parts, to_above, to_below)
    own_grad_one = scatter_end(own_grad_one, move_z(to_above, 1), move_z(to_below, -1))
    grad_input = (grad_middle + norm_back(own_hidden, factor_one[:TOK], gain_one, own_grad_one)).astype(low)
    attn_sums = jnp.sum(attn_parts.reshape(FSDP, TOK, 3 * HD).astype(wide), axis=0)

    own_weight = lax.dynamic_slice_in_dim(qkv_weight, place * TOK, TOK, 0)
    gain_part = jnp.sum(attn_sums * own_weight.astype(wide), axis=1, keepdims=True)
    gain_upper, gain_lower = halves(gain_part / attn_gain.astype(wide)[:, None])
    shards = jnp.concatenate([attn_sums.astype(low), gain_upper, gain_lower, jnp.zeros((TOK, 126), low)], axis=1)

    dense_sums, expert_sums, _ = together(dense_sums, expert_sums, qkv_grads)
    dense_shards = lax.all_gather(dense_sums[:, : base + 256], "expert", axis=0)
    dense_shards, shards = together(dense_shards, shards)
    attn_shards = lax.all_gather(shards, "expert", axis=0)
    put_row = jnp.arange(SH_PAD * EXPERTS * FSDP // 2)
    source, within = put_row // half_out, put_row % half_out
    target = SH_ROWS * (within // SH_PAD) + SH_PART * source + within % SH_PAD
    target = jnp.where(within % SH_PAD < SH_PART, target, -1)
    spread = (target[:, None] == jnp.arange(half_in)[None, :]).astype(low)
    put_row = jnp.arange(EXPERTS * SH_PAD)
    target = SH_PART * (put_row // SH_PAD) + put_row % SH_PAD
    target = jnp.where(put_row % SH_PAD < SH_PART, target, -1)
    spread_rows = (jnp.arange(SH_ROWS)[:, None] == target[None, :]).astype(low)
    spread, spread_rows, _ = together(spread, spread_rows, sent)
    grad_shared_gate, grad_shared_up, grad_shared_down, grad_w_out = finish_dense(dense_shards, spread, spread_rows)
    grad_w_query, grad_w_key, grad_w_value, grad_attn_gain = finish(attn_shards)
    grad_expert_gate = expert_sums[:, :FF].astype(wide)[:, None]
    grad_expert_up = expert_sums[:, FF : 2 * FF].astype(wide)[:, None]
    grad_expert_down = unpack_tiles(expert_sums[:, 2 * FF :], 1).astype(wide)[:, None]
    small_sums = dense_sums[:, base + 256 :].astype(wide)
    return (
        layer_out[None],
        grad_input[None],
        grad_attn_gain[:, 0],
        grad_w_query,
        grad_w_key,
        grad_w_value,
        grad_w_out,
        small_sums[:, 0] + small_sums[:, 1],
        small_sums[:, 2 : 2 + EXPERTS],
        grad_shared_gate,
        grad_shared_up,
        grad_shared_down,
        grad_expert_gate,
        grad_expert_up,
        grad_expert_down,
    )


def solution(mesh):
    in_specs = (
        P("expert", "fsdp", None),
        P("expert", "fsdp", None),
        P("expert", None),
        P("expert", "fsdp", None),
        P("fsdp"),
        P("fsdp", None),
        P("fsdp", None),
        P("fsdp", None),
        P("fsdp", None),
        P("fsdp"),
        P("fsdp", None),
        P("fsdp", None),
        P("fsdp", None),
        P("fsdp", None),
        P("fsdp", "expert", None),
        P("fsdp", "expert", None),
        P("fsdp", "expert", None),
    )
    out_specs = (
        P("expert", "fsdp", None),
        P("expert", "fsdp", None),
        P("fsdp"),
        P("fsdp", None),
        P("fsdp", None),
        P("fsdp", None),
        P("fsdp", None),
        P("fsdp"),
        P("fsdp", None),
        P("fsdp", None),
        P("fsdp", None),
        P("fsdp", None),
        P("fsdp", "expert", None),
        P("fsdp", "expert", None),
        P("fsdp", "expert", None),
    )
    return jax.shard_map(
        per_device, mesh=mesh, in_specs=in_specs, out_specs=out_specs, check_vma=False
    )
```

```python
import jax
import jax.numpy as jnp
from jax import lax
from jax.experimental import pallas as pl
from jax.experimental.pallas import tpu as pltpu
from jax.sharding import PartitionSpec as P

D = 2048
H = 16
KV = 4
HD = 128
FF = 1408
SH = 2816
TOPK = 2
TOK = 128
LENGTH = 2048
SEQS = 8
EXPERTS = 8
FSDP = 16
ALL = SEQS * TOK
CAP = 42
SLOTS = SEQS * CAP
SH_ROWS = SH // FSDP
SH_PART = SH_ROWS // EXPERTS
SH_PAD = 24
SH_OWN = FSDP * SH_PAD
QBLOCK = 256

eps_norm = 1e-06
rope_base = 600000.0
masked_fill = -1e30
low = jnp.bfloat16
wide = jnp.float32


def shift_pairs(step):
    return [(z * 2 + c, ((z + step) % 4) * 2 + c) for z in range(4) for c in range(2)]


core_pairs = [(z * 2 + c, z * 2 + 1 - c) for z in range(4) for c in range(2)]


def move_z(block, step):
    return lax.ppermute(block, "expert", shift_pairs(step))


def swap_core(block):
    return lax.ppermute(block, "expert", core_pairs)


def together(*values):
    return lax.optimization_barrier(values)


TOP = TOK // 2


def first_pieces(block):
    return move_z(block, 1), move_z(block, -1)


def other_pieces(block, below, above):
    upper, lower = move_z(below[:TOP], 1), move_z(above[TOP:], -1)
    mine = [block, above, upper, lower, below]
    return mine + [swap_core(piece) for piece in mine]


def gather_pieces(block):
    return other_pieces(block, *first_pieces(block))


PIECES = [(4 * side + block, start) for side in (0, 1) for block, start in ((0, 0), (1, 0), (2, 0), (2, TOP), (3, 0))]


def load_pieces(refs, rows_ref, extra_ref, sems):
    copies = []
    for index, (ref, (block, start)) in enumerate(zip(refs, PIECES)):
        count = min(ref.shape[0], TOK - start)
        copies.append(
            pltpu.make_async_copy(
                ref.at[pl.ds(0, count), :], rows_ref.at[pl.ds(block * TOK + start, count), :], sems.at[2 * index]
            )
        )
        if extra_ref is not None and ref.shape[0] > count:
            copies.append(
                pltpu.make_async_copy(
                    ref.at[pl.ds(count, 16), :], extra_ref.at[pl.ds(block * 16, 16), :], sems.at[2 * index + 1]
                )
            )
    for copy in copies:
        copy.start()
    return copies


def scatter_start(mine, received):
    chip = mine.reshape(4, TOK, -1).astype(wide) + received.reshape(4, TOK, -1).astype(wide)
    from_below = move_z(chip[2, :TOP].astype(low), 1)
    from_above = move_z(chip[2, TOP:].astype(low), -1)
    to_above = jnp.concatenate([chip[1, :TOP] + from_below.astype(wide), chip[1, TOP:]], axis=0)
    to_below = jnp.concatenate([chip[3, :TOP], chip[3, TOP:] + from_above.astype(wide)], axis=0)
    return chip[0], to_above.astype(low), to_below.astype(low)


def scatter_end(own, first, second):
    return own + first.astype(wide) + second.astype(wide)


def scatter_rows(mine, other):
    own, to_above, to_below = scatter_start(mine, swap_core(other))
    return scatter_end(own, move_z(to_above, 1), move_z(to_below, -1))


def exchange(mine, other):
    got = swap_core(other)
    chip = jnp.stack([mine[1:], got[1:]], axis=1)
    return mine[0], got[0], *[move_z(chip[step - 1], step) for step in (1, 2, 3)]


def source_owners(expert):
    return jnp.stack([((expert // 2 - index // 2) % 4) * 2 + ((expert % 2) ^ (index % 2)) for index in range(EXPERTS)])


def relative_owner(expert, block):
    return ((expert // 2 + block % 4) % 4) * 2 + ((expert % 2) ^ (block // 4))


def pack_tiles(block):
    rows, columns = block.shape[0] // 8, block.shape[1] // 128
    tiles = block.reshape(rows, 8, columns, 128).transpose(2, 1, 0, 3)
    return tiles.reshape(columns * 8, rows * 128)


def unpack_tiles(block, count):
    rows, columns = block.shape[1] // 128, block.shape[0] // (8 * count)
    tiles = block.reshape(count, columns, 8, rows, 128).transpose(0, 3, 2, 1, 4)
    return tiles.reshape(count * rows * 8, columns * 128)


def product(left, right, contract):
    return lax.dot_general(left, right, (contract, ((), ())), preferred_element_type=wide)


def mm(left, right):
    return product(left, right, ((1,), (0,)))


def mm_t(left, right):
    return product(left, right, ((1,), (1,)))


def t_mm(left, right):
    return product(left, right, ((0,), (0,)))


def segment_columns(seg_blocks_ref):
    return seg_blocks_ref[...].T


def block_scores(qkv_ref, seg_row_ref, columns, start, reach):
    query = qkv_ref[pl.ds(start, QBLOCK), 0:HD]
    key = qkv_ref[pl.ds(0, reach), HD : 2 * HD]
    scores = mm_t(query, key) * HD ** (-0.5)
    query_pos = start + lax.broadcasted_iota(jnp.int32, (QBLOCK, reach), 0)
    key_pos = lax.broadcasted_iota(jnp.int32, (QBLOCK, reach), 1)
    block = start // TOK
    column = jnp.concatenate([columns[:, block : block + 1], columns[:, block + 1 : block + 2]], axis=0)
    same = column == seg_row_ref[:, pl.ds(0, reach)]
    return jnp.where(same & (query_pos >= key_pos), scores, masked_fill)


def attend_kernel(qkv_ref, seg_row_ref, seg_blocks_ref, mixed_ref, total_ref):
    columns = segment_columns(seg_blocks_ref)
    for block in range(LENGTH // QBLOCK):
        start, reach = block * QBLOCK, (block + 1) * QBLOCK
        scores = block_scores(qkv_ref, seg_row_ref, columns, start, reach)
        largest = jnp.max(scores, axis=-1, keepdims=True)
        exponent = jnp.exp(scores - largest)
        totals = jnp.sum(exponent, axis=-1, keepdims=True)
        probs_low = (exponent * (1.0 / totals)).astype(low)
        value = qkv_ref[pl.ds(0, reach), 2 * HD : 3 * HD]
        mixed_ref[pl.ds(start, QBLOCK), :] = mm(probs_low, value).astype(low)
        total_ref[pl.ds(start, QBLOCK), :] = largest + jnp.log(totals)


def attend_back_kernel(
    qkv_ref, grad_ref, total_ref, seg_row_ref, seg_blocks_ref, cos_ref, sin_ref, out_ref, key_acc, value_acc
):
    columns = segment_columns(seg_blocks_ref)
    key_acc[...] = jnp.zeros_like(key_acc)
    value_acc[...] = jnp.zeros_like(value_acc)

    def turn_back(value, rows):
        return value * cos_ref[rows, :] + pltpu.roll(value, HD // 2, 1) * sin_ref[rows, :]

    for block in range(LENGTH // QBLOCK):
        start, reach = block * QBLOCK, (block + 1) * QBLOCK
        rows, span = pl.ds(start, QBLOCK), pl.ds(0, reach)
        scores = block_scores(qkv_ref, seg_row_ref, columns, start, reach)
        probs = jnp.exp(scores - total_ref[rows, :])
        grad = grad_ref[rows, :]
        grad_probs = mm_t(grad, qkv_ref[span, 2 * HD : 3 * HD])
        inner = jnp.sum(probs * grad_probs, axis=-1, keepdims=True)
        grad_scores = (probs * (grad_probs - inner)).astype(low)
        scale = HD ** (-0.5)
        grad_query = mm(grad_scores, qkv_ref[span, HD : 2 * HD]) * scale
        out_ref[rows, 0:HD] = turn_back(grad_query, rows).astype(low)
        key_acc[span, :] += t_mm(grad_scores, qkv_ref[rows, 0:HD]) * scale
        value_acc[span, :] += t_mm(probs.astype(low), grad)
    for block in range(LENGTH // QBLOCK):
        rows = pl.ds(block * QBLOCK, QBLOCK)
        out_ref[rows, HD : 2 * HD] = turn_back(key_acc[rows, :], rows).astype(low)
        out_ref[rows, 2 * HD : 3 * HD] = value_acc[rows, :].astype(low)


vmem = pl.BlockSpec(memory_space=pltpu.VMEM)
smem = pl.BlockSpec(memory_space=pltpu.SMEM)
anywhere = pl.BlockSpec(memory_space=pl.ANY)
kernel_params = pltpu.CompilerParams(vmem_limit_bytes=48 * 1024 * 1024)


def attend(qkv, seg_row, seg_blocks):
    return pl.pallas_call(
        attend_kernel,
        out_shape=(
            jax.ShapeDtypeStruct((LENGTH, HD), low),
            jax.ShapeDtypeStruct((LENGTH, 1), wide),
        ),
        in_specs=[vmem] * 3,
        out_specs=(vmem, vmem),
        compiler_params=kernel_params,
        cost_estimate=pl.CostEstimate(
            flops=2 * LENGTH * LENGTH * HD, bytes_accessed=4 * LENGTH * HD * 2, transcendentals=LENGTH * LENGTH // 2
        ),
        name="attend",
    )(qkv, seg_row, seg_blocks)


def attend_back(qkv, grad, total, seg_row, seg_blocks, cos_all, sin_all):
    return pl.pallas_call(
        attend_back_kernel,
        out_shape=jax.ShapeDtypeStruct((LENGTH, 3 * HD), low),
        in_specs=[vmem] * 7,
        out_specs=vmem,
        scratch_shapes=[pltpu.VMEM((LENGTH, HD), wide), pltpu.VMEM((LENGTH, HD), wide)],
        compiler_params=kernel_params,
        cost_estimate=pl.CostEstimate(
            flops=5 * LENGTH * LENGTH * HD, bytes_accessed=8 * LENGTH * HD * 2, transcendentals=LENGTH * LENGTH // 2
        ),
        name="attend_back",
    )(qkv, grad, total, seg_row, seg_blocks, cos_all, sin_all)


ROWS = 256
FF_TILES = [(start, min(256, FF - start)) for start in range(0, FF, 256)]


def params(mebibytes):
    return pltpu.CompilerParams(vmem_limit_bytes=mebibytes * 1024 * 1024)


def cost(flops, moved, special=0):
    return pl.CostEstimate(flops=int(flops), bytes_accessed=int(moved), transcendentals=int(special))


def project_kernel(*refs):
    pieces, (attn_ref, cos_ref, sin_ref) = refs[:10], refs[10:13]
    normed_ref, sent_ref, factor_ref, gains_ref, ids_ref, hidden, sems = refs[13:]
    copies = load_pieces(pieces, hidden, ids_ref, sems)
    pick = lax.broadcasted_iota(jnp.int32, (16, TOK), 0) == lax.broadcasted_iota(jnp.int32, (16, TOK), 1)
    gains_ref[...] = mm_t(pick.astype(wide).astype(low), attn_ref[:, 768:896])
    for copy in copies:
        copy.wait()
    gain = gains_ref[0:1, :]

    @pl.loop(0, ALL // ROWS)
    def step(index):
        rows = pl.ds(index * ROWS, ROWS)
        values = hidden[rows, :].astype(wide)
        factor = lax.rsqrt(jnp.mean(values * values, axis=-1, keepdims=True) + eps_norm)
        factor_ref[rows, :] = factor
        normed = (values * factor * gain).astype(low)
        normed_ref[rows, :] = normed
        raw = mm(normed, attn_ref[:, 0:512])

        def turn(value):
            return (value * cos_ref[...] + pltpu.roll(value, HD // 2, 1) * sin_ref[...]).astype(low)

        key = turn(raw[:, 2 * HD : 3 * HD])
        value = raw[:, 3 * HD :].astype(low)
        for head in range(2):
            query = turn(raw[:, head * HD : (head + 1) * HD])
            for part in range(2):
                place = pl.ds(index * 4 * TOK + (2 * part + head) * TOK, TOK)
                within = slice(part * TOK, (part + 1) * TOK)
                sent_ref[place, 0:HD] = query[within]
                sent_ref[place, HD : 2 * HD] = key[within]
                sent_ref[place, 2 * HD : 3 * HD] = value[within]


def project(pieces, attn_all, cos_two, sin_two):
    return pl.pallas_call(
        project_kernel,
        out_shape=(
            jax.ShapeDtypeStruct((ALL, D), low),
            jax.ShapeDtypeStruct((LENGTH, 3 * HD), low),
            jax.ShapeDtypeStruct((ALL, 1), wide),
            jax.ShapeDtypeStruct((16, D), wide),
            jax.ShapeDtypeStruct((SEQS * 16, D), low),
        ),
        in_specs=[anywhere] * 10 + [vmem] * 3,
        out_specs=tuple([vmem] * 5),
        scratch_shapes=[pltpu.VMEM((ALL, D), low), pltpu.SemaphoreType.DMA((20,))],
        compiler_params=params(40),
        cost_estimate=cost(2.2e9, 16e6),
        name="project",
    )(*pieces, attn_all, cos_two, sin_two)


def mix_back_kernel(place_ref, *refs):
    pieces, weight_ref, mixed_ref = refs[:10], refs[10], refs[11]
    sent_ref, mine_ref, other_ref, grad_ref, sems = refs[12:]
    for copy in load_pieces(pieces, grad_ref, None, sems):
        copy.wait()
    for index in range(ALL // ROWS):
        grad = mm_t(grad_ref[pl.ds(index * ROWS, ROWS), :], weight_ref[...]).astype(low)
        for part in range(2):
            for head in range(2):
                place = pl.ds(index * 4 * TOK + (2 * part + head) * TOK, TOK)
                sent_ref[place, :] = grad[part * TOK : (part + 1) * TOK, head * HD : (head + 1) * HD]
    for index in range(EXPERTS):
        columns = pl.ds(pl.multiple_of(place_ref[index] * 256, 256), 256)
        target = mine_ref if index < 4 else other_ref
        target[index % 4] = t_mm(mixed_ref[...], grad_ref[:, columns]).astype(low)


def mix_back(owners, pieces, weight, mixed):
    blocks = jax.ShapeDtypeStruct((4, 256, 256), low)
    return pl.pallas_call(
        mix_back_kernel,
        out_shape=(jax.ShapeDtypeStruct((LENGTH, HD), low), blocks, blocks),
        in_specs=[smem] + [anywhere] * 10 + [vmem] * 2,
        out_specs=(vmem, vmem, vmem),
        scratch_shapes=[pltpu.VMEM((ALL, D), low), pltpu.SemaphoreType.DMA((20,))],
        compiler_params=params(60),
        cost_estimate=cost(2.2e9, 10e6),
        name="mix_back",
    )(owners, *pieces, weight, mixed)


def collect_kernel(core_ref, grads_ref, query_ref, mine_ref, other_ref):
    first = core_ref[0] == 0

    @pl.loop(0, SEQS)
    def step(index):
        rows = pl.ds(index * TOK, TOK)
        swapped = pl.ds(((index + SEQS // 2) % SEQS) * TOK, TOK)
        one = grads_ref[pl.ds(index * 2 * TOK, TOK), :]
        two = grads_ref[pl.ds(index * 2 * TOK + TOK, TOK), :]
        query_ref[rows, 0:HD] = one[:, :HD]
        query_ref[rows, HD : 2 * HD] = two[:, :HD]
        total = one[:, HD:].astype(wide) + two[:, HD:].astype(wide)
        lower = jnp.concatenate([total[:, : HD // 2], total[:, HD : HD + HD // 2]], axis=1)
        upper = jnp.concatenate([total[:, HD // 2 : HD], total[:, HD + HD // 2 :]], axis=1)
        mine_ref[rows, :] = jnp.where(first, lower, upper)
        other_ref[swapped, :] = jnp.where(first, upper, lower).astype(low)


def collect(core, grads):
    return pl.pallas_call(
        collect_kernel,
        out_shape=(
            jax.ShapeDtypeStruct((ALL, 2 * HD), low),
            jax.ShapeDtypeStruct((ALL, HD), wide),
            jax.ShapeDtypeStruct((ALL, HD), low),
        ),
        in_specs=[smem, vmem],
        out_specs=(vmem, vmem, vmem),
        compiler_params=params(32),
        cost_estimate=cost(1e6, 4e6),
        name="collect",
    )(core, grads)


def qkv_weights_kernel(place_ref, normed_ref, query_ref, mine_ref, got_ref, *refs):
    parts, (out_ref, grad_ref) = refs[:5], refs[5:]
    grad_ref[:, 0 : 2 * HD] = query_ref[...]
    grad_ref[:, 2 * HD : 3 * HD] = (mine_ref[...] + got_ref[...].astype(wide)).astype(low)
    for index in range(EXPERTS):
        step, side = index // 2, index % 2
        rows = pl.ds(pl.multiple_of(place_ref[index] * 256, 256), 256)
        out_ref[rows, 3 * HD : 3 * HD + 256] = parts[step + 1][side] if step else parts[side][...]
    for index in range(D // ROWS):
        rows = pl.ds(index * ROWS, ROWS)
        out_ref[rows, 0 : 3 * HD] = t_mm(normed_ref[:, rows], grad_ref[...]).astype(low)


def qkv_weights(places, normed, query, mine, got, parts):
    return pl.pallas_call(
        qkv_weights_kernel,
        out_shape=(jax.ShapeDtypeStruct((D, 3 * HD + 256), low), jax.ShapeDtypeStruct((ALL, 3 * HD), low)),
        in_specs=[smem] + [vmem] * 9,
        out_specs=(vmem, vmem),
        compiler_params=params(40),
        cost_estimate=cost(1.6e9, 10e6),
        name="qkv_weights",
    )(places, normed, query, mine, got, *parts)


def finish_kernel(shards_ref, query_ref, key_ref, value_ref, out_ref, gain_ref):
    gain = jnp.zeros((TOK, TOK), wide)
    for source in range(EXPERTS):
        query_ref[:, source * 256 : (source + 1) * 256] = shards_ref[source, :, 0:256].astype(wide)
        out_ref[:, source * 256 : (source + 1) * 256] = shards_ref[source, :, 384:640].astype(wide)
        gain = gain + shards_ref[source, :, 640:768].astype(wide)
    for pair in range(KV):
        one = shards_ref[2 * pair, :, 256:384].astype(wide)
        two = shards_ref[2 * pair + 1, :, 256:384].astype(wide)
        columns = slice(pair * HD, (pair + 1) * HD)
        key_ref[:, columns] = jnp.concatenate([one[:, : HD // 2], two[:, : HD // 2]], axis=1)
        value_ref[:, columns] = jnp.concatenate([one[:, HD // 2 :], two[:, HD // 2 :]], axis=1)
    gain_ref[...] = jnp.sum(gain, axis=1, keepdims=True)


def finish(shards):
    widths = (H * HD, KV * HD, KV * HD, H * HD, 1)
    return pl.pallas_call(
        finish_kernel,
        out_shape=tuple(jax.ShapeDtypeStruct((TOK, width), wide) for width in widths),
        in_specs=[vmem],
        out_specs=tuple([vmem] * 5),
        compiler_params=params(32),
        cost_estimate=cost(1e6, 4e6),
        name="finish",
    )(shards)


def finish_dense_kernel(shards_ref, spread_ref, spread_rows_ref, gate_ref, up_ref, down_ref, small_ref, left, rows_in):
    width = SH_OWN // 2
    small = jnp.zeros((TOK, TOK), wide)
    for source in range(EXPERTS):
        for part in range(4):
            left[part * TOK : (part + 1) * TOK, source * width : (source + 1) * width] = shards_ref[
                source, :, part * width : (part + 1) * width
            ]
        packed = shards_ref[source, :, 2 * SH_OWN : 3 * SH_OWN].astype(wide)
        rows_in[source * SH_PAD : (source + 1) * SH_PAD, :] = pack_rows(packed)
        small = small + shards_ref[source, :, 3 * SH_OWN :].astype(wide)
    small_ref[...] = small
    for start in range(0, SH // 2, 256):
        count = min(256, SH // 2 - start)
        both = mm(left[...], spread_ref[:, start : start + count])
        for part in range(4):
            target = gate_ref if part < 2 else up_ref
            begin = (part % 2) * (SH // 2) + start
            target[:, begin : begin + count] = both[part * TOK : (part + 1) * TOK]
    down_ref[...] = mm(spread_rows_ref[...], rows_in[...].astype(low))


def finish_dense(shards, spread, spread_rows):
    shapes = [(TOK, SH), (TOK, SH), (SH_ROWS, D), (TOK, TOK)]
    return pl.pallas_call(
        finish_dense_kernel,
        out_shape=tuple(jax.ShapeDtypeStruct(shape, wide) for shape in shapes),
        in_specs=[vmem] * 3,
        out_specs=tuple([vmem] * 4),
        scratch_shapes=[
            pltpu.VMEM((4 * TOK, EXPERTS * SH_OWN // 2), low),
            pltpu.VMEM((EXPERTS * SH_PAD, D), wide),
        ],
        compiler_params=params(40),
        cost_estimate=cost(2.2e9, 12e6),
        name="finish_dense",
    )(shards, spread, spread_rows)


def halves(value):
    upper = value.astype(low)
    return upper, (value - upper.astype(wide)).astype(low)


def silu_parts(gate_value):
    sig = 1.0 / (1.0 + jnp.exp(-gate_value))
    return sig, gate_value * sig


def swiglu_back(sig, act, up_value, grad):
    return (grad * up_value * (sig + act * (1.0 - sig))).astype(low), (grad * act).astype(low)


def pack_rows(block):
    count, width = block.shape[0] // 8, block.shape[1] // 128
    return jnp.concatenate(
        [
            jnp.concatenate(
                [block[8 * i : 8 * i + 8, 128 * j : 128 * j + 128] for i in range(count)], axis=1
            )
            for j in range(width)
        ],
        axis=0,
    )


def slab(buffer, out_ref, sems, step):
    target = out_ref.at[pl.ds(step * ROWS, ROWS), pl.ds(0, buffer.shape[2])]
    return pltpu.make_async_copy(buffer.at[step % 2], target, sems.at[step % 2])


def send_slabs(tokens_ref, grad_ref, down_rows, out_ref, buffer, sems):
    width = grad_ref.shape[1]
    count = width // 2 // FSDP
    for step in range(D // ROWS):
        slot = step % 2
        if step >= 2:
            slab(buffer, out_ref, sems, step - 2).wait()
        buffer[slot, :, 0:width] = t_mm(tokens_ref[:, pl.ds(step * ROWS, ROWS)], grad_ref[...]).astype(low)
        down = down_rows(step)
        for part in range(2):
            packed = pack_rows(down[part * count : (part + 1) * count]).astype(low)
            buffer[slot, part * TOK : (part + 1) * TOK, width:] = packed
        slab(buffer, out_ref, sems, step).start()
    for step in (D // ROWS - 2, D // ROWS - 1):
        slab(buffer, out_ref, sems, step).wait()


def unpack(target, pair, stage, row, start, width):
    count = 2 * width // FSDP
    both = [
        pack_rows(stage[row + part * TOK : row + (part + 1) * TOK, start : start + width].astype(wide))
        for part in range(2)
    ]
    target[pair * count : (pair + 1) * count, :] = jnp.concatenate(both, axis=0).astype(low)


def experts_kernel(*refs):
    expert_ref, slots_hbm, routes_ref, router_hbm = refs[:4]
    pieces, cot_pieces, pack_ref = refs[4:14], refs[14:24], refs[24]
    out_ref, gates_ref, parts_ref, gated_out, grad_in_out = refs[25:30]
    normed_ref, cot_ref, incoming, hidden, gated, grad_rows, grad_ref, grad_in = refs[30:38]
    router_ref, w_in, w_down, stage, slots_ref, raw, gate_parts, buffer = refs[38:46]
    piece_sems, cot_sems, sems, slab_sems = refs[46:]
    base = 3 * SH_OWN
    half_d = D // 2

    def stage_down(part):
        return pltpu.make_async_copy(
            pack_ref.at[pl.ds(part * half_d, half_d), pl.ds(base + 2 * FF, FF)], stage, sems.at[part]
        )

    copies = [
        pltpu.make_async_copy(router_hbm, router_ref, sems.at[2]),
        pltpu.make_async_copy(slots_hbm, slots_ref, sems.at[3]),
        pltpu.make_async_copy(pack_ref.at[:, pl.ds(base, 2 * FF)], w_in, sems.at[4]),
    ]
    copies[0].start()
    piece_copies = load_pieces(pieces, normed_ref, None, piece_sems)
    copies[1].start()
    stage_down(0).start()
    cot_copies = load_pieces(cot_pieces, cot_ref, None, cot_sems)
    copies[2].start()
    expert = expert_ref[0]
    lane = lax.broadcasted_iota(jnp.int32, (ROWS, 128), 1)
    for copy in piece_copies + copies[:1]:
        copy.wait()
    for step in range(ALL // ROWS):
        rows = pl.ds(step * ROWS, ROWS)
        logits = mm(normed_ref[rows, :], router_ref[...])
        first, second = routes_ref[rows, 0:1], routes_ref[rows, 1:2]
        chosen_first = jnp.sum(jnp.where(lane == first + 2, logits, 0.0), axis=1, keepdims=True)
        chosen_second = jnp.sum(jnp.where(lane == second + 2, logits, 0.0), axis=1, keepdims=True)
        gate_first = 1.0 / (1.0 + jnp.exp(chosen_second - chosen_first))
        gate_second = 1.0 / (1.0 + jnp.exp(chosen_first - chosen_second))
        here = jnp.where(first == expert, gate_first, 0.0) + jnp.where(second == expert, gate_second, 0.0)
        upper, lower = halves(here)
        parts = jnp.where(lane == 0, upper.astype(wide), 0.0) + jnp.where(lane == 1, lower.astype(wide), 0.0)
        gate_parts[rows, :] = parts.astype(low)
        if step == 0:
            both_gates = jnp.where(lane == 0, gate_first, 0.0) + jnp.where(lane == 1, gate_second, 0.0)
            gates_ref[...] = both_gates[:TOK]
    copies[1].wait()
    for step in range(D // ROWS):
        columns = pl.ds(step * ROWS, ROWS)
        incoming[:, columns] = mm(slots_ref[...], normed_ref[:, columns]).astype(low)
    stage_down(0).wait()
    for copy in cot_copies:
        copy.wait()
    for step in range(D // ROWS):
        columns = pl.ds(step * ROWS, ROWS)
        grad_rows[:, columns] = mm(slots_ref[...], cot_ref[:, columns]).astype(low)
        if step < 4:
            unpack(w_down, step, stage, step * 2 * TOK, 0, FF)
    stage_down(1).start()
    slot_parts = mm(slots_ref[...], gate_parts[...])
    slot_gate = slot_parts[:, 0:1] + slot_parts[:, 1:2]
    copies[2].wait()
    for step in range(2 * FF // ROWS):
        columns = pl.ds(step * ROWS, ROWS)
        raw[:, columns] = mm(incoming[...], w_in[:, columns])
    stage_down(1).wait()
    for step in range(4):
        unpack(w_down, 4 + step, stage, step * 2 * TOK, 0, FF)
    for start, width in FF_TILES:
        gate, up = raw[:, start : start + width], raw[:, FF + start : FF + start + width]
        hidden[:, start : start + width] = (silu_parts(gate)[1] * up).astype(low)
    slot_grad = jnp.zeros((SLOTS, 1), wide)
    for step in range(D // ROWS):
        columns = pl.ds(step * ROWS, ROWS)
        rows = mm(hidden[...], w_down[:, columns]).astype(low).astype(wide)
        cot = grad_rows[:, columns].astype(wide)
        gated[:, columns] = (rows * slot_gate).astype(low)
        grad_rows[:, columns] = (cot * slot_gate).astype(low)
        slot_grad = slot_grad + jnp.sum(rows * cot, axis=1, keepdims=True)
    gated_copy = pltpu.make_async_copy(gated, gated_out, sems.at[5])
    gated_copy.start()
    for start, width in FF_TILES:
        grad_hidden = mm_t(grad_rows[...], w_down[pl.ds(start, width), :])
        sig, act = silu_parts(raw[:, start : start + width])
        grad_gate, grad_up = swiglu_back(sig, act, raw[:, FF + start : FF + start + width], grad_hidden)
        grad_ref[:, start : start + width] = grad_gate
        grad_ref[:, FF + start : FF + start + width] = grad_up
    for step in range(D // ROWS):
        columns = pl.ds(step * ROWS, ROWS)
        grad_in[:, columns] = mm_t(grad_ref[...], w_in[columns, :]).astype(low)
    grad_copy = pltpu.make_async_copy(grad_in, grad_in_out, sems.at[6])
    grad_copy.start()
    upper, lower = halves(slot_grad)
    slot_lane = lax.broadcasted_iota(jnp.int32, (SLOTS, 128), 1)
    parts_ref[...] = (
        jnp.where(slot_lane == expert, upper.astype(wide), 0.0)
        + jnp.where(slot_lane == expert + 8, lower.astype(wide), 0.0)
    ).astype(low)

    def down_rows(step):
        count = 2 * FF // FSDP
        return t_mm(hidden[:, step * count : (step + 1) * count], grad_rows[...])

    send_slabs(incoming, grad_ref, down_rows, out_ref, buffer, slab_sems)
    gated_copy.wait()
    grad_copy.wait()


def experts(expert, slots, routes, router, pieces, cot_pieces, pack):
    rows = [(SLOTS, D), (SLOTS, FF), (SLOTS, D), (SLOTS, D), (SLOTS, 2 * FF), (SLOTS, D)]
    return pl.pallas_call(
        experts_kernel,
        out_shape=(
            jax.ShapeDtypeStruct((D, 3 * FF), low),
            jax.ShapeDtypeStruct((TOK, 128), wide),
            jax.ShapeDtypeStruct((SLOTS, 128), low),
            jax.ShapeDtypeStruct((SLOTS, D), low),
            jax.ShapeDtypeStruct((SLOTS, D), low),
        ),
        in_specs=[smem, anywhere, vmem] + [anywhere] * 22,
        out_specs=(anywhere, vmem, vmem, anywhere, anywhere),
        scratch_shapes=[pltpu.VMEM((ALL, D), low), pltpu.VMEM((ALL, D), low)]
        + [pltpu.VMEM(shape, low) for shape in rows]
        + [
            pltpu.VMEM((D, 128), low),
            pltpu.VMEM((D, 2 * FF), low),
            pltpu.VMEM((FF, D), low),
            pltpu.VMEM((D // 2, FF), low),
            pltpu.VMEM((SLOTS, ALL), low),
            pltpu.VMEM((SLOTS, 2 * FF), wide),
            pltpu.VMEM((ALL, 128), low),
            pltpu.VMEM((2, ROWS, 3 * FF), low),
            pltpu.SemaphoreType.DMA((20,)),
            pltpu.SemaphoreType.DMA((20,)),
            pltpu.SemaphoreType.DMA((7,)),
            pltpu.SemaphoreType.DMA((2,)),
        ],
        compiler_params=params(60),
        cost_estimate=cost(24e9, 60e6, 1e6),
        name="experts",
    )(expert, slots, routes, router, *pieces, *cot_pieces, pack)


def shared_kernel(*refs):
    slots_t_hbm, pieces, cot_pieces = refs[0], refs[1:11], refs[11:21]
    pack_ref, grad_in_hbm, parts_ref = refs[21:24]
    grad_mine, grad_other, hidden_out, grad_out, down_out = refs[24:29]
    normed_ref, cot_ref, grad_ref, hidden, grad_hidden_ref, w_in, w_down, stage, slots_t_ref, grad_in = refs[29:39]
    piece_sems, cot_sems, sems = refs[39:]
    half_d = D // 2

    def stage_shared(part):
        return pltpu.make_async_copy(
            pack_ref.at[pl.ds(part * half_d, half_d), pl.ds(2 * SH_OWN, SH_OWN)], stage.at[part], sems.at[part]
        )

    stage_shared(0).start()
    stage_shared(1).start()
    piece_copies = load_pieces(pieces, normed_ref, None, piece_sems)
    copies = [
        pltpu.make_async_copy(pack_ref.at[:, pl.ds(0, 2 * SH_OWN)], w_in, sems.at[2]),
        pltpu.make_async_copy(slots_t_hbm, slots_t_ref, sems.at[3]),
        pltpu.make_async_copy(grad_in_hbm, grad_in, sems.at[4]),
    ]
    copies[0].start()
    cot_copies = load_pieces(cot_pieces, cot_ref, None, cot_sems)
    copies[1].start()
    copies[2].start()
    for part in range(2):
        stage_shared(part).wait()
        for pair in range(4):
            unpack(w_down, part * 4 + pair, stage.at[part], pair * 2 * TOK, 0, SH_OWN)
    for copy in piece_copies + copies[:1] + cot_copies:
        copy.wait()
    for step in range(ALL // ROWS):
        rows = pl.ds(step * ROWS, ROWS)
        both = mm(normed_ref[rows, :], w_in[...])
        sig, act = silu_parts(both[:, :SH_OWN])
        up = both[:, SH_OWN:]
        hidden[rows, :] = (act * up).astype(low)
        grad_gate, grad_up = swiglu_back(sig, act, up, mm_t(cot_ref[rows, :], w_down[...]))
        grad_hidden_ref[rows, 0:SH_OWN] = grad_gate
        grad_hidden_ref[rows, SH_OWN : 2 * SH_OWN] = grad_up
    sent = [
        pltpu.make_async_copy(hidden, hidden_out, sems.at[5]),
        pltpu.make_async_copy(grad_hidden_ref, grad_out, sems.at[6]),
        pltpu.make_async_copy(w_down, down_out, sems.at[7]),
    ]
    for copy in sent:
        copy.start()
    for copy in copies[1:]:
        copy.wait()
    half = ALL // 2
    for side, target in ((1, grad_other), (0, grad_mine)):
        for step in range(half // ROWS):
            rows = pl.ds(side * half + step * ROWS, ROWS)
            for tile in range(D // 512):
                columns = pl.ds(tile * 512, 512)
                grad_ref[rows, columns] = (
                    mm_t(grad_hidden_ref[rows, :], w_in[columns, :]) + mm(slots_t_ref[rows, :], grad_in[:, columns])
                ).astype(low)
            grad_ref[rows, D : D + 128] = mm(slots_t_ref[rows, :], parts_ref[...]).astype(low)
        copy = pltpu.make_async_copy(grad_ref.at[pl.ds(side * half, half), :], target, sems.at[8 + side])
        copy.start()
        sent.append(copy)
    for copy in sent:
        copy.wait()


def shared(slots_t, pieces, cot_pieces, pack, grad_in, parts):
    outs = [(ALL // 2, D + 128)] * 2 + [(ALL, SH_OWN), (ALL, 2 * SH_OWN), (SH_OWN, D)]
    return pl.pallas_call(
        shared_kernel,
        out_shape=tuple(jax.ShapeDtypeStruct(shape, low) for shape in outs),
        in_specs=[anywhere] * 23 + [vmem],
        out_specs=tuple([anywhere] * 5),
        scratch_shapes=[
            pltpu.VMEM((ALL, D), low),
            pltpu.VMEM((ALL, D), low),
            pltpu.VMEM((ALL, D + 128), low),
            pltpu.VMEM((ALL, SH_OWN), low),
            pltpu.VMEM((ALL, 2 * SH_OWN), low),
            pltpu.VMEM((D, 2 * SH_OWN), low),
            pltpu.VMEM((SH_OWN, D), low),
            pltpu.VMEM((2, D // 2, SH_OWN), low),
            pltpu.VMEM((ALL, SLOTS), low),
            pltpu.VMEM((SLOTS, D), low),
            pltpu.SemaphoreType.DMA((20,)),
            pltpu.SemaphoreType.DMA((20,)),
            pltpu.SemaphoreType.DMA((10,)),
        ],
        compiler_params=params(60),
        cost_estimate=cost(9.5e9, 30e6, 1e6),
        name="shared",
    )(slots_t, *pieces, *cot_pieces, pack, grad_in, parts)


def shared_weights_kernel(*refs):
    pieces, cot_pieces, hidden_ref, grad_ref = refs[:10], refs[10:20], refs[20], refs[21]
    out_ref, normed_ref, cot_ref, buffer, down, piece_sems, cot_sems, sems = refs[22:]
    cot_copies = load_pieces(cot_pieces, cot_ref, None, cot_sems)
    copies = load_pieces(pieces, normed_ref, None, piece_sems)
    for copy in cot_copies:
        copy.wait()
    for tile in range(D // ROWS):
        part = pl.ds(tile * ROWS, ROWS)
        down[:, part] = t_mm(hidden_ref[...], cot_ref[:, part])
    for copy in copies:
        copy.wait()
    count = 2 * SH_PAD
    send_slabs(
        normed_ref, grad_ref, lambda step: down[step * count : (step + 1) * count, :], out_ref, buffer, sems
    )


def shared_weights(pieces, cot_pieces, hidden, grad):
    return pl.pallas_call(
        shared_weights_kernel,
        out_shape=jax.ShapeDtypeStruct((D, 3 * SH_OWN + 128), low),
        in_specs=[anywhere] * 20 + [vmem] * 2,
        out_specs=anywhere,
        scratch_shapes=[
            pltpu.VMEM((ALL, D), low),
            pltpu.VMEM((ALL, D), low),
            pltpu.VMEM((2, ROWS, 3 * SH_OWN), low),
            pltpu.VMEM((SH_OWN, D), wide),
            pltpu.SemaphoreType.DMA((20,)),
            pltpu.SemaphoreType.DMA((20,)),
            pltpu.SemaphoreType.DMA((2,)),
        ],
        compiler_params=params(60),
        cost_estimate=cost(5e9, 18e6),
        name="shared_weights",
    )(*pieces, *cot_pieces, hidden, grad)


def out_rows_kernel(place_ref, *refs):
    parts, out_ref = refs[:5], refs[5]
    for index in range(EXPERTS):
        step, side = index // 2, index % 2
        columns = pl.ds(pl.multiple_of(place_ref[index] * 256, 256), 256)
        out_ref[:, columns] = parts[step + 1][side] if step else parts[side][...]


def out_rows(places, parts):
    return pl.pallas_call(
        out_rows_kernel,
        out_shape=jax.ShapeDtypeStruct((256, D), low),
        in_specs=[smem] + [vmem] * 5,
        out_specs=vmem,
        compiler_params=params(32),
        cost_estimate=cost(0, 2e6),
        name="out_rows",
    )(places, *parts)


def back_two_kernel(*refs):
    own_ref, first_ref, second_ref, middle_ref, cot_ref, gains_ref, gates_ref, routes_ref, _ = refs[:9]
    block_ref, grad_ref, pack_ref, small_ref, sem = refs[9:]
    total = own_ref[...] + first_ref[...].astype(wide) + second_ref[...].astype(wide)
    lane = lax.broadcasted_iota(jnp.int32, (TOK, 128), 1)
    extra = total[:, D:]
    first, second = routes_ref[:, 0:1], routes_ref[:, 1:2]

    def taken(route):
        return jnp.sum(jnp.where((lane == route) | (lane == route + 8), extra, 0.0), axis=1, keepdims=True)

    gate_first, gate_second = gates_ref[:, 0:1], gates_ref[:, 1:2]
    taken_first, taken_second = taken(first), taken(second)
    inner = gate_first * taken_first + gate_second * taken_second
    chosen_first, chosen_second = gate_first * (taken_first - inner), gate_second * (taken_second - inner)
    logits = jnp.where(lane == first, chosen_first, 0.0) + jnp.where(lane == second, chosen_second, 0.0)
    grad = total[:, :D]
    for index in range(EXPERTS):
        grad = grad + logits[:, index : index + 1] * gains_ref[2 + index : 3 + index, :]
    middle = middle_ref[...]
    factor = lax.rsqrt(jnp.mean(middle * middle, axis=-1, keepdims=True) + eps_norm)
    scaled = grad * gains_ref[1:2, :]
    mean = jnp.mean(scaled * middle, axis=-1, keepdims=True)
    result = cot_ref[...].astype(wide) + factor * scaled - middle * (factor * factor * factor * mean)
    grad_ref[...] = result
    block_ref[...] = result.astype(low)
    gain = jnp.sum(grad * middle * factor, axis=0, keepdims=True)
    gain_upper, gain_lower = halves(gain)
    normed = (middle * factor * gains_ref[1:2, :]).astype(low)
    logit_upper, logit_lower = halves(logits.T[0:EXPERTS, :])
    router = mm(logit_upper, normed) + mm(logit_lower, normed)
    small = [gain_upper.astype(wide), gain_lower.astype(wide), router, jnp.zeros((118, D), wide)]
    small_ref[...] = jnp.concatenate(small, axis=0).T.astype(low)
    copy = pltpu.make_async_copy(small_ref, pack_ref.at[:, pl.ds(3 * SH_OWN, 128)], sem)
    copy.start()
    copy.wait()


def back_two(*operands):
    return pl.pallas_call(
        back_two_kernel,
        out_shape=(
            jax.ShapeDtypeStruct((TOK, D), low),
            jax.ShapeDtypeStruct((TOK, D), wide),
            jax.ShapeDtypeStruct((D, 3 * SH_OWN + 128), low),
        ),
        in_specs=[vmem] * 8 + [anywhere],
        out_specs=(vmem, vmem, anywhere),
        scratch_shapes=[pltpu.VMEM((D, 128), low), pltpu.SemaphoreType.DMA],
        input_output_aliases={8: 2},
        compiler_params=params(60),
        cost_estimate=cost(1e7, 6e6),
        name="back_two",
    )(*operands)


def norm_factor(values):
    return lax.rsqrt(jnp.mean(values * values, axis=-1, keepdims=True) + eps_norm)


def norm_back(values, factor, gain, grad):
    scaled = grad * gain
    inner = jnp.mean(scaled * values, axis=-1, keepdims=True)
    return factor * scaled - values * (factor * factor * factor * inner)


def per_device(
    hidden_in,
    cotangent,
    segments,
    routes,
    attn_gain,
    w_query,
    w_key,
    w_value,
    w_out,
    ffn_gain,
    w_router,
    shared_gate,
    shared_up,
    shared_down,
    expert_gate,
    expert_up,
    expert_down,
):
    expert = lax.axis_index("expert")
    z, core = expert // 2, expert % 2
    place = lax.axis_index("fsdp")

    misc = jnp.concatenate(
        [attn_gain[:, None], ffn_gain[:, None], w_router, jnp.zeros((TOK, 118), low)], axis=1
    )
    attn_pack = jnp.concatenate(
        [
            lax.dynamic_slice_in_dim(w_query, 256 * expert, 256, 1),
            lax.dynamic_slice_in_dim(w_key, HD * z, HD, 1),
            lax.dynamic_slice_in_dim(w_value, HD * z, HD, 1),
            lax.dynamic_slice_in_dim(w_out, 256 * expert, 256, 1),
            misc,
        ],
        axis=1,
    )
    attn_all = lax.all_gather(attn_pack, "fsdp", axis=0, tiled=True)
    half_in, half_out = SH // 2, SH_OWN // 2
    sel_column = jnp.arange(half_out)
    picked = SH_ROWS * (sel_column // SH_PAD) + SH_PART * expert + sel_column % SH_PAD
    picked = jnp.where(sel_column % SH_PAD < SH_PART, picked, -1)
    select = (jnp.arange(half_in)[:, None] == picked[None, :]).astype(low)
    own_shared = mm(
        jnp.concatenate(
            [shared_gate[:, :half_in], shared_gate[:, half_in:], shared_up[:, :half_in], shared_up[:, half_in:]],
            axis=0,
        ),
        select,
    ).astype(low)
    own_down = jnp.pad(
        lax.dynamic_slice_in_dim(shared_down, SH_PART * expert, SH_PART, 0),
        ((0, SH_PAD - SH_PART), (0, 0)),
    )
    ffn_pack = jnp.concatenate(
        [
            own_shared[:TOK],
            own_shared[TOK : 2 * TOK],
            own_shared[2 * TOK : 3 * TOK],
            own_shared[3 * TOK :],
            pack_tiles(own_down),
            expert_gate[:, 0],
            expert_up[:, 0],
            pack_tiles(expert_down[:, 0]),
        ],
        axis=1,
    )
    ffn_all = lax.all_gather(ffn_pack, "fsdp", axis=0, tiled=True)

    ids = jnp.concatenate(
        [
            segments.astype(low),
            jnp.pad(routes[0].reshape(1, TOK * TOPK), ((0, 0), (0, LENGTH - TOK * TOPK))).astype(low),
            jnp.zeros((14, LENGTH), low),
        ],
        axis=0,
    )
    hidden_pieces = gather_pieces(jnp.concatenate([hidden_in[0], ids], axis=0))
    cot_block, *hidden_pieces = together(cotangent[0], *hidden_pieces)
    cot_pieces = gather_pieces(cot_block)

    inverse_freq = rope_base ** (-jnp.arange(HD // 2, dtype=wide) * 2.0 / HD)
    angles = jnp.arange(LENGTH).astype(wide)[:, None] * inverse_freq[None, :]
    cosine, sine = jnp.cos(angles), jnp.sin(angles)
    cos_all = jnp.concatenate([cosine, cosine], axis=1)
    sin_back = jnp.concatenate([sine, -sine], axis=1)
    cos_own = lax.dynamic_slice_in_dim(cos_all, place * TOK, TOK, 0)
    sin_own = -lax.dynamic_slice_in_dim(sin_back, place * TOK, TOK, 0)
    cos_two, sin_two = jnp.concatenate([cos_own, cos_own]), jnp.concatenate([sin_own, sin_own])
    attn_all, cos_two, sin_two, cos_all, sin_back = together(attn_all, cos_two, sin_two, cos_all, sin_back)
    normed_one, sent, factor_one, gains, ids_all = project(hidden_pieces, attn_all, cos_two, sin_two)
    qkv = lax.all_to_all(sent, "fsdp", split_axis=0, concat_axis=0, tiled=True)

    ids_all = ids_all.reshape(SEQS, 16, D)
    seg_row = lax.dynamic_slice_in_dim(ids_all[:, 0].astype(wide), place // 2, 1, 0)
    seg_blocks = jnp.pad(seg_row.reshape(FSDP, TOK), ((0, TOK - FSDP), (0, 0)))
    route_all = ids_all[:, 1, : TOK * TOPK].astype(jnp.int32).reshape(ALL, TOPK)
    hit = jnp.any(route_all == expert, axis=1).astype(wide)
    order = jnp.arange(ALL)
    rank = mm(hit.astype(low)[None, :], (order[:, None] < order[None, :]).astype(low))
    slot_bool = (rank.astype(jnp.int32) == jnp.arange(SLOTS)[:, None]) & (hit > 0.5)[None, :]
    slots = slot_bool.astype(low)
    slots_t = slot_bool.T.astype(low)
    out_columns = attn_all[:, 512:768].reshape(EXPERTS, 256, 256)
    owners = jnp.stack([relative_owner(expert, block) for block in range(EXPERTS)])
    out_blocks = [lax.dynamic_index_in_dim(out_columns, owners[block], 0) for block in range(EXPERTS)]
    out_mine, out_other = jnp.concatenate(out_blocks[:4]), jnp.concatenate(out_blocks[4:])
    out_mine, out_other, _ = together(out_mine, out_other, sent)
    w_out_own = out_rows(source_owners(expert), exchange(out_mine, out_other))
    router = attn_all[:, 768:896]
    is_first = core == 0
    kv_weight = attn_all[:, 256:512].reshape(D, 2, 2, HD // 2)
    kv_weight = jnp.where(is_first, kv_weight[:, :, 0], kv_weight[:, :, 1]).reshape(D, HD)
    qkv_weight = jnp.concatenate([attn_all[:, :256], kv_weight], axis=1)
    route_own = route_all[:TOK]
    qkv, seg_row, seg_blocks, route_all, slots, slots_t, w_out_own, router, qkv_weight, route_own, *cot_pieces = together(
        qkv, seg_row, seg_blocks, route_all, slots, slots_t, w_out_own, router, qkv_weight, route_own, *cot_pieces
    )
    mixed_head, log_total = attend(qkv, seg_row, seg_blocks)
    mixed = (
        lax.all_to_all(mixed_head, "fsdp", split_axis=0, concat_axis=0, tiled=True)
        .reshape(SEQS, 2, TOK, HD)
        .transpose(0, 2, 1, 3)
        .reshape(ALL, 2 * HD)
    )
    own_hidden = hidden_in[0].astype(wide)
    half = ALL // 2
    middle = own_hidden + scatter_rows(
        mm(mixed[:half], w_out_own).astype(low), mm(mixed[half:], w_out_own).astype(low)
    )
    factor_two = norm_factor(middle)
    gain_one, gain_two = gains[0:1], gains[1:2]
    normed_block = (middle * factor_two * gain_two).astype(low)

    base = 3 * SH_OWN
    normed_pieces = gather_pieces(normed_block)
    expert_grads, gates, slot_parts, gated_rows, grad_in = experts(
        expert[None], slots, route_all, router, normed_pieces, cot_pieces, ffn_all
    )
    expert_sums = lax.psum_scatter(expert_grads, "fsdp", scatter_dimension=0, tiled=True)
    grad_mine, grad_other, hidden_shared, grad_shared, shared_down_w = shared(
        slots_t, normed_pieces, cot_pieces, ffn_all, grad_in, slot_parts
    )
    own_grad, to_above, to_below = scatter_start(grad_mine, swap_core(grad_other))
    to_above, to_below, hidden_shared, grad_shared = together(to_above, to_below, hidden_shared, grad_shared)
    from_below, from_above = move_z(to_above, 1), move_z(to_below, -1)
    shared_grads = shared_weights(normed_pieces, cot_pieces, hidden_shared, grad_shared)
    from_below, from_above, shared_grads = together(from_below, from_above, shared_grads)
    back_block, grad_middle, shared_grads = back_two(
        own_grad, from_below, from_above, middle, cotangent[0], gains, gates, route_own, shared_grads
    )
    back_block, hidden_shared, gated_rows = together(back_block, hidden_shared, gated_rows)
    below, above = first_pieces(back_block)
    result_other = (mm(hidden_shared[half:], shared_down_w) + mm(slots_t[half:], gated_rows)).astype(low)
    result_mine = (mm(hidden_shared[:half], shared_down_w) + mm(slots_t[:half], gated_rows)).astype(low)
    below, above, result_other, result_mine = together(below, above, result_other, result_mine)
    back_pieces = other_pieces(back_block, below, above)

    sent_back, out_mine, out_other = mix_back(owners, back_pieces, w_out_own, mixed)
    grad_head = lax.all_to_all(sent_back, "fsdp", split_axis=0, concat_axis=0, tiled=True)
    grads_head = attend_back(qkv, grad_head, log_total, seg_row, seg_blocks, cos_all, sin_back)
    grads_qkv = lax.all_to_all(grads_head, "fsdp", split_axis=0, concat_axis=0, tiled=True)
    shared_grads, expert_sums, _ = together(shared_grads, expert_sums, grads_head)
    shared_sums = lax.psum_scatter(shared_grads, "fsdp", scatter_dimension=0, tiled=True)

    result_other, result_mine, _ = together(result_other, result_mine, sent_back)
    result_got = swap_core(result_other)
    result_got, out_mine, out_other = together(result_got, out_mine, out_other)
    out_parts = exchange(out_mine, out_other)
    result_own, to_above, to_below = scatter_start(result_mine, result_got)
    result_own = scatter_end(result_own, move_z(to_above, 1), move_z(to_below, -1))
    layer_out = (middle + result_own).astype(low)
    grads_qkv, layer_out, *out_parts = together(grads_qkv, layer_out, *out_parts)

    grad_query, kv_mine, kv_other = collect(core[None], grads_qkv)
    attn_grads, grad_qkv = qkv_weights(
        source_owners(expert), normed_one, grad_query, kv_mine, swap_core(kv_other), out_parts
    )
    attn_parts = lax.all_to_all(attn_grads, "fsdp", split_axis=0, concat_axis=0, tiled=True)

    grad_normed_other = mm_t(grad_qkv[half:], qkv_weight).astype(low)
    grad_normed_mine = mm_t(grad_qkv[:half], qkv_weight).astype(low)
    own_grad_one, to_above, to_below = scatter_start(grad_normed_mine, swap_core(grad_normed_other))
    attn_parts, to_above, to_below = together(attn_parts, to_above, to_below)
    own_grad_one = scatter_end(own_grad_one, move_z(to_above, 1), move_z(to_below, -1))
    grad_input = (grad_middle + norm_back(own_hidden, factor_one[:TOK], gain_one, own_grad_one)).astype(low)
    attn_sums = jnp.sum(attn_parts.reshape(FSDP, TOK, 3 * HD + 256).astype(wide), axis=0)

    own_weight = lax.dynamic_slice_in_dim(qkv_weight, place * TOK, TOK, 0)
    gain_part = jnp.sum(attn_sums[:, : 3 * HD] * own_weight.astype(wide), axis=1, keepdims=True)
    gain_upper, gain_lower = halves(gain_part / attn_gain.astype(wide)[:, None])
    shards = jnp.concatenate([attn_sums.astype(low), gain_upper, gain_lower, jnp.zeros((TOK, 126), low)], axis=1)

    shared_sums, expert_sums, _ = together(shared_sums, expert_sums, attn_grads)
    shared_shards = lax.all_gather(shared_sums, "expert", axis=0)
    shared_shards, shards = together(shared_shards, shards)
    attn_shards = lax.all_gather(shards, "expert", axis=0)
    put_row = jnp.arange(SH_PAD * EXPERTS * FSDP // 2)
    source, within = put_row // half_out, put_row % half_out
    target = SH_ROWS * (within // SH_PAD) + SH_PART * source + within % SH_PAD
    target = jnp.where(within % SH_PAD < SH_PART, target, -1)
    spread = (target[:, None] == jnp.arange(half_in)[None, :]).astype(low)
    put_row = jnp.arange(EXPERTS * SH_PAD)
    target = SH_PART * (put_row // SH_PAD) + put_row % SH_PAD
    target = jnp.where(put_row % SH_PAD < SH_PART, target, -1)
    spread_rows = (jnp.arange(SH_ROWS)[:, None] == target[None, :]).astype(low)
    spread, spread_rows, _ = together(spread, spread_rows, sent)
    grad_shared_gate, grad_shared_up, grad_shared_down, small_sums = finish_dense(shared_shards, spread, spread_rows)
    grad_w_query, grad_w_key, grad_w_value, grad_w_out, grad_attn_gain = finish(attn_shards)
    grad_expert_gate = expert_sums[:, :FF].astype(wide)[:, None]
    grad_expert_up = expert_sums[:, FF : 2 * FF].astype(wide)[:, None]
    grad_expert_down = unpack_tiles(expert_sums[:, 2 * FF :], 1).astype(wide)[:, None]
    return (
        layer_out[None],
        grad_input[None],
        grad_attn_gain[:, 0],
        grad_w_query,
        grad_w_key,
        grad_w_value,
        grad_w_out,
        small_sums[:, 0] + small_sums[:, 1],
        small_sums[:, 2 : 2 + EXPERTS],
        grad_shared_gate,
        grad_shared_up,
        grad_shared_down,
        grad_expert_gate,
        grad_expert_up,
        grad_expert_down,
    )


def solution(mesh):
    in_specs = (
        P("expert", "fsdp", None),
        P("expert", "fsdp", None),
        P("expert", None),
        P("expert", "fsdp", None),
        P("fsdp"),
        P("fsdp", None),
        P("fsdp", None),
        P("fsdp", None),
        P("fsdp", None),
        P("fsdp"),
        P("fsdp", None),
        P("fsdp", None),
        P("fsdp", None),
        P("fsdp", None),
        P("fsdp", "expert", None),
        P("fsdp", "expert", None),
        P("fsdp", "expert", None),
    )
    out_specs = (
        P("expert", "fsdp", None),
        P("expert", "fsdp", None),
        P("fsdp"),
        P("fsdp", None),
        P("fsdp", None),
        P("fsdp", None),
        P("fsdp", None),
        P("fsdp"),
        P("fsdp", None),
        P("fsdp", None),
        P("fsdp", None),
        P("fsdp", None),
        P("fsdp", "expert", None),
        P("fsdp", "expert", None),
        P("fsdp", "expert", None),
    )
    return jax.shard_map(
        per_device, mesh=mesh, in_specs=in_specs, out_specs=out_specs, check_vma=False
    )
```

```python
import jax
import jax.numpy as jnp
from jax import lax
from jax.experimental import pallas as pl
from jax.experimental.pallas import tpu as pltpu
from jax.sharding import PartitionSpec as P

D = 2048
H = 16
KV = 4
HD = 128
FF = 1408
SH = 2816
TOPK = 2
TOK = 128
LENGTH = 2048
SEQS = 8
EXPERTS = 8
FSDP = 16
ALL = SEQS * TOK
CAP = 42
SLOTS = SEQS * CAP
SH_ROWS = SH // FSDP
SH_PART = SH_ROWS // EXPERTS
SH_PAD = 24
SH_OWN = FSDP * SH_PAD
QBLOCK = 256

eps_norm = 1e-06
rope_base = 600000.0
masked_fill = -1e30
low = jnp.bfloat16
wide = jnp.float32


def shift_pairs(step):
    return [(z * 2 + c, ((z + step) % 4) * 2 + c) for z in range(4) for c in range(2)]


core_pairs = [(z * 2 + c, z * 2 + 1 - c) for z in range(4) for c in range(2)]


def move_z(block, step):
    return lax.ppermute(block, "expert", shift_pairs(step))


def swap_core(block):
    return lax.ppermute(block, "expert", core_pairs)


def together(*values):
    return lax.optimization_barrier(values)


TOP = TOK // 2


def first_pieces(block):
    return move_z(block, 1), move_z(block, -1)


def other_pieces(block, below, above):
    upper, lower = move_z(below[:TOP], 1), move_z(above[TOP:], -1)
    mine = [block, above, upper, lower, below]
    return mine + [swap_core(piece) for piece in mine]


def gather_pieces(block):
    return other_pieces(block, *first_pieces(block))


PIECES = [(4 * side + block, start) for side in (0, 1) for block, start in ((0, 0), (1, 0), (2, 0), (2, TOP), (3, 0))]


def load_pieces(refs, rows_ref, extra_ref, sems):
    copies = []
    for index, (ref, (block, start)) in enumerate(zip(refs, PIECES)):
        count = min(ref.shape[0], TOK - start)
        copies.append(
            pltpu.make_async_copy(
                ref.at[pl.ds(0, count), :], rows_ref.at[pl.ds(block * TOK + start, count), :], sems.at[2 * index]
            )
        )
        if extra_ref is not None and ref.shape[0] > count:
            copies.append(
                pltpu.make_async_copy(
                    ref.at[pl.ds(count, 16), :], extra_ref.at[pl.ds(block * 16, 16), :], sems.at[2 * index + 1]
                )
            )
    for copy in copies:
        copy.start()
    return copies


def scatter_start(mine, received):
    chip = mine.reshape(4, TOK, -1).astype(wide) + received.reshape(4, TOK, -1).astype(wide)
    from_below = move_z(chip[2, :TOP].astype(low), 1)
    from_above = move_z(chip[2, TOP:].astype(low), -1)
    to_above = jnp.concatenate([chip[1, :TOP] + from_below.astype(wide), chip[1, TOP:]], axis=0)
    to_below = jnp.concatenate([chip[3, :TOP], chip[3, TOP:] + from_above.astype(wide)], axis=0)
    return chip[0], to_above.astype(low), to_below.astype(low)


def scatter_end(own, first, second):
    return own + first.astype(wide) + second.astype(wide)


def scatter_rows(mine, other):
    own, to_above, to_below = scatter_start(mine, swap_core(other))
    return scatter_end(own, move_z(to_above, 1), move_z(to_below, -1))


def exchange(mine, other):
    got = swap_core(other)
    chip = jnp.stack([mine[1:], got[1:]], axis=1)
    return mine[0], got[0], *[move_z(chip[step - 1], step) for step in (1, 2, 3)]


def source_owners(expert):
    return jnp.stack([((expert // 2 - index // 2) % 4) * 2 + ((expert % 2) ^ (index % 2)) for index in range(EXPERTS)])


def relative_owner(expert, block):
    return ((expert // 2 + block % 4) % 4) * 2 + ((expert % 2) ^ (block // 4))


def pack_tiles(block):
    rows, columns = block.shape[0] // 8, block.shape[1] // 128
    tiles = block.reshape(rows, 8, columns, 128).transpose(2, 1, 0, 3)
    return tiles.reshape(columns * 8, rows * 128)


def unpack_tiles(block, count):
    rows, columns = block.shape[1] // 128, block.shape[0] // (8 * count)
    tiles = block.reshape(count, columns, 8, rows, 128).transpose(0, 3, 2, 1, 4)
    return tiles.reshape(count * rows * 8, columns * 128)


def product(left, right, contract):
    return lax.dot_general(left, right, (contract, ((), ())), preferred_element_type=wide)


def mm(left, right):
    return product(left, right, ((1,), (0,)))


def mm_t(left, right):
    return product(left, right, ((1,), (1,)))


def t_mm(left, right):
    return product(left, right, ((0,), (0,)))


def segment_columns(seg_blocks_ref):
    return seg_blocks_ref[...].T


def block_scores(qkv_ref, seg_row_ref, columns, start, reach):
    query = qkv_ref[pl.ds(start, QBLOCK), 0:HD]
    key = qkv_ref[pl.ds(0, reach), HD : 2 * HD]
    scores = mm_t(query, key) * HD ** (-0.5)
    query_pos = start + lax.broadcasted_iota(jnp.int32, (QBLOCK, reach), 0)
    key_pos = lax.broadcasted_iota(jnp.int32, (QBLOCK, reach), 1)
    block = start // TOK
    column = jnp.concatenate([columns[:, block : block + 1], columns[:, block + 1 : block + 2]], axis=0)
    same = column == seg_row_ref[:, pl.ds(0, reach)]
    return jnp.where(same & (query_pos >= key_pos), scores, masked_fill)


def attend_kernel(qkv_ref, seg_row_ref, seg_blocks_ref, mixed_ref, total_ref):
    columns = segment_columns(seg_blocks_ref)
    for block in range(LENGTH // QBLOCK):
        start, reach = block * QBLOCK, (block + 1) * QBLOCK
        scores = block_scores(qkv_ref, seg_row_ref, columns, start, reach)
        largest = jnp.max(scores, axis=-1, keepdims=True)
        exponent = jnp.exp(scores - largest)
        totals = jnp.sum(exponent, axis=-1, keepdims=True)
        probs_low = (exponent * (1.0 / totals)).astype(low)
        value = qkv_ref[pl.ds(0, reach), 2 * HD : 3 * HD]
        mixed_ref[pl.ds(start, QBLOCK), :] = mm(probs_low, value).astype(low)
        total_ref[pl.ds(start, QBLOCK), :] = largest + jnp.log(totals)


def attend_back_kernel(
    qkv_ref, grad_ref, total_ref, seg_row_ref, seg_blocks_ref, cos_ref, sin_ref, out_ref, small_ref, key_acc, value_acc
):
    columns = segment_columns(seg_blocks_ref)
    key_acc[...] = jnp.zeros_like(key_acc)
    value_acc[...] = jnp.zeros_like(value_acc)

    def turn_back(value, rows):
        return value * cos_ref[rows, :] + pltpu.roll(value, HD // 2, 1) * sin_ref[rows, :]

    for block in range(LENGTH // QBLOCK):
        start, reach = block * QBLOCK, (block + 1) * QBLOCK
        rows, span = pl.ds(start, QBLOCK), pl.ds(0, reach)
        scores = block_scores(qkv_ref, seg_row_ref, columns, start, reach)
        probs = jnp.exp(scores - total_ref[rows, :])
        tall = [pl.ds((start // TOK + part) * TALL, TOK) for part in range(QBLOCK // TOK)]
        grad = jnp.concatenate([grad_ref[part, :] for part in tall], axis=0)
        grad_probs = mm_t(grad, qkv_ref[span, 2 * HD : 3 * HD])
        inner = jnp.sum(probs * grad_probs, axis=-1, keepdims=True)
        grad_scores = (probs * (grad_probs - inner)).astype(low)
        scale = HD ** (-0.5)
        grad_query = mm(grad_scores, qkv_ref[span, HD : 2 * HD]) * scale
        out_ref[rows, 0:HD] = turn_back(grad_query, rows).astype(low)
        key_acc[span, :] += t_mm(grad_scores, qkv_ref[rows, 0:HD]) * scale
        value_acc[span, :] += t_mm(probs.astype(low), grad)
    for block in range(LENGTH // QBLOCK):
        rows = pl.ds(block * QBLOCK, QBLOCK)
        out_ref[rows, HD : 2 * HD] = turn_back(key_acc[rows, :], rows).astype(low)
        out_ref[rows, 2 * HD : 3 * HD] = value_acc[rows, :].astype(low)
    small = grad_ref[pl.ds(TOK, 16), :].astype(wide)
    for index in range(1, FSDP):
        small = small + grad_ref[pl.ds(index * TALL + TOK, 16), :].astype(wide)
    small_ref[...] = small


vmem = pl.BlockSpec(memory_space=pltpu.VMEM)
smem = pl.BlockSpec(memory_space=pltpu.SMEM)
anywhere = pl.BlockSpec(memory_space=pl.ANY)
kernel_params = pltpu.CompilerParams(vmem_limit_bytes=48 * 1024 * 1024)


def attend(qkv, seg_row, seg_blocks):
    return pl.pallas_call(
        attend_kernel,
        out_shape=(
            jax.ShapeDtypeStruct((LENGTH, HD), low),
            jax.ShapeDtypeStruct((LENGTH, 1), wide),
        ),
        in_specs=[vmem] * 3,
        out_specs=(vmem, vmem),
        compiler_params=kernel_params,
        cost_estimate=pl.CostEstimate(
            flops=2 * LENGTH * LENGTH * HD, bytes_accessed=4 * LENGTH * HD * 2, transcendentals=LENGTH * LENGTH // 2
        ),
        name="attend",
    )(qkv, seg_row, seg_blocks)


def attend_back(qkv, grad, total, seg_row, seg_blocks, cos_all, sin_all):
    return pl.pallas_call(
        attend_back_kernel,
        out_shape=(jax.ShapeDtypeStruct((LENGTH, 3 * HD), low), jax.ShapeDtypeStruct((16, TOK), wide)),
        in_specs=[vmem] * 7,
        out_specs=(vmem, vmem),
        scratch_shapes=[pltpu.VMEM((LENGTH, HD), wide), pltpu.VMEM((LENGTH, HD), wide)],
        compiler_params=kernel_params,
        cost_estimate=pl.CostEstimate(
            flops=5 * LENGTH * LENGTH * HD, bytes_accessed=8 * LENGTH * HD * 2, transcendentals=LENGTH * LENGTH // 2
        ),
        name="attend_back",
    )(qkv, grad, total, seg_row, seg_blocks, cos_all, sin_all)


ROWS = 256
FF_TILES = [(start, min(256, FF - start)) for start in range(0, FF, 256)]


def params(mebibytes):
    return pltpu.CompilerParams(vmem_limit_bytes=mebibytes * 1024 * 1024)


def cost(flops, moved, special=0):
    return pl.CostEstimate(flops=int(flops), bytes_accessed=int(moved), transcendentals=int(special))


def project_kernel(*refs):
    pieces, (attn_ref, cos_ref, sin_ref) = refs[:10], refs[10:13]
    normed_ref, sent_ref, factor_ref, gains_ref, ids_ref, hidden, sems = refs[13:]
    copies = load_pieces(pieces, hidden, ids_ref, sems)
    pick = lax.broadcasted_iota(jnp.int32, (16, TOK), 0) == lax.broadcasted_iota(jnp.int32, (16, TOK), 1)
    gains_ref[...] = mm_t(pick.astype(wide).astype(low), attn_ref[:, 768:896])
    for copy in copies:
        copy.wait()
    gain = gains_ref[0:1, :]

    @pl.loop(0, ALL // ROWS)
    def step(index):
        rows = pl.ds(index * ROWS, ROWS)
        values = hidden[rows, :].astype(wide)
        factor = lax.rsqrt(jnp.mean(values * values, axis=-1, keepdims=True) + eps_norm)
        factor_ref[rows, :] = factor
        normed = (values * factor * gain).astype(low)
        normed_ref[rows, :] = normed
        raw = mm(normed, attn_ref[:, 0:512])

        def turn(value):
            return (value * cos_ref[...] + pltpu.roll(value, HD // 2, 1) * sin_ref[...]).astype(low)

        key = turn(raw[:, 2 * HD : 3 * HD])
        value = raw[:, 3 * HD :].astype(low)
        for head in range(2):
            query = turn(raw[:, head * HD : (head + 1) * HD])
            for part in range(2):
                place = pl.ds(index * 4 * TOK + (2 * part + head) * TOK, TOK)
                within = slice(part * TOK, (part + 1) * TOK)
                sent_ref[place, 0:HD] = query[within]
                sent_ref[place, HD : 2 * HD] = key[within]
                sent_ref[place, 2 * HD : 3 * HD] = value[within]


def project(pieces, attn_all, cos_two, sin_two):
    return pl.pallas_call(
        project_kernel,
        out_shape=(
            jax.ShapeDtypeStruct((ALL, D), low),
            jax.ShapeDtypeStruct((LENGTH, 3 * HD), low),
            jax.ShapeDtypeStruct((ALL, 1), wide),
            jax.ShapeDtypeStruct((16, D), wide),
            jax.ShapeDtypeStruct((SEQS * 16, D), low),
        ),
        in_specs=[anywhere] * 10 + [vmem] * 3,
        out_specs=tuple([vmem] * 5),
        scratch_shapes=[pltpu.VMEM((ALL, D), low), pltpu.SemaphoreType.DMA((20,))],
        compiler_params=params(40),
        cost_estimate=cost(2.2e9, 16e6),
        name="project",
    )(*pieces, attn_all, cos_two, sin_two)


TALL = TOK + 16


def mix_back_kernel(place_ref, *refs):
    pieces, weight_ref, mixed_ref, small_ref = refs[:10], refs[10], refs[11], refs[12]
    sent_ref, mine_ref, other_ref, grad_ref, sems = refs[13:]
    for index in range(FSDP):
        sent_ref[pl.ds(index * TALL + TOK, 16), :] = small_ref[:, index * TOK : (index + 1) * TOK]
    for copy in load_pieces(pieces, grad_ref, None, sems):
        copy.wait()
    for index in range(ALL // ROWS):
        grad = mm_t(grad_ref[pl.ds(index * ROWS, ROWS), :], weight_ref[...]).astype(low)
        for part in range(2):
            for head in range(2):
                place = pl.ds((index * 4 + 2 * part + head) * TALL, TOK)
                sent_ref[place, :] = grad[part * TOK : (part + 1) * TOK, head * HD : (head + 1) * HD]
    for index in range(EXPERTS):
        columns = pl.ds(pl.multiple_of(place_ref[index] * 256, 256), 256)
        target = mine_ref if index < 4 else other_ref
        target[index % 4] = t_mm(mixed_ref[...], grad_ref[:, columns]).astype(low)


def mix_back(owners, pieces, weight, mixed, small):
    blocks = jax.ShapeDtypeStruct((4, 256, 256), low)
    return pl.pallas_call(
        mix_back_kernel,
        out_shape=(jax.ShapeDtypeStruct((FSDP * TALL, HD), low), blocks, blocks),
        in_specs=[smem] + [anywhere] * 10 + [vmem] * 3,
        out_specs=(vmem, vmem, vmem),
        scratch_shapes=[pltpu.VMEM((ALL, D), low), pltpu.SemaphoreType.DMA((20,))],
        compiler_params=params(60),
        cost_estimate=cost(2.2e9, 10e6),
        name="mix_back",
    )(owners, *pieces, weight, mixed, small)


def collect_kernel(core_ref, grads_ref, query_ref, mine_ref, other_ref):
    first = core_ref[0] == 0

    @pl.loop(0, SEQS)
    def step(index):
        rows = pl.ds(index * TOK, TOK)
        swapped = pl.ds(((index + SEQS // 2) % SEQS) * TOK, TOK)
        one = grads_ref[pl.ds(index * 2 * TOK, TOK), :]
        two = grads_ref[pl.ds(index * 2 * TOK + TOK, TOK), :]
        query_ref[rows, 0:HD] = one[:, :HD]
        query_ref[rows, HD : 2 * HD] = two[:, :HD]
        total = one[:, HD:].astype(wide) + two[:, HD:].astype(wide)
        lower = jnp.concatenate([total[:, : HD // 2], total[:, HD : HD + HD // 2]], axis=1)
        upper = jnp.concatenate([total[:, HD // 2 : HD], total[:, HD + HD // 2 :]], axis=1)
        mine_ref[rows, :] = jnp.where(first, lower, upper)
        other_ref[swapped, :] = jnp.where(first, upper, lower).astype(low)


def collect(core, grads):
    return pl.pallas_call(
        collect_kernel,
        out_shape=(
            jax.ShapeDtypeStruct((ALL, 2 * HD), low),
            jax.ShapeDtypeStruct((ALL, HD), wide),
            jax.ShapeDtypeStruct((ALL, HD), low),
        ),
        in_specs=[smem, vmem],
        out_specs=(vmem, vmem, vmem),
        compiler_params=params(32),
        cost_estimate=cost(1e6, 4e6),
        name="collect",
    )(core, grads)


def qkv_weights_kernel(place_ref, normed_ref, query_ref, mine_ref, got_ref, *refs):
    parts, (out_ref, grad_ref) = refs[:5], refs[5:]
    grad_ref[:, 0 : 2 * HD] = query_ref[...]
    grad_ref[:, 2 * HD : 3 * HD] = (mine_ref[...] + got_ref[...].astype(wide)).astype(low)
    for index in range(EXPERTS):
        step, side = index // 2, index % 2
        rows = pl.ds(pl.multiple_of(place_ref[index] * 256, 256), 256)
        out_ref[rows, 3 * HD : 3 * HD + 256] = parts[step + 1][side] if step else parts[side][...]
    for index in range(D // ROWS):
        rows = pl.ds(index * ROWS, ROWS)
        out_ref[rows, 0 : 3 * HD] = t_mm(normed_ref[:, rows], grad_ref[...]).astype(low)


def qkv_weights(places, normed, query, mine, got, parts):
    return pl.pallas_call(
        qkv_weights_kernel,
        out_shape=(jax.ShapeDtypeStruct((D, 3 * HD + 256), low), jax.ShapeDtypeStruct((ALL, 3 * HD), low)),
        in_specs=[smem] + [vmem] * 9,
        out_specs=(vmem, vmem),
        compiler_params=params(40),
        cost_estimate=cost(1.6e9, 10e6),
        name="qkv_weights",
    )(places, normed, query, mine, got, *parts)


def finish_kernel(shards_ref, query_ref, key_ref, value_ref, out_ref, gain_ref):
    gain = jnp.zeros((TOK, TOK), wide)
    for source in range(EXPERTS):
        query_ref[:, source * 256 : (source + 1) * 256] = shards_ref[source, :, 0:256].astype(wide)
        out_ref[:, source * 256 : (source + 1) * 256] = shards_ref[source, :, 384:640].astype(wide)
        gain = gain + shards_ref[source, :, 640:768].astype(wide)
    for pair in range(KV):
        one = shards_ref[2 * pair, :, 256:384].astype(wide)
        two = shards_ref[2 * pair + 1, :, 256:384].astype(wide)
        columns = slice(pair * HD, (pair + 1) * HD)
        key_ref[:, columns] = jnp.concatenate([one[:, : HD // 2], two[:, : HD // 2]], axis=1)
        value_ref[:, columns] = jnp.concatenate([one[:, HD // 2 :], two[:, HD // 2 :]], axis=1)
    gain_ref[...] = gain


def finish(shards):
    widths = (H * HD, KV * HD, KV * HD, H * HD, TOK)
    return pl.pallas_call(
        finish_kernel,
        out_shape=tuple(jax.ShapeDtypeStruct((TOK, width), wide) for width in widths),
        in_specs=[vmem],
        out_specs=tuple([vmem] * 5),
        compiler_params=params(32),
        cost_estimate=cost(1e6, 4e6),
        name="finish",
    )(shards)


def finish_dense_kernel(shards_ref, spread_ref, spread_rows_ref, gate_ref, up_ref, down_ref, left, rows_in):
    width = SH_OWN // 2
    for source in range(EXPERTS):
        for part in range(4):
            left[part * TOK : (part + 1) * TOK, source * width : (source + 1) * width] = shards_ref[
                source, :, part * width : (part + 1) * width
            ]
        packed = shards_ref[source, :, 2 * SH_OWN : 3 * SH_OWN].astype(wide)
        rows_in[source * SH_PAD : (source + 1) * SH_PAD, :] = pack_rows(packed)
    for start in range(0, SH // 2, 256):
        count = min(256, SH // 2 - start)
        both = mm(left[...], spread_ref[:, start : start + count])
        for part in range(4):
            target = gate_ref if part < 2 else up_ref
            begin = (part % 2) * (SH // 2) + start
            target[:, begin : begin + count] = both[part * TOK : (part + 1) * TOK]
    down_ref[...] = mm(spread_rows_ref[...], rows_in[...].astype(low))


def finish_dense(shards, spread, spread_rows):
    shapes = [(TOK, SH), (TOK, SH), (SH_ROWS, D)]
    return pl.pallas_call(
        finish_dense_kernel,
        out_shape=tuple(jax.ShapeDtypeStruct(shape, wide) for shape in shapes),
        in_specs=[vmem] * 3,
        out_specs=tuple([vmem] * 3),
        scratch_shapes=[
            pltpu.VMEM((4 * TOK, EXPERTS * SH_OWN // 2), low),
            pltpu.VMEM((EXPERTS * SH_PAD, D), wide),
        ],
        compiler_params=params(40),
        cost_estimate=cost(2.2e9, 12e6),
        name="finish_dense",
    )(shards, spread, spread_rows)


def halves(value):
    upper = value.astype(low)
    return upper, (value - upper.astype(wide)).astype(low)


def silu_parts(gate_value):
    sig = 1.0 / (1.0 + jnp.exp(-gate_value))
    return sig, gate_value * sig


def swiglu_back(sig, act, up_value, grad):
    return (grad * up_value * (sig + act * (1.0 - sig))).astype(low), (grad * act).astype(low)


def pack_rows(block):
    count, width = block.shape[0] // 8, block.shape[1] // 128
    return jnp.concatenate(
        [
            jnp.concatenate(
                [block[8 * i : 8 * i + 8, 128 * j : 128 * j + 128] for i in range(count)], axis=1
            )
            for j in range(width)
        ],
        axis=0,
    )


def slab(buffer, out_ref, sems, step, start):
    target = out_ref.at[pl.ds(step * ROWS, ROWS), pl.ds(start, buffer.shape[2])]
    return pltpu.make_async_copy(buffer.at[step % 2], target, sems.at[step % 2])


def send_slabs(tokens_ref, grad_ref, down_rows, out_ref, buffer, sems, start):
    width = grad_ref.shape[1]
    count = width // 2 // FSDP
    for step in range(D // ROWS):
        slot = step % 2
        if step >= 2:
            slab(buffer, out_ref, sems, step - 2, start).wait()
        buffer[slot, :, 0:width] = t_mm(tokens_ref[:, pl.ds(step * ROWS, ROWS)], grad_ref[...]).astype(low)
        down = down_rows(step)
        for part in range(2):
            packed = pack_rows(down[part * count : (part + 1) * count]).astype(low)
            buffer[slot, part * TOK : (part + 1) * TOK, width:] = packed
        slab(buffer, out_ref, sems, step, start).start()
    for step in (D // ROWS - 2, D // ROWS - 1):
        slab(buffer, out_ref, sems, step, start).wait()


def ffn_kernel(*refs):
    expert_ref, slots_hbm, slots_t_hbm, routes_ref, router_hbm = refs[:5]
    pieces, cot_pieces, pack_ref = refs[5:15], refs[15:25], refs[25]
    grad_mine, grad_other, gates_ref = refs[26:29]
    outs = refs[29:37]
    normed_ref, cot_ref, grad_ref = refs[37:40]
    kept = refs[40:48]
    hidden_s, grad_s, incoming, hidden_e, gated, grad_rows, grad_e, w_down_s = kept
    w_in_s, w_in, w_down, slots_ref, slots_t_ref = refs[48:53]
    raw, gate_parts, grad_in, piece_sems, cot_sems, sems, out_sems = refs[53:]
    base = 3 * SH_OWN
    half_d = D // 2

    def stage_shared(part):
        return pltpu.make_async_copy(
            pack_ref.at[pl.ds(part * half_d, half_d), pl.ds(2 * SH_OWN, SH_OWN)],
            grad_ref.at[:, pl.ds(FF + part * SH_OWN, SH_OWN)],
            sems.at[part],
        )

    def stage_down(part):
        return pltpu.make_async_copy(
            pack_ref.at[pl.ds(part * half_d, half_d), pl.ds(base + 2 * FF, FF)],
            grad_ref.at[:, pl.ds(0, FF)],
            sems.at[2 + part],
        )

    def unpack(target, pair, row, start, width):
        count = 2 * width // FSDP
        both = [
            pack_rows(grad_ref[row + part * TOK : row + (part + 1) * TOK, start : start + width].astype(wide))
            for part in range(2)
        ]
        target[pair * count : (pair + 1) * count, :] = jnp.concatenate(both, axis=0).astype(low)

    copies = [
        pltpu.make_async_copy(router_hbm, w_in_s.at[:, pl.ds(2 * SH_OWN, 128)], sems.at[4]),
        pltpu.make_async_copy(pack_ref.at[:, pl.ds(0, 2 * SH_OWN)], w_in_s.at[:, pl.ds(0, 2 * SH_OWN)], sems.at[5]),
        pltpu.make_async_copy(slots_hbm, slots_ref, sems.at[6]),
        pltpu.make_async_copy(pack_ref.at[:, pl.ds(base, 2 * FF)], w_in, sems.at[7]),
        pltpu.make_async_copy(slots_t_hbm, slots_t_ref, sems.at[8]),
    ]
    stage_shared(0).start()
    stage_shared(1).start()
    copies[0].start()
    copies[1].start()
    piece_copies = load_pieces(pieces, normed_ref, None, piece_sems)
    cot_copies = load_pieces(cot_pieces, cot_ref, None, cot_sems)
    stage_down(0).start()
    for copy in copies[2:]:
        copy.start()

    def send(index):
        copy = pltpu.make_async_copy(kept[index], outs[index], out_sems.at[index])
        copy.start()
        return copy

    expert = expert_ref[0]
    lane = lax.broadcasted_iota(jnp.int32, (ROWS, 128), 1)
    for part in range(2):
        stage_shared(part).wait()
        for pair in range(4):
            unpack(w_down_s, part * 4 + pair, pair * 2 * TOK, FF + part * SH_OWN, SH_OWN)
    for copy in piece_copies + cot_copies + copies[:2]:
        copy.wait()
    stage_down(0).wait()
    for step in range(ALL // ROWS):
        unpack(w_down, step, step * 2 * TOK, 0, FF)
        rows = pl.ds(step * ROWS, ROWS)
        both = mm(normed_ref[rows, :], w_in_s[...])
        sig, act = silu_parts(both[:, :SH_OWN])
        up = both[:, SH_OWN : 2 * SH_OWN]
        hidden_s[rows, :] = (act * up).astype(low)
        grad_hidden = mm_t(cot_ref[rows, :], w_down_s[...])
        grad_gate, grad_up = swiglu_back(sig, act, up, grad_hidden)
        grad_s[rows, 0:SH_OWN] = grad_gate
        grad_s[rows, SH_OWN : 2 * SH_OWN] = grad_up
        logits = both[:, 2 * SH_OWN :]
        first, second = routes_ref[rows, 0:1], routes_ref[rows, 1:2]
        chosen_first = jnp.sum(jnp.where(lane == first + 2, logits, 0.0), axis=1, keepdims=True)
        chosen_second = jnp.sum(jnp.where(lane == second + 2, logits, 0.0), axis=1, keepdims=True)
        gate_first = 1.0 / (1.0 + jnp.exp(chosen_second - chosen_first))
        gate_second = 1.0 / (1.0 + jnp.exp(chosen_first - chosen_second))
        here = jnp.where(first == expert, gate_first, 0.0) + jnp.where(second == expert, gate_second, 0.0)
        upper, lower = halves(here)
        parts = jnp.where(lane == 0, upper.astype(wide), 0.0) + jnp.where(lane == 1, lower.astype(wide), 0.0)
        gate_parts[rows, :] = parts.astype(low)
        if step == 0:
            both_gates = jnp.where(lane == 0, gate_first, 0.0) + jnp.where(lane == 1, gate_second, 0.0)
            gates_ref[...] = both_gates[:TOK]
    stage_down(1).start()
    sent = [send(0), send(1), send(7)]
    copies[2].wait()
    for step in range(D // ROWS):
        columns = pl.ds(step * ROWS, ROWS)
        incoming[:, columns] = mm(slots_ref[...], normed_ref[:, columns]).astype(low)
        grad_rows[:, columns] = mm(slots_ref[...], cot_ref[:, columns]).astype(low)
    slot_parts = mm(slots_ref[...], gate_parts[...])
    slot_gate = slot_parts[:, 0:1] + slot_parts[:, 1:2]
    sent.append(send(2))
    copies[3].wait()
    stage_down(1).wait()
    for step in range(4):
        unpack(w_down, 4 + step, step * 2 * TOK, 0, FF)
    for step in range(2 * FF // ROWS):
        columns = pl.ds(step * ROWS, ROWS)
        raw[:, columns] = mm(incoming[...], w_in[:, columns])
    for start, width in FF_TILES:
        gate, up = raw[:, start : start + width], raw[:, FF + start : FF + start + width]
        hidden_e[:, start : start + width] = (silu_parts(gate)[1] * up).astype(low)
    sent.append(send(3))
    slot_grad = jnp.zeros((SLOTS, 1), wide)
    for step in range(D // ROWS):
        columns = pl.ds(step * ROWS, ROWS)
        rows = mm(hidden_e[...], w_down[:, columns]).astype(low).astype(wide)
        cot = grad_rows[:, columns].astype(wide)
        gated[:, columns] = (rows * slot_gate).astype(low)
        grad_rows[:, columns] = (cot * slot_gate).astype(low)
        slot_grad = slot_grad + jnp.sum(rows * cot, axis=1, keepdims=True)
    sent += [send(4), send(5)]
    for start, width in FF_TILES:
        grad_hidden = mm_t(grad_rows[...], w_down[pl.ds(start, width), :])
        sig, act = silu_parts(raw[:, start : start + width])
        grad_gate, grad_up = swiglu_back(sig, act, raw[:, FF + start : FF + start + width], grad_hidden)
        grad_e[:, start : start + width] = grad_gate
        grad_e[:, FF + start : FF + start + width] = grad_up
    sent.append(send(6))
    for step in range(D // ROWS):
        columns = pl.ds(step * ROWS, ROWS)
        grad_in[:, columns] = mm_t(grad_e[...], w_in[columns, :]).astype(low)
    upper, lower = halves(slot_grad)
    slot_lane = lax.broadcasted_iota(jnp.int32, (SLOTS, 128), 1)
    slot_parts = (
        jnp.where(slot_lane == expert, upper.astype(wide), 0.0)
        + jnp.where(slot_lane == expert + 8, lower.astype(wide), 0.0)
    ).astype(low)
    copies[4].wait()
    half = ALL // 2
    for side, target in ((1, grad_other), (0, grad_mine)):
        for step in range(half // ROWS):
            rows = pl.ds(side * half + step * ROWS, ROWS)
            for tile in range(D // 512):
                columns = pl.ds(tile * 512, 512)
                grad_ref[rows, columns] = (
                    mm_t(grad_s[rows, :], w_in_s[columns, 0 : 2 * SH_OWN])
                    + mm(slots_t_ref[rows, :], grad_in[:, columns])
                ).astype(low)
            grad_ref[rows, D : D + 128] = mm(slots_t_ref[rows, :], slot_parts).astype(low)
        copy = pltpu.make_async_copy(grad_ref.at[pl.ds(side * half, half), :], target, sems.at[9 + side])
        copy.start()
        sent.append(copy)
    for copy in sent:
        copy.wait()


def ffn(expert, slots, slots_t, routes, router, pieces, cot_pieces, pack):
    kept = [(ALL, SH_OWN), (ALL, 2 * SH_OWN), (SLOTS, D), (SLOTS, FF), (SLOTS, D), (SLOTS, D), (SLOTS, 2 * FF)]
    kept.append((SH_OWN, D))
    grads = [(ALL // 2, D + 128)] * 2
    return pl.pallas_call(
        ffn_kernel,
        out_shape=tuple(
            [jax.ShapeDtypeStruct(shape, low) for shape in grads]
            + [jax.ShapeDtypeStruct((TOK, 128), wide)]
            + [jax.ShapeDtypeStruct(shape, low) for shape in kept]
        ),
        in_specs=[smem, anywhere, anywhere, vmem] + [anywhere] * 22,
        out_specs=tuple([anywhere] * 2 + [vmem] + [anywhere] * 8),
        scratch_shapes=[pltpu.VMEM((ALL, D), low), pltpu.VMEM((ALL, D), low), pltpu.VMEM((ALL, D + 128), low)]
        + [pltpu.VMEM(shape, low) for shape in kept]
        + [
            pltpu.VMEM((D, 2 * SH_OWN + 128), low),
            pltpu.VMEM((D, 2 * FF), low),
            pltpu.VMEM((FF, D), low),
            pltpu.VMEM((SLOTS, ALL), low),
            pltpu.VMEM((ALL, SLOTS), low),
            pltpu.VMEM((SLOTS, 2 * FF), wide),
            pltpu.VMEM((ALL, 128), low),
            pltpu.VMEM((SLOTS, D), low),
            pltpu.SemaphoreType.DMA((20,)),
            pltpu.SemaphoreType.DMA((20,)),
            pltpu.SemaphoreType.DMA((11,)),
            pltpu.SemaphoreType.DMA((8,)),
        ],
        compiler_params=params(60),
        cost_estimate=cost(27e9, 50e6, 1e6),
        name="ffn",
    )(expert, slots, slots_t, routes, router, *pieces, *cot_pieces, pack)


def shared_weights_kernel(*refs):
    pieces, cot_pieces, hidden_ref, grad_ref = refs[:10], refs[10:20], refs[20], refs[21]
    out_ref, normed_ref, cot_ref, buffer, down, piece_sems, cot_sems, sems = refs[22:]
    cot_copies = load_pieces(cot_pieces, cot_ref, None, cot_sems)
    copies = load_pieces(pieces, normed_ref, None, piece_sems)
    for copy in cot_copies:
        copy.wait()
    for tile in range(D // ROWS):
        part = pl.ds(tile * ROWS, ROWS)
        down[:, part] = t_mm(hidden_ref[...], cot_ref[:, part])
    for copy in copies:
        copy.wait()
    count = 2 * SH_PAD
    send_slabs(
        normed_ref, grad_ref, lambda step: down[step * count : (step + 1) * count, :], out_ref, buffer, sems, 0
    )


def shared_weights(pieces, cot_pieces, hidden, grad):
    return pl.pallas_call(
        shared_weights_kernel,
        out_shape=jax.ShapeDtypeStruct((D, 3 * SH_OWN + 3 * FF), low),
        in_specs=[anywhere] * 20 + [vmem] * 2,
        out_specs=anywhere,
        scratch_shapes=[
            pltpu.VMEM((ALL, D), low),
            pltpu.VMEM((ALL, D), low),
            pltpu.VMEM((2, ROWS, 3 * SH_OWN), low),
            pltpu.VMEM((SH_OWN, D), wide),
            pltpu.SemaphoreType.DMA((20,)),
            pltpu.SemaphoreType.DMA((20,)),
            pltpu.SemaphoreType.DMA((2,)),
        ],
        compiler_params=params(60),
        cost_estimate=cost(5e9, 18e6),
        name="shared_weights",
    )(*pieces, *cot_pieces, hidden, grad)


def expert_weights_kernel(_, incoming_ref, hidden_ref, grad_rows_ref, grad_ref, out_ref, buffer, sems):
    def down_rows(step):
        count = 2 * FF // FSDP
        return t_mm(hidden_ref[:, step * count : (step + 1) * count], grad_rows_ref[...])

    send_slabs(incoming_ref, grad_ref, down_rows, out_ref, buffer, sems, 3 * SH_OWN)


def expert_weights(*operands):
    return pl.pallas_call(
        expert_weights_kernel,
        out_shape=jax.ShapeDtypeStruct((D, 3 * SH_OWN + 3 * FF), low),
        in_specs=[anywhere] + [vmem] * 4,
        out_specs=anywhere,
        scratch_shapes=[pltpu.VMEM((2, ROWS, 3 * FF), low), pltpu.SemaphoreType.DMA((2,))],
        input_output_aliases={0: 0},
        compiler_params=params(48),
        cost_estimate=cost(6e9, 24e6),
        name="expert_weights",
    )(*operands)


def out_rows_kernel(place_ref, *refs):
    parts, out_ref = refs[:5], refs[5]
    for index in range(EXPERTS):
        step, side = index // 2, index % 2
        columns = pl.ds(pl.multiple_of(place_ref[index] * 256, 256), 256)
        out_ref[:, columns] = parts[step + 1][side] if step else parts[side][...]


def out_rows(places, parts):
    return pl.pallas_call(
        out_rows_kernel,
        out_shape=jax.ShapeDtypeStruct((256, D), low),
        in_specs=[smem] + [vmem] * 5,
        out_specs=vmem,
        compiler_params=params(32),
        cost_estimate=cost(0, 2e6),
        name="out_rows",
    )(places, *parts)


def back_two_kernel(
    own_ref, first_ref, second_ref, middle_ref, cot_ref, gains_ref, gates_ref, routes_ref, block_ref, grad_ref, total_ref, logits_ref
):
    total = own_ref[...] + first_ref[...].astype(wide) + second_ref[...].astype(wide)
    lane = lax.broadcasted_iota(jnp.int32, (TOK, 128), 1)
    extra = total[:, D:]
    first, second = routes_ref[:, 0:1], routes_ref[:, 1:2]

    def taken(route):
        return jnp.sum(jnp.where((lane == route) | (lane == route + 8), extra, 0.0), axis=1, keepdims=True)

    gate_first, gate_second = gates_ref[:, 0:1], gates_ref[:, 1:2]
    taken_first, taken_second = taken(first), taken(second)
    inner = gate_first * taken_first + gate_second * taken_second
    chosen_first, chosen_second = gate_first * (taken_first - inner), gate_second * (taken_second - inner)
    logits = jnp.where(lane == first, chosen_first, 0.0) + jnp.where(lane == second, chosen_second, 0.0)
    grad = total[:, :D]
    for index in range(EXPERTS):
        grad = grad + logits[:, index : index + 1] * gains_ref[2 + index : 3 + index, :]
    middle = middle_ref[...]
    factor = lax.rsqrt(jnp.mean(middle * middle, axis=-1, keepdims=True) + eps_norm)
    scaled = grad * gains_ref[1:2, :]
    mean = jnp.mean(scaled * middle, axis=-1, keepdims=True)
    result = cot_ref[...].astype(wide) + factor * scaled - middle * (factor * factor * factor * mean)
    grad_ref[...] = result
    block_ref[...] = result.astype(low)
    total_ref[...] = grad
    logits_ref[...] = logits


def back_two(*operands):
    return pl.pallas_call(
        back_two_kernel,
        out_shape=(
            jax.ShapeDtypeStruct((TOK, D), low),
            jax.ShapeDtypeStruct((TOK, D), wide),
            jax.ShapeDtypeStruct((TOK, D), wide),
            jax.ShapeDtypeStruct((TOK, 128), wide),
        ),
        in_specs=[vmem] * 8,
        out_specs=(vmem, vmem, vmem, vmem),
        compiler_params=params(32),
        cost_estimate=cost(1e7, 6e6),
        name="back_two",
    )(*operands)


def small_rows_kernel(total_ref, logits_ref, middle_ref, gains_ref, out_ref):
    middle = middle_ref[...]
    factor = lax.rsqrt(jnp.mean(middle * middle, axis=-1, keepdims=True) + eps_norm)
    gain_upper, gain_lower = halves(jnp.sum(total_ref[...] * middle * factor, axis=0, keepdims=True))
    normed = (middle * factor * gains_ref[1:2, :]).astype(low)
    logit_upper, logit_lower = halves(logits_ref[...].T[0:EXPERTS, :])
    router = mm(logit_upper, normed) + mm(logit_lower, normed)
    small = [gain_upper.astype(wide), gain_lower.astype(wide), router, jnp.zeros((6, D), wide)]
    out_ref[...] = jnp.concatenate(small, axis=0).astype(low)


def small_rows(*operands):
    return pl.pallas_call(
        small_rows_kernel,
        out_shape=jax.ShapeDtypeStruct((16, D), low),
        in_specs=[vmem] * 4,
        out_specs=vmem,
        compiler_params=params(32),
        cost_estimate=cost(1e7, 3e6),
        name="small_rows",
    )(*operands)


def norm_factor(values):
    return lax.rsqrt(jnp.mean(values * values, axis=-1, keepdims=True) + eps_norm)


def norm_back(values, factor, gain, grad):
    scaled = grad * gain
    inner = jnp.mean(scaled * values, axis=-1, keepdims=True)
    return factor * scaled - values * (factor * factor * factor * inner)


def per_device(
    hidden_in,
    cotangent,
    segments,
    routes,
    attn_gain,
    w_query,
    w_key,
    w_value,
    w_out,
    ffn_gain,
    w_router,
    shared_gate,
    shared_up,
    shared_down,
    expert_gate,
    expert_up,
    expert_down,
):
    expert = lax.axis_index("expert")
    z, core = expert // 2, expert % 2
    place = lax.axis_index("fsdp")

    misc = jnp.concatenate(
        [attn_gain[:, None], ffn_gain[:, None], w_router, jnp.zeros((TOK, 118), low)], axis=1
    )
    attn_pack = jnp.concatenate(
        [
            lax.dynamic_slice_in_dim(w_query, 256 * expert, 256, 1),
            lax.dynamic_slice_in_dim(w_key, HD * z, HD, 1),
            lax.dynamic_slice_in_dim(w_value, HD * z, HD, 1),
            lax.dynamic_slice_in_dim(w_out, 256 * expert, 256, 1),
            misc,
        ],
        axis=1,
    )
    attn_all = lax.all_gather(attn_pack, "fsdp", axis=0, tiled=True)
    half_in, half_out = SH // 2, SH_OWN // 2
    sel_column = jnp.arange(half_out)
    picked = SH_ROWS * (sel_column // SH_PAD) + SH_PART * expert + sel_column % SH_PAD
    picked = jnp.where(sel_column % SH_PAD < SH_PART, picked, -1)
    select = (jnp.arange(half_in)[:, None] == picked[None, :]).astype(low)
    own_shared = mm(
        jnp.concatenate(
            [shared_gate[:, :half_in], shared_gate[:, half_in:], shared_up[:, :half_in], shared_up[:, half_in:]],
            axis=0,
        ),
        select,
    ).astype(low)
    own_down = jnp.pad(
        lax.dynamic_slice_in_dim(shared_down, SH_PART * expert, SH_PART, 0),
        ((0, SH_PAD - SH_PART), (0, 0)),
    )
    ffn_pack = jnp.concatenate(
        [
            own_shared[:TOK],
            own_shared[TOK : 2 * TOK],
            own_shared[2 * TOK : 3 * TOK],
            own_shared[3 * TOK :],
            pack_tiles(own_down),
            expert_gate[:, 0],
            expert_up[:, 0],
            pack_tiles(expert_down[:, 0]),
        ],
        axis=1,
    )
    ffn_all = lax.all_gather(ffn_pack, "fsdp", axis=0, tiled=True)

    ids = jnp.concatenate(
        [
            segments.astype(low),
            jnp.pad(routes[0].reshape(1, TOK * TOPK), ((0, 0), (0, LENGTH - TOK * TOPK))).astype(low),
            jnp.zeros((14, LENGTH), low),
        ],
        axis=0,
    )
    hidden_pieces = gather_pieces(jnp.concatenate([hidden_in[0], ids], axis=0))
    cot_block, *hidden_pieces = together(cotangent[0], *hidden_pieces)
    cot_pieces = gather_pieces(cot_block)

    inverse_freq = rope_base ** (-jnp.arange(HD // 2, dtype=wide) * 2.0 / HD)
    angles = jnp.arange(LENGTH).astype(wide)[:, None] * inverse_freq[None, :]
    cosine, sine = jnp.cos(angles), jnp.sin(angles)
    cos_all = jnp.concatenate([cosine, cosine], axis=1)
    sin_back = jnp.concatenate([sine, -sine], axis=1)
    cos_own = lax.dynamic_slice_in_dim(cos_all, place * TOK, TOK, 0)
    sin_own = -lax.dynamic_slice_in_dim(sin_back, place * TOK, TOK, 0)
    cos_two, sin_two = jnp.concatenate([cos_own, cos_own]), jnp.concatenate([sin_own, sin_own])
    put_row = jnp.arange(SH_PAD * EXPERTS * FSDP // 2)
    source, within = put_row // half_out, put_row % half_out
    target = SH_ROWS * (within // SH_PAD) + SH_PART * source + within % SH_PAD
    target = jnp.where(within % SH_PAD < SH_PART, target, -1)
    spread = (target[:, None] == jnp.arange(half_in)[None, :]).astype(low)
    put_row = jnp.arange(EXPERTS * SH_PAD)
    target = SH_PART * (put_row // SH_PAD) + put_row % SH_PAD
    target = jnp.where(put_row % SH_PAD < SH_PART, target, -1)
    spread_rows = (jnp.arange(SH_ROWS)[:, None] == target[None, :]).astype(low)
    attn_all, cos_two, sin_two, cos_all, sin_back, spread, spread_rows = together(
        attn_all, cos_two, sin_two, cos_all, sin_back, spread, spread_rows
    )
    normed_one, sent, factor_one, gains, ids_all = project(hidden_pieces, attn_all, cos_two, sin_two)
    qkv = lax.all_to_all(sent, "fsdp", split_axis=0, concat_axis=0, tiled=True)

    ids_all = ids_all.reshape(SEQS, 16, D)
    seg_row = lax.dynamic_slice_in_dim(ids_all[:, 0].astype(wide), place // 2, 1, 0)
    seg_blocks = jnp.pad(seg_row.reshape(FSDP, TOK), ((0, TOK - FSDP), (0, 0)))
    route_all = ids_all[:, 1, : TOK * TOPK].astype(jnp.int32).reshape(ALL, TOPK)
    hit = jnp.any(route_all == expert, axis=1).astype(wide)
    order = jnp.arange(ALL)
    rank = mm(hit.astype(low)[None, :], (order[:, None] < order[None, :]).astype(low))
    slot_bool = (rank.astype(jnp.int32) == jnp.arange(SLOTS)[:, None]) & (hit > 0.5)[None, :]
    slots = slot_bool.astype(low)
    slots_t = slot_bool.T.astype(low)
    out_columns = attn_all[:, 512:768].reshape(EXPERTS, 256, 256)
    owners = jnp.stack([relative_owner(expert, block) for block in range(EXPERTS)])
    out_blocks = [lax.dynamic_index_in_dim(out_columns, owners[block], 0) for block in range(EXPERTS)]
    out_mine, out_other = jnp.concatenate(out_blocks[:4]), jnp.concatenate(out_blocks[4:])
    out_mine, out_other, _ = together(out_mine, out_other, sent)
    w_out_own = out_rows(source_owners(expert), exchange(out_mine, out_other))
    router = attn_all[:, 768:896]
    is_first = core == 0
    kv_weight = attn_all[:, 256:512].reshape(D, 2, 2, HD // 2)
    kv_weight = jnp.where(is_first, kv_weight[:, :, 0], kv_weight[:, :, 1]).reshape(D, HD)
    qkv_weight = jnp.concatenate([attn_all[:, :256], kv_weight], axis=1)
    route_own = route_all[:TOK]
    qkv, seg_row, seg_blocks, route_all, slots, slots_t, w_out_own, router, qkv_weight, route_own, *cot_pieces = together(
        qkv, seg_row, seg_blocks, route_all, slots, slots_t, w_out_own, router, qkv_weight, route_own, *cot_pieces
    )
    mixed_head, log_total = attend(qkv, seg_row, seg_blocks)
    mixed = (
        lax.all_to_all(mixed_head, "fsdp", split_axis=0, concat_axis=0, tiled=True)
        .reshape(SEQS, 2, TOK, HD)
        .transpose(0, 2, 1, 3)
        .reshape(ALL, 2 * HD)
    )
    own_hidden = hidden_in[0].astype(wide)
    half = ALL // 2
    middle = own_hidden + scatter_rows(
        mm(mixed[:half], w_out_own).astype(low), mm(mixed[half:], w_out_own).astype(low)
    )
    factor_two = norm_factor(middle)
    gain_one, gain_two = gains[0:1], gains[1:2]
    normed_block = (middle * factor_two * gain_two).astype(low)

    base = 3 * SH_OWN
    normed_pieces = gather_pieces(normed_block)
    (
        grad_mine,
        grad_other,
        gates,
        hidden_shared,
        grad_shared,
        incoming,
        hidden_expert,
        gated_rows,
        grad_rows,
        grad_expert,
        shared_down_w,
    ) = ffn(expert[None], slots, slots_t, route_all, router, normed_pieces, cot_pieces, ffn_all)
    received = swap_core(grad_other)
    ffn_grads = shared_weights(normed_pieces, cot_pieces, hidden_shared, grad_shared)
    received, ffn_grads = together(received, ffn_grads)
    own_grad, to_above, to_below = scatter_start(grad_mine, received)
    to_above, to_below, ffn_grads = together(to_above, to_below, ffn_grads)
    from_below, from_above = move_z(to_above, 1), move_z(to_below, -1)
    ffn_grads = expert_weights(ffn_grads, incoming, hidden_expert, grad_rows, grad_expert)
    from_below, from_above, ffn_grads = together(from_below, from_above, ffn_grads)
    ffn_sums = lax.psum_scatter(ffn_grads, "fsdp", scatter_dimension=0, tiled=True)
    back_block, grad_middle, grad_two, grad_logits = back_two(
        own_grad, from_below, from_above, middle, cotangent[0], gains, gates, route_own
    )
    back_block, hidden_shared, gated_rows = together(back_block, hidden_shared, gated_rows)
    below, above = first_pieces(back_block)
    small = small_rows(grad_two, grad_logits, middle, gains)
    result_other = (mm(hidden_shared[half:], shared_down_w) + mm(slots_t[half:], gated_rows)).astype(low)
    result_mine = (mm(hidden_shared[:half], shared_down_w) + mm(slots_t[:half], gated_rows)).astype(low)
    below, above, result_other, result_mine, small = together(below, above, result_other, result_mine, small)
    back_pieces = other_pieces(back_block, below, above)

    sent_back, out_mine, out_other = mix_back(owners, back_pieces, w_out_own, mixed, small)
    grad_head = lax.all_to_all(sent_back, "fsdp", split_axis=0, concat_axis=0, tiled=True)
    grads_head, small_sums = attend_back(qkv, grad_head, log_total, seg_row, seg_blocks, cos_all, sin_back)
    grads_qkv = lax.all_to_all(grads_head, "fsdp", split_axis=0, concat_axis=0, tiled=True)
    result_other, result_mine, _ = together(result_other, result_mine, sent_back)
    result_got = swap_core(result_other)
    result_got, out_mine, out_other = together(result_got, out_mine, out_other)
    out_parts = exchange(out_mine, out_other)
    result_own, to_above, to_below = scatter_start(result_mine, result_got)
    result_own = scatter_end(result_own, move_z(to_above, 1), move_z(to_below, -1))
    layer_out = (middle + result_own).astype(low)
    grads_qkv, layer_out, *out_parts = together(grads_qkv, layer_out, *out_parts)

    grad_query, kv_mine, kv_other = collect(core[None], grads_qkv)
    attn_grads, grad_qkv = qkv_weights(
        source_owners(expert), normed_one, grad_query, kv_mine, swap_core(kv_other), out_parts
    )
    attn_parts = lax.all_to_all(attn_grads, "fsdp", split_axis=0, concat_axis=0, tiled=True)

    grad_normed_other = mm_t(grad_qkv[half:], qkv_weight).astype(low)
    grad_normed_mine = mm_t(grad_qkv[:half], qkv_weight).astype(low)
    own_grad_one, to_above, to_below = scatter_start(grad_normed_mine, swap_core(grad_normed_other))
    attn_parts, to_above, to_below = together(attn_parts, to_above, to_below)
    own_grad_one = scatter_end(own_grad_one, move_z(to_above, 1), move_z(to_below, -1))
    grad_input = (grad_middle + norm_back(own_hidden, factor_one[:TOK], gain_one, own_grad_one)).astype(low)
    attn_sums = jnp.sum(attn_parts.reshape(FSDP, TOK, 3 * HD + 256).astype(wide), axis=0)

    own_weight = lax.dynamic_slice_in_dim(qkv_weight, place * TOK, TOK, 0)
    gain_part = jnp.sum(attn_sums[:, : 3 * HD] * own_weight.astype(wide), axis=1, keepdims=True)
    gain_upper, gain_lower = halves(gain_part / attn_gain.astype(wide)[:, None])
    small = [gain_upper, gain_lower, small_sums.T.astype(low), jnp.zeros((TOK, 110), low)]
    shards = jnp.concatenate([attn_sums.astype(low), *small], axis=1)

    ffn_sums, _ = together(ffn_sums, to_above)
    shared_shards = lax.all_gather(ffn_sums[:, :base], "expert", axis=0)
    shared_shards, shards = together(shared_shards, shards)
    attn_shards = lax.all_gather(shards, "expert", axis=0)
    grad_shared_gate, grad_shared_up, grad_shared_down = finish_dense(shared_shards, spread, spread_rows)
    grad_w_query, grad_w_key, grad_w_value, grad_w_out, small = finish(attn_shards)
    grad_expert_gate = ffn_sums[:, base : base + FF].astype(wide)[:, None]
    grad_expert_up = ffn_sums[:, base + FF : base + 2 * FF].astype(wide)[:, None]
    grad_expert_down = unpack_tiles(ffn_sums[:, base + 2 * FF :], 1).astype(wide)[:, None]
    return (
        layer_out[None],
        grad_input[None],
        small[:, 0] + small[:, 1],
        grad_w_query,
        grad_w_key,
        grad_w_value,
        grad_w_out,
        small[:, 2] + small[:, 3],
        small[:, 4 : 4 + EXPERTS],
        grad_shared_gate,
        grad_shared_up,
        grad_shared_down,
        grad_expert_gate,
        grad_expert_up,
        grad_expert_down,
    )


def solution(mesh):
    in_specs = (
        P("expert", "fsdp", None),
        P("expert", "fsdp", None),
        P("expert", None),
        P("expert", "fsdp", None),
        P("fsdp"),
        P("fsdp", None),
        P("fsdp", None),
        P("fsdp", None),
        P("fsdp", None),
        P("fsdp"),
        P("fsdp", None),
        P("fsdp", None),
        P("fsdp", None),
        P("fsdp", None),
        P("fsdp", "expert", None),
        P("fsdp", "expert", None),
        P("fsdp", "expert", None),
    )
    out_specs = (
        P("expert", "fsdp", None),
        P("expert", "fsdp", None),
        P("fsdp"),
        P("fsdp", None),
        P("fsdp", None),
        P("fsdp", None),
        P("fsdp", None),
        P("fsdp"),
        P("fsdp", None),
        P("fsdp", None),
        P("fsdp", None),
        P("fsdp", None),
        P("fsdp", "expert", None),
        P("fsdp", "expert", None),
        P("fsdp", "expert", None),
    )
    return jax.shard_map(
        per_device, mesh=mesh, in_specs=in_specs, out_specs=out_specs, check_vma=False
    )
```

```python
import jax
import jax.numpy as jnp
from jax import lax
from jax.experimental import pallas as pl
from jax.experimental.pallas import tpu as pltpu
from jax.sharding import PartitionSpec as P

D = 2048
H = 16
KV = 4
HD = 128
FF = 1408
SH = 2816
TOPK = 2
TOK = 128
LENGTH = 2048
SEQS = 8
EXPERTS = 8
FSDP = 16
ALL = SEQS * TOK
CAP = 42
SLOTS = SEQS * CAP
SH_ROWS = SH // FSDP
SH_PART = SH_ROWS // EXPERTS
SH_PAD = 24
SH_OWN = FSDP * SH_PAD
QBLOCK = 256

eps_norm = 1e-06
rope_base = 600000.0
masked_fill = -1e30
low = jnp.bfloat16
wide = jnp.float32


def shift_pairs(step):
    return [(z * 2 + c, ((z + step) % 4) * 2 + c) for z in range(4) for c in range(2)]


core_pairs = [(z * 2 + c, z * 2 + 1 - c) for z in range(4) for c in range(2)]


def move_z(block, step):
    return lax.ppermute(block, "expert", shift_pairs(step))


def swap_core(block):
    return lax.ppermute(block, "expert", core_pairs)


def together(*values):
    return lax.optimization_barrier(values)


TOP = TOK // 2


def first_pieces(block):
    return move_z(block, 1), move_z(block, -1)


def other_pieces(block, below, above):
    upper, lower = move_z(below[:TOP], 1), move_z(above[TOP:], -1)
    mine = [block, above, upper, lower, below]
    return mine + [swap_core(piece) for piece in mine]


def gather_pieces(block):
    return other_pieces(block, *first_pieces(block))


PIECES = [(4 * side + block, start) for side in (0, 1) for block, start in ((0, 0), (1, 0), (2, 0), (2, TOP), (3, 0))]


def load_pieces(refs, rows_ref, extra_ref, sems):
    copies = []
    for index, (ref, (block, start)) in enumerate(zip(refs, PIECES)):
        count = min(ref.shape[0], TOK - start)
        copies.append(
            pltpu.make_async_copy(
                ref.at[pl.ds(0, count), :], rows_ref.at[pl.ds(block * TOK + start, count), :], sems.at[2 * index]
            )
        )
        if extra_ref is not None and ref.shape[0] > count:
            copies.append(
                pltpu.make_async_copy(
                    ref.at[pl.ds(count, 16), :], extra_ref.at[pl.ds(block * 16, 16), :], sems.at[2 * index + 1]
                )
            )
    for copy in copies:
        copy.start()
    return copies


def scatter_start(mine, received):
    chip = mine.reshape(4, TOK, -1).astype(wide) + received.reshape(4, TOK, -1).astype(wide)
    from_below = move_z(chip[2, :TOP].astype(low), 1)
    from_above = move_z(chip[2, TOP:].astype(low), -1)
    to_above = jnp.concatenate([chip[1, :TOP] + from_below.astype(wide), chip[1, TOP:]], axis=0)
    to_below = jnp.concatenate([chip[3, :TOP], chip[3, TOP:] + from_above.astype(wide)], axis=0)
    return chip[0], to_above.astype(low), to_below.astype(low)


def scatter_end(own, first, second):
    return own + first.astype(wide) + second.astype(wide)


def scatter_rows(mine, other):
    own, to_above, to_below = scatter_start(mine, swap_core(other))
    return scatter_end(own, move_z(to_above, 1), move_z(to_below, -1))


def exchange(mine, other):
    got = swap_core(other)
    chip = jnp.stack([mine[1:], got[1:]], axis=1)
    return mine[0], got[0], *[move_z(chip[step - 1], step) for step in (1, 2, 3)]


def source_owners(expert):
    return jnp.stack([((expert // 2 - index // 2) % 4) * 2 + ((expert % 2) ^ (index % 2)) for index in range(EXPERTS)])


def relative_owner(expert, block):
    return ((expert // 2 + block % 4) % 4) * 2 + ((expert % 2) ^ (block // 4))


def pack_tiles(block):
    rows, columns = block.shape[0] // 8, block.shape[1] // 128
    tiles = block.reshape(rows, 8, columns, 128).transpose(2, 1, 0, 3)
    return tiles.reshape(columns * 8, rows * 128)


def unpack_tiles(block, count):
    rows, columns = block.shape[1] // 128, block.shape[0] // (8 * count)
    tiles = block.reshape(count, columns, 8, rows, 128).transpose(0, 3, 2, 1, 4)
    return tiles.reshape(count * rows * 8, columns * 128)


def product(left, right, contract):
    return lax.dot_general(left, right, (contract, ((), ())), preferred_element_type=wide)


def mm(left, right):
    return product(left, right, ((1,), (0,)))


def mm_t(left, right):
    return product(left, right, ((1,), (1,)))


def t_mm(left, right):
    return product(left, right, ((0,), (0,)))


def segment_columns(seg_blocks_ref):
    return seg_blocks_ref[...].T


def block_scores(qkv_ref, seg_row_ref, columns, start, reach):
    query = qkv_ref[pl.ds(start, QBLOCK), 0:HD]
    key = qkv_ref[pl.ds(0, reach), HD : 2 * HD]
    scores = mm_t(query, key) * HD ** (-0.5)
    query_pos = start + lax.broadcasted_iota(jnp.int32, (QBLOCK, reach), 0)
    key_pos = lax.broadcasted_iota(jnp.int32, (QBLOCK, reach), 1)
    block = start // TOK
    column = jnp.concatenate([columns[:, block : block + 1], columns[:, block + 1 : block + 2]], axis=0)
    same = column == seg_row_ref[:, pl.ds(0, reach)]
    return jnp.where(same & (query_pos >= key_pos), scores, masked_fill)


def attend_kernel(qkv_ref, seg_row_ref, seg_blocks_ref, mixed_ref, total_ref):
    columns = segment_columns(seg_blocks_ref)
    for block in range(LENGTH // QBLOCK):
        start, reach = block * QBLOCK, (block + 1) * QBLOCK
        scores = block_scores(qkv_ref, seg_row_ref, columns, start, reach)
        largest = jnp.max(scores, axis=-1, keepdims=True)
        exponent = jnp.exp(scores - largest)
        totals = jnp.sum(exponent, axis=-1, keepdims=True)
        probs_low = (exponent * (1.0 / totals)).astype(low)
        value = qkv_ref[pl.ds(0, reach), 2 * HD : 3 * HD]
        mixed_ref[pl.ds(start, QBLOCK), :] = mm(probs_low, value).astype(low)
        total_ref[pl.ds(start, QBLOCK), :] = largest + jnp.log(totals)


def attend_back_kernel(
    qkv_ref, grad_ref, total_ref, seg_row_ref, seg_blocks_ref, cos_ref, sin_ref, out_ref, small_ref, key_acc, value_acc
):
    columns = segment_columns(seg_blocks_ref)
    key_acc[...] = jnp.zeros_like(key_acc)
    value_acc[...] = jnp.zeros_like(value_acc)

    def turn_back(value, rows):
        return value * cos_ref[rows, :] + pltpu.roll(value, HD // 2, 1) * sin_ref[rows, :]

    for block in range(LENGTH // QBLOCK):
        start, reach = block * QBLOCK, (block + 1) * QBLOCK
        rows, span = pl.ds(start, QBLOCK), pl.ds(0, reach)
        scores = block_scores(qkv_ref, seg_row_ref, columns, start, reach)
        probs = jnp.exp(scores - total_ref[rows, :])
        tall = [pl.ds((start // TOK + part) * TALL, TOK) for part in range(QBLOCK // TOK)]
        grad = jnp.concatenate([grad_ref[part, :] for part in tall], axis=0)
        grad_probs = mm_t(grad, qkv_ref[span, 2 * HD : 3 * HD])
        inner = jnp.sum(probs * grad_probs, axis=-1, keepdims=True)
        grad_scores = (probs * (grad_probs - inner)).astype(low)
        scale = HD ** (-0.5)
        grad_query = mm(grad_scores, qkv_ref[span, HD : 2 * HD]) * scale
        out_ref[rows, 0:HD] = turn_back(grad_query, rows).astype(low)
        key_acc[span, :] += t_mm(grad_scores, qkv_ref[rows, 0:HD]) * scale
        value_acc[span, :] += t_mm(probs.astype(low), grad)
    for block in range(LENGTH // QBLOCK):
        rows = pl.ds(block * QBLOCK, QBLOCK)
        out_ref[rows, HD : 2 * HD] = turn_back(key_acc[rows, :], rows).astype(low)
        out_ref[rows, 2 * HD : 3 * HD] = value_acc[rows, :].astype(low)
    small = grad_ref[pl.ds(TOK, 16), :].astype(wide)
    for index in range(1, FSDP):
        small = small + grad_ref[pl.ds(index * TALL + TOK, 16), :].astype(wide)
    small_ref[...] = small


vmem = pl.BlockSpec(memory_space=pltpu.VMEM)
smem = pl.BlockSpec(memory_space=pltpu.SMEM)
anywhere = pl.BlockSpec(memory_space=pl.ANY)
kernel_params = pltpu.CompilerParams(vmem_limit_bytes=48 * 1024 * 1024)


def attend(qkv, seg_row, seg_blocks):
    return pl.pallas_call(
        attend_kernel,
        out_shape=(
            jax.ShapeDtypeStruct((LENGTH, HD), low),
            jax.ShapeDtypeStruct((LENGTH, 1), wide),
        ),
        in_specs=[vmem] * 3,
        out_specs=(vmem, vmem),
        compiler_params=kernel_params,
        cost_estimate=pl.CostEstimate(
            flops=2 * LENGTH * LENGTH * HD, bytes_accessed=4 * LENGTH * HD * 2, transcendentals=LENGTH * LENGTH // 2
        ),
        name="attend",
    )(qkv, seg_row, seg_blocks)


def attend_back(qkv, grad, total, seg_row, seg_blocks, cos_all, sin_all):
    return pl.pallas_call(
        attend_back_kernel,
        out_shape=(jax.ShapeDtypeStruct((LENGTH, 3 * HD), low), jax.ShapeDtypeStruct((16, TOK), wide)),
        in_specs=[vmem] * 7,
        out_specs=(vmem, vmem),
        scratch_shapes=[pltpu.VMEM((LENGTH, HD), wide), pltpu.VMEM((LENGTH, HD), wide)],
        compiler_params=kernel_params,
        cost_estimate=pl.CostEstimate(
            flops=5 * LENGTH * LENGTH * HD, bytes_accessed=8 * LENGTH * HD * 2, transcendentals=LENGTH * LENGTH // 2
        ),
        name="attend_back",
    )(qkv, grad, total, seg_row, seg_blocks, cos_all, sin_all)


ROWS = 256
FF_TILES = [(start, min(256, FF - start)) for start in range(0, FF, 256)]


def params(mebibytes):
    return pltpu.CompilerParams(vmem_limit_bytes=mebibytes * 1024 * 1024)


def cost(flops, moved, special=0):
    return pl.CostEstimate(flops=int(flops), bytes_accessed=int(moved), transcendentals=int(special))


def project_kernel(*refs):
    pieces, (attn_ref, cos_ref, sin_ref) = refs[:10], refs[10:13]
    normed_ref, sent_ref, factor_ref, gains_ref, ids_ref, hidden, sems = refs[13:]
    copies = load_pieces(pieces, hidden, ids_ref, sems)
    pick = lax.broadcasted_iota(jnp.int32, (16, TOK), 0) == lax.broadcasted_iota(jnp.int32, (16, TOK), 1)
    gains_ref[...] = mm_t(pick.astype(wide).astype(low), attn_ref[:, 768:896])
    for copy in copies:
        copy.wait()
    gain = gains_ref[0:1, :]

    @pl.loop(0, ALL // ROWS)
    def step(index):
        rows = pl.ds(index * ROWS, ROWS)
        values = hidden[rows, :].astype(wide)
        factor = lax.rsqrt(jnp.mean(values * values, axis=-1, keepdims=True) + eps_norm)
        factor_ref[rows, :] = factor
        normed = (values * factor * gain).astype(low)
        normed_ref[rows, :] = normed
        raw = mm(normed, attn_ref[:, 0:512])

        def turn(value):
            return (value * cos_ref[...] + pltpu.roll(value, HD // 2, 1) * sin_ref[...]).astype(low)

        key = turn(raw[:, 2 * HD : 3 * HD])
        value = raw[:, 3 * HD :].astype(low)
        for head in range(2):
            query = turn(raw[:, head * HD : (head + 1) * HD])
            for part in range(2):
                place = pl.ds(index * 4 * TOK + (2 * part + head) * TOK, TOK)
                within = slice(part * TOK, (part + 1) * TOK)
                sent_ref[place, 0:HD] = query[within]
                sent_ref[place, HD : 2 * HD] = key[within]
                sent_ref[place, 2 * HD : 3 * HD] = value[within]


def project(pieces, attn_all, cos_two, sin_two):
    return pl.pallas_call(
        project_kernel,
        out_shape=(
            jax.ShapeDtypeStruct((ALL, D), low),
            jax.ShapeDtypeStruct((LENGTH, 3 * HD), low),
            jax.ShapeDtypeStruct((ALL, 1), wide),
            jax.ShapeDtypeStruct((16, D), wide),
            jax.ShapeDtypeStruct((SEQS * 16, D), low),
        ),
        in_specs=[anywhere] * 10 + [vmem] * 3,
        out_specs=tuple([vmem] * 5),
        scratch_shapes=[pltpu.VMEM((ALL, D), low), pltpu.SemaphoreType.DMA((20,))],
        compiler_params=params(40),
        cost_estimate=cost(2.2e9, 16e6),
        name="project",
    )(*pieces, attn_all, cos_two, sin_two)


TALL = TOK + 16


def mix_back_kernel(place_ref, *refs):
    pieces, weight_ref, mixed_ref, small_ref = refs[:10], refs[10], refs[11], refs[12]
    sent_ref, mine_ref, other_ref, grad_ref, sems = refs[13:]
    for index in range(FSDP):
        sent_ref[pl.ds(index * TALL + TOK, 16), :] = small_ref[:, index * TOK : (index + 1) * TOK]
    for copy in load_pieces(pieces, grad_ref, None, sems):
        copy.wait()
    for index in range(ALL // ROWS):
        grad = mm_t(grad_ref[pl.ds(index * ROWS, ROWS), :], weight_ref[...]).astype(low)
        for part in range(2):
            for head in range(2):
                place = pl.ds((index * 4 + 2 * part + head) * TALL, TOK)
                sent_ref[place, :] = grad[part * TOK : (part + 1) * TOK, head * HD : (head + 1) * HD]
    for index in range(EXPERTS):
        columns = pl.ds(pl.multiple_of(place_ref[index] * 256, 256), 256)
        target = mine_ref if index < 4 else other_ref
        target[index % 4] = t_mm(mixed_ref[...], grad_ref[:, columns]).astype(low)


def mix_back(owners, pieces, weight, mixed, small):
    blocks = jax.ShapeDtypeStruct((4, 256, 256), low)
    return pl.pallas_call(
        mix_back_kernel,
        out_shape=(jax.ShapeDtypeStruct((FSDP * TALL, HD), low), blocks, blocks),
        in_specs=[smem] + [anywhere] * 10 + [vmem] * 3,
        out_specs=(vmem, vmem, vmem),
        scratch_shapes=[pltpu.VMEM((ALL, D), low), pltpu.SemaphoreType.DMA((20,))],
        compiler_params=params(60),
        cost_estimate=cost(2.2e9, 10e6),
        name="mix_back",
    )(owners, *pieces, weight, mixed, small)


def collect_kernel(core_ref, grads_ref, query_ref, mine_ref, other_ref):
    first = core_ref[0] == 0

    @pl.loop(0, SEQS)
    def step(index):
        rows = pl.ds(index * TOK, TOK)
        swapped = pl.ds(((index + SEQS // 2) % SEQS) * TOK, TOK)
        one = grads_ref[pl.ds(index * 2 * TOK, TOK), :]
        two = grads_ref[pl.ds(index * 2 * TOK + TOK, TOK), :]
        query_ref[rows, 0:HD] = one[:, :HD]
        query_ref[rows, HD : 2 * HD] = two[:, :HD]
        total = one[:, HD:].astype(wide) + two[:, HD:].astype(wide)
        lower = jnp.concatenate([total[:, : HD // 2], total[:, HD : HD + HD // 2]], axis=1)
        upper = jnp.concatenate([total[:, HD // 2 : HD], total[:, HD + HD // 2 :]], axis=1)
        mine_ref[rows, :] = jnp.where(first, lower, upper)
        other_ref[swapped, :] = jnp.where(first, upper, lower).astype(low)


def collect(core, grads):
    return pl.pallas_call(
        collect_kernel,
        out_shape=(
            jax.ShapeDtypeStruct((ALL, 2 * HD), low),
            jax.ShapeDtypeStruct((ALL, HD), wide),
            jax.ShapeDtypeStruct((ALL, HD), low),
        ),
        in_specs=[smem, vmem],
        out_specs=(vmem, vmem, vmem),
        compiler_params=params(32),
        cost_estimate=cost(1e6, 4e6),
        name="collect",
    )(core, grads)


def qkv_weights_kernel(place_ref, normed_ref, query_ref, mine_ref, got_ref, *refs):
    parts, (out_ref, grad_ref) = refs[:5], refs[5:]
    grad_ref[:, 0 : 2 * HD] = query_ref[...]
    grad_ref[:, 2 * HD : 3 * HD] = (mine_ref[...] + got_ref[...].astype(wide)).astype(low)
    for index in range(EXPERTS):
        step, side = index // 2, index % 2
        rows = pl.ds(pl.multiple_of(place_ref[index] * 256, 256), 256)
        out_ref[rows, 3 * HD : 3 * HD + 256] = parts[step + 1][side] if step else parts[side][...]
    for index in range(D // ROWS):
        rows = pl.ds(index * ROWS, ROWS)
        out_ref[rows, 0 : 3 * HD] = t_mm(normed_ref[:, rows], grad_ref[...]).astype(low)


def qkv_weights(places, normed, query, mine, got, parts):
    return pl.pallas_call(
        qkv_weights_kernel,
        out_shape=(jax.ShapeDtypeStruct((D, 3 * HD + 256), low), jax.ShapeDtypeStruct((ALL, 3 * HD), low)),
        in_specs=[smem] + [vmem] * 9,
        out_specs=(vmem, vmem),
        compiler_params=params(40),
        cost_estimate=cost(1.6e9, 10e6),
        name="qkv_weights",
    )(places, normed, query, mine, got, *parts)


def finish_kernel(shards_ref, query_ref, key_ref, value_ref, out_ref, gain_ref):
    gain = jnp.zeros((TOK, TOK), wide)
    for source in range(EXPERTS):
        query_ref[:, source * 256 : (source + 1) * 256] = shards_ref[source, :, 0:256].astype(wide)
        out_ref[:, source * 256 : (source + 1) * 256] = shards_ref[source, :, 384:640].astype(wide)
        gain = gain + shards_ref[source, :, 640:768].astype(wide)
    for pair in range(KV):
        one = shards_ref[2 * pair, :, 256:384].astype(wide)
        two = shards_ref[2 * pair + 1, :, 256:384].astype(wide)
        columns = slice(pair * HD, (pair + 1) * HD)
        key_ref[:, columns] = jnp.concatenate([one[:, : HD // 2], two[:, : HD // 2]], axis=1)
        value_ref[:, columns] = jnp.concatenate([one[:, HD // 2 :], two[:, HD // 2 :]], axis=1)
    gain_ref[...] = gain


def finish(shards):
    widths = (H * HD, KV * HD, KV * HD, H * HD, TOK)
    return pl.pallas_call(
        finish_kernel,
        out_shape=tuple(jax.ShapeDtypeStruct((TOK, width), wide) for width in widths),
        in_specs=[vmem],
        out_specs=tuple([vmem] * 5),
        compiler_params=params(32),
        cost_estimate=cost(1e6, 4e6),
        name="finish",
    )(shards)


def finish_dense_kernel(shards_ref, spread_ref, spread_rows_ref, gate_ref, up_ref, down_ref, left, rows_in):
    width = SH_OWN // 2
    for source in range(EXPERTS):
        for part in range(4):
            left[part * TOK : (part + 1) * TOK, source * width : (source + 1) * width] = shards_ref[
                source, :, part * width : (part + 1) * width
            ]
        packed = shards_ref[source, :, 2 * SH_OWN : 3 * SH_OWN].astype(wide)
        rows_in[source * SH_PAD : (source + 1) * SH_PAD, :] = pack_rows(packed)
    for start in range(0, SH // 2, 256):
        count = min(256, SH // 2 - start)
        both = mm(left[...], spread_ref[:, start : start + count])
        for part in range(4):
            target = gate_ref if part < 2 else up_ref
            begin = (part % 2) * (SH // 2) + start
            target[:, begin : begin + count] = both[part * TOK : (part + 1) * TOK]
    down_ref[...] = mm(spread_rows_ref[...], rows_in[...].astype(low))


def finish_dense(shards, spread, spread_rows):
    shapes = [(TOK, SH), (TOK, SH), (SH_ROWS, D)]
    return pl.pallas_call(
        finish_dense_kernel,
        out_shape=tuple(jax.ShapeDtypeStruct(shape, wide) for shape in shapes),
        in_specs=[vmem] * 3,
        out_specs=tuple([vmem] * 3),
        scratch_shapes=[
            pltpu.VMEM((4 * TOK, EXPERTS * SH_OWN // 2), low),
            pltpu.VMEM((EXPERTS * SH_PAD, D), wide),
        ],
        compiler_params=params(40),
        cost_estimate=cost(2.2e9, 12e6),
        name="finish_dense",
    )(shards, spread, spread_rows)


def halves(value):
    upper = value.astype(low)
    return upper, (value - upper.astype(wide)).astype(low)


def silu_parts(gate_value):
    sig = 1.0 / (1.0 + jnp.exp(-gate_value))
    return sig, gate_value * sig


def swiglu_back(sig, act, up_value, grad):
    return (grad * up_value * (sig + act * (1.0 - sig))).astype(low), (grad * act).astype(low)


def pack_rows(block):
    count, width = block.shape[0] // 8, block.shape[1] // 128
    return jnp.concatenate(
        [
            jnp.concatenate(
                [block[8 * i : 8 * i + 8, 128 * j : 128 * j + 128] for i in range(count)], axis=1
            )
            for j in range(width)
        ],
        axis=0,
    )


def slab(buffer, out_ref, sems, step, start, width):
    target = out_ref.at[pl.ds(step * ROWS, ROWS), pl.ds(start, width)]
    return pltpu.make_async_copy(buffer.at[step % 2, :, pl.ds(0, width)], target, sems.at[step % 2])


def send_slabs(tokens_ref, grad_ref, down_rows, out_ref, buffer, sems, start):
    width = grad_ref.shape[1]
    count = width // 2 // FSDP
    place = (start, width + width // 2)
    for step in range(D // ROWS):
        slot = step % 2
        if step >= 2:
            slab(buffer, out_ref, sems, step - 2, *place).wait()
        buffer[slot, :, 0:width] = t_mm(tokens_ref[:, pl.ds(step * ROWS, ROWS)], grad_ref[...]).astype(low)
        down = down_rows(step)
        for part in range(2):
            packed = pack_rows(down[part * count : (part + 1) * count]).astype(low)
            buffer[slot, part * TOK : (part + 1) * TOK, width : width + width // 2] = packed
        slab(buffer, out_ref, sems, step, *place).start()
    for step in (D // ROWS - 2, D // ROWS - 1):
        slab(buffer, out_ref, sems, step, *place).wait()


def ffn_kernel(*refs):
    expert_ref, slots_hbm, slots_t_hbm, routes_ref, router_hbm = refs[:5]
    pieces, cot_pieces, pack_ref = refs[5:15], refs[15:25], refs[25]
    grad_mine, grad_other, gates_ref, out_ref = refs[26:30]
    outs = refs[30:33]
    normed_ref, cot_ref, grad_ref = refs[33:36]
    kept = refs[36:44]
    hidden_s, grad_s, incoming, hidden_e, gated, grad_rows, grad_e, w_down_s = kept
    w_in_s, w_in, w_down, slots_ref, slots_t_ref = refs[44:49]
    raw, gate_parts, grad_in, buffer, piece_sems, cot_sems, sems, out_sems, slab_sems = refs[49:]
    base = 3 * SH_OWN
    half_d = D // 2

    def stage_shared(part):
        return pltpu.make_async_copy(
            pack_ref.at[pl.ds(part * half_d, half_d), pl.ds(2 * SH_OWN, SH_OWN)],
            grad_ref.at[:, pl.ds(FF + part * SH_OWN, SH_OWN)],
            sems.at[part],
        )

    def stage_down(part):
        return pltpu.make_async_copy(
            pack_ref.at[pl.ds(part * half_d, half_d), pl.ds(base + 2 * FF, FF)],
            grad_ref.at[:, pl.ds(0, FF)],
            sems.at[2 + part],
        )

    def unpack(target, pair, row, start, width):
        count = 2 * width // FSDP
        both = [
            pack_rows(grad_ref[row + part * TOK : row + (part + 1) * TOK, start : start + width].astype(wide))
            for part in range(2)
        ]
        target[pair * count : (pair + 1) * count, :] = jnp.concatenate(both, axis=0).astype(low)

    copies = [
        pltpu.make_async_copy(router_hbm, w_in_s.at[:, pl.ds(2 * SH_OWN, 128)], sems.at[4]),
        pltpu.make_async_copy(pack_ref.at[:, pl.ds(0, 2 * SH_OWN)], w_in_s.at[:, pl.ds(0, 2 * SH_OWN)], sems.at[5]),
        pltpu.make_async_copy(slots_hbm, slots_ref, sems.at[6]),
        pltpu.make_async_copy(pack_ref.at[:, pl.ds(base, 2 * FF)], w_in, sems.at[7]),
        pltpu.make_async_copy(slots_t_hbm, slots_t_ref, sems.at[8]),
    ]
    stage_shared(0).start()
    stage_shared(1).start()
    copies[0].start()
    copies[1].start()
    piece_copies = load_pieces(pieces, normed_ref, None, piece_sems)
    cot_copies = load_pieces(cot_pieces, cot_ref, None, cot_sems)
    stage_down(0).start()
    for copy in copies[2:]:
        copy.start()

    def send(index, source):
        copy = pltpu.make_async_copy(source, outs[index], out_sems.at[index])
        copy.start()
        return copy

    expert = expert_ref[0]
    lane = lax.broadcasted_iota(jnp.int32, (ROWS, 128), 1)
    for part in range(2):
        stage_shared(part).wait()
        for pair in range(4):
            unpack(w_down_s, part * 4 + pair, pair * 2 * TOK, FF + part * SH_OWN, SH_OWN)
    for copy in piece_copies + cot_copies + copies[:2]:
        copy.wait()
    stage_down(0).wait()
    for step in range(ALL // ROWS):
        unpack(w_down, step, step * 2 * TOK, 0, FF)
        rows = pl.ds(step * ROWS, ROWS)
        both = mm(normed_ref[rows, :], w_in_s[...])
        sig, act = silu_parts(both[:, :SH_OWN])
        up = both[:, SH_OWN : 2 * SH_OWN]
        hidden_s[rows, :] = (act * up).astype(low)
        grad_hidden = mm_t(cot_ref[rows, :], w_down_s[...])
        grad_gate, grad_up = swiglu_back(sig, act, up, grad_hidden)
        grad_s[rows, 0:SH_OWN] = grad_gate
        grad_s[rows, SH_OWN : 2 * SH_OWN] = grad_up
        logits = both[:, 2 * SH_OWN :]
        first, second = routes_ref[rows, 0:1], routes_ref[rows, 1:2]
        chosen_first = jnp.sum(jnp.where(lane == first + 2, logits, 0.0), axis=1, keepdims=True)
        chosen_second = jnp.sum(jnp.where(lane == second + 2, logits, 0.0), axis=1, keepdims=True)
        gate_first = 1.0 / (1.0 + jnp.exp(chosen_second - chosen_first))
        gate_second = 1.0 / (1.0 + jnp.exp(chosen_first - chosen_second))
        here = jnp.where(first == expert, gate_first, 0.0) + jnp.where(second == expert, gate_second, 0.0)
        upper, lower = halves(here)
        parts = jnp.where(lane == 0, upper.astype(wide), 0.0) + jnp.where(lane == 1, lower.astype(wide), 0.0)
        gate_parts[rows, :] = parts.astype(low)
        if step == 0:
            both_gates = jnp.where(lane == 0, gate_first, 0.0) + jnp.where(lane == 1, gate_second, 0.0)
            gates_ref[...] = both_gates[:TOK]
    stage_down(1).start()
    sent = [send(0, hidden_s)]
    down_copy = send(1, w_down_s)
    copies[2].wait()
    for step in range(D // ROWS):
        columns = pl.ds(step * ROWS, ROWS)
        incoming[:, columns] = mm(slots_ref[...], normed_ref[:, columns]).astype(low)
        grad_rows[:, columns] = mm(slots_ref[...], cot_ref[:, columns]).astype(low)
    slot_parts = mm(slots_ref[...], gate_parts[...])
    slot_gate = slot_parts[:, 0:1] + slot_parts[:, 1:2]
    copies[3].wait()
    stage_down(1).wait()
    for step in range(4):
        unpack(w_down, 4 + step, step * 2 * TOK, 0, FF)
    for step in range(2 * FF // ROWS):
        columns = pl.ds(step * ROWS, ROWS)
        raw[:, columns] = mm(incoming[...], w_in[:, columns])
    for start, width in FF_TILES:
        gate, up = raw[:, start : start + width], raw[:, FF + start : FF + start + width]
        hidden_e[:, start : start + width] = (silu_parts(gate)[1] * up).astype(low)
    slot_grad = jnp.zeros((SLOTS, 1), wide)
    for step in range(D // ROWS):
        columns = pl.ds(step * ROWS, ROWS)
        rows = mm(hidden_e[...], w_down[:, columns]).astype(low).astype(wide)
        cot = grad_rows[:, columns].astype(wide)
        gated[:, columns] = (rows * slot_gate).astype(low)
        grad_rows[:, columns] = (cot * slot_gate).astype(low)
        slot_grad = slot_grad + jnp.sum(rows * cot, axis=1, keepdims=True)
    sent.append(send(2, gated))
    for start, width in FF_TILES:
        grad_hidden = mm_t(grad_rows[...], w_down[pl.ds(start, width), :])
        sig, act = silu_parts(raw[:, start : start + width])
        grad_gate, grad_up = swiglu_back(sig, act, raw[:, FF + start : FF + start + width], grad_hidden)
        grad_e[:, start : start + width] = grad_gate
        grad_e[:, FF + start : FF + start + width] = grad_up
    for step in range(D // ROWS):
        columns = pl.ds(step * ROWS, ROWS)
        grad_in[:, columns] = mm_t(grad_e[...], w_in[columns, :]).astype(low)
    upper, lower = halves(slot_grad)
    slot_lane = lax.broadcasted_iota(jnp.int32, (SLOTS, 128), 1)
    slot_parts = (
        jnp.where(slot_lane == expert, upper.astype(wide), 0.0)
        + jnp.where(slot_lane == expert + 8, lower.astype(wide), 0.0)
    ).astype(low)
    copies[4].wait()
    half = ALL // 2
    for side, target in ((1, grad_other), (0, grad_mine)):
        for step in range(half // ROWS):
            rows = pl.ds(side * half + step * ROWS, ROWS)
            for tile in range(D // 512):
                columns = pl.ds(tile * 512, 512)
                grad_ref[rows, columns] = (
                    mm_t(grad_s[rows, :], w_in_s[columns, 0 : 2 * SH_OWN])
                    + mm(slots_t_ref[rows, :], grad_in[:, columns])
                ).astype(low)
            grad_ref[rows, D : D + 128] = mm(slots_t_ref[rows, :], slot_parts).astype(low)
        copy = pltpu.make_async_copy(grad_ref.at[pl.ds(side * half, half), :], target, sems.at[9 + side])
        copy.start()
        sent.append(copy)

    def expert_down(step):
        count = 2 * FF // FSDP
        return t_mm(hidden_e[:, step * count : (step + 1) * count], grad_rows[...])

    def shared_down(step):
        count = 2 * SH_PAD
        return w_down_s[step * count : (step + 1) * count, :].astype(wide)

    down_copy.wait()
    for step in range(D // ROWS):
        columns = pl.ds(step * ROWS, ROWS)
        w_down_s[:, columns] = t_mm(hidden_s[...], cot_ref[:, columns]).astype(low)
    send_slabs(incoming, grad_e, expert_down, out_ref, buffer, slab_sems, base)
    send_slabs(normed_ref, grad_s, shared_down, out_ref, buffer, slab_sems, 0)
    for copy in sent:
        copy.wait()


def ffn(expert, slots, slots_t, routes, router, pieces, cot_pieces, pack):
    outs = [(D, 3 * SH_OWN + 3 * FF), (ALL, SH_OWN), (SH_OWN, D), (SLOTS, D)]
    kept = [(ALL, SH_OWN), (ALL, 2 * SH_OWN), (SLOTS, D), (SLOTS, FF), (SLOTS, D), (SLOTS, D), (SLOTS, 2 * FF)]
    kept.append((SH_OWN, D))
    grads = [(ALL // 2, D + 128)] * 2
    return pl.pallas_call(
        ffn_kernel,
        out_shape=tuple(
            [jax.ShapeDtypeStruct(shape, low) for shape in grads]
            + [jax.ShapeDtypeStruct((TOK, 128), wide)]
            + [jax.ShapeDtypeStruct(shape, low) for shape in outs]
        ),
        in_specs=[smem, anywhere, anywhere, vmem] + [anywhere] * 22,
        out_specs=tuple([anywhere] * 2 + [vmem] + [anywhere] * 4),
        scratch_shapes=[pltpu.VMEM((ALL, D), low), pltpu.VMEM((ALL, D), low), pltpu.VMEM((ALL, D + 128), low)]
        + [pltpu.VMEM(shape, low) for shape in kept]
        + [
            pltpu.VMEM((D, 2 * SH_OWN + 128), low),
            pltpu.VMEM((D, 2 * FF), low),
            pltpu.VMEM((FF, D), low),
            pltpu.VMEM((SLOTS, ALL), low),
            pltpu.VMEM((ALL, SLOTS), low),
            pltpu.VMEM((SLOTS, 2 * FF), wide),
            pltpu.VMEM((ALL, 128), low),
            pltpu.VMEM((SLOTS, D), low),
            pltpu.VMEM((2, ROWS, 3 * FF), low),
            pltpu.SemaphoreType.DMA((20,)),
            pltpu.SemaphoreType.DMA((20,)),
            pltpu.SemaphoreType.DMA((11,)),
            pltpu.SemaphoreType.DMA((3,)),
            pltpu.SemaphoreType.DMA((2,)),
        ],
        compiler_params=params(60),
        cost_estimate=cost(38e9, 70e6, 1e6),
        name="ffn",
    )(expert, slots, slots_t, routes, router, *pieces, *cot_pieces, pack)


def out_rows_kernel(place_ref, *refs):
    parts, out_ref = refs[:5], refs[5]
    for index in range(EXPERTS):
        step, side = index // 2, index % 2
        columns = pl.ds(pl.multiple_of(place_ref[index] * 256, 256), 256)
        out_ref[:, columns] = parts[step + 1][side] if step else parts[side][...]


def out_rows(places, parts):
    return pl.pallas_call(
        out_rows_kernel,
        out_shape=jax.ShapeDtypeStruct((256, D), low),
        in_specs=[smem] + [vmem] * 5,
        out_specs=vmem,
        compiler_params=params(32),
        cost_estimate=cost(0, 2e6),
        name="out_rows",
    )(places, *parts)


def back_two_kernel(
    own_ref, first_ref, second_ref, middle_ref, cot_ref, gains_ref, gates_ref, routes_ref, block_ref, grad_ref, total_ref, logits_ref
):
    total = own_ref[...] + first_ref[...].astype(wide) + second_ref[...].astype(wide)
    lane = lax.broadcasted_iota(jnp.int32, (TOK, 128), 1)
    extra = total[:, D:]
    first, second = routes_ref[:, 0:1], routes_ref[:, 1:2]

    def taken(route):
        return jnp.sum(jnp.where((lane == route) | (lane == route + 8), extra, 0.0), axis=1, keepdims=True)

    gate_first, gate_second = gates_ref[:, 0:1], gates_ref[:, 1:2]
    taken_first, taken_second = taken(first), taken(second)
    inner = gate_first * taken_first + gate_second * taken_second
    chosen_first, chosen_second = gate_first * (taken_first - inner), gate_second * (taken_second - inner)
    logits = jnp.where(lane == first, chosen_first, 0.0) + jnp.where(lane == second, chosen_second, 0.0)
    grad = total[:, :D]
    for index in range(EXPERTS):
        grad = grad + logits[:, index : index + 1] * gains_ref[2 + index : 3 + index, :]
    middle = middle_ref[...]
    factor = lax.rsqrt(jnp.mean(middle * middle, axis=-1, keepdims=True) + eps_norm)
    scaled = grad * gains_ref[1:2, :]
    mean = jnp.mean(scaled * middle, axis=-1, keepdims=True)
    result = cot_ref[...].astype(wide) + factor * scaled - middle * (factor * factor * factor * mean)
    grad_ref[...] = result
    block_ref[...] = result.astype(low)
    total_ref[...] = grad
    logits_ref[...] = logits


def back_two(*operands):
    return pl.pallas_call(
        back_two_kernel,
        out_shape=(
            jax.ShapeDtypeStruct((TOK, D), low),
            jax.ShapeDtypeStruct((TOK, D), wide),
            jax.ShapeDtypeStruct((TOK, D), wide),
            jax.ShapeDtypeStruct((TOK, 128), wide),
        ),
        in_specs=[vmem] * 8,
        out_specs=(vmem, vmem, vmem, vmem),
        compiler_params=params(32),
        cost_estimate=cost(1e7, 6e6),
        name="back_two",
    )(*operands)


def small_rows_kernel(total_ref, logits_ref, middle_ref, gains_ref, out_ref):
    middle = middle_ref[...]
    factor = lax.rsqrt(jnp.mean(middle * middle, axis=-1, keepdims=True) + eps_norm)
    gain_upper, gain_lower = halves(jnp.sum(total_ref[...] * middle * factor, axis=0, keepdims=True))
    normed = (middle * factor * gains_ref[1:2, :]).astype(low)
    logit_upper, logit_lower = halves(logits_ref[...].T[0:EXPERTS, :])
    router = mm(logit_upper, normed) + mm(logit_lower, normed)
    small = [gain_upper.astype(wide), gain_lower.astype(wide), router, jnp.zeros((6, D), wide)]
    out_ref[...] = jnp.concatenate(small, axis=0).astype(low)


def small_rows(*operands):
    return pl.pallas_call(
        small_rows_kernel,
        out_shape=jax.ShapeDtypeStruct((16, D), low),
        in_specs=[vmem] * 4,
        out_specs=vmem,
        compiler_params=params(32),
        cost_estimate=cost(1e7, 3e6),
        name="small_rows",
    )(*operands)


def norm_factor(values):
    return lax.rsqrt(jnp.mean(values * values, axis=-1, keepdims=True) + eps_norm)


def norm_back(values, factor, gain, grad):
    scaled = grad * gain
    inner = jnp.mean(scaled * values, axis=-1, keepdims=True)
    return factor * scaled - values * (factor * factor * factor * inner)


def per_device(
    hidden_in,
    cotangent,
    segments,
    routes,
    attn_gain,
    w_query,
    w_key,
    w_value,
    w_out,
    ffn_gain,
    w_router,
    shared_gate,
    shared_up,
    shared_down,
    expert_gate,
    expert_up,
    expert_down,
):
    expert = lax.axis_index("expert")
    z, core = expert // 2, expert % 2
    place = lax.axis_index("fsdp")

    misc = jnp.concatenate(
        [attn_gain[:, None], ffn_gain[:, None], w_router, jnp.zeros((TOK, 118), low)], axis=1
    )
    attn_pack = jnp.concatenate(
        [
            lax.dynamic_slice_in_dim(w_query, 256 * expert, 256, 1),
            lax.dynamic_slice_in_dim(w_key, HD * z, HD, 1),
            lax.dynamic_slice_in_dim(w_value, HD * z, HD, 1),
            lax.dynamic_slice_in_dim(w_out, 256 * expert, 256, 1),
            misc,
        ],
        axis=1,
    )
    attn_all = lax.all_gather(attn_pack, "fsdp", axis=0, tiled=True)
    half_in, half_out = SH // 2, SH_OWN // 2
    sel_column = jnp.arange(half_out)
    picked = SH_ROWS * (sel_column // SH_PAD) + SH_PART * expert + sel_column % SH_PAD
    picked = jnp.where(sel_column % SH_PAD < SH_PART, picked, -1)
    select = (jnp.arange(half_in)[:, None] == picked[None, :]).astype(low)
    own_shared = mm(
        jnp.concatenate(
            [shared_gate[:, :half_in], shared_gate[:, half_in:], shared_up[:, :half_in], shared_up[:, half_in:]],
            axis=0,
        ),
        select,
    ).astype(low)
    own_down = jnp.pad(
        lax.dynamic_slice_in_dim(shared_down, SH_PART * expert, SH_PART, 0),
        ((0, SH_PAD - SH_PART), (0, 0)),
    )
    ffn_pack = jnp.concatenate(
        [
            own_shared[:TOK],
            own_shared[TOK : 2 * TOK],
            own_shared[2 * TOK : 3 * TOK],
            own_shared[3 * TOK :],
            pack_tiles(own_down),
            expert_gate[:, 0],
            expert_up[:, 0],
            pack_tiles(expert_down[:, 0]),
        ],
        axis=1,
    )
    ffn_all = lax.all_gather(ffn_pack, "fsdp", axis=0, tiled=True)

    ids = jnp.concatenate(
        [
            segments.astype(low),
            jnp.pad(routes[0].reshape(1, TOK * TOPK), ((0, 0), (0, LENGTH - TOK * TOPK))).astype(low),
            jnp.zeros((14, LENGTH), low),
        ],
        axis=0,
    )
    hidden_pieces = gather_pieces(jnp.concatenate([hidden_in[0], ids], axis=0))
    cot_block, *hidden_pieces = together(cotangent[0], *hidden_pieces)
    cot_first = first_pieces(cot_block)

    inverse_freq = rope_base ** (-jnp.arange(HD // 2, dtype=wide) * 2.0 / HD)
    angles = jnp.arange(LENGTH).astype(wide)[:, None] * inverse_freq[None, :]
    cosine, sine = jnp.cos(angles), jnp.sin(angles)
    cos_all = jnp.concatenate([cosine, cosine], axis=1)
    sin_back = jnp.concatenate([sine, -sine], axis=1)
    cos_own = lax.dynamic_slice_in_dim(cos_all, place * TOK, TOK, 0)
    sin_own = -lax.dynamic_slice_in_dim(sin_back, place * TOK, TOK, 0)
    cos_two, sin_two = jnp.concatenate([cos_own, cos_own]), jnp.concatenate([sin_own, sin_own])
    put_row = jnp.arange(SH_PAD * EXPERTS * FSDP // 2)
    source, within = put_row // half_out, put_row % half_out
    target = SH_ROWS * (within // SH_PAD) + SH_PART * source + within % SH_PAD
    target = jnp.where(within % SH_PAD < SH_PART, target, -1)
    spread = (target[:, None] == jnp.arange(half_in)[None, :]).astype(low)
    put_row = jnp.arange(EXPERTS * SH_PAD)
    target = SH_PART * (put_row // SH_PAD) + put_row % SH_PAD
    target = jnp.where(put_row % SH_PAD < SH_PART, target, -1)
    spread_rows = (jnp.arange(SH_ROWS)[:, None] == target[None, :]).astype(low)
    attn_all, cos_two, sin_two, cos_all, sin_back = together(attn_all, cos_two, sin_two, cos_all, sin_back)
    normed_one, sent, factor_one, gains, ids_all = project(hidden_pieces, attn_all, cos_two, sin_two)

    sent, cot_block, *cot_first = together(sent, cot_block, *cot_first)
    cot_pieces = other_pieces(cot_block, *cot_first)
    qkv = lax.all_to_all(sent, "fsdp", split_axis=0, concat_axis=0, tiled=True)

    ids_all = ids_all.reshape(SEQS, 16, D)
    seg_row = lax.dynamic_slice_in_dim(ids_all[:, 0].astype(wide), place // 2, 1, 0)
    seg_blocks = jnp.pad(seg_row.reshape(FSDP, TOK), ((0, TOK - FSDP), (0, 0)))
    route_all = ids_all[:, 1, : TOK * TOPK].astype(jnp.int32).reshape(ALL, TOPK)
    hit = jnp.any(route_all == expert, axis=1).astype(wide)
    order = jnp.arange(ALL)
    rank = mm(hit.astype(low)[None, :], (order[:, None] < order[None, :]).astype(low))
    slot_bool = (rank.astype(jnp.int32) == jnp.arange(SLOTS)[:, None]) & (hit > 0.5)[None, :]
    slots = slot_bool.astype(low)
    slots_t = slot_bool.T.astype(low)
    out_columns = attn_all[:, 512:768].reshape(EXPERTS, 256, 256)
    owners = jnp.stack([relative_owner(expert, block) for block in range(EXPERTS)])
    out_blocks = [lax.dynamic_index_in_dim(out_columns, owners[block], 0) for block in range(EXPERTS)]
    out_mine, out_other = jnp.concatenate(out_blocks[:4]), jnp.concatenate(out_blocks[4:])
    out_mine, out_other, _ = together(out_mine, out_other, sent)
    w_out_own = out_rows(source_owners(expert), exchange(out_mine, out_other))
    router = attn_all[:, 768:896]
    is_first = core == 0
    kv_weight = attn_all[:, 256:512].reshape(D, 2, 2, HD // 2)
    kv_weight = jnp.where(is_first, kv_weight[:, :, 0], kv_weight[:, :, 1]).reshape(D, HD)
    qkv_weight = jnp.concatenate([attn_all[:, :256], kv_weight], axis=1)
    route_own = route_all[:TOK]
    qkv, seg_row, seg_blocks, route_all, slots, slots_t, w_out_own, router, qkv_weight, route_own, *cot_pieces = together(
        qkv, seg_row, seg_blocks, route_all, slots, slots_t, w_out_own, router, qkv_weight, route_own, *cot_pieces
    )
    mixed_head, log_total = attend(qkv, seg_row, seg_blocks)
    mixed = (
        lax.all_to_all(mixed_head, "fsdp", split_axis=0, concat_axis=0, tiled=True)
        .reshape(SEQS, 2, TOK, HD)
        .transpose(0, 2, 1, 3)
        .reshape(ALL, 2 * HD)
    )
    own_hidden = hidden_in[0].astype(wide)
    half = ALL // 2
    middle = own_hidden + scatter_rows(
        mm(mixed[:half], w_out_own).astype(low), mm(mixed[half:], w_out_own).astype(low)
    )
    factor_two = norm_factor(middle)
    gain_one, gain_two = gains[0:1], gains[1:2]
    normed_block = (middle * factor_two * gain_two).astype(low)

    base = 3 * SH_OWN
    normed_pieces = gather_pieces(normed_block)
    grad_mine, grad_other, gates, ffn_grads, hidden_shared, shared_down_w, gated_rows = ffn(
        expert[None], slots, slots_t, route_all, router, normed_pieces, cot_pieces, ffn_all
    )
    ffn_sums = lax.psum_scatter(ffn_grads, "fsdp", scatter_dimension=0, tiled=True)
    own_grad, to_above, to_below = scatter_start(grad_mine, swap_core(grad_other))
    from_below, from_above = move_z(to_above, 1), move_z(to_below, -1)
    back_block, grad_middle, grad_two, grad_logits = back_two(
        own_grad, from_below, from_above, middle, cotangent[0], gains, gates, route_own
    )
    back_block, hidden_shared, gated_rows = together(back_block, hidden_shared, gated_rows)
    below, above = first_pieces(back_block)
    small = small_rows(grad_two, grad_logits, middle, gains)
    result_other = (mm(hidden_shared[half:], shared_down_w) + mm(slots_t[half:], gated_rows)).astype(low)
    result_mine = (mm(hidden_shared[:half], shared_down_w) + mm(slots_t[:half], gated_rows)).astype(low)
    below, above, result_other, result_mine, small = together(below, above, result_other, result_mine, small)
    back_pieces = other_pieces(back_block, below, above)

    sent_back, out_mine, out_other = mix_back(owners, back_pieces, w_out_own, mixed, small)
    grad_head = lax.all_to_all(sent_back, "fsdp", split_axis=0, concat_axis=0, tiled=True)
    grads_head, small_sums = attend_back(qkv, grad_head, log_total, seg_row, seg_blocks, cos_all, sin_back)
    grads_qkv = lax.all_to_all(grads_head, "fsdp", split_axis=0, concat_axis=0, tiled=True)
    result_other, result_mine, _ = together(result_other, result_mine, sent_back)
    result_got = swap_core(result_other)
    result_got, out_mine, out_other = together(result_got, out_mine, out_other)
    out_parts = exchange(out_mine, out_other)
    result_own, to_above, to_below = scatter_start(result_mine, result_got)
    result_own = scatter_end(result_own, move_z(to_above, 1), move_z(to_below, -1))
    layer_out = (middle + result_own).astype(low)
    grads_qkv, layer_out, *out_parts = together(grads_qkv, layer_out, *out_parts)

    grad_query, kv_mine, kv_other = collect(core[None], grads_qkv)
    attn_grads, grad_qkv = qkv_weights(
        source_owners(expert), normed_one, grad_query, kv_mine, swap_core(kv_other), out_parts
    )
    attn_parts = lax.all_to_all(attn_grads, "fsdp", split_axis=0, concat_axis=0, tiled=True)

    grad_normed_other = mm_t(grad_qkv[half:], qkv_weight).astype(low)
    grad_normed_mine = mm_t(grad_qkv[:half], qkv_weight).astype(low)
    own_grad_one, to_above, to_below = scatter_start(grad_normed_mine, swap_core(grad_normed_other))
    attn_parts, to_above, to_below = together(attn_parts, to_above, to_below)
    own_grad_one = scatter_end(own_grad_one, move_z(to_above, 1), move_z(to_below, -1))
    grad_input = (grad_middle + norm_back(own_hidden, factor_one[:TOK], gain_one, own_grad_one)).astype(low)
    ffn_sums, _ = together(ffn_sums, attn_grads)
    shared_shards = lax.all_gather(ffn_sums[:, :base], "expert", axis=0)
    attn_parts, shared_shards = together(attn_parts, shared_shards)
    attn_sums = jnp.sum(attn_parts.reshape(FSDP, TOK, 3 * HD + 256).astype(wide), axis=0)

    own_weight = lax.dynamic_slice_in_dim(qkv_weight, place * TOK, TOK, 0)
    gain_part = jnp.sum(attn_sums[:, : 3 * HD] * own_weight.astype(wide), axis=1, keepdims=True)
    gain_upper, gain_lower = halves(gain_part / attn_gain.astype(wide)[:, None])
    small = [gain_upper, gain_lower, small_sums.T.astype(low), jnp.zeros((TOK, 110), low)]
    shards = jnp.concatenate([attn_sums.astype(low), *small], axis=1)

    attn_shards = lax.all_gather(shards, "expert", axis=0)
    grad_shared_gate, grad_shared_up, grad_shared_down = finish_dense(shared_shards, spread, spread_rows)
    grad_w_query, grad_w_key, grad_w_value, grad_w_out, small = finish(attn_shards)
    grad_expert_gate = ffn_sums[:, base : base + FF].astype(wide)[:, None]
    grad_expert_up = ffn_sums[:, base + FF : base + 2 * FF].astype(wide)[:, None]
    grad_expert_down = unpack_tiles(ffn_sums[:, base + 2 * FF :], 1).astype(wide)[:, None]
    return (
        layer_out[None],
        grad_input[None],
        small[:, 0] + small[:, 1],
        grad_w_query,
        grad_w_key,
        grad_w_value,
        grad_w_out,
        small[:, 2] + small[:, 3],
        small[:, 4 : 4 + EXPERTS],
        grad_shared_gate,
        grad_shared_up,
        grad_shared_down,
        grad_expert_gate,
        grad_expert_up,
        grad_expert_down,
    )


def solution(mesh):
    in_specs = (
        P("expert", "fsdp", None),
        P("expert", "fsdp", None),
        P("expert", None),
        P("expert", "fsdp", None),
        P("fsdp"),
        P("fsdp", None),
        P("fsdp", None),
        P("fsdp", None),
        P("fsdp", None),
        P("fsdp"),
        P("fsdp", None),
        P("fsdp", None),
        P("fsdp", None),
        P("fsdp", None),
        P("fsdp", "expert", None),
        P("fsdp", "expert", None),
        P("fsdp", "expert", None),
    )
    out_specs = (
        P("expert", "fsdp", None),
        P("expert", "fsdp", None),
        P("fsdp"),
        P("fsdp", None),
        P("fsdp", None),
        P("fsdp", None),
        P("fsdp", None),
        P("fsdp"),
        P("fsdp", None),
        P("fsdp", None),
        P("fsdp", None),
        P("fsdp", None),
        P("fsdp", "expert", None),
        P("fsdp", "expert", None),
        P("fsdp", "expert", None),
    )
    return jax.shard_map(
        per_device, mesh=mesh, in_specs=in_specs, out_specs=out_specs, check_vma=False
    )
```

```python
import jax
import jax.numpy as jnp
from jax import lax
from jax.experimental import pallas as pl
from jax.experimental.pallas import tpu as pltpu
from jax.sharding import PartitionSpec as P

D = 2048
H = 16
KV = 4
HD = 128
FF = 1408
SH = 2816
TOPK = 2
TOK = 128
LENGTH = 2048
SEQS = 8
EXPERTS = 8
FSDP = 16
ALL = SEQS * TOK
CAP = 42
SLOTS = SEQS * CAP
SH_ROWS = SH // FSDP
SH_PART = SH_ROWS // EXPERTS
SH_PAD = 24
SH_OWN = FSDP * SH_PAD
QBLOCK = 256

eps_norm = 1e-06
rope_base = 600000.0
masked_fill = -1e30
low = jnp.bfloat16
wide = jnp.float32


def shift_pairs(step):
    return [(z * 2 + c, ((z + step) % 4) * 2 + c) for z in range(4) for c in range(2)]


core_pairs = [(z * 2 + c, z * 2 + 1 - c) for z in range(4) for c in range(2)]


def move_z(block, step):
    return lax.ppermute(block, "expert", shift_pairs(step))


def swap_core(block):
    return lax.ppermute(block, "expert", core_pairs)


def together(*values):
    return lax.optimization_barrier(values)


TOP = TOK // 2


def first_pieces(block):
    return move_z(block, 1), move_z(block, -1)


def other_pieces(block, below, above):
    upper, lower = move_z(below[:TOP], 1), move_z(above[TOP:], -1)
    mine = [block, above, upper, lower, below]
    return mine + [swap_core(piece) for piece in mine]


def gather_pieces(block):
    return other_pieces(block, *first_pieces(block))


PIECES = [(4 * side + block, start) for side in (0, 1) for block, start in ((0, 0), (1, 0), (2, 0), (2, TOP), (3, 0))]


def load_pieces(refs, rows_ref, extra_ref, sems):
    copies = []
    for index, (ref, (block, start)) in enumerate(zip(refs, PIECES)):
        count = min(ref.shape[0], TOK - start)
        copies.append(
            pltpu.make_async_copy(
                ref.at[pl.ds(0, count), :], rows_ref.at[pl.ds(block * TOK + start, count), :], sems.at[2 * index]
            )
        )
        if extra_ref is not None and ref.shape[0] > count:
            copies.append(
                pltpu.make_async_copy(
                    ref.at[pl.ds(count, 16), :], extra_ref.at[pl.ds(block * 16, 16), :], sems.at[2 * index + 1]
                )
            )
    for copy in copies:
        copy.start()
    return copies


def scatter_start(mine, received):
    chip = mine.reshape(4, TOK, -1).astype(wide) + received.reshape(4, TOK, -1).astype(wide)
    from_below = move_z(chip[2, :TOP].astype(low), 1)
    from_above = move_z(chip[2, TOP:].astype(low), -1)
    to_above = jnp.concatenate([chip[1, :TOP] + from_below.astype(wide), chip[1, TOP:]], axis=0)
    to_below = jnp.concatenate([chip[3, :TOP], chip[3, TOP:] + from_above.astype(wide)], axis=0)
    return chip[0], to_above.astype(low), to_below.astype(low)


def scatter_end(own, first, second):
    return own + first.astype(wide) + second.astype(wide)


def scatter_rows(mine, other):
    own, to_above, to_below = scatter_start(mine, swap_core(other))
    return scatter_end(own, move_z(to_above, 1), move_z(to_below, -1))


def exchange(mine, got):
    chip = jnp.stack([mine[1:], got[1:]], axis=1)
    return mine[0], got[0], *[move_z(chip[step - 1], step) for step in (1, 2, 3)]


def source_owners(expert):
    return jnp.stack([((expert // 2 - index // 2) % 4) * 2 + ((expert % 2) ^ (index % 2)) for index in range(EXPERTS)])


def relative_owner(expert, block):
    return ((expert // 2 + block % 4) % 4) * 2 + ((expert % 2) ^ (block // 4))


def pack_tiles(block):
    rows, columns = block.shape[0] // 8, block.shape[1] // 128
    tiles = block.reshape(rows, 8, columns, 128).transpose(2, 1, 0, 3)
    return tiles.reshape(columns * 8, rows * 128)


def unpack_tiles(block, count):
    rows, columns = block.shape[1] // 128, block.shape[0] // (8 * count)
    tiles = block.reshape(count, columns, 8, rows, 128).transpose(0, 3, 2, 1, 4)
    return tiles.reshape(count * rows * 8, columns * 128)


def product(left, right, contract):
    return lax.dot_general(left, right, (contract, ((), ())), preferred_element_type=wide)


def mm(left, right):
    return product(left, right, ((1,), (0,)))


def mm_t(left, right):
    return product(left, right, ((1,), (1,)))


def t_mm(left, right):
    return product(left, right, ((0,), (0,)))


def segment_columns(seg_blocks_ref):
    return seg_blocks_ref[...].T


def block_scores(qkv_ref, seg_row_ref, columns, start, reach):
    query = qkv_ref[pl.ds(start, QBLOCK), 0:HD]
    key = qkv_ref[pl.ds(0, reach), HD : 2 * HD]
    scores = mm_t(query, key) * HD ** (-0.5)
    query_pos = start + lax.broadcasted_iota(jnp.int32, (QBLOCK, reach), 0)
    key_pos = lax.broadcasted_iota(jnp.int32, (QBLOCK, reach), 1)
    block = start // TOK
    column = jnp.concatenate([columns[:, block : block + 1], columns[:, block + 1 : block + 2]], axis=0)
    same = column == seg_row_ref[:, pl.ds(0, reach)]
    return jnp.where(same & (query_pos >= key_pos), scores, masked_fill)


def attend_kernel(qkv_ref, seg_row_ref, seg_blocks_ref, mixed_ref, total_ref):
    columns = segment_columns(seg_blocks_ref)
    for block in range(LENGTH // QBLOCK):
        start, reach = block * QBLOCK, (block + 1) * QBLOCK
        scores = block_scores(qkv_ref, seg_row_ref, columns, start, reach)
        largest = jnp.max(scores, axis=-1, keepdims=True)
        exponent = jnp.exp(scores - largest)
        totals = jnp.sum(exponent, axis=-1, keepdims=True)
        probs_low = (exponent * (1.0 / totals)).astype(low)
        value = qkv_ref[pl.ds(0, reach), 2 * HD : 3 * HD]
        mixed_ref[pl.ds(start, QBLOCK), :] = mm(probs_low, value).astype(low)
        total_ref[pl.ds(start, QBLOCK), :] = largest + jnp.log(totals)


def attend_back_kernel(
    qkv_ref, grad_ref, total_ref, seg_row_ref, seg_blocks_ref, cos_ref, sin_ref, out_ref, small_ref, key_acc, value_acc
):
    columns = segment_columns(seg_blocks_ref)
    key_acc[...] = jnp.zeros_like(key_acc)
    value_acc[...] = jnp.zeros_like(value_acc)

    def turn_back(value, rows):
        return value * cos_ref[rows, :] + pltpu.roll(value, HD // 2, 1) * sin_ref[rows, :]

    for block in range(LENGTH // QBLOCK):
        start, reach = block * QBLOCK, (block + 1) * QBLOCK
        rows, span = pl.ds(start, QBLOCK), pl.ds(0, reach)
        scores = block_scores(qkv_ref, seg_row_ref, columns, start, reach)
        probs = jnp.exp(scores - total_ref[rows, :])
        tall = [pl.ds((start // TOK + part) * TALL, TOK) for part in range(QBLOCK // TOK)]
        grad = jnp.concatenate([grad_ref[part, :] for part in tall], axis=0)
        grad_probs = mm_t(grad, qkv_ref[span, 2 * HD : 3 * HD])
        inner = jnp.sum(probs * grad_probs, axis=-1, keepdims=True)
        grad_scores = (probs * (grad_probs - inner)).astype(low)
        scale = HD ** (-0.5)
        grad_query = mm(grad_scores, qkv_ref[span, HD : 2 * HD]) * scale
        out_ref[rows, 0:HD] = turn_back(grad_query, rows).astype(low)
        key_acc[span, :] += t_mm(grad_scores, qkv_ref[rows, 0:HD]) * scale
        value_acc[span, :] += t_mm(probs.astype(low), grad)
    for block in range(LENGTH // QBLOCK):
        rows = pl.ds(block * QBLOCK, QBLOCK)
        out_ref[rows, HD : 2 * HD] = turn_back(key_acc[rows, :], rows).astype(low)
        out_ref[rows, 2 * HD : 3 * HD] = value_acc[rows, :].astype(low)
    small = grad_ref[pl.ds(TOK, 16), :].astype(wide)
    for index in range(1, FSDP):
        small = small + grad_ref[pl.ds(index * TALL + TOK, 16), :].astype(wide)
    small_ref[...] = small


vmem = pl.BlockSpec(memory_space=pltpu.VMEM)
smem = pl.BlockSpec(memory_space=pltpu.SMEM)
anywhere = pl.BlockSpec(memory_space=pl.ANY)
kernel_params = pltpu.CompilerParams(vmem_limit_bytes=48 * 1024 * 1024)


def attend(qkv, seg_row, seg_blocks):
    return pl.pallas_call(
        attend_kernel,
        out_shape=(
            jax.ShapeDtypeStruct((LENGTH, HD), low),
            jax.ShapeDtypeStruct((LENGTH, 1), wide),
        ),
        in_specs=[vmem] * 3,
        out_specs=(vmem, vmem),
        compiler_params=kernel_params,
        cost_estimate=pl.CostEstimate(
            flops=2 * LENGTH * LENGTH * HD, bytes_accessed=4 * LENGTH * HD * 2, transcendentals=LENGTH * LENGTH // 2
        ),
        name="attend",
    )(qkv, seg_row, seg_blocks)


def attend_back(qkv, grad, total, seg_row, seg_blocks, cos_all, sin_all):
    return pl.pallas_call(
        attend_back_kernel,
        out_shape=(jax.ShapeDtypeStruct((LENGTH, 3 * HD), low), jax.ShapeDtypeStruct((16, TOK), wide)),
        in_specs=[vmem] * 7,
        out_specs=(vmem, vmem),
        scratch_shapes=[pltpu.VMEM((LENGTH, HD), wide), pltpu.VMEM((LENGTH, HD), wide)],
        compiler_params=kernel_params,
        cost_estimate=pl.CostEstimate(
            flops=5 * LENGTH * LENGTH * HD, bytes_accessed=8 * LENGTH * HD * 2, transcendentals=LENGTH * LENGTH // 2
        ),
        name="attend_back",
    )(qkv, grad, total, seg_row, seg_blocks, cos_all, sin_all)


ROWS = 256
FF_TILES = [(start, min(256, FF - start)) for start in range(0, FF, 256)]


def params(mebibytes):
    return pltpu.CompilerParams(vmem_limit_bytes=mebibytes * 1024 * 1024)


def cost(flops, moved, special=0):
    return pl.CostEstimate(flops=int(flops), bytes_accessed=int(moved), transcendentals=int(special))


def project_kernel(*refs):
    pieces, (attn_ref, cos_ref, sin_ref) = refs[:10], refs[10:13]
    normed_ref, sent_ref, factor_ref, gains_ref, ids_ref, hidden, sems = refs[13:]
    copies = load_pieces(pieces, hidden, ids_ref, sems)
    pick = lax.broadcasted_iota(jnp.int32, (16, TOK), 0) == lax.broadcasted_iota(jnp.int32, (16, TOK), 1)
    gains_ref[...] = mm_t(pick.astype(wide).astype(low), attn_ref[:, 768:896])
    for copy in copies:
        copy.wait()
    gain = gains_ref[0:1, :]

    @pl.loop(0, ALL // ROWS)
    def step(index):
        rows = pl.ds(index * ROWS, ROWS)
        values = hidden[rows, :].astype(wide)
        factor = lax.rsqrt(jnp.mean(values * values, axis=-1, keepdims=True) + eps_norm)
        factor_ref[rows, :] = factor
        normed = (values * factor * gain).astype(low)
        normed_ref[rows, :] = normed
        raw = mm(normed, attn_ref[:, 0:512])

        def turn(value):
            return (value * cos_ref[...] + pltpu.roll(value, HD // 2, 1) * sin_ref[...]).astype(low)

        key = turn(raw[:, 2 * HD : 3 * HD])
        value = raw[:, 3 * HD :].astype(low)
        for head in range(2):
            query = turn(raw[:, head * HD : (head + 1) * HD])
            for part in range(2):
                place = pl.ds(index * 4 * TOK + (2 * part + head) * TOK, TOK)
                within = slice(part * TOK, (part + 1) * TOK)
                sent_ref[place, 0:HD] = query[within]
                sent_ref[place, HD : 2 * HD] = key[within]
                sent_ref[place, 2 * HD : 3 * HD] = value[within]


def project(pieces, attn_all, cos_two, sin_two):
    return pl.pallas_call(
        project_kernel,
        out_shape=(
            jax.ShapeDtypeStruct((ALL, D), low),
            jax.ShapeDtypeStruct((LENGTH, 3 * HD), low),
            jax.ShapeDtypeStruct((ALL, 1), wide),
            jax.ShapeDtypeStruct((16, D), wide),
            jax.ShapeDtypeStruct((SEQS * 16, D), low),
        ),
        in_specs=[anywhere] * 10 + [vmem] * 3,
        out_specs=tuple([vmem] * 5),
        scratch_shapes=[pltpu.VMEM((ALL, D), low), pltpu.SemaphoreType.DMA((20,))],
        compiler_params=params(40),
        cost_estimate=cost(2.2e9, 16e6),
        name="project",
    )(*pieces, attn_all, cos_two, sin_two)


TALL = TOK + 16


def mix_back_kernel(place_ref, *refs):
    pieces, weight_ref, mixed_ref, small_ref = refs[:10], refs[10], refs[11], refs[12]
    sent_ref, mine_ref, other_ref, grad_ref, sems = refs[13:]
    for index in range(FSDP):
        sent_ref[pl.ds(index * TALL + TOK, 16), :] = small_ref[:, index * TOK : (index + 1) * TOK]
    for copy in load_pieces(pieces, grad_ref, None, sems):
        copy.wait()
    for index in range(ALL // ROWS):
        grad = mm_t(grad_ref[pl.ds(index * ROWS, ROWS), :], weight_ref[...]).astype(low)
        for part in range(2):
            for head in range(2):
                place = pl.ds((index * 4 + 2 * part + head) * TALL, TOK)
                sent_ref[place, :] = grad[part * TOK : (part + 1) * TOK, head * HD : (head + 1) * HD]
    for index in range(EXPERTS):
        columns = pl.ds(pl.multiple_of(place_ref[index] * 256, 256), 256)
        target = mine_ref if index < 4 else other_ref
        target[index % 4] = t_mm(mixed_ref[...], grad_ref[:, columns]).astype(low)


def mix_back(owners, pieces, weight, mixed, small):
    blocks = jax.ShapeDtypeStruct((4, 256, 256), low)
    return pl.pallas_call(
        mix_back_kernel,
        out_shape=(jax.ShapeDtypeStruct((FSDP * TALL, HD), low), blocks, blocks),
        in_specs=[smem] + [anywhere] * 10 + [vmem] * 3,
        out_specs=(vmem, vmem, vmem),
        scratch_shapes=[pltpu.VMEM((ALL, D), low), pltpu.SemaphoreType.DMA((20,))],
        compiler_params=params(60),
        cost_estimate=cost(2.2e9, 10e6),
        name="mix_back",
    )(owners, *pieces, weight, mixed, small)


def collect_kernel(core_ref, grads_ref, query_ref, mine_ref, other_ref):
    first = core_ref[0] == 0

    @pl.loop(0, SEQS)
    def step(index):
        rows = pl.ds(index * TOK, TOK)
        swapped = pl.ds(((index + SEQS // 2) % SEQS) * TOK, TOK)
        one = grads_ref[pl.ds(index * 2 * TOK, TOK), :]
        two = grads_ref[pl.ds(index * 2 * TOK + TOK, TOK), :]
        query_ref[rows, 0:HD] = one[:, :HD]
        query_ref[rows, HD : 2 * HD] = two[:, :HD]
        total = one[:, HD:].astype(wide) + two[:, HD:].astype(wide)
        lower = jnp.concatenate([total[:, : HD // 2], total[:, HD : HD + HD // 2]], axis=1)
        upper = jnp.concatenate([total[:, HD // 2 : HD], total[:, HD + HD // 2 :]], axis=1)
        mine_ref[rows, :] = jnp.where(first, lower, upper)
        other_ref[swapped, :] = jnp.where(first, upper, lower).astype(low)


def collect(core, grads):
    return pl.pallas_call(
        collect_kernel,
        out_shape=(
            jax.ShapeDtypeStruct((ALL, 2 * HD), low),
            jax.ShapeDtypeStruct((ALL, HD), wide),
            jax.ShapeDtypeStruct((ALL, HD), low),
        ),
        in_specs=[smem, vmem],
        out_specs=(vmem, vmem, vmem),
        compiler_params=params(32),
        cost_estimate=cost(1e6, 4e6),
        name="collect",
    )(core, grads)


def gather_rows_kernel(place_ref, *refs):
    parts, out_ref = refs[:5], refs[5]
    for index in range(EXPERTS):
        step, side = index // 2, index % 2
        rows = pl.ds(pl.multiple_of(place_ref[index] * 256, 256), 256)
        out_ref[rows, :] = parts[step + 1][side] if step else parts[side][...]


def gather_out(places, parts):
    return pl.pallas_call(
        gather_rows_kernel,
        out_shape=jax.ShapeDtypeStruct((D, 256), low),
        in_specs=[smem] + [vmem] * 5,
        out_specs=vmem,
        compiler_params=params(32),
        cost_estimate=cost(0, 2e6),
        name="gather_out",
    )(places, *parts)


def qkv_weights_kernel(normed_hbm, query_ref, mine_ref, got_ref, out_ref, grad_ref, normed_ref, sems):
    copies = []
    for index in range(D // ROWS):
        columns = pl.ds(index * ROWS, ROWS)
        copies.append(pltpu.make_async_copy(normed_hbm.at[:, columns], normed_ref.at[:, columns], sems.at[index]))
        copies[index].start()
    grad_ref[:, 0 : 2 * HD] = query_ref[...]
    grad_ref[:, 2 * HD : 3 * HD] = (mine_ref[...] + got_ref[...].astype(wide)).astype(low)
    for index in range(D // ROWS):
        rows = pl.ds(index * ROWS, ROWS)
        copies[index].wait()
        out_ref[rows, :] = t_mm(normed_ref[:, rows], grad_ref[...]).astype(low)


def qkv_weights(normed, query, mine, got):
    return pl.pallas_call(
        qkv_weights_kernel,
        out_shape=(jax.ShapeDtypeStruct((D, 3 * HD), low), jax.ShapeDtypeStruct((ALL, 3 * HD), low)),
        in_specs=[anywhere] + [vmem] * 3,
        out_specs=(vmem, vmem),
        scratch_shapes=[pltpu.VMEM((ALL, D), low), pltpu.SemaphoreType.DMA((D // ROWS,))],
        compiler_params=params(60),
        cost_estimate=cost(1.6e9, 8e6),
        name="qkv_weights",
    )(normed, query, mine, got)


def finish_kernel(shards_ref, query_ref, key_ref, value_ref, out_ref, gain_ref):
    gain = jnp.zeros((TOK, TOK), wide)
    for source in range(EXPERTS):
        query_ref[:, source * 256 : (source + 1) * 256] = shards_ref[source, :, 0:256].astype(wide)
        out_ref[:, source * 256 : (source + 1) * 256] = shards_ref[source, :, 384:640].astype(wide)
        gain = gain + shards_ref[source, :, 640:768].astype(wide)
    for pair in range(KV):
        one = shards_ref[2 * pair, :, 256:384].astype(wide)
        two = shards_ref[2 * pair + 1, :, 256:384].astype(wide)
        columns = slice(pair * HD, (pair + 1) * HD)
        key_ref[:, columns] = jnp.concatenate([one[:, : HD // 2], two[:, : HD // 2]], axis=1)
        value_ref[:, columns] = jnp.concatenate([one[:, HD // 2 :], two[:, HD // 2 :]], axis=1)
    gain_ref[...] = gain


def finish(shards):
    widths = (H * HD, KV * HD, KV * HD, H * HD, TOK)
    return pl.pallas_call(
        finish_kernel,
        out_shape=tuple(jax.ShapeDtypeStruct((TOK, width), wide) for width in widths),
        in_specs=[vmem],
        out_specs=tuple([vmem] * 5),
        compiler_params=params(32),
        cost_estimate=cost(1e6, 4e6),
        name="finish",
    )(shards)


def finish_dense_kernel(shards_ref, spread_ref, spread_rows_ref, gate_ref, up_ref, down_ref, left, rows_in):
    width = SH_OWN // 2
    for source in range(EXPERTS):
        for part in range(4):
            left[part * TOK : (part + 1) * TOK, source * width : (source + 1) * width] = shards_ref[
                source, :, part * width : (part + 1) * width
            ]
        packed = shards_ref[source, :, 2 * SH_OWN : 3 * SH_OWN].astype(wide)
        rows_in[source * SH_PAD : (source + 1) * SH_PAD, :] = pack_rows(packed)
    for start in range(0, SH // 2, 256):
        count = min(256, SH // 2 - start)
        both = mm(left[...], spread_ref[:, start : start + count])
        for part in range(4):
            target = gate_ref if part < 2 else up_ref
            begin = (part % 2) * (SH // 2) + start
            target[:, begin : begin + count] = both[part * TOK : (part + 1) * TOK]
    down_ref[...] = mm(spread_rows_ref[...], rows_in[...].astype(low))


def finish_dense(shards, spread, spread_rows):
    shapes = [(TOK, SH), (TOK, SH), (SH_ROWS, D)]
    return pl.pallas_call(
        finish_dense_kernel,
        out_shape=tuple(jax.ShapeDtypeStruct(shape, wide) for shape in shapes),
        in_specs=[vmem] * 3,
        out_specs=tuple([vmem] * 3),
        scratch_shapes=[
            pltpu.VMEM((4 * TOK, EXPERTS * SH_OWN // 2), low),
            pltpu.VMEM((EXPERTS * SH_PAD, D), wide),
        ],
        compiler_params=params(40),
        cost_estimate=cost(2.2e9, 12e6),
        name="finish_dense",
    )(shards, spread, spread_rows)


def halves(value):
    upper = value.astype(low)
    return upper, (value - upper.astype(wide)).astype(low)


def silu_parts(gate_value):
    sig = 1.0 / (1.0 + jnp.exp(-gate_value))
    return sig, gate_value * sig


def swiglu_back(sig, act, up_value, grad):
    return (grad * up_value * (sig + act * (1.0 - sig))).astype(low), (grad * act).astype(low)


def pack_rows(block):
    count, width = block.shape[0] // 8, block.shape[1] // 128
    return jnp.concatenate(
        [
            jnp.concatenate(
                [block[8 * i : 8 * i + 8, 128 * j : 128 * j + 128] for i in range(count)], axis=1
            )
            for j in range(width)
        ],
        axis=0,
    )


def slab(buffer, out_ref, sems, step, start, width):
    target = out_ref.at[pl.ds(step * ROWS, ROWS), pl.ds(start, width)]
    return pltpu.make_async_copy(buffer.at[step % 2, :, pl.ds(0, width)], target, sems.at[step % 2])


def send_slabs(tokens_ref, grad_ref, down_rows, out_ref, buffer, sems, start):
    width = grad_ref.shape[1]
    count = width // 2 // FSDP
    place = (start, width + width // 2)
    for step in range(D // ROWS):
        slot = step % 2
        if step >= 2:
            slab(buffer, out_ref, sems, step - 2, *place).wait()
        buffer[slot, :, 0:width] = t_mm(tokens_ref[:, pl.ds(step * ROWS, ROWS)], grad_ref[...]).astype(low)
        down = down_rows(step)
        for part in range(2):
            packed = pack_rows(down[part * count : (part + 1) * count]).astype(low)
            buffer[slot, part * TOK : (part + 1) * TOK, width : width + width // 2] = packed
        slab(buffer, out_ref, sems, step, *place).start()
    for step in (D // ROWS - 2, D // ROWS - 1):
        slab(buffer, out_ref, sems, step, *place).wait()


def ffn_kernel(*refs):
    expert_ref, slots_hbm, slots_t_hbm, routes_ref, router_hbm = refs[:5]
    pieces, cot_pieces, pack_ref = refs[5:15], refs[15:25], refs[25]
    grad_mine, grad_other, gates_ref, out_ref = refs[26:30]
    outs = refs[30:33]
    normed_ref, cot_ref, grad_ref = refs[33:36]
    kept = refs[36:44]
    hidden_s, grad_s, incoming, hidden_e, gated, grad_rows, grad_e, w_down_s = kept
    w_in_s, w_in, w_down, slots_ref, slots_t_ref = refs[44:49]
    raw, gate_parts, grad_in, buffer, piece_sems, cot_sems, sems, out_sems, slab_sems = refs[49:]
    base = 3 * SH_OWN
    half_d = D // 2

    def stage_shared(part):
        return pltpu.make_async_copy(
            pack_ref.at[pl.ds(part * half_d, half_d), pl.ds(2 * SH_OWN, SH_OWN)],
            grad_ref.at[:, pl.ds(FF + part * SH_OWN, SH_OWN)],
            sems.at[part],
        )

    def stage_down(part):
        return pltpu.make_async_copy(
            pack_ref.at[pl.ds(part * half_d, half_d), pl.ds(base + 2 * FF, FF)],
            grad_ref.at[:, pl.ds(0, FF)],
            sems.at[2 + part],
        )

    def unpack(target, pair, row, start, width):
        count = 2 * width // FSDP
        both = [
            pack_rows(grad_ref[row + part * TOK : row + (part + 1) * TOK, start : start + width].astype(wide))
            for part in range(2)
        ]
        target[pair * count : (pair + 1) * count, :] = jnp.concatenate(both, axis=0).astype(low)

    copies = [
        pltpu.make_async_copy(router_hbm, w_in_s.at[:, pl.ds(2 * SH_OWN, 128)], sems.at[4]),
        pltpu.make_async_copy(pack_ref.at[:, pl.ds(0, 2 * SH_OWN)], w_in_s.at[:, pl.ds(0, 2 * SH_OWN)], sems.at[5]),
        pltpu.make_async_copy(slots_hbm, slots_ref, sems.at[6]),
        pltpu.make_async_copy(pack_ref.at[:, pl.ds(base, 2 * FF)], w_in, sems.at[7]),
        pltpu.make_async_copy(slots_t_hbm, slots_t_ref, sems.at[8]),
    ]
    stage_shared(0).start()
    stage_shared(1).start()
    copies[0].start()
    copies[1].start()
    piece_copies = load_pieces(pieces, normed_ref, None, piece_sems)
    cot_copies = load_pieces(cot_pieces, cot_ref, None, cot_sems)
    stage_down(0).start()
    for copy in copies[2:]:
        copy.start()

    def send(index, source):
        copy = pltpu.make_async_copy(source, outs[index], out_sems.at[index])
        copy.start()
        return copy

    expert = expert_ref[0]
    lane = lax.broadcasted_iota(jnp.int32, (ROWS, 128), 1)
    for part in range(2):
        stage_shared(part).wait()
        for pair in range(4):
            unpack(w_down_s, part * 4 + pair, pair * 2 * TOK, FF + part * SH_OWN, SH_OWN)
    for copy in piece_copies + cot_copies + copies[:2]:
        copy.wait()
    stage_down(0).wait()
    for step in range(ALL // ROWS):
        unpack(w_down, step, step * 2 * TOK, 0, FF)
        rows = pl.ds(step * ROWS, ROWS)
        both = mm(normed_ref[rows, :], w_in_s[...])
        sig, act = silu_parts(both[:, :SH_OWN])
        up = both[:, SH_OWN : 2 * SH_OWN]
        hidden_s[rows, :] = (act * up).astype(low)
        grad_hidden = mm_t(cot_ref[rows, :], w_down_s[...])
        grad_gate, grad_up = swiglu_back(sig, act, up, grad_hidden)
        grad_s[rows, 0:SH_OWN] = grad_gate
        grad_s[rows, SH_OWN : 2 * SH_OWN] = grad_up
        logits = both[:, 2 * SH_OWN :]
        first, second = routes_ref[rows, 0:1], routes_ref[rows, 1:2]
        chosen_first = jnp.sum(jnp.where(lane == first + 2, logits, 0.0), axis=1, keepdims=True)
        chosen_second = jnp.sum(jnp.where(lane == second + 2, logits, 0.0), axis=1, keepdims=True)
        gate_first = 1.0 / (1.0 + jnp.exp(chosen_second - chosen_first))
        gate_second = 1.0 / (1.0 + jnp.exp(chosen_first - chosen_second))
        here = jnp.where(first == expert, gate_first, 0.0) + jnp.where(second == expert, gate_second, 0.0)
        upper, lower = halves(here)
        parts = jnp.where(lane == 0, upper.astype(wide), 0.0) + jnp.where(lane == 1, lower.astype(wide), 0.0)
        gate_parts[rows, :] = parts.astype(low)
        if step == 0:
            both_gates = jnp.where(lane == 0, gate_first, 0.0) + jnp.where(lane == 1, gate_second, 0.0)
            gates_ref[...] = both_gates[:TOK]
    stage_down(1).start()
    sent = [send(0, hidden_s)]
    down_copy = send(1, w_down_s)
    copies[2].wait()
    for step in range(D // ROWS):
        columns = pl.ds(step * ROWS, ROWS)
        incoming[:, columns] = mm(slots_ref[...], normed_ref[:, columns]).astype(low)
        grad_rows[:, columns] = mm(slots_ref[...], cot_ref[:, columns]).astype(low)
    slot_parts = mm(slots_ref[...], gate_parts[...])
    slot_gate = slot_parts[:, 0:1] + slot_parts[:, 1:2]
    copies[3].wait()
    stage_down(1).wait()
    for step in range(4):
        unpack(w_down, 4 + step, step * 2 * TOK, 0, FF)
    for step in range(2 * FF // ROWS):
        columns = pl.ds(step * ROWS, ROWS)
        raw[:, columns] = mm(incoming[...], w_in[:, columns])
    for start, width in FF_TILES:
        gate, up = raw[:, start : start + width], raw[:, FF + start : FF + start + width]
        hidden_e[:, start : start + width] = (silu_parts(gate)[1] * up).astype(low)
    slot_grad = jnp.zeros((SLOTS, 1), wide)
    for step in range(D // ROWS):
        columns = pl.ds(step * ROWS, ROWS)
        rows = mm(hidden_e[...], w_down[:, columns]).astype(low).astype(wide)
        cot = grad_rows[:, columns].astype(wide)
        gated[:, columns] = (rows * slot_gate).astype(low)
        grad_rows[:, columns] = (cot * slot_gate).astype(low)
        slot_grad = slot_grad + jnp.sum(rows * cot, axis=1, keepdims=True)
    sent.append(send(2, gated))
    for start, width in FF_TILES:
        grad_hidden = mm_t(grad_rows[...], w_down[pl.ds(start, width), :])
        sig, act = silu_parts(raw[:, start : start + width])
        grad_gate, grad_up = swiglu_back(sig, act, raw[:, FF + start : FF + start + width], grad_hidden)
        grad_e[:, start : start + width] = grad_gate
        grad_e[:, FF + start : FF + start + width] = grad_up
    for step in range(D // ROWS):
        columns = pl.ds(step * ROWS, ROWS)
        grad_in[:, columns] = mm_t(grad_e[...], w_in[columns, :]).astype(low)
    upper, lower = halves(slot_grad)
    slot_lane = lax.broadcasted_iota(jnp.int32, (SLOTS, 128), 1)
    slot_parts = (
        jnp.where(slot_lane == expert, upper.astype(wide), 0.0)
        + jnp.where(slot_lane == expert + 8, lower.astype(wide), 0.0)
    ).astype(low)
    copies[4].wait()
    half = ALL // 2
    for side, target in ((1, grad_other), (0, grad_mine)):
        for step in range(half // ROWS):
            rows = pl.ds(side * half + step * ROWS, ROWS)
            for tile in range(D // 512):
                columns = pl.ds(tile * 512, 512)
                grad_ref[rows, columns] = (
                    mm_t(grad_s[rows, :], w_in_s[columns, 0 : 2 * SH_OWN])
                    + mm(slots_t_ref[rows, :], grad_in[:, columns])
                ).astype(low)
            grad_ref[rows, D : D + 128] = mm(slots_t_ref[rows, :], slot_parts).astype(low)
        copy = pltpu.make_async_copy(grad_ref.at[pl.ds(side * half, half), :], target, sems.at[9 + side])
        copy.start()
        sent.append(copy)

    def expert_down(step):
        count = 2 * FF // FSDP
        return t_mm(hidden_e[:, step * count : (step + 1) * count], grad_rows[...])

    def shared_down(step):
        count = 2 * SH_PAD
        return w_down_s[step * count : (step + 1) * count, :].astype(wide)

    down_copy.wait()
    for step in range(D // ROWS):
        columns = pl.ds(step * ROWS, ROWS)
        w_down_s[:, columns] = t_mm(hidden_s[...], cot_ref[:, columns]).astype(low)
    send_slabs(incoming, grad_e, expert_down, out_ref, buffer, slab_sems, base)
    send_slabs(normed_ref, grad_s, shared_down, out_ref, buffer, slab_sems, 0)
    for copy in sent:
        copy.wait()


def ffn(expert, slots, slots_t, routes, router, pieces, cot_pieces, pack):
    outs = [(D, 3 * SH_OWN + 3 * FF), (ALL, SH_OWN), (SH_OWN, D), (SLOTS, D)]
    kept = [(ALL, SH_OWN), (ALL, 2 * SH_OWN), (SLOTS, D), (SLOTS, FF), (SLOTS, D), (SLOTS, D), (SLOTS, 2 * FF)]
    kept.append((SH_OWN, D))
    grads = [(ALL // 2, D + 128)] * 2
    return pl.pallas_call(
        ffn_kernel,
        out_shape=tuple(
            [jax.ShapeDtypeStruct(shape, low) for shape in grads]
            + [jax.ShapeDtypeStruct((TOK, 128), wide)]
            + [jax.ShapeDtypeStruct(shape, low) for shape in outs]
        ),
        in_specs=[smem, anywhere, anywhere, vmem] + [anywhere] * 22,
        out_specs=tuple([anywhere] * 2 + [vmem] + [anywhere] * 4),
        scratch_shapes=[pltpu.VMEM((ALL, D), low), pltpu.VMEM((ALL, D), low), pltpu.VMEM((ALL, D + 128), low)]
        + [pltpu.VMEM(shape, low) for shape in kept]
        + [
            pltpu.VMEM((D, 2 * SH_OWN + 128), low),
            pltpu.VMEM((D, 2 * FF), low),
            pltpu.VMEM((FF, D), low),
            pltpu.VMEM((SLOTS, ALL), low),
            pltpu.VMEM((ALL, SLOTS), low),
            pltpu.VMEM((SLOTS, 2 * FF), wide),
            pltpu.VMEM((ALL, 128), low),
            pltpu.VMEM((SLOTS, D), low),
            pltpu.VMEM((2, ROWS, 3 * FF), low),
            pltpu.SemaphoreType.DMA((20,)),
            pltpu.SemaphoreType.DMA((20,)),
            pltpu.SemaphoreType.DMA((11,)),
            pltpu.SemaphoreType.DMA((3,)),
            pltpu.SemaphoreType.DMA((2,)),
        ],
        compiler_params=params(60),
        cost_estimate=cost(38e9, 70e6, 1e6),
        name="ffn",
    )(expert, slots, slots_t, routes, router, *pieces, *cot_pieces, pack)


def out_rows_kernel(place_ref, *refs):
    parts, out_ref = refs[:5], refs[5]
    for index in range(EXPERTS):
        step, side = index // 2, index % 2
        columns = pl.ds(pl.multiple_of(place_ref[index] * 256, 256), 256)
        out_ref[:, columns] = parts[step + 1][side] if step else parts[side][...]


def out_rows(places, parts):
    return pl.pallas_call(
        out_rows_kernel,
        out_shape=jax.ShapeDtypeStruct((256, D), low),
        in_specs=[smem] + [vmem] * 5,
        out_specs=vmem,
        compiler_params=params(32),
        cost_estimate=cost(0, 2e6),
        name="out_rows",
    )(places, *parts)


def back_two_kernel(
    own_ref, first_ref, second_ref, middle_ref, cot_ref, gains_ref, gates_ref, routes_ref, block_ref, grad_ref, total_ref, logits_ref
):
    total = own_ref[...] + first_ref[...].astype(wide) + second_ref[...].astype(wide)
    lane = lax.broadcasted_iota(jnp.int32, (TOK, 128), 1)
    extra = total[:, D:]
    first, second = routes_ref[:, 0:1], routes_ref[:, 1:2]

    def taken(route):
        return jnp.sum(jnp.where((lane == route) | (lane == route + 8), extra, 0.0), axis=1, keepdims=True)

    gate_first, gate_second = gates_ref[:, 0:1], gates_ref[:, 1:2]
    taken_first, taken_second = taken(first), taken(second)
    inner = gate_first * taken_first + gate_second * taken_second
    chosen_first, chosen_second = gate_first * (taken_first - inner), gate_second * (taken_second - inner)
    logits = jnp.where(lane == first, chosen_first, 0.0) + jnp.where(lane == second, chosen_second, 0.0)
    grad = total[:, :D]
    for index in range(EXPERTS):
        grad = grad + logits[:, index : index + 1] * gains_ref[2 + index : 3 + index, :]
    middle = middle_ref[...]
    factor = lax.rsqrt(jnp.mean(middle * middle, axis=-1, keepdims=True) + eps_norm)
    scaled = grad * gains_ref[1:2, :]
    mean = jnp.mean(scaled * middle, axis=-1, keepdims=True)
    result = cot_ref[...].astype(wide) + factor * scaled - middle * (factor * factor * factor * mean)
    grad_ref[...] = result
    block_ref[...] = result.astype(low)
    total_ref[...] = grad
    logits_ref[...] = logits


def back_two(*operands):
    return pl.pallas_call(
        back_two_kernel,
        out_shape=(
            jax.ShapeDtypeStruct((TOK, D), low),
            jax.ShapeDtypeStruct((TOK, D), wide),
            jax.ShapeDtypeStruct((TOK, D), wide),
            jax.ShapeDtypeStruct((TOK, 128), wide),
        ),
        in_specs=[vmem] * 8,
        out_specs=(vmem, vmem, vmem, vmem),
        compiler_params=params(32),
        cost_estimate=cost(1e7, 6e6),
        name="back_two",
    )(*operands)


def small_rows_kernel(total_ref, logits_ref, middle_ref, gains_ref, out_ref):
    middle = middle_ref[...]
    factor = lax.rsqrt(jnp.mean(middle * middle, axis=-1, keepdims=True) + eps_norm)
    gain_upper, gain_lower = halves(jnp.sum(total_ref[...] * middle * factor, axis=0, keepdims=True))
    normed = (middle * factor * gains_ref[1:2, :]).astype(low)
    logit_upper, logit_lower = halves(logits_ref[...].T[0:EXPERTS, :])
    router = mm(logit_upper, normed) + mm(logit_lower, normed)
    small = [gain_upper.astype(wide), gain_lower.astype(wide), router, jnp.zeros((6, D), wide)]
    out_ref[...] = jnp.concatenate(small, axis=0).astype(low)


def small_rows(*operands):
    return pl.pallas_call(
        small_rows_kernel,
        out_shape=jax.ShapeDtypeStruct((16, D), low),
        in_specs=[vmem] * 4,
        out_specs=vmem,
        compiler_params=params(32),
        cost_estimate=cost(1e7, 3e6),
        name="small_rows",
    )(*operands)


def norm_factor(values):
    return lax.rsqrt(jnp.mean(values * values, axis=-1, keepdims=True) + eps_norm)


def norm_back(values, factor, gain, grad):
    scaled = grad * gain
    inner = jnp.mean(scaled * values, axis=-1, keepdims=True)
    return factor * scaled - values * (factor * factor * factor * inner)


def per_device(
    hidden_in,
    cotangent,
    segments,
    routes,
    attn_gain,
    w_query,
    w_key,
    w_value,
    w_out,
    ffn_gain,
    w_router,
    shared_gate,
    shared_up,
    shared_down,
    expert_gate,
    expert_up,
    expert_down,
):
    expert = lax.axis_index("expert")
    z, core = expert // 2, expert % 2
    place = lax.axis_index("fsdp")

    misc = jnp.concatenate(
        [attn_gain[:, None], ffn_gain[:, None], w_router, jnp.zeros((TOK, 118), low)], axis=1
    )
    attn_pack = jnp.concatenate(
        [
            lax.dynamic_slice_in_dim(w_query, 256 * expert, 256, 1),
            lax.dynamic_slice_in_dim(w_key, HD * z, HD, 1),
            lax.dynamic_slice_in_dim(w_value, HD * z, HD, 1),
            lax.dynamic_slice_in_dim(w_out, 256 * expert, 256, 1),
            misc,
        ],
        axis=1,
    )
    attn_all = lax.all_gather(attn_pack, "fsdp", axis=0, tiled=True)
    half_in, half_out = SH // 2, SH_OWN // 2
    sel_column = jnp.arange(half_out)
    picked = SH_ROWS * (sel_column // SH_PAD) + SH_PART * expert + sel_column % SH_PAD
    picked = jnp.where(sel_column % SH_PAD < SH_PART, picked, -1)
    select = (jnp.arange(half_in)[:, None] == picked[None, :]).astype(low)
    own_shared = mm(
        jnp.concatenate(
            [shared_gate[:, :half_in], shared_gate[:, half_in:], shared_up[:, :half_in], shared_up[:, half_in:]],
            axis=0,
        ),
        select,
    ).astype(low)
    own_down = jnp.pad(
        lax.dynamic_slice_in_dim(shared_down, SH_PART * expert, SH_PART, 0),
        ((0, SH_PAD - SH_PART), (0, 0)),
    )
    ffn_pack = jnp.concatenate(
        [
            own_shared[:TOK],
            own_shared[TOK : 2 * TOK],
            own_shared[2 * TOK : 3 * TOK],
            own_shared[3 * TOK :],
            pack_tiles(own_down),
            expert_gate[:, 0],
            expert_up[:, 0],
            pack_tiles(expert_down[:, 0]),
        ],
        axis=1,
    )
    ffn_all = lax.all_gather(ffn_pack, "fsdp", axis=0, tiled=True)

    ids = jnp.concatenate(
        [
            segments.astype(low),
            jnp.pad(routes[0].reshape(1, TOK * TOPK), ((0, 0), (0, LENGTH - TOK * TOPK))).astype(low),
            jnp.zeros((14, LENGTH), low),
        ],
        axis=0,
    )
    hidden_pieces = gather_pieces(jnp.concatenate([hidden_in[0], ids], axis=0))
    cot_block, *hidden_pieces = together(cotangent[0], *hidden_pieces)
    cot_first = first_pieces(cot_block)

    inverse_freq = rope_base ** (-jnp.arange(HD // 2, dtype=wide) * 2.0 / HD)
    angles = jnp.arange(LENGTH).astype(wide)[:, None] * inverse_freq[None, :]
    cosine, sine = jnp.cos(angles), jnp.sin(angles)
    cos_all = jnp.concatenate([cosine, cosine], axis=1)
    sin_back = jnp.concatenate([sine, -sine], axis=1)
    cos_own = lax.dynamic_slice_in_dim(cos_all, place * TOK, TOK, 0)
    sin_own = -lax.dynamic_slice_in_dim(sin_back, place * TOK, TOK, 0)
    cos_two, sin_two = jnp.concatenate([cos_own, cos_own]), jnp.concatenate([sin_own, sin_own])
    put_row = jnp.arange(SH_PAD * EXPERTS * FSDP // 2)
    source, within = put_row // half_out, put_row % half_out
    target = SH_ROWS * (within // SH_PAD) + SH_PART * source + within % SH_PAD
    target = jnp.where(within % SH_PAD < SH_PART, target, -1)
    spread = (target[:, None] == jnp.arange(half_in)[None, :]).astype(low)
    put_row = jnp.arange(EXPERTS * SH_PAD)
    target = SH_PART * (put_row // SH_PAD) + put_row % SH_PAD
    target = jnp.where(put_row % SH_PAD < SH_PART, target, -1)
    spread_rows = (jnp.arange(SH_ROWS)[:, None] == target[None, :]).astype(low)
    attn_all, cos_two, sin_two, cos_all, sin_back = together(attn_all, cos_two, sin_two, cos_all, sin_back)
    normed_one, sent, factor_one, gains, ids_all = project(hidden_pieces, attn_all, cos_two, sin_two)

    sent, cot_block, *cot_first = together(sent, cot_block, *cot_first)
    cot_pieces = other_pieces(cot_block, *cot_first)
    qkv = lax.all_to_all(sent, "fsdp", split_axis=0, concat_axis=0, tiled=True)

    ids_all = ids_all.reshape(SEQS, 16, D)
    seg_row = lax.dynamic_slice_in_dim(ids_all[:, 0].astype(wide), place // 2, 1, 0)
    seg_blocks = jnp.pad(seg_row.reshape(FSDP, TOK), ((0, TOK - FSDP), (0, 0)))
    route_all = ids_all[:, 1, : TOK * TOPK].astype(jnp.int32).reshape(ALL, TOPK)
    hit = jnp.any(route_all == expert, axis=1).astype(wide)
    order = jnp.arange(ALL)
    rank = mm(hit.astype(low)[None, :], (order[:, None] < order[None, :]).astype(low))
    slot_bool = (rank.astype(jnp.int32) == jnp.arange(SLOTS)[:, None]) & (hit > 0.5)[None, :]
    slots = slot_bool.astype(low)
    slots_t = slot_bool.T.astype(low)
    out_columns = attn_all[:, 512:768].reshape(EXPERTS, 256, 256)
    owners = jnp.stack([relative_owner(expert, block) for block in range(EXPERTS)])
    out_blocks = [lax.dynamic_index_in_dim(out_columns, owners[block], 0) for block in range(EXPERTS)]
    out_mine, out_other = jnp.concatenate(out_blocks[:4]), jnp.concatenate(out_blocks[4:])
    out_mine, out_other, _ = together(out_mine, out_other, sent)
    w_out_own = out_rows(source_owners(expert), exchange(out_mine, swap_core(out_other)))
    router = attn_all[:, 768:896]
    is_first = core == 0
    kv_weight = attn_all[:, 256:512].reshape(D, 2, 2, HD // 2)
    kv_weight = jnp.where(is_first, kv_weight[:, :, 0], kv_weight[:, :, 1]).reshape(D, HD)
    qkv_weight = jnp.concatenate([attn_all[:, :256], kv_weight], axis=1)
    route_own = route_all[:TOK]
    qkv, seg_row, seg_blocks, route_all, slots, slots_t, w_out_own, router, qkv_weight, route_own, *cot_pieces = together(
        qkv, seg_row, seg_blocks, route_all, slots, slots_t, w_out_own, router, qkv_weight, route_own, *cot_pieces
    )
    mixed_head, log_total = attend(qkv, seg_row, seg_blocks)
    mixed = (
        lax.all_to_all(mixed_head, "fsdp", split_axis=0, concat_axis=0, tiled=True)
        .reshape(SEQS, 2, TOK, HD)
        .transpose(0, 2, 1, 3)
        .reshape(ALL, 2 * HD)
    )
    own_hidden = hidden_in[0].astype(wide)
    half = ALL // 2
    middle = own_hidden + scatter_rows(
        mm(mixed[:half], w_out_own).astype(low), mm(mixed[half:], w_out_own).astype(low)
    )
    factor_two = norm_factor(middle)
    gain_one, gain_two = gains[0:1], gains[1:2]
    normed_block = (middle * factor_two * gain_two).astype(low)

    base = 3 * SH_OWN
    normed_pieces = gather_pieces(normed_block)
    grad_mine, grad_other, gates, ffn_grads, hidden_shared, shared_down_w, gated_rows = ffn(
        expert[None], slots, slots_t, route_all, router, normed_pieces, cot_pieces, ffn_all
    )
    ffn_sums = lax.psum_scatter(ffn_grads, "fsdp", scatter_dimension=0, tiled=True)
    own_grad, to_above, to_below = scatter_start(grad_mine, swap_core(grad_other))
    from_below, from_above = move_z(to_above, 1), move_z(to_below, -1)
    back_block, grad_middle, grad_two, grad_logits = back_two(
        own_grad, from_below, from_above, middle, cotangent[0], gains, gates, route_own
    )
    back_block, hidden_shared, gated_rows = together(back_block, hidden_shared, gated_rows)
    below, above = first_pieces(back_block)
    small = small_rows(grad_two, grad_logits, middle, gains)
    result_other = (mm(hidden_shared[half:], shared_down_w) + mm(slots_t[half:], gated_rows)).astype(low)
    result_mine = (mm(hidden_shared[:half], shared_down_w) + mm(slots_t[:half], gated_rows)).astype(low)
    below, above, result_other, result_mine, small = together(below, above, result_other, result_mine, small)
    back_pieces = other_pieces(back_block, below, above)

    sent_back, out_mine, out_other = mix_back(owners, back_pieces, w_out_own, mixed, small)
    grad_head = lax.all_to_all(sent_back, "fsdp", split_axis=0, concat_axis=0, tiled=True)
    result_other, out_other, _ = together(result_other, out_other, sent_back)
    result_got, out_got = swap_core(result_other), swap_core(out_other)
    grad_head, result_got, out_got = together(grad_head, result_got, out_got)
    grads_head, small_sums = attend_back(qkv, grad_head, log_total, seg_row, seg_blocks, cos_all, sin_back)
    grads_qkv = lax.all_to_all(grads_head, "fsdp", split_axis=0, concat_axis=0, tiled=True)
    out_grads = gather_out(source_owners(expert), exchange(out_mine, out_got))
    result_own, to_above, to_below = scatter_start(result_mine, result_got)
    result_own = scatter_end(result_own, move_z(to_above, 1), move_z(to_below, -1))
    layer_out = (middle + result_own).astype(low)
    grads_qkv, layer_out, out_grads = together(grads_qkv, layer_out, out_grads)
    out_parts = lax.all_to_all(out_grads, "fsdp", split_axis=0, concat_axis=0, tiled=True)

    grad_query, kv_mine, kv_other = collect(core[None], grads_qkv)
    attn_grads, grad_qkv = qkv_weights(normed_one, grad_query, kv_mine, swap_core(kv_other))
    attn_grads, out_parts = together(attn_grads, out_parts)
    attn_parts = lax.all_to_all(attn_grads, "fsdp", split_axis=0, concat_axis=0, tiled=True)

    grad_normed_other = mm_t(grad_qkv[half:], qkv_weight).astype(low)
    grad_normed_mine = mm_t(grad_qkv[:half], qkv_weight).astype(low)
    own_grad_one, to_above, to_below = scatter_start(grad_normed_mine, swap_core(grad_normed_other))
    attn_parts, to_above, to_below = together(attn_parts, to_above, to_below)
    own_grad_one = scatter_end(own_grad_one, move_z(to_above, 1), move_z(to_below, -1))
    grad_input = (grad_middle + norm_back(own_hidden, factor_one[:TOK], gain_one, own_grad_one)).astype(low)
    ffn_sums, _ = together(ffn_sums, attn_grads)
    shared_shards = lax.all_gather(ffn_sums[:, :base], "expert", axis=0)
    attn_parts, shared_shards = together(attn_parts, shared_shards)
    attn_sums = jnp.sum(attn_parts.reshape(FSDP, TOK, 3 * HD).astype(wide), axis=0)
    out_sums = jnp.sum(out_parts.reshape(FSDP, TOK, 256).astype(wide), axis=0)

    own_weight = lax.dynamic_slice_in_dim(qkv_weight, place * TOK, TOK, 0)
    gain_part = jnp.sum(attn_sums * own_weight.astype(wide), axis=1, keepdims=True)
    gain_upper, gain_lower = halves(gain_part / attn_gain.astype(wide)[:, None])
    small = [gain_upper, gain_lower, small_sums.T.astype(low), jnp.zeros((TOK, 110), low)]
    shards = jnp.concatenate([attn_sums.astype(low), out_sums.astype(low), *small], axis=1)

    attn_shards = lax.all_gather(shards, "expert", axis=0)
    grad_shared_gate, grad_shared_up, grad_shared_down = finish_dense(shared_shards, spread, spread_rows)
    grad_w_query, grad_w_key, grad_w_value, grad_w_out, small = finish(attn_shards)
    grad_expert_gate = ffn_sums[:, base : base + FF].astype(wide)[:, None]
    grad_expert_up = ffn_sums[:, base + FF : base + 2 * FF].astype(wide)[:, None]
    grad_expert_down = unpack_tiles(ffn_sums[:, base + 2 * FF :], 1).astype(wide)[:, None]
    return (
        layer_out[None],
        grad_input[None],
        small[:, 0] + small[:, 1],
        grad_w_query,
        grad_w_key,
        grad_w_value,
        grad_w_out,
        small[:, 2] + small[:, 3],
        small[:, 4 : 4 + EXPERTS],
        grad_shared_gate,
        grad_shared_up,
        grad_shared_down,
        grad_expert_gate,
        grad_expert_up,
        grad_expert_down,
    )


def solution(mesh):
    in_specs = (
        P("expert", "fsdp", None),
        P("expert", "fsdp", None),
        P("expert", None),
        P("expert", "fsdp", None),
        P("fsdp"),
        P("fsdp", None),
        P("fsdp", None),
        P("fsdp", None),
        P("fsdp", None),
        P("fsdp"),
        P("fsdp", None),
        P("fsdp", None),
        P("fsdp", None),
        P("fsdp", None),
        P("fsdp", "expert", None),
        P("fsdp", "expert", None),
        P("fsdp", "expert", None),
    )
    out_specs = (
        P("expert", "fsdp", None),
        P("expert", "fsdp", None),
        P("fsdp"),
        P("fsdp", None),
        P("fsdp", None),
        P("fsdp", None),
        P("fsdp", None),
        P("fsdp"),
        P("fsdp", None),
        P("fsdp", None),
        P("fsdp", None),
        P("fsdp", None),
        P("fsdp", "expert", None),
        P("fsdp", "expert", None),
        P("fsdp", "expert", None),
    )
    return jax.shard_map(
        per_device, mesh=mesh, in_specs=in_specs, out_specs=out_specs, check_vma=False
    )
```

```python
import jax
import jax.numpy as jnp
from jax import lax
from jax.experimental import pallas as pl
from jax.experimental.pallas import tpu as pltpu
from jax.sharding import PartitionSpec as P

D = 2048
H = 16
KV = 4
HD = 128
FF = 1408
SH = 2816
TOPK = 2
TOK = 128
LENGTH = 2048
SEQS = 8
EXPERTS = 8
FSDP = 16
ALL = SEQS * TOK
CAP = 42
SLOTS = SEQS * CAP
SH_ROWS = SH // FSDP
SH_PART = SH_ROWS // EXPERTS
SH_PAD = 24
SH_OWN = FSDP * SH_PAD
QBLOCK = 256

eps_norm = 1e-06
rope_base = 600000.0
masked_fill = -1e30
low = jnp.bfloat16
wide = jnp.float32


def shift_pairs(step):
    return [(z * 2 + c, ((z + step) % 4) * 2 + c) for z in range(4) for c in range(2)]


core_pairs = [(z * 2 + c, z * 2 + 1 - c) for z in range(4) for c in range(2)]


def move_z(block, step):
    return lax.ppermute(block, "expert", shift_pairs(step))


def swap_core(block):
    return lax.ppermute(block, "expert", core_pairs)


def together(*values):
    return lax.optimization_barrier(values)


TOP = TOK // 2


def first_pieces(block):
    return move_z(block, 1), move_z(block, -1)


def other_pieces(block, below, above):
    upper, lower = move_z(below[:TOP], 1), move_z(above[TOP:], -1)
    mine = [block, above, upper, lower, below]
    return mine + [swap_core(piece) for piece in mine]


def gather_pieces(block):
    return other_pieces(block, *first_pieces(block))


PIECES = [(4 * side + block, start) for side in (0, 1) for block, start in ((0, 0), (1, 0), (2, 0), (2, TOP), (3, 0))]


def load_pieces(refs, rows_ref, extra_ref, sems):
    copies = []
    for index, (ref, (block, start)) in enumerate(zip(refs, PIECES)):
        count = min(ref.shape[0], TOK - start)
        copies.append(
            pltpu.make_async_copy(
                ref.at[pl.ds(0, count), :], rows_ref.at[pl.ds(block * TOK + start, count), :], sems.at[2 * index]
            )
        )
        if extra_ref is not None and ref.shape[0] > count:
            copies.append(
                pltpu.make_async_copy(
                    ref.at[pl.ds(count, 16), :], extra_ref.at[pl.ds(block * 16, 16), :], sems.at[2 * index + 1]
                )
            )
    for copy in copies:
        copy.start()
    return copies


def scatter_start(mine, received):
    chip = mine.reshape(4, TOK, -1).astype(wide) + received.reshape(4, TOK, -1).astype(wide)
    from_below = move_z(chip[2, :TOP].astype(low), 1)
    from_above = move_z(chip[2, TOP:].astype(low), -1)
    to_above = jnp.concatenate([chip[1, :TOP] + from_below.astype(wide), chip[1, TOP:]], axis=0)
    to_below = jnp.concatenate([chip[3, :TOP], chip[3, TOP:] + from_above.astype(wide)], axis=0)
    return chip[0], to_above.astype(low), to_below.astype(low)


def scatter_end(own, first, second):
    return own + first.astype(wide) + second.astype(wide)


def scatter_rows(mine, other):
    own, to_above, to_below = scatter_start(mine, swap_core(other))
    return scatter_end(own, move_z(to_above, 1), move_z(to_below, -1))


def exchange(mine, got):
    chip = jnp.stack([mine[1:], got[1:]], axis=1)
    return mine[0], got[0], *[move_z(chip[step - 1], step) for step in (1, 2, 3)]


def source_owners(expert):
    return jnp.stack([((expert // 2 - index // 2) % 4) * 2 + ((expert % 2) ^ (index % 2)) for index in range(EXPERTS)])


def relative_owner(expert, block):
    return ((expert // 2 + block % 4) % 4) * 2 + ((expert % 2) ^ (block // 4))


def pack_tiles(block):
    rows, columns = block.shape[0] // 8, block.shape[1] // 128
    tiles = block.reshape(rows, 8, columns, 128).transpose(2, 1, 0, 3)
    return tiles.reshape(columns * 8, rows * 128)


def unpack_tiles(block, count):
    rows, columns = block.shape[1] // 128, block.shape[0] // (8 * count)
    tiles = block.reshape(count, columns, 8, rows, 128).transpose(0, 3, 2, 1, 4)
    return tiles.reshape(count * rows * 8, columns * 128)


def product(left, right, contract):
    return lax.dot_general(left, right, (contract, ((), ())), preferred_element_type=wide)


def mm(left, right):
    return product(left, right, ((1,), (0,)))


def mm_t(left, right):
    return product(left, right, ((1,), (1,)))


def t_mm(left, right):
    return product(left, right, ((0,), (0,)))


def segment_columns(seg_blocks_ref):
    return seg_blocks_ref[...].T


def block_scores(qkv_ref, seg_row_ref, columns, start, reach):
    query = qkv_ref[pl.ds(start, QBLOCK), 0:HD]
    key = qkv_ref[pl.ds(0, reach), HD : 2 * HD]
    scores = mm_t(query, key) * HD ** (-0.5)
    query_pos = start + lax.broadcasted_iota(jnp.int32, (QBLOCK, reach), 0)
    key_pos = lax.broadcasted_iota(jnp.int32, (QBLOCK, reach), 1)
    block = start // TOK
    column = jnp.concatenate([columns[:, block : block + 1], columns[:, block + 1 : block + 2]], axis=0)
    same = column == seg_row_ref[:, pl.ds(0, reach)]
    return jnp.where(same & (query_pos >= key_pos), scores, masked_fill)


def attend_kernel(qkv_ref, seg_row_ref, seg_blocks_ref, mixed_ref, total_ref):
    columns = segment_columns(seg_blocks_ref)
    for block in range(LENGTH // QBLOCK):
        start, reach = block * QBLOCK, (block + 1) * QBLOCK
        scores = block_scores(qkv_ref, seg_row_ref, columns, start, reach)
        largest = jnp.max(scores, axis=-1, keepdims=True)
        exponent = jnp.exp(scores - largest)
        totals = jnp.sum(exponent, axis=-1, keepdims=True)
        probs_low = (exponent * (1.0 / totals)).astype(low)
        value = qkv_ref[pl.ds(0, reach), 2 * HD : 3 * HD]
        mixed_ref[pl.ds(start, QBLOCK), :] = mm(probs_low, value).astype(low)
        total_ref[pl.ds(start, QBLOCK), :] = largest + jnp.log(totals)


def attend_back_kernel(
    qkv_ref, grad_ref, total_ref, seg_row_ref, seg_blocks_ref, cos_ref, sin_ref, out_ref, small_ref, key_acc, value_acc
):
    columns = segment_columns(seg_blocks_ref)
    key_acc[...] = jnp.zeros_like(key_acc)
    value_acc[...] = jnp.zeros_like(value_acc)

    def turn_back(value, rows):
        return value * cos_ref[rows, :] + pltpu.roll(value, HD // 2, 1) * sin_ref[rows, :]

    for block in range(LENGTH // QBLOCK):
        start, reach = block * QBLOCK, (block + 1) * QBLOCK
        rows, span = pl.ds(start, QBLOCK), pl.ds(0, reach)
        scores = block_scores(qkv_ref, seg_row_ref, columns, start, reach)
        probs = jnp.exp(scores - total_ref[rows, :])
        tall = [pl.ds((start // TOK + part) * TALL, TOK) for part in range(QBLOCK // TOK)]
        grad = jnp.concatenate([grad_ref[part, :] for part in tall], axis=0)
        grad_probs = mm_t(grad, qkv_ref[span, 2 * HD : 3 * HD])
        inner = jnp.sum(probs * grad_probs, axis=-1, keepdims=True)
        grad_scores = (probs * (grad_probs - inner)).astype(low)
        scale = HD ** (-0.5)
        grad_query = mm(grad_scores, qkv_ref[span, HD : 2 * HD]) * scale
        out_ref[rows, 0:HD] = turn_back(grad_query, rows).astype(low)
        key_acc[span, :] += t_mm(grad_scores, qkv_ref[rows, 0:HD]) * scale
        value_acc[span, :] += t_mm(probs.astype(low), grad)
    for block in range(LENGTH // QBLOCK):
        rows = pl.ds(block * QBLOCK, QBLOCK)
        out_ref[rows, HD : 2 * HD] = turn_back(key_acc[rows, :], rows).astype(low)
        out_ref[rows, 2 * HD : 3 * HD] = value_acc[rows, :].astype(low)
    small = grad_ref[pl.ds(TOK, 16), :].astype(wide)
    for index in range(1, FSDP):
        small = small + grad_ref[pl.ds(index * TALL + TOK, 16), :].astype(wide)
    small_ref[...] = small


vmem = pl.BlockSpec(memory_space=pltpu.VMEM)
smem = pl.BlockSpec(memory_space=pltpu.SMEM)
anywhere = pl.BlockSpec(memory_space=pl.ANY)
kernel_params = pltpu.CompilerParams(vmem_limit_bytes=48 * 1024 * 1024)


def attend(qkv, seg_row, seg_blocks):
    return pl.pallas_call(
        attend_kernel,
        out_shape=(
            jax.ShapeDtypeStruct((LENGTH, HD), low),
            jax.ShapeDtypeStruct((LENGTH, 1), wide),
        ),
        in_specs=[vmem] * 3,
        out_specs=(vmem, vmem),
        compiler_params=kernel_params,
        cost_estimate=pl.CostEstimate(
            flops=2 * LENGTH * LENGTH * HD, bytes_accessed=4 * LENGTH * HD * 2, transcendentals=LENGTH * LENGTH // 2
        ),
        name="attend",
    )(qkv, seg_row, seg_blocks)


def attend_back(qkv, grad, total, seg_row, seg_blocks, cos_all, sin_all):
    return pl.pallas_call(
        attend_back_kernel,
        out_shape=(jax.ShapeDtypeStruct((LENGTH, 3 * HD), low), jax.ShapeDtypeStruct((16, TOK), wide)),
        in_specs=[vmem] * 7,
        out_specs=(vmem, vmem),
        scratch_shapes=[pltpu.VMEM((LENGTH, HD), wide), pltpu.VMEM((LENGTH, HD), wide)],
        compiler_params=kernel_params,
        cost_estimate=pl.CostEstimate(
            flops=5 * LENGTH * LENGTH * HD, bytes_accessed=8 * LENGTH * HD * 2, transcendentals=LENGTH * LENGTH // 2
        ),
        name="attend_back",
    )(qkv, grad, total, seg_row, seg_blocks, cos_all, sin_all)


ROWS = 256
FF_TILES = [(start, min(256, FF - start)) for start in range(0, FF, 256)]


def params(mebibytes):
    return pltpu.CompilerParams(vmem_limit_bytes=mebibytes * 1024 * 1024)


def cost(flops, moved, special=0):
    return pl.CostEstimate(flops=int(flops), bytes_accessed=int(moved), transcendentals=int(special))


def project_kernel(*refs):
    pieces, (attn_ref, cos_ref, sin_ref) = refs[:10], refs[10:13]
    normed_ref, sent_ref, factor_ref, gains_ref, ids_ref, hidden, sems = refs[13:]
    copies = load_pieces(pieces, hidden, ids_ref, sems)
    pick = lax.broadcasted_iota(jnp.int32, (16, TOK), 0) == lax.broadcasted_iota(jnp.int32, (16, TOK), 1)
    gains_ref[...] = mm_t(pick.astype(wide).astype(low), attn_ref[:, 768:896])
    for copy in copies:
        copy.wait()
    gain = gains_ref[0:1, :]

    @pl.loop(0, ALL // ROWS)
    def step(index):
        rows = pl.ds(index * ROWS, ROWS)
        values = hidden[rows, :].astype(wide)
        factor = lax.rsqrt(jnp.mean(values * values, axis=-1, keepdims=True) + eps_norm)
        factor_ref[rows, :] = factor
        normed = (values * factor * gain).astype(low)
        normed_ref[rows, :] = normed
        raw = mm(normed, attn_ref[:, 0:512])

        def turn(value):
            return (value * cos_ref[...] + pltpu.roll(value, HD // 2, 1) * sin_ref[...]).astype(low)

        key = turn(raw[:, 2 * HD : 3 * HD])
        value = raw[:, 3 * HD :].astype(low)
        for head in range(2):
            query = turn(raw[:, head * HD : (head + 1) * HD])
            for part in range(2):
                place = pl.ds(index * 4 * TOK + (2 * part + head) * TOK, TOK)
                within = slice(part * TOK, (part + 1) * TOK)
                sent_ref[place, 0:HD] = query[within]
                sent_ref[place, HD : 2 * HD] = key[within]
                sent_ref[place, 2 * HD : 3 * HD] = value[within]


def project(pieces, attn_all, cos_two, sin_two):
    return pl.pallas_call(
        project_kernel,
        out_shape=(
            jax.ShapeDtypeStruct((ALL, D), low),
            jax.ShapeDtypeStruct((LENGTH, 3 * HD), low),
            jax.ShapeDtypeStruct((ALL, 1), wide),
            jax.ShapeDtypeStruct((16, D), wide),
            jax.ShapeDtypeStruct((SEQS * 16, D), low),
        ),
        in_specs=[anywhere] * 10 + [vmem] * 3,
        out_specs=tuple([vmem] * 5),
        scratch_shapes=[pltpu.VMEM((ALL, D), low), pltpu.SemaphoreType.DMA((20,))],
        compiler_params=params(40),
        cost_estimate=cost(2.2e9, 16e6),
        name="project",
    )(*pieces, attn_all, cos_two, sin_two)


TALL = TOK + 16


def mix_back_kernel(place_ref, *refs):
    pieces, weight_ref, mixed_ref, small_ref = refs[:10], refs[10], refs[11], refs[12]
    sent_ref, mine_ref, other_ref, grad_ref, sems = refs[13:]
    for index in range(FSDP):
        sent_ref[pl.ds(index * TALL + TOK, 16), :] = small_ref[:, index * TOK : (index + 1) * TOK]
    for copy in load_pieces(pieces, grad_ref, None, sems):
        copy.wait()
    for index in range(ALL // ROWS):
        grad = mm_t(grad_ref[pl.ds(index * ROWS, ROWS), :], weight_ref[...]).astype(low)
        for part in range(2):
            for head in range(2):
                place = pl.ds((index * 4 + 2 * part + head) * TALL, TOK)
                sent_ref[place, :] = grad[part * TOK : (part + 1) * TOK, head * HD : (head + 1) * HD]
    for index in range(EXPERTS):
        columns = pl.ds(pl.multiple_of(place_ref[index] * 256, 256), 256)
        target = mine_ref if index < 4 else other_ref
        target[index % 4] = t_mm(mixed_ref[...], grad_ref[:, columns]).astype(low)


def mix_back(owners, pieces, weight, mixed, small):
    blocks = jax.ShapeDtypeStruct((4, 256, 256), low)
    return pl.pallas_call(
        mix_back_kernel,
        out_shape=(jax.ShapeDtypeStruct((FSDP * TALL, HD), low), blocks, blocks),
        in_specs=[smem] + [anywhere] * 10 + [vmem] * 3,
        out_specs=(vmem, vmem, vmem),
        scratch_shapes=[pltpu.VMEM((ALL, D), low), pltpu.SemaphoreType.DMA((20,))],
        compiler_params=params(60),
        cost_estimate=cost(2.2e9, 10e6),
        name="mix_back",
    )(owners, *pieces, weight, mixed, small)


def collect_kernel(core_ref, grads_ref, query_ref, mine_ref, other_ref):
    first = core_ref[0] == 0

    @pl.loop(0, SEQS)
    def step(index):
        rows = pl.ds(index * TOK, TOK)
        swapped = pl.ds(((index + SEQS // 2) % SEQS) * TOK, TOK)
        one = grads_ref[pl.ds(index * 2 * TOK, TOK), :]
        two = grads_ref[pl.ds(index * 2 * TOK + TOK, TOK), :]
        query_ref[rows, 0:HD] = one[:, :HD]
        query_ref[rows, HD : 2 * HD] = two[:, :HD]
        total = one[:, HD:].astype(wide) + two[:, HD:].astype(wide)
        lower = jnp.concatenate([total[:, : HD // 2], total[:, HD : HD + HD // 2]], axis=1)
        upper = jnp.concatenate([total[:, HD // 2 : HD], total[:, HD + HD // 2 :]], axis=1)
        mine_ref[rows, :] = jnp.where(first, lower, upper)
        other_ref[swapped, :] = jnp.where(first, upper, lower).astype(low)


def collect(core, grads):
    return pl.pallas_call(
        collect_kernel,
        out_shape=(
            jax.ShapeDtypeStruct((ALL, 2 * HD), low),
            jax.ShapeDtypeStruct((ALL, HD), wide),
            jax.ShapeDtypeStruct((ALL, HD), low),
        ),
        in_specs=[smem, vmem],
        out_specs=(vmem, vmem, vmem),
        compiler_params=params(32),
        cost_estimate=cost(1e6, 4e6),
        name="collect",
    )(core, grads)


def gather_rows_kernel(place_ref, *refs):
    parts, out_ref = refs[:5], refs[5]
    for index in range(EXPERTS):
        step, side = index // 2, index % 2
        rows = pl.ds(pl.multiple_of(place_ref[index] * 256, 256), 256)
        out_ref[rows, :] = parts[step + 1][side] if step else parts[side][...]


def gather_out(places, parts):
    return pl.pallas_call(
        gather_rows_kernel,
        out_shape=jax.ShapeDtypeStruct((D, 256), low),
        in_specs=[smem] + [vmem] * 5,
        out_specs=vmem,
        compiler_params=params(32),
        cost_estimate=cost(0, 2e6),
        name="gather_out",
    )(places, *parts)


def qkv_weights_kernel(normed_hbm, query_ref, mine_ref, got_ref, out_ref, grad_ref, normed_ref, sems):
    copies = []
    for index in range(D // ROWS):
        columns = pl.ds(index * ROWS, ROWS)
        copies.append(pltpu.make_async_copy(normed_hbm.at[:, columns], normed_ref.at[:, columns], sems.at[index]))
        copies[index].start()
    grad_ref[:, 0 : 2 * HD] = query_ref[...]
    grad_ref[:, 2 * HD : 3 * HD] = (mine_ref[...] + got_ref[...].astype(wide)).astype(low)
    for index in range(D // ROWS):
        rows = pl.ds(index * ROWS, ROWS)
        copies[index].wait()
        out_ref[rows, :] = t_mm(normed_ref[:, rows], grad_ref[...]).astype(low)


def qkv_weights(normed, query, mine, got):
    return pl.pallas_call(
        qkv_weights_kernel,
        out_shape=(jax.ShapeDtypeStruct((D, 3 * HD), low), jax.ShapeDtypeStruct((ALL, 3 * HD), low)),
        in_specs=[anywhere] + [vmem] * 3,
        out_specs=(vmem, vmem),
        scratch_shapes=[pltpu.VMEM((ALL, D), low), pltpu.SemaphoreType.DMA((D // ROWS,))],
        compiler_params=params(60),
        cost_estimate=cost(1.6e9, 8e6),
        name="qkv_weights",
    )(normed, query, mine, got)


def finish_kernel(shards_ref, query_ref, key_ref, value_ref, out_ref, gain_ref):
    gain = jnp.zeros((TOK, TOK), wide)
    for source in range(EXPERTS):
        query_ref[:, source * 256 : (source + 1) * 256] = shards_ref[source, :, 0:256].astype(wide)
        out_ref[:, source * 256 : (source + 1) * 256] = shards_ref[source, :, 384:640].astype(wide)
        gain = gain + shards_ref[source, :, 640:768].astype(wide)
    for pair in range(KV):
        one = shards_ref[2 * pair, :, 256:384].astype(wide)
        two = shards_ref[2 * pair + 1, :, 256:384].astype(wide)
        columns = slice(pair * HD, (pair + 1) * HD)
        key_ref[:, columns] = jnp.concatenate([one[:, : HD // 2], two[:, : HD // 2]], axis=1)
        value_ref[:, columns] = jnp.concatenate([one[:, HD // 2 :], two[:, HD // 2 :]], axis=1)
    gain_ref[...] = gain


def finish(shards):
    widths = (H * HD, KV * HD, KV * HD, H * HD, TOK)
    return pl.pallas_call(
        finish_kernel,
        out_shape=tuple(jax.ShapeDtypeStruct((TOK, width), wide) for width in widths),
        in_specs=[vmem],
        out_specs=tuple([vmem] * 5),
        compiler_params=params(32),
        cost_estimate=cost(1e6, 4e6),
        name="finish",
    )(shards)


def finish_dense_kernel(shards_ref, spread_ref, spread_rows_ref, gate_ref, up_ref, down_ref, left, rows_in):
    width = SH_OWN // 2
    for source in range(EXPERTS):
        for part in range(4):
            left[part * TOK : (part + 1) * TOK, source * width : (source + 1) * width] = shards_ref[
                source, :, part * width : (part + 1) * width
            ]
        packed = shards_ref[source, :, 2 * SH_OWN : 3 * SH_OWN].astype(wide)
        rows_in[source * SH_PAD : (source + 1) * SH_PAD, :] = pack_rows(packed)
    for start in range(0, SH // 2, 256):
        count = min(256, SH // 2 - start)
        both = mm(left[...], spread_ref[:, start : start + count])
        for part in range(4):
            target = gate_ref if part < 2 else up_ref
            begin = (part % 2) * (SH // 2) + start
            target[:, begin : begin + count] = both[part * TOK : (part + 1) * TOK]
    down_ref[...] = mm(spread_rows_ref[...], rows_in[...].astype(low))


def finish_dense(shards, spread, spread_rows):
    shapes = [(TOK, SH), (TOK, SH), (SH_ROWS, D)]
    return pl.pallas_call(
        finish_dense_kernel,
        out_shape=tuple(jax.ShapeDtypeStruct(shape, wide) for shape in shapes),
        in_specs=[vmem] * 3,
        out_specs=tuple([vmem] * 3),
        scratch_shapes=[
            pltpu.VMEM((4 * TOK, EXPERTS * SH_OWN // 2), low),
            pltpu.VMEM((EXPERTS * SH_PAD, D), wide),
        ],
        compiler_params=params(40),
        cost_estimate=cost(2.2e9, 12e6),
        name="finish_dense",
    )(shards, spread, spread_rows)


def halves(value):
    upper = value.astype(low)
    return upper, (value - upper.astype(wide)).astype(low)


def silu_parts(gate_value):
    sig = 1.0 / (1.0 + jnp.exp(-gate_value))
    return sig, gate_value * sig


def swiglu_back(sig, act, up_value, grad):
    return (grad * up_value * (sig + act * (1.0 - sig))).astype(low), (grad * act).astype(low)


def pack_rows(block):
    count, width = block.shape[0] // 8, block.shape[1] // 128
    return jnp.concatenate(
        [
            jnp.concatenate(
                [block[8 * i : 8 * i + 8, 128 * j : 128 * j + 128] for i in range(count)], axis=1
            )
            for j in range(width)
        ],
        axis=0,
    )


def slab(buffer, out_ref, sems, step, start, width):
    target = out_ref.at[pl.ds(step * ROWS, ROWS), pl.ds(start, width)]
    return pltpu.make_async_copy(buffer.at[step % 2, :, pl.ds(0, width)], target, sems.at[step % 2])


def send_slabs(tokens_ref, grad_ref, down_rows, out_ref, buffer, sems, start):
    width = grad_ref.shape[1]
    count = width // 2 // FSDP
    place = (start, width + width // 2)
    for step in range(D // ROWS):
        slot = step % 2
        if step >= 2:
            slab(buffer, out_ref, sems, step - 2, *place).wait()
        buffer[slot, :, 0:width] = t_mm(tokens_ref[:, pl.ds(step * ROWS, ROWS)], grad_ref[...]).astype(low)
        down = down_rows(step)
        for part in range(2):
            packed = pack_rows(down[part * count : (part + 1) * count]).astype(low)
            buffer[slot, part * TOK : (part + 1) * TOK, width : width + width // 2] = packed
        slab(buffer, out_ref, sems, step, *place).start()
    for step in (D // ROWS - 2, D // ROWS - 1):
        slab(buffer, out_ref, sems, step, *place).wait()


def ffn_kernel(*refs):
    expert_ref, slots_hbm, slots_t_hbm, routes_ref, router_hbm = refs[:5]
    pieces, cot_pieces, pack_ref = refs[5:15], refs[15:25], refs[25]
    grad_mine, grad_other, gates_ref, out_ref = refs[26:30]
    outs = refs[30:33]
    normed_ref, cot_ref, grad_ref = refs[33:36]
    kept = refs[36:44]
    hidden_s, grad_s, incoming, hidden_e, gated, grad_rows, grad_e, w_down_s = kept
    w_in_s, w_in, w_down, slots_ref, slots_t_ref = refs[44:49]
    raw, gate_parts, grad_in, buffer, piece_sems, cot_sems, sems, out_sems, slab_sems = refs[49:]
    base = 3 * SH_OWN
    half_d = D // 2

    def stage_shared(part):
        return pltpu.make_async_copy(
            pack_ref.at[pl.ds(part * half_d, half_d), pl.ds(2 * SH_OWN, SH_OWN)],
            grad_ref.at[:, pl.ds(FF + part * SH_OWN, SH_OWN)],
            sems.at[part],
        )

    def stage_down(part):
        return pltpu.make_async_copy(
            pack_ref.at[pl.ds(part * half_d, half_d), pl.ds(base + 2 * FF, FF)],
            grad_ref.at[:, pl.ds(0, FF)],
            sems.at[2 + part],
        )

    def unpack(target, pair, row, start, width):
        count = 2 * width // FSDP
        both = [
            pack_rows(grad_ref[row + part * TOK : row + (part + 1) * TOK, start : start + width].astype(wide))
            for part in range(2)
        ]
        target[pair * count : (pair + 1) * count, :] = jnp.concatenate(both, axis=0).astype(low)

    copies = [
        pltpu.make_async_copy(router_hbm, w_in_s.at[:, pl.ds(2 * SH_OWN, 128)], sems.at[4]),
        pltpu.make_async_copy(pack_ref.at[:, pl.ds(0, 2 * SH_OWN)], w_in_s.at[:, pl.ds(0, 2 * SH_OWN)], sems.at[5]),
        pltpu.make_async_copy(slots_hbm, slots_ref, sems.at[6]),
        pltpu.make_async_copy(pack_ref.at[:, pl.ds(base, 2 * FF)], w_in, sems.at[7]),
        pltpu.make_async_copy(slots_t_hbm, slots_t_ref, sems.at[8]),
    ]
    stage_shared(0).start()
    stage_shared(1).start()
    copies[0].start()
    copies[1].start()
    piece_copies = load_pieces(pieces, normed_ref, None, piece_sems)
    cot_copies = load_pieces(cot_pieces, cot_ref, None, cot_sems)
    stage_down(0).start()
    for copy in copies[2:]:
        copy.start()

    def send(index, source):
        copy = pltpu.make_async_copy(source, outs[index], out_sems.at[index])
        copy.start()
        return copy

    expert = expert_ref[0]
    lane = lax.broadcasted_iota(jnp.int32, (ROWS, 128), 1)
    for part in range(2):
        stage_shared(part).wait()
        for pair in range(4):
            unpack(w_down_s, part * 4 + pair, pair * 2 * TOK, FF + part * SH_OWN, SH_OWN)
    for copy in piece_copies + cot_copies + copies[:2]:
        copy.wait()
    stage_down(0).wait()
    for step in range(ALL // ROWS):
        unpack(w_down, step, step * 2 * TOK, 0, FF)
        rows = pl.ds(step * ROWS, ROWS)
        both = mm(normed_ref[rows, :], w_in_s[...])
        sig, act = silu_parts(both[:, :SH_OWN])
        up = both[:, SH_OWN : 2 * SH_OWN]
        hidden_s[rows, :] = (act * up).astype(low)
        grad_hidden = mm_t(cot_ref[rows, :], w_down_s[...])
        grad_gate, grad_up = swiglu_back(sig, act, up, grad_hidden)
        grad_s[rows, 0:SH_OWN] = grad_gate
        grad_s[rows, SH_OWN : 2 * SH_OWN] = grad_up
        logits = both[:, 2 * SH_OWN :]
        first, second = routes_ref[rows, 0:1], routes_ref[rows, 1:2]
        chosen_first = jnp.sum(jnp.where(lane == first + 2, logits, 0.0), axis=1, keepdims=True)
        chosen_second = jnp.sum(jnp.where(lane == second + 2, logits, 0.0), axis=1, keepdims=True)
        gate_first = 1.0 / (1.0 + jnp.exp(chosen_second - chosen_first))
        gate_second = 1.0 / (1.0 + jnp.exp(chosen_first - chosen_second))
        here = jnp.where(first == expert, gate_first, 0.0) + jnp.where(second == expert, gate_second, 0.0)
        upper, lower = halves(here)
        parts = jnp.where(lane == 0, upper.astype(wide), 0.0) + jnp.where(lane == 1, lower.astype(wide), 0.0)
        gate_parts[rows, :] = parts.astype(low)
        if step == 0:
            both_gates = jnp.where(lane == 0, gate_first, 0.0) + jnp.where(lane == 1, gate_second, 0.0)
            gates_ref[...] = both_gates[:TOK]
    stage_down(1).start()
    sent = [send(0, hidden_s)]
    down_copy = send(1, w_down_s)
    copies[2].wait()
    for step in range(D // ROWS):
        columns = pl.ds(step * ROWS, ROWS)
        incoming[:, columns] = mm(slots_ref[...], normed_ref[:, columns]).astype(low)
        grad_rows[:, columns] = mm(slots_ref[...], cot_ref[:, columns]).astype(low)
    slot_parts = mm(slots_ref[...], gate_parts[...])
    slot_gate = slot_parts[:, 0:1] + slot_parts[:, 1:2]
    copies[3].wait()
    stage_down(1).wait()
    for step in range(4):
        unpack(w_down, 4 + step, step * 2 * TOK, 0, FF)
    for step in range(2 * FF // ROWS):
        columns = pl.ds(step * ROWS, ROWS)
        raw[:, columns] = mm(incoming[...], w_in[:, columns])
    for start, width in FF_TILES:
        gate, up = raw[:, start : start + width], raw[:, FF + start : FF + start + width]
        hidden_e[:, start : start + width] = (silu_parts(gate)[1] * up).astype(low)
    slot_grad = jnp.zeros((SLOTS, 1), wide)
    for step in range(D // ROWS):
        columns = pl.ds(step * ROWS, ROWS)
        rows = mm(hidden_e[...], w_down[:, columns]).astype(low).astype(wide)
        cot = grad_rows[:, columns].astype(wide)
        gated[:, columns] = (rows * slot_gate).astype(low)
        grad_rows[:, columns] = (cot * slot_gate).astype(low)
        slot_grad = slot_grad + jnp.sum(rows * cot, axis=1, keepdims=True)
    sent.append(send(2, gated))
    for start, width in FF_TILES:
        grad_hidden = mm_t(grad_rows[...], w_down[pl.ds(start, width), :])
        sig, act = silu_parts(raw[:, start : start + width])
        grad_gate, grad_up = swiglu_back(sig, act, raw[:, FF + start : FF + start + width], grad_hidden)
        grad_e[:, start : start + width] = grad_gate
        grad_e[:, FF + start : FF + start + width] = grad_up
    for step in range(D // ROWS):
        columns = pl.ds(step * ROWS, ROWS)
        grad_in[:, columns] = mm_t(grad_e[...], w_in[columns, :]).astype(low)
    upper, lower = halves(slot_grad)
    slot_lane = lax.broadcasted_iota(jnp.int32, (SLOTS, 128), 1)
    slot_parts = (
        jnp.where(slot_lane == expert, upper.astype(wide), 0.0)
        + jnp.where(slot_lane == expert + 8, lower.astype(wide), 0.0)
    ).astype(low)
    copies[4].wait()
    half = ALL // 2
    for side, target in ((1, grad_other), (0, grad_mine)):
        for step in range(half // ROWS):
            rows = pl.ds(side * half + step * ROWS, ROWS)
            for tile in range(D // 512):
                columns = pl.ds(tile * 512, 512)
                grad_ref[rows, columns] = (
                    mm_t(grad_s[rows, :], w_in_s[columns, 0 : 2 * SH_OWN])
                    + mm(slots_t_ref[rows, :], grad_in[:, columns])
                ).astype(low)
            grad_ref[rows, D : D + 128] = mm(slots_t_ref[rows, :], slot_parts).astype(low)
        copy = pltpu.make_async_copy(grad_ref.at[pl.ds(side * half, half), :], target, sems.at[9 + side])
        copy.start()
        sent.append(copy)

    def expert_down(step):
        count = 2 * FF // FSDP
        return t_mm(hidden_e[:, step * count : (step + 1) * count], grad_rows[...])

    def shared_down(step):
        count = 2 * SH_PAD
        return w_down_s[step * count : (step + 1) * count, :].astype(wide)

    down_copy.wait()
    for step in range(D // ROWS):
        columns = pl.ds(step * ROWS, ROWS)
        w_down_s[:, columns] = t_mm(hidden_s[...], cot_ref[:, columns]).astype(low)
    send_slabs(incoming, grad_e, expert_down, out_ref, buffer, slab_sems, base)
    send_slabs(normed_ref, grad_s, shared_down, out_ref, buffer, slab_sems, 0)
    for copy in sent:
        copy.wait()


def ffn(expert, slots, slots_t, routes, router, pieces, cot_pieces, pack):
    outs = [(D, 3 * SH_OWN + 3 * FF), (ALL, SH_OWN), (SH_OWN, D), (SLOTS, D)]
    kept = [(ALL, SH_OWN), (ALL, 2 * SH_OWN), (SLOTS, D), (SLOTS, FF), (SLOTS, D), (SLOTS, D), (SLOTS, 2 * FF)]
    kept.append((SH_OWN, D))
    grads = [(ALL // 2, D + 128)] * 2
    return pl.pallas_call(
        ffn_kernel,
        out_shape=tuple(
            [jax.ShapeDtypeStruct(shape, low) for shape in grads]
            + [jax.ShapeDtypeStruct((TOK, 128), wide)]
            + [jax.ShapeDtypeStruct(shape, low) for shape in outs]
        ),
        in_specs=[smem, anywhere, anywhere, vmem] + [anywhere] * 22,
        out_specs=tuple([anywhere] * 2 + [vmem] + [anywhere] * 4),
        scratch_shapes=[pltpu.VMEM((ALL, D), low), pltpu.VMEM((ALL, D), low), pltpu.VMEM((ALL, D + 128), low)]
        + [pltpu.VMEM(shape, low) for shape in kept]
        + [
            pltpu.VMEM((D, 2 * SH_OWN + 128), low),
            pltpu.VMEM((D, 2 * FF), low),
            pltpu.VMEM((FF, D), low),
            pltpu.VMEM((SLOTS, ALL), low),
            pltpu.VMEM((ALL, SLOTS), low),
            pltpu.VMEM((SLOTS, 2 * FF), wide),
            pltpu.VMEM((ALL, 128), low),
            pltpu.VMEM((SLOTS, D), low),
            pltpu.VMEM((2, ROWS, 3 * FF), low),
            pltpu.SemaphoreType.DMA((20,)),
            pltpu.SemaphoreType.DMA((20,)),
            pltpu.SemaphoreType.DMA((11,)),
            pltpu.SemaphoreType.DMA((3,)),
            pltpu.SemaphoreType.DMA((2,)),
        ],
        compiler_params=params(60),
        cost_estimate=cost(38e9, 70e6, 1e6),
        name="ffn",
    )(expert, slots, slots_t, routes, router, *pieces, *cot_pieces, pack)


def out_rows_kernel(place_ref, *refs):
    parts, out_ref = refs[:5], refs[5]
    for index in range(EXPERTS):
        step, side = index // 2, index % 2
        columns = pl.ds(pl.multiple_of(place_ref[index] * 256, 256), 256)
        out_ref[:, columns] = parts[step + 1][side] if step else parts[side][...]


def out_rows(places, parts):
    return pl.pallas_call(
        out_rows_kernel,
        out_shape=jax.ShapeDtypeStruct((256, D), low),
        in_specs=[smem] + [vmem] * 5,
        out_specs=vmem,
        compiler_params=params(32),
        cost_estimate=cost(0, 2e6),
        name="out_rows",
    )(places, *parts)


def back_two_kernel(
    own_ref, first_ref, second_ref, middle_ref, cot_ref, gains_ref, gates_ref, routes_ref, block_ref, grad_ref, total_ref, logits_ref
):
    total = own_ref[...] + first_ref[...].astype(wide) + second_ref[...].astype(wide)
    lane = lax.broadcasted_iota(jnp.int32, (TOK, 128), 1)
    extra = total[:, D:]
    first, second = routes_ref[:, 0:1], routes_ref[:, 1:2]

    def taken(route):
        return jnp.sum(jnp.where((lane == route) | (lane == route + 8), extra, 0.0), axis=1, keepdims=True)

    gate_first, gate_second = gates_ref[:, 0:1], gates_ref[:, 1:2]
    taken_first, taken_second = taken(first), taken(second)
    inner = gate_first * taken_first + gate_second * taken_second
    chosen_first, chosen_second = gate_first * (taken_first - inner), gate_second * (taken_second - inner)
    logits = jnp.where(lane == first, chosen_first, 0.0) + jnp.where(lane == second, chosen_second, 0.0)
    grad = total[:, :D]
    for index in range(EXPERTS):
        grad = grad + logits[:, index : index + 1] * gains_ref[2 + index : 3 + index, :]
    middle = middle_ref[...]
    factor = lax.rsqrt(jnp.mean(middle * middle, axis=-1, keepdims=True) + eps_norm)
    scaled = grad * gains_ref[1:2, :]
    mean = jnp.mean(scaled * middle, axis=-1, keepdims=True)
    result = cot_ref[...].astype(wide) + factor * scaled - middle * (factor * factor * factor * mean)
    grad_ref[...] = result
    block_ref[...] = result.astype(low)
    total_ref[...] = grad
    logits_ref[...] = logits


def back_two(*operands):
    return pl.pallas_call(
        back_two_kernel,
        out_shape=(
            jax.ShapeDtypeStruct((TOK, D), low),
            jax.ShapeDtypeStruct((TOK, D), wide),
            jax.ShapeDtypeStruct((TOK, D), wide),
            jax.ShapeDtypeStruct((TOK, 128), wide),
        ),
        in_specs=[vmem] * 8,
        out_specs=(vmem, vmem, vmem, vmem),
        compiler_params=params(32),
        cost_estimate=cost(1e7, 6e6),
        name="back_two",
    )(*operands)


def small_rows_kernel(total_ref, logits_ref, middle_ref, gains_ref, out_ref):
    middle = middle_ref[...]
    factor = lax.rsqrt(jnp.mean(middle * middle, axis=-1, keepdims=True) + eps_norm)
    gain_upper, gain_lower = halves(jnp.sum(total_ref[...] * middle * factor, axis=0, keepdims=True))
    normed = (middle * factor * gains_ref[1:2, :]).astype(low)
    logit_upper, logit_lower = halves(logits_ref[...].T[0:EXPERTS, :])
    router = mm(logit_upper, normed) + mm(logit_lower, normed)
    small = [gain_upper.astype(wide), gain_lower.astype(wide), router, jnp.zeros((6, D), wide)]
    out_ref[...] = jnp.concatenate(small, axis=0).astype(low)


def small_rows(*operands):
    return pl.pallas_call(
        small_rows_kernel,
        out_shape=jax.ShapeDtypeStruct((16, D), low),
        in_specs=[vmem] * 4,
        out_specs=vmem,
        compiler_params=params(32),
        cost_estimate=cost(1e7, 3e6),
        name="small_rows",
    )(*operands)


def norm_factor(values):
    return lax.rsqrt(jnp.mean(values * values, axis=-1, keepdims=True) + eps_norm)


def norm_back(values, factor, gain, grad):
    scaled = grad * gain
    inner = jnp.mean(scaled * values, axis=-1, keepdims=True)
    return factor * scaled - values * (factor * factor * factor * inner)


def per_device(
    hidden_in,
    cotangent,
    segments,
    routes,
    attn_gain,
    w_query,
    w_key,
    w_value,
    w_out,
    ffn_gain,
    w_router,
    shared_gate,
    shared_up,
    shared_down,
    expert_gate,
    expert_up,
    expert_down,
):
    expert = lax.axis_index("expert")
    z, core = expert // 2, expert % 2
    place = lax.axis_index("fsdp")

    misc = jnp.concatenate(
        [attn_gain[:, None], ffn_gain[:, None], w_router, jnp.zeros((TOK, 118), low)], axis=1
    )
    attn_pack = jnp.concatenate(
        [
            lax.dynamic_slice_in_dim(w_query, 256 * expert, 256, 1),
            lax.dynamic_slice_in_dim(w_key, HD * z, HD, 1),
            lax.dynamic_slice_in_dim(w_value, HD * z, HD, 1),
            lax.dynamic_slice_in_dim(w_out, 256 * expert, 256, 1),
            misc,
        ],
        axis=1,
    )
    attn_all = lax.all_gather(attn_pack, "fsdp", axis=0, tiled=True)
    half_in, half_out = SH // 2, SH_OWN // 2
    sel_column = jnp.arange(half_out)
    picked = SH_ROWS * (sel_column // SH_PAD) + SH_PART * expert + sel_column % SH_PAD
    picked = jnp.where(sel_column % SH_PAD < SH_PART, picked, -1)
    select = (jnp.arange(half_in)[:, None] == picked[None, :]).astype(low)
    own_shared = mm(
        jnp.concatenate(
            [shared_gate[:, :half_in], shared_gate[:, half_in:], shared_up[:, :half_in], shared_up[:, half_in:]],
            axis=0,
        ),
        select,
    ).astype(low)
    own_down = jnp.pad(
        lax.dynamic_slice_in_dim(shared_down, SH_PART * expert, SH_PART, 0),
        ((0, SH_PAD - SH_PART), (0, 0)),
    )
    ffn_pack = jnp.concatenate(
        [
            own_shared[:TOK],
            own_shared[TOK : 2 * TOK],
            own_shared[2 * TOK : 3 * TOK],
            own_shared[3 * TOK :],
            pack_tiles(own_down),
            expert_gate[:, 0],
            expert_up[:, 0],
            pack_tiles(expert_down[:, 0]),
        ],
        axis=1,
    )
    ffn_all = lax.all_gather(ffn_pack, "fsdp", axis=0, tiled=True)

    ids = jnp.concatenate(
        [
            segments.astype(low),
            jnp.pad(routes[0].reshape(1, TOK * TOPK), ((0, 0), (0, LENGTH - TOK * TOPK))).astype(low),
            jnp.zeros((14, LENGTH), low),
        ],
        axis=0,
    )
    hidden_pieces = gather_pieces(jnp.concatenate([hidden_in[0], ids], axis=0))
    cot_block, *hidden_pieces = together(cotangent[0], *hidden_pieces)
    cot_first = first_pieces(cot_block)

    inverse_freq = rope_base ** (-jnp.arange(HD // 2, dtype=wide) * 2.0 / HD)
    angles = jnp.arange(LENGTH).astype(wide)[:, None] * inverse_freq[None, :]
    cosine, sine = jnp.cos(angles), jnp.sin(angles)
    cos_all = jnp.concatenate([cosine, cosine], axis=1)
    sin_back = jnp.concatenate([sine, -sine], axis=1)
    cos_own = lax.dynamic_slice_in_dim(cos_all, place * TOK, TOK, 0)
    sin_own = -lax.dynamic_slice_in_dim(sin_back, place * TOK, TOK, 0)
    cos_two, sin_two = jnp.concatenate([cos_own, cos_own]), jnp.concatenate([sin_own, sin_own])
    put_row = jnp.arange(SH_PAD * EXPERTS * FSDP // 2)
    source, within = put_row // half_out, put_row % half_out
    target = SH_ROWS * (within // SH_PAD) + SH_PART * source + within % SH_PAD
    target = jnp.where(within % SH_PAD < SH_PART, target, -1)
    spread = (target[:, None] == jnp.arange(half_in)[None, :]).astype(low)
    put_row = jnp.arange(EXPERTS * SH_PAD)
    target = SH_PART * (put_row // SH_PAD) + put_row % SH_PAD
    target = jnp.where(put_row % SH_PAD < SH_PART, target, -1)
    spread_rows = (jnp.arange(SH_ROWS)[:, None] == target[None, :]).astype(low)
    attn_all, cos_two, sin_two, cos_all, sin_back = together(attn_all, cos_two, sin_two, cos_all, sin_back)
    normed_one, sent, factor_one, gains, ids_all = project(hidden_pieces, attn_all, cos_two, sin_two)

    sent, cot_block, *cot_first = together(sent, cot_block, *cot_first)
    cot_pieces = other_pieces(cot_block, *cot_first)
    qkv = lax.all_to_all(sent, "fsdp", split_axis=0, concat_axis=0, tiled=True)

    ids_all = ids_all.reshape(SEQS, 16, D)
    seg_row = lax.dynamic_slice_in_dim(ids_all[:, 0].astype(wide), place // 2, 1, 0)
    seg_blocks = jnp.pad(seg_row.reshape(FSDP, TOK), ((0, TOK - FSDP), (0, 0)))
    route_all = ids_all[:, 1, : TOK * TOPK].astype(jnp.int32).reshape(ALL, TOPK)
    hit = jnp.any(route_all == expert, axis=1).astype(wide)
    order = jnp.arange(ALL)
    rank = mm(hit.astype(low)[None, :], (order[:, None] < order[None, :]).astype(low))
    slot_bool = (rank.astype(jnp.int32) == jnp.arange(SLOTS)[:, None]) & (hit > 0.5)[None, :]
    slots = slot_bool.astype(low)
    slots_t = slot_bool.T.astype(low)
    out_columns = attn_all[:, 512:768].reshape(EXPERTS, 256, 256)
    owners = jnp.stack([relative_owner(expert, block) for block in range(EXPERTS)])
    out_blocks = [lax.dynamic_index_in_dim(out_columns, owners[block], 0) for block in range(EXPERTS)]
    out_mine, out_other = jnp.concatenate(out_blocks[:4]), jnp.concatenate(out_blocks[4:])
    out_mine, out_other, _ = together(out_mine, out_other, sent)
    w_out_own = out_rows(source_owners(expert), exchange(out_mine, swap_core(out_other)))
    router = attn_all[:, 768:896]
    is_first = core == 0
    kv_weight = attn_all[:, 256:512].reshape(D, 2, 2, HD // 2)
    kv_weight = jnp.where(is_first, kv_weight[:, :, 0], kv_weight[:, :, 1]).reshape(D, HD)
    qkv_weight = jnp.concatenate([attn_all[:, :256], kv_weight], axis=1)
    route_own = route_all[:TOK]
    qkv, seg_row, seg_blocks, route_all, slots, slots_t, w_out_own, router, qkv_weight, route_own, *cot_pieces = together(
        qkv, seg_row, seg_blocks, route_all, slots, slots_t, w_out_own, router, qkv_weight, route_own, *cot_pieces
    )
    mixed_head, log_total = attend(qkv, seg_row, seg_blocks)
    mixed = (
        lax.all_to_all(mixed_head, "fsdp", split_axis=0, concat_axis=0, tiled=True)
        .reshape(SEQS, 2, TOK, HD)
        .transpose(0, 2, 1, 3)
        .reshape(ALL, 2 * HD)
    )
    own_hidden = hidden_in[0].astype(wide)
    half = ALL // 2
    middle = own_hidden + scatter_rows(
        mm(mixed[:half], w_out_own).astype(low), mm(mixed[half:], w_out_own).astype(low)
    )
    factor_two = norm_factor(middle)
    gain_one, gain_two = gains[0:1], gains[1:2]
    normed_block = (middle * factor_two * gain_two).astype(low)

    base = 3 * SH_OWN
    normed_pieces = gather_pieces(normed_block)
    grad_mine, grad_other, gates, ffn_grads, hidden_shared, shared_down_w, gated_rows = ffn(
        expert[None], slots, slots_t, route_all, router, normed_pieces, cot_pieces, ffn_all
    )
    ffn_sums = lax.psum_scatter(ffn_grads, "fsdp", scatter_dimension=0, tiled=True)
    own_grad, to_above, to_below = scatter_start(grad_mine, swap_core(grad_other))
    from_below, from_above = move_z(to_above, 1), move_z(to_below, -1)
    back_block, grad_middle, grad_two, grad_logits = back_two(
        own_grad, from_below, from_above, middle, cotangent[0], gains, gates, route_own
    )
    back_block, hidden_shared, gated_rows = together(back_block, hidden_shared, gated_rows)
    below, above = first_pieces(back_block)
    small = small_rows(grad_two, grad_logits, middle, gains)
    result_other = (mm(hidden_shared[half:], shared_down_w) + mm(slots_t[half:], gated_rows)).astype(low)
    result_mine = (mm(hidden_shared[:half], shared_down_w) + mm(slots_t[:half], gated_rows)).astype(low)
    below, above, result_other, result_mine, small = together(below, above, result_other, result_mine, small)
    back_pieces = other_pieces(back_block, below, above)

    sent_back, out_mine, out_other = mix_back(owners, back_pieces, w_out_own, mixed, small)
    grad_head = lax.all_to_all(sent_back, "fsdp", split_axis=0, concat_axis=0, tiled=True)
    grads_head, small_sums = attend_back(qkv, grad_head, log_total, seg_row, seg_blocks, cos_all, sin_back)
    grads_qkv = lax.all_to_all(grads_head, "fsdp", split_axis=0, concat_axis=0, tiled=True)
    result_other, result_mine, _ = together(result_other, result_mine, sent_back)
    result_got = swap_core(result_other)
    result_got, out_mine, out_other = together(result_got, out_mine, out_other)
    out_grads = gather_out(source_owners(expert), exchange(out_mine, swap_core(out_other)))
    result_own, to_above, to_below = scatter_start(result_mine, result_got)
    result_own = scatter_end(result_own, move_z(to_above, 1), move_z(to_below, -1))
    layer_out = (middle + result_own).astype(low)
    grads_qkv, layer_out, out_grads = together(grads_qkv, layer_out, out_grads)
    out_parts = lax.all_to_all(out_grads, "fsdp", split_axis=0, concat_axis=0, tiled=True)

    grad_query, kv_mine, kv_other = collect(core[None], grads_qkv)
    attn_grads, grad_qkv = qkv_weights(normed_one, grad_query, kv_mine, swap_core(kv_other))
    grad_normed_other = mm_t(grad_qkv[half:], qkv_weight).astype(low)
    grad_normed_mine = mm_t(grad_qkv[:half], qkv_weight).astype(low)
    ffn_sums, _ = together(ffn_sums, grads_qkv)
    attn_grads, out_parts, grad_normed_other, grad_normed_mine, shared_sums = together(
        attn_grads, out_parts, grad_normed_other, grad_normed_mine, ffn_sums[:, :base]
    )
    attn_parts = lax.all_to_all(attn_grads, "fsdp", split_axis=0, concat_axis=0, tiled=True)

    own_grad_one, to_above, to_below = scatter_start(grad_normed_mine, swap_core(grad_normed_other))
    attn_parts, to_above, to_below = together(attn_parts, to_above, to_below)
    own_grad_one = scatter_end(own_grad_one, move_z(to_above, 1), move_z(to_below, -1))
    grad_input = (grad_middle + norm_back(own_hidden, factor_one[:TOK], gain_one, own_grad_one)).astype(low)
    shared_shards = lax.all_gather(shared_sums, "expert", axis=0)
    attn_parts, shared_shards = together(attn_parts, shared_shards)
    attn_sums = jnp.sum(attn_parts.reshape(FSDP, TOK, 3 * HD).astype(wide), axis=0)
    out_sums = jnp.sum(out_parts.reshape(FSDP, TOK, 256).astype(wide), axis=0)

    own_weight = lax.dynamic_slice_in_dim(qkv_weight, place * TOK, TOK, 0)
    gain_part = jnp.sum(attn_sums * own_weight.astype(wide), axis=1, keepdims=True)
    gain_upper, gain_lower = halves(gain_part / attn_gain.astype(wide)[:, None])
    small = [gain_upper, gain_lower, small_sums.T.astype(low), jnp.zeros((TOK, 110), low)]
    shards = jnp.concatenate([attn_sums.astype(low), out_sums.astype(low), *small], axis=1)

    attn_shards = lax.all_gather(shards, "expert", axis=0)
    grad_shared_gate, grad_shared_up, grad_shared_down = finish_dense(shared_shards, spread, spread_rows)
    grad_w_query, grad_w_key, grad_w_value, grad_w_out, small = finish(attn_shards)
    grad_expert_gate = ffn_sums[:, base : base + FF].astype(wide)[:, None]
    grad_expert_up = ffn_sums[:, base + FF : base + 2 * FF].astype(wide)[:, None]
    grad_expert_down = unpack_tiles(ffn_sums[:, base + 2 * FF :], 1).astype(wide)[:, None]
    return (
        layer_out[None],
        grad_input[None],
        small[:, 0] + small[:, 1],
        grad_w_query,
        grad_w_key,
        grad_w_value,
        grad_w_out,
        small[:, 2] + small[:, 3],
        small[:, 4 : 4 + EXPERTS],
        grad_shared_gate,
        grad_shared_up,
        grad_shared_down,
        grad_expert_gate,
        grad_expert_up,
        grad_expert_down,
    )


def solution(mesh):
    in_specs = (
        P("expert", "fsdp", None),
        P("expert", "fsdp", None),
        P("expert", None),
        P("expert", "fsdp", None),
        P("fsdp"),
        P("fsdp", None),
        P("fsdp", None),
        P("fsdp", None),
        P("fsdp", None),
        P("fsdp"),
        P("fsdp", None),
        P("fsdp", None),
        P("fsdp", None),
        P("fsdp", None),
        P("fsdp", "expert", None),
        P("fsdp", "expert", None),
        P("fsdp", "expert", None),
    )
    out_specs = (
        P("expert", "fsdp", None),
        P("expert", "fsdp", None),
        P("fsdp"),
        P("fsdp", None),
        P("fsdp", None),
        P("fsdp", None),
        P("fsdp", None),
        P("fsdp"),
        P("fsdp", None),
        P("fsdp", None),
        P("fsdp", None),
        P("fsdp", None),
        P("fsdp", "expert", None),
        P("fsdp", "expert", None),
        P("fsdp", "expert", None),
    )
    return jax.shard_map(
        per_device, mesh=mesh, in_specs=in_specs, out_specs=out_specs, check_vma=False
    )
```

```python
import jax
import jax.numpy as jnp
from jax import lax
from jax.experimental import pallas as pl
from jax.experimental.pallas import tpu as pltpu
from jax.sharding import PartitionSpec as P

D = 2048
H = 16
KV = 4
HD = 128
FF = 1408
SH = 2816
TOPK = 2
TOK = 128
LENGTH = 2048
SEQS = 8
EXPERTS = 8
FSDP = 16
ALL = SEQS * TOK
CAP = 42
SLOTS = SEQS * CAP
SH_ROWS = SH // FSDP
SH_PART = SH_ROWS // EXPERTS
SH_PAD = 24
SH_OWN = FSDP * SH_PAD
QBLOCK = 256

eps_norm = 1e-06
rope_base = 600000.0
masked_fill = -1e30
low = jnp.bfloat16
wide = jnp.float32


def shift_pairs(step):
    return [(z * 2 + c, ((z + step) % 4) * 2 + c) for z in range(4) for c in range(2)]


core_pairs = [(z * 2 + c, z * 2 + 1 - c) for z in range(4) for c in range(2)]


def move_z(block, step):
    return lax.ppermute(block, "expert", shift_pairs(step))


def swap_core(block):
    return lax.ppermute(block, "expert", core_pairs)


def together(*values):
    return lax.optimization_barrier(values)


TOP = TOK // 2


def first_pieces(block):
    return move_z(block, 1), move_z(block, -1)


def other_pieces(block, below, above):
    upper, lower = move_z(below[:TOP], 1), move_z(above[TOP:], -1)
    mine = [block, above, upper, lower, below]
    return mine + [swap_core(piece) for piece in mine]


def gather_pieces(block):
    return other_pieces(block, *first_pieces(block))


PIECES = [(4 * side + block, start) for side in (0, 1) for block, start in ((0, 0), (1, 0), (2, 0), (2, TOP), (3, 0))]


def load_pieces(refs, rows_ref, extra_ref, sems):
    copies = []
    for index, (ref, (block, start)) in enumerate(zip(refs, PIECES)):
        count = min(ref.shape[0], TOK - start)
        copies.append(
            pltpu.make_async_copy(
                ref.at[pl.ds(0, count), :], rows_ref.at[pl.ds(block * TOK + start, count), :], sems.at[2 * index]
            )
        )
        if extra_ref is not None and ref.shape[0] > count:
            copies.append(
                pltpu.make_async_copy(
                    ref.at[pl.ds(count, 16), :], extra_ref.at[pl.ds(block * 16, 16), :], sems.at[2 * index + 1]
                )
            )
    for copy in copies:
        copy.start()
    return copies


def scatter_start(mine, received):
    chip = mine.reshape(4, TOK, -1).astype(wide) + received.reshape(4, TOK, -1).astype(wide)
    from_below = move_z(chip[2, :TOP].astype(low), 1)
    from_above = move_z(chip[2, TOP:].astype(low), -1)
    to_above = jnp.concatenate([chip[1, :TOP] + from_below.astype(wide), chip[1, TOP:]], axis=0)
    to_below = jnp.concatenate([chip[3, :TOP], chip[3, TOP:] + from_above.astype(wide)], axis=0)
    return chip[0], to_above.astype(low), to_below.astype(low)


def scatter_end(own, first, second):
    return own + first.astype(wide) + second.astype(wide)


def scatter_rows(mine, other):
    own, to_above, to_below = scatter_start(mine, swap_core(other))
    return scatter_end(own, move_z(to_above, 1), move_z(to_below, -1))


def exchange(mine, got):
    chip = jnp.stack([mine[1:], got[1:]], axis=1)
    return mine[0], got[0], *[move_z(chip[step - 1], step) for step in (1, 2, 3)]


def source_owners(expert):
    return jnp.stack([((expert // 2 - index // 2) % 4) * 2 + ((expert % 2) ^ (index % 2)) for index in range(EXPERTS)])


def relative_owner(expert, block):
    return ((expert // 2 + block % 4) % 4) * 2 + ((expert % 2) ^ (block // 4))


def pack_tiles(block):
    rows, columns = block.shape[0] // 8, block.shape[1] // 128
    tiles = block.reshape(rows, 8, columns, 128).transpose(2, 1, 0, 3)
    return tiles.reshape(columns * 8, rows * 128)


def unpack_tiles(block, count):
    rows, columns = block.shape[1] // 128, block.shape[0] // (8 * count)
    tiles = block.reshape(count, columns, 8, rows, 128).transpose(0, 3, 2, 1, 4)
    return tiles.reshape(count * rows * 8, columns * 128)


def product(left, right, contract):
    return lax.dot_general(left, right, (contract, ((), ())), preferred_element_type=wide)


def mm(left, right):
    return product(left, right, ((1,), (0,)))


def mm_t(left, right):
    return product(left, right, ((1,), (1,)))


def t_mm(left, right):
    return product(left, right, ((0,), (0,)))


def segment_columns(seg_blocks_ref):
    return seg_blocks_ref[...].T


def block_scores(qkv_ref, seg_row_ref, columns, start, reach):
    query = qkv_ref[pl.ds(start, QBLOCK), 0:HD]
    key = qkv_ref[pl.ds(0, reach), HD : 2 * HD]
    scores = mm_t(query, key) * HD ** (-0.5)
    query_pos = start + lax.broadcasted_iota(jnp.int32, (QBLOCK, reach), 0)
    key_pos = lax.broadcasted_iota(jnp.int32, (QBLOCK, reach), 1)
    block = start // TOK
    column = jnp.concatenate([columns[:, block : block + 1], columns[:, block + 1 : block + 2]], axis=0)
    same = column == seg_row_ref[:, pl.ds(0, reach)]
    return jnp.where(same & (query_pos >= key_pos), scores, masked_fill)


def attend_kernel(qkv_ref, seg_row_ref, seg_blocks_ref, mixed_ref, total_ref):
    columns = segment_columns(seg_blocks_ref)
    for block in range(LENGTH // QBLOCK):
        start, reach = block * QBLOCK, (block + 1) * QBLOCK
        scores = block_scores(qkv_ref, seg_row_ref, columns, start, reach)
        largest = jnp.max(scores, axis=-1, keepdims=True)
        exponent = jnp.exp(scores - largest)
        totals = jnp.sum(exponent, axis=-1, keepdims=True)
        probs_low = (exponent * (1.0 / totals)).astype(low)
        value = qkv_ref[pl.ds(0, reach), 2 * HD : 3 * HD]
        mixed_ref[pl.ds(start, QBLOCK), :] = mm(probs_low, value).astype(low)
        total_ref[pl.ds(start, QBLOCK), :] = largest + jnp.log(totals)


def attend_back_kernel(
    qkv_ref, grad_ref, total_ref, seg_row_ref, seg_blocks_ref, cos_ref, sin_ref, out_ref, small_ref, key_acc, value_acc
):
    columns = segment_columns(seg_blocks_ref)
    key_acc[...] = jnp.zeros_like(key_acc)
    value_acc[...] = jnp.zeros_like(value_acc)

    def turn_back(value, rows):
        return value * cos_ref[rows, :] + pltpu.roll(value, HD // 2, 1) * sin_ref[rows, :]

    for block in range(LENGTH // QBLOCK):
        start, reach = block * QBLOCK, (block + 1) * QBLOCK
        rows, span = pl.ds(start, QBLOCK), pl.ds(0, reach)
        scores = block_scores(qkv_ref, seg_row_ref, columns, start, reach)
        probs = jnp.exp(scores - total_ref[rows, :])
        tall = [pl.ds((start // TOK + part) * TALL, TOK) for part in range(QBLOCK // TOK)]
        grad = jnp.concatenate([grad_ref[part, :] for part in tall], axis=0)
        grad_probs = mm_t(grad, qkv_ref[span, 2 * HD : 3 * HD])
        inner = jnp.sum(probs * grad_probs, axis=-1, keepdims=True)
        grad_scores = (probs * (grad_probs - inner)).astype(low)
        scale = HD ** (-0.5)
        grad_query = mm(grad_scores, qkv_ref[span, HD : 2 * HD]) * scale
        out_ref[rows, 0:HD] = turn_back(grad_query, rows).astype(low)
        key_acc[span, :] += t_mm(grad_scores, qkv_ref[rows, 0:HD]) * scale
        value_acc[span, :] += t_mm(probs.astype(low), grad)
    for block in range(LENGTH // QBLOCK):
        rows = pl.ds(block * QBLOCK, QBLOCK)
        out_ref[rows, HD : 2 * HD] = turn_back(key_acc[rows, :], rows).astype(low)
        out_ref[rows, 2 * HD : 3 * HD] = value_acc[rows, :].astype(low)
    small = grad_ref[pl.ds(TOK, 16), :].astype(wide)
    for index in range(1, FSDP):
        small = small + grad_ref[pl.ds(index * TALL + TOK, 16), :].astype(wide)
    small_ref[...] = small


vmem = pl.BlockSpec(memory_space=pltpu.VMEM)
smem = pl.BlockSpec(memory_space=pltpu.SMEM)
anywhere = pl.BlockSpec(memory_space=pl.ANY)
kernel_params = pltpu.CompilerParams(vmem_limit_bytes=48 * 1024 * 1024)


def attend(qkv, seg_row, seg_blocks):
    return pl.pallas_call(
        attend_kernel,
        out_shape=(
            jax.ShapeDtypeStruct((LENGTH, HD), low),
            jax.ShapeDtypeStruct((LENGTH, 1), wide),
        ),
        in_specs=[vmem] * 3,
        out_specs=(vmem, vmem),
        compiler_params=kernel_params,
        cost_estimate=pl.CostEstimate(
            flops=2 * LENGTH * LENGTH * HD, bytes_accessed=4 * LENGTH * HD * 2, transcendentals=LENGTH * LENGTH // 2
        ),
        name="attend",
    )(qkv, seg_row, seg_blocks)


def attend_back(qkv, grad, total, seg_row, seg_blocks, cos_all, sin_all):
    return pl.pallas_call(
        attend_back_kernel,
        out_shape=(jax.ShapeDtypeStruct((LENGTH, 3 * HD), low), jax.ShapeDtypeStruct((16, TOK), wide)),
        in_specs=[vmem] * 7,
        out_specs=(vmem, vmem),
        scratch_shapes=[pltpu.VMEM((LENGTH, HD), wide), pltpu.VMEM((LENGTH, HD), wide)],
        compiler_params=kernel_params,
        cost_estimate=pl.CostEstimate(
            flops=5 * LENGTH * LENGTH * HD, bytes_accessed=8 * LENGTH * HD * 2, transcendentals=LENGTH * LENGTH // 2
        ),
        name="attend_back",
    )(qkv, grad, total, seg_row, seg_blocks, cos_all, sin_all)


ROWS = 256
FF_TILES = [(start, min(256, FF - start)) for start in range(0, FF, 256)]


def params(mebibytes):
    return pltpu.CompilerParams(vmem_limit_bytes=mebibytes * 1024 * 1024)


def cost(flops, moved, special=0):
    return pl.CostEstimate(flops=int(flops), bytes_accessed=int(moved), transcendentals=int(special))


def project_kernel(*refs):
    pieces, (attn_ref, cos_ref, sin_ref) = refs[:10], refs[10:13]
    normed_ref, sent_ref, factor_ref, gains_ref, ids_ref, hidden, sems = refs[13:]
    copies = load_pieces(pieces, hidden, ids_ref, sems)
    pick = lax.broadcasted_iota(jnp.int32, (16, TOK), 0) == lax.broadcasted_iota(jnp.int32, (16, TOK), 1)
    gains_ref[...] = mm_t(pick.astype(wide).astype(low), attn_ref[:, 768:896])
    for copy in copies:
        copy.wait()
    gain = gains_ref[0:1, :]

    @pl.loop(0, ALL // ROWS)
    def step(index):
        rows = pl.ds(index * ROWS, ROWS)
        values = hidden[rows, :].astype(wide)
        factor = lax.rsqrt(jnp.mean(values * values, axis=-1, keepdims=True) + eps_norm)
        factor_ref[rows, :] = factor
        normed = (values * factor * gain).astype(low)
        normed_ref[rows, :] = normed
        raw = mm(normed, attn_ref[:, 0:512])

        def turn(value):
            return (value * cos_ref[...] + pltpu.roll(value, HD // 2, 1) * sin_ref[...]).astype(low)

        key = turn(raw[:, 2 * HD : 3 * HD])
        value = raw[:, 3 * HD :].astype(low)
        for head in range(2):
            query = turn(raw[:, head * HD : (head + 1) * HD])
            for part in range(2):
                place = pl.ds(index * 4 * TOK + (2 * part + head) * TOK, TOK)
                within = slice(part * TOK, (part + 1) * TOK)
                sent_ref[place, 0:HD] = query[within]
                sent_ref[place, HD : 2 * HD] = key[within]
                sent_ref[place, 2 * HD : 3 * HD] = value[within]


def project(pieces, attn_all, cos_two, sin_two):
    return pl.pallas_call(
        project_kernel,
        out_shape=(
            jax.ShapeDtypeStruct((ALL, D), low),
            jax.ShapeDtypeStruct((LENGTH, 3 * HD), low),
            jax.ShapeDtypeStruct((ALL, 1), wide),
            jax.ShapeDtypeStruct((16, D), wide),
            jax.ShapeDtypeStruct((SEQS * 16, D), low),
        ),
        in_specs=[anywhere] * 10 + [vmem] * 3,
        out_specs=tuple([vmem] * 5),
        scratch_shapes=[pltpu.VMEM((ALL, D), low), pltpu.SemaphoreType.DMA((20,))],
        compiler_params=params(40),
        cost_estimate=cost(2.2e9, 16e6),
        name="project",
    )(*pieces, attn_all, cos_two, sin_two)


TALL = TOK + 16


def mix_back_kernel(*refs):
    pieces, weight_ref, small_ref = refs[:10], refs[10], refs[11]
    sent_ref, grad_ref, sems = refs[12:]
    for index in range(FSDP):
        sent_ref[pl.ds(index * TALL + TOK, 16), :] = small_ref[:, index * TOK : (index + 1) * TOK]
    for copy in load_pieces(pieces, grad_ref, None, sems):
        copy.wait()
    for index in range(ALL // ROWS):
        grad = mm_t(grad_ref[pl.ds(index * ROWS, ROWS), :], weight_ref[...]).astype(low)
        for part in range(2):
            for head in range(2):
                place = pl.ds((index * 4 + 2 * part + head) * TALL, TOK)
                sent_ref[place, :] = grad[part * TOK : (part + 1) * TOK, head * HD : (head + 1) * HD]


def mix_back(pieces, weight, small):
    return pl.pallas_call(
        mix_back_kernel,
        out_shape=(jax.ShapeDtypeStruct((FSDP * TALL, HD), low), jax.ShapeDtypeStruct((ALL, D), low)),
        in_specs=[anywhere] * 10 + [vmem] * 2,
        out_specs=(vmem, vmem),
        scratch_shapes=[pltpu.SemaphoreType.DMA((20,))],
        compiler_params=params(60),
        cost_estimate=cost(1.1e9, 10e6),
        name="mix_back",
    )(*pieces, weight, small)


def out_weights_kernel(place_ref, mixed_ref, grad_ref, mine_ref, other_ref):
    for index in range(EXPERTS):
        columns = pl.ds(pl.multiple_of(place_ref[index] * 256, 256), 256)
        target = mine_ref if index < 4 else other_ref
        target[index % 4] = t_mm(mixed_ref[...], grad_ref[:, columns]).astype(low)


def out_weights(owners, mixed, grad):
    blocks = jax.ShapeDtypeStruct((4, 256, 256), low)
    return pl.pallas_call(
        out_weights_kernel,
        out_shape=(blocks, blocks),
        in_specs=[smem, vmem, vmem],
        out_specs=(vmem, vmem),
        compiler_params=params(32),
        cost_estimate=cost(1.1e9, 6e6),
        name="out_weights",
    )(owners, mixed, grad)


def collect_kernel(core_ref, grads_ref, query_ref, mine_ref, other_ref):
    first = core_ref[0] == 0

    @pl.loop(0, SEQS)
    def step(index):
        rows = pl.ds(index * TOK, TOK)
        swapped = pl.ds(((index + SEQS // 2) % SEQS) * TOK, TOK)
        one = grads_ref[pl.ds(index * 2 * TOK, TOK), :]
        two = grads_ref[pl.ds(index * 2 * TOK + TOK, TOK), :]
        query_ref[rows, 0:HD] = one[:, :HD]
        query_ref[rows, HD : 2 * HD] = two[:, :HD]
        total = one[:, HD:].astype(wide) + two[:, HD:].astype(wide)
        lower = jnp.concatenate([total[:, : HD // 2], total[:, HD : HD + HD // 2]], axis=1)
        upper = jnp.concatenate([total[:, HD // 2 : HD], total[:, HD + HD // 2 :]], axis=1)
        mine_ref[rows, :] = jnp.where(first, lower, upper)
        other_ref[swapped, :] = jnp.where(first, upper, lower).astype(low)


def collect(core, grads):
    return pl.pallas_call(
        collect_kernel,
        out_shape=(
            jax.ShapeDtypeStruct((ALL, 2 * HD), low),
            jax.ShapeDtypeStruct((ALL, HD), wide),
            jax.ShapeDtypeStruct((ALL, HD), low),
        ),
        in_specs=[smem, vmem],
        out_specs=(vmem, vmem, vmem),
        compiler_params=params(32),
        cost_estimate=cost(1e6, 4e6),
        name="collect",
    )(core, grads)


def gather_rows_kernel(place_ref, *refs):
    parts, out_ref = refs[:5], refs[5]
    for index in range(EXPERTS):
        step, side = index // 2, index % 2
        rows = pl.ds(pl.multiple_of(place_ref[index] * 256, 256), 256)
        out_ref[rows, :] = parts[step + 1][side] if step else parts[side][...]


def gather_out(places, parts):
    return pl.pallas_call(
        gather_rows_kernel,
        out_shape=jax.ShapeDtypeStruct((D, 256), low),
        in_specs=[smem] + [vmem] * 5,
        out_specs=vmem,
        compiler_params=params(32),
        cost_estimate=cost(0, 2e6),
        name="gather_out",
    )(places, *parts)


def qkv_weights_kernel(normed_hbm, query_ref, mine_ref, got_ref, out_ref, grad_ref, normed_ref, sems):
    copies = []
    for index in range(D // ROWS):
        columns = pl.ds(index * ROWS, ROWS)
        copies.append(pltpu.make_async_copy(normed_hbm.at[:, columns], normed_ref.at[:, columns], sems.at[index]))
        copies[index].start()
    grad_ref[:, 0 : 2 * HD] = query_ref[...]
    grad_ref[:, 2 * HD : 3 * HD] = (mine_ref[...] + got_ref[...].astype(wide)).astype(low)
    for index in range(D // ROWS):
        rows = pl.ds(index * ROWS, ROWS)
        copies[index].wait()
        out_ref[rows, :] = t_mm(normed_ref[:, rows], grad_ref[...]).astype(low)


def qkv_weights(normed, query, mine, got):
    return pl.pallas_call(
        qkv_weights_kernel,
        out_shape=(jax.ShapeDtypeStruct((D, 3 * HD), low), jax.ShapeDtypeStruct((ALL, 3 * HD), low)),
        in_specs=[anywhere] + [vmem] * 3,
        out_specs=(vmem, vmem),
        scratch_shapes=[pltpu.VMEM((ALL, D), low), pltpu.SemaphoreType.DMA((D // ROWS,))],
        compiler_params=params(60),
        cost_estimate=cost(1.6e9, 8e6),
        name="qkv_weights",
    )(normed, query, mine, got)


def finish_kernel(shards_ref, query_ref, key_ref, value_ref, out_ref, gain_ref):
    gain = jnp.zeros((TOK, TOK), wide)
    for source in range(EXPERTS):
        query_ref[:, source * 256 : (source + 1) * 256] = shards_ref[source, :, 0:256].astype(wide)
        out_ref[:, source * 256 : (source + 1) * 256] = shards_ref[source, :, 384:640].astype(wide)
        gain = gain + shards_ref[source, :, 640:768].astype(wide)
    for pair in range(KV):
        one = shards_ref[2 * pair, :, 256:384].astype(wide)
        two = shards_ref[2 * pair + 1, :, 256:384].astype(wide)
        columns = slice(pair * HD, (pair + 1) * HD)
        key_ref[:, columns] = jnp.concatenate([one[:, : HD // 2], two[:, : HD // 2]], axis=1)
        value_ref[:, columns] = jnp.concatenate([one[:, HD // 2 :], two[:, HD // 2 :]], axis=1)
    gain_ref[...] = gain


def finish(shards):
    widths = (H * HD, KV * HD, KV * HD, H * HD, TOK)
    return pl.pallas_call(
        finish_kernel,
        out_shape=tuple(jax.ShapeDtypeStruct((TOK, width), wide) for width in widths),
        in_specs=[vmem],
        out_specs=tuple([vmem] * 5),
        compiler_params=params(32),
        cost_estimate=cost(1e6, 4e6),
        name="finish",
    )(shards)


def finish_dense_kernel(shards_ref, spread_ref, spread_rows_ref, gate_ref, up_ref, down_ref, left, rows_in):
    width = SH_OWN // 2
    for source in range(EXPERTS):
        for part in range(4):
            left[part * TOK : (part + 1) * TOK, source * width : (source + 1) * width] = shards_ref[
                source, :, part * width : (part + 1) * width
            ]
        packed = shards_ref[source, :, 2 * SH_OWN : 3 * SH_OWN].astype(wide)
        rows_in[source * SH_PAD : (source + 1) * SH_PAD, :] = pack_rows(packed)
    for start in range(0, SH // 2, 256):
        count = min(256, SH // 2 - start)
        both = mm(left[...], spread_ref[:, start : start + count])
        for part in range(4):
            target = gate_ref if part < 2 else up_ref
            begin = (part % 2) * (SH // 2) + start
            target[:, begin : begin + count] = both[part * TOK : (part + 1) * TOK]
    down_ref[...] = mm(spread_rows_ref[...], rows_in[...].astype(low))


def finish_dense(shards, spread, spread_rows):
    shapes = [(TOK, SH), (TOK, SH), (SH_ROWS, D)]
    return pl.pallas_call(
        finish_dense_kernel,
        out_shape=tuple(jax.ShapeDtypeStruct(shape, wide) for shape in shapes),
        in_specs=[vmem] * 3,
        out_specs=tuple([vmem] * 3),
        scratch_shapes=[
            pltpu.VMEM((4 * TOK, EXPERTS * SH_OWN // 2), low),
            pltpu.VMEM((EXPERTS * SH_PAD, D), wide),
        ],
        compiler_params=params(40),
        cost_estimate=cost(2.2e9, 12e6),
        name="finish_dense",
    )(shards, spread, spread_rows)


def halves(value):
    upper = value.astype(low)
    return upper, (value - upper.astype(wide)).astype(low)


def silu_parts(gate_value):
    sig = 1.0 / (1.0 + jnp.exp(-gate_value))
    return sig, gate_value * sig


def swiglu_back(sig, act, up_value, grad):
    return (grad * up_value * (sig + act * (1.0 - sig))).astype(low), (grad * act).astype(low)


def pack_rows(block):
    count, width = block.shape[0] // 8, block.shape[1] // 128
    return jnp.concatenate(
        [
            jnp.concatenate(
                [block[8 * i : 8 * i + 8, 128 * j : 128 * j + 128] for i in range(count)], axis=1
            )
            for j in range(width)
        ],
        axis=0,
    )


def slab(buffer, out_ref, sems, step, start, width):
    target = out_ref.at[pl.ds(step * ROWS, ROWS), pl.ds(start, width)]
    return pltpu.make_async_copy(buffer.at[step % 2, :, pl.ds(0, width)], target, sems.at[step % 2])


def send_slabs(tokens_ref, grad_ref, down_rows, out_ref, buffer, sems, start):
    width = grad_ref.shape[1]
    count = width // 2 // FSDP
    place = (start, width + width // 2)
    for step in range(D // ROWS):
        slot = step % 2
        if step >= 2:
            slab(buffer, out_ref, sems, step - 2, *place).wait()
        buffer[slot, :, 0:width] = t_mm(tokens_ref[:, pl.ds(step * ROWS, ROWS)], grad_ref[...]).astype(low)
        down = down_rows(step)
        for part in range(2):
            packed = pack_rows(down[part * count : (part + 1) * count]).astype(low)
            buffer[slot, part * TOK : (part + 1) * TOK, width : width + width // 2] = packed
        slab(buffer, out_ref, sems, step, *place).start()
    for step in (D // ROWS - 2, D // ROWS - 1):
        slab(buffer, out_ref, sems, step, *place).wait()


def ffn_kernel(*refs):
    expert_ref, slots_hbm, slots_t_hbm, routes_ref, router_hbm = refs[:5]
    pieces, cot_pieces, pack_ref = refs[5:15], refs[15:25], refs[25]
    grad_mine, grad_other, gates_ref, out_ref = refs[26:30]
    outs = refs[30:33]
    normed_ref, cot_ref, grad_ref = refs[33:36]
    kept = refs[36:44]
    hidden_s, grad_s, incoming, hidden_e, gated, grad_rows, grad_e, w_down_s = kept
    w_in_s, w_in, w_down, slots_ref, slots_t_ref = refs[44:49]
    raw, gate_parts, grad_in, buffer, piece_sems, cot_sems, sems, out_sems, slab_sems = refs[49:]
    base = 3 * SH_OWN
    half_d = D // 2

    def stage_shared(part):
        return pltpu.make_async_copy(
            pack_ref.at[pl.ds(part * half_d, half_d), pl.ds(2 * SH_OWN, SH_OWN)],
            grad_ref.at[:, pl.ds(FF + part * SH_OWN, SH_OWN)],
            sems.at[part],
        )

    def stage_down(part):
        return pltpu.make_async_copy(
            pack_ref.at[pl.ds(part * half_d, half_d), pl.ds(base + 2 * FF, FF)],
            grad_ref.at[:, pl.ds(0, FF)],
            sems.at[2 + part],
        )

    def unpack(target, pair, row, start, width):
        count = 2 * width // FSDP
        both = [
            pack_rows(grad_ref[row + part * TOK : row + (part + 1) * TOK, start : start + width].astype(wide))
            for part in range(2)
        ]
        target[pair * count : (pair + 1) * count, :] = jnp.concatenate(both, axis=0).astype(low)

    copies = [
        pltpu.make_async_copy(router_hbm, w_in_s.at[:, pl.ds(2 * SH_OWN, 128)], sems.at[4]),
        pltpu.make_async_copy(pack_ref.at[:, pl.ds(0, 2 * SH_OWN)], w_in_s.at[:, pl.ds(0, 2 * SH_OWN)], sems.at[5]),
        pltpu.make_async_copy(slots_hbm, slots_ref, sems.at[6]),
        pltpu.make_async_copy(pack_ref.at[:, pl.ds(base, 2 * FF)], w_in, sems.at[7]),
        pltpu.make_async_copy(slots_t_hbm, slots_t_ref, sems.at[8]),
    ]
    stage_shared(0).start()
    stage_shared(1).start()
    copies[0].start()
    copies[1].start()
    piece_copies = load_pieces(pieces, normed_ref, None, piece_sems)
    cot_copies = load_pieces(cot_pieces, cot_ref, None, cot_sems)
    stage_down(0).start()
    for copy in copies[2:]:
        copy.start()

    def send(index, source):
        copy = pltpu.make_async_copy(source, outs[index], out_sems.at[index])
        copy.start()
        return copy

    expert = expert_ref[0]
    lane = lax.broadcasted_iota(jnp.int32, (ROWS, 128), 1)
    for part in range(2):
        stage_shared(part).wait()
        for pair in range(4):
            unpack(w_down_s, part * 4 + pair, pair * 2 * TOK, FF + part * SH_OWN, SH_OWN)
    for copy in piece_copies + cot_copies + copies[:2]:
        copy.wait()
    stage_down(0).wait()
    for step in range(ALL // ROWS):
        unpack(w_down, step, step * 2 * TOK, 0, FF)
        rows = pl.ds(step * ROWS, ROWS)
        both = mm(normed_ref[rows, :], w_in_s[...])
        sig, act = silu_parts(both[:, :SH_OWN])
        up = both[:, SH_OWN : 2 * SH_OWN]
        hidden_s[rows, :] = (act * up).astype(low)
        grad_hidden = mm_t(cot_ref[rows, :], w_down_s[...])
        grad_gate, grad_up = swiglu_back(sig, act, up, grad_hidden)
        grad_s[rows, 0:SH_OWN] = grad_gate
        grad_s[rows, SH_OWN : 2 * SH_OWN] = grad_up
        logits = both[:, 2 * SH_OWN :]
        first, second = routes_ref[rows, 0:1], routes_ref[rows, 1:2]
        chosen_first = jnp.sum(jnp.where(lane == first + 2, logits, 0.0), axis=1, keepdims=True)
        chosen_second = jnp.sum(jnp.where(lane == second + 2, logits, 0.0), axis=1, keepdims=True)
        gate_first = 1.0 / (1.0 + jnp.exp(chosen_second - chosen_first))
        gate_second = 1.0 / (1.0 + jnp.exp(chosen_first - chosen_second))
        here = jnp.where(first == expert, gate_first, 0.0) + jnp.where(second == expert, gate_second, 0.0)
        upper, lower = halves(here)
        parts = jnp.where(lane == 0, upper.astype(wide), 0.0) + jnp.where(lane == 1, lower.astype(wide), 0.0)
        gate_parts[rows, :] = parts.astype(low)
        if step == 0:
            both_gates = jnp.where(lane == 0, gate_first, 0.0) + jnp.where(lane == 1, gate_second, 0.0)
            gates_ref[...] = both_gates[:TOK]
    stage_down(1).start()
    sent = [send(0, hidden_s)]
    down_copy = send(1, w_down_s)
    copies[2].wait()
    for step in range(D // ROWS):
        columns = pl.ds(step * ROWS, ROWS)
        incoming[:, columns] = mm(slots_ref[...], normed_ref[:, columns]).astype(low)
        grad_rows[:, columns] = mm(slots_ref[...], cot_ref[:, columns]).astype(low)
    slot_parts = mm(slots_ref[...], gate_parts[...])
    slot_gate = slot_parts[:, 0:1] + slot_parts[:, 1:2]
    copies[3].wait()
    stage_down(1).wait()
    for step in range(4):
        unpack(w_down, 4 + step, step * 2 * TOK, 0, FF)
    for step in range(2 * FF // ROWS):
        columns = pl.ds(step * ROWS, ROWS)
        raw[:, columns] = mm(incoming[...], w_in[:, columns])
    for start, width in FF_TILES:
        gate, up = raw[:, start : start + width], raw[:, FF + start : FF + start + width]
        hidden_e[:, start : start + width] = (silu_parts(gate)[1] * up).astype(low)
    slot_grad = jnp.zeros((SLOTS, 1), wide)
    for step in range(D // ROWS):
        columns = pl.ds(step * ROWS, ROWS)
        rows = mm(hidden_e[...], w_down[:, columns]).astype(low).astype(wide)
        cot = grad_rows[:, columns].astype(wide)
        gated[:, columns] = (rows * slot_gate).astype(low)
        grad_rows[:, columns] = (cot * slot_gate).astype(low)
        slot_grad = slot_grad + jnp.sum(rows * cot, axis=1, keepdims=True)
    sent.append(send(2, gated))
    for start, width in FF_TILES:
        grad_hidden = mm_t(grad_rows[...], w_down[pl.ds(start, width), :])
        sig, act = silu_parts(raw[:, start : start + width])
        grad_gate, grad_up = swiglu_back(sig, act, raw[:, FF + start : FF + start + width], grad_hidden)
        grad_e[:, start : start + width] = grad_gate
        grad_e[:, FF + start : FF + start + width] = grad_up
    for step in range(D // ROWS):
        columns = pl.ds(step * ROWS, ROWS)
        grad_in[:, columns] = mm_t(grad_e[...], w_in[columns, :]).astype(low)
    upper, lower = halves(slot_grad)
    slot_lane = lax.broadcasted_iota(jnp.int32, (SLOTS, 128), 1)
    slot_parts = (
        jnp.where(slot_lane == expert, upper.astype(wide), 0.0)
        + jnp.where(slot_lane == expert + 8, lower.astype(wide), 0.0)
    ).astype(low)
    copies[4].wait()
    half = ALL // 2
    for side, target in ((1, grad_other), (0, grad_mine)):
        for step in range(half // ROWS):
            rows = pl.ds(side * half + step * ROWS, ROWS)
            for tile in range(D // 512):
                columns = pl.ds(tile * 512, 512)
                grad_ref[rows, columns] = (
                    mm_t(grad_s[rows, :], w_in_s[columns, 0 : 2 * SH_OWN])
                    + mm(slots_t_ref[rows, :], grad_in[:, columns])
                ).astype(low)
            grad_ref[rows, D : D + 128] = mm(slots_t_ref[rows, :], slot_parts).astype(low)
        copy = pltpu.make_async_copy(grad_ref.at[pl.ds(side * half, half), :], target, sems.at[9 + side])
        copy.start()
        sent.append(copy)

    def expert_down(step):
        count = 2 * FF // FSDP
        return t_mm(hidden_e[:, step * count : (step + 1) * count], grad_rows[...])

    def shared_down(step):
        count = 2 * SH_PAD
        return w_down_s[step * count : (step + 1) * count, :].astype(wide)

    down_copy.wait()
    for step in range(D // ROWS):
        columns = pl.ds(step * ROWS, ROWS)
        w_down_s[:, columns] = t_mm(hidden_s[...], cot_ref[:, columns]).astype(low)
    send_slabs(incoming, grad_e, expert_down, out_ref, buffer, slab_sems, base)
    send_slabs(normed_ref, grad_s, shared_down, out_ref, buffer, slab_sems, 0)
    for copy in sent:
        copy.wait()


def ffn(expert, slots, slots_t, routes, router, pieces, cot_pieces, pack):
    outs = [(D, 3 * SH_OWN + 3 * FF), (ALL, SH_OWN), (SH_OWN, D), (SLOTS, D)]
    kept = [(ALL, SH_OWN), (ALL, 2 * SH_OWN), (SLOTS, D), (SLOTS, FF), (SLOTS, D), (SLOTS, D), (SLOTS, 2 * FF)]
    kept.append((SH_OWN, D))
    grads = [(ALL // 2, D + 128)] * 2
    return pl.pallas_call(
        ffn_kernel,
        out_shape=tuple(
            [jax.ShapeDtypeStruct(shape, low) for shape in grads]
            + [jax.ShapeDtypeStruct((TOK, 128), wide)]
            + [jax.ShapeDtypeStruct(shape, low) for shape in outs]
        ),
        in_specs=[smem, anywhere, anywhere, vmem] + [anywhere] * 22,
        out_specs=tuple([anywhere] * 2 + [vmem] + [anywhere] * 4),
        scratch_shapes=[pltpu.VMEM((ALL, D), low), pltpu.VMEM((ALL, D), low), pltpu.VMEM((ALL, D + 128), low)]
        + [pltpu.VMEM(shape, low) for shape in kept]
        + [
            pltpu.VMEM((D, 2 * SH_OWN + 128), low),
            pltpu.VMEM((D, 2 * FF), low),
            pltpu.VMEM((FF, D), low),
            pltpu.VMEM((SLOTS, ALL), low),
            pltpu.VMEM((ALL, SLOTS), low),
            pltpu.VMEM((SLOTS, 2 * FF), wide),
            pltpu.VMEM((ALL, 128), low),
            pltpu.VMEM((SLOTS, D), low),
            pltpu.VMEM((2, ROWS, 3 * FF), low),
            pltpu.SemaphoreType.DMA((20,)),
            pltpu.SemaphoreType.DMA((20,)),
            pltpu.SemaphoreType.DMA((11,)),
            pltpu.SemaphoreType.DMA((3,)),
            pltpu.SemaphoreType.DMA((2,)),
        ],
        compiler_params=params(60),
        cost_estimate=cost(38e9, 70e6, 1e6),
        name="ffn",
    )(expert, slots, slots_t, routes, router, *pieces, *cot_pieces, pack)


def out_rows_kernel(place_ref, *refs):
    parts, out_ref = refs[:5], refs[5]
    for index in range(EXPERTS):
        step, side = index // 2, index % 2
        columns = pl.ds(pl.multiple_of(place_ref[index] * 256, 256), 256)
        out_ref[:, columns] = parts[step + 1][side] if step else parts[side][...]


def out_rows(places, parts):
    return pl.pallas_call(
        out_rows_kernel,
        out_shape=jax.ShapeDtypeStruct((256, D), low),
        in_specs=[smem] + [vmem] * 5,
        out_specs=vmem,
        compiler_params=params(32),
        cost_estimate=cost(0, 2e6),
        name="out_rows",
    )(places, *parts)


def back_two_kernel(
    own_ref, first_ref, second_ref, middle_ref, cot_ref, gains_ref, gates_ref, routes_ref, block_ref, grad_ref, total_ref, logits_ref
):
    total = own_ref[...] + first_ref[...].astype(wide) + second_ref[...].astype(wide)
    lane = lax.broadcasted_iota(jnp.int32, (TOK, 128), 1)
    extra = total[:, D:]
    first, second = routes_ref[:, 0:1], routes_ref[:, 1:2]

    def taken(route):
        return jnp.sum(jnp.where((lane == route) | (lane == route + 8), extra, 0.0), axis=1, keepdims=True)

    gate_first, gate_second = gates_ref[:, 0:1], gates_ref[:, 1:2]
    taken_first, taken_second = taken(first), taken(second)
    inner = gate_first * taken_first + gate_second * taken_second
    chosen_first, chosen_second = gate_first * (taken_first - inner), gate_second * (taken_second - inner)
    logits = jnp.where(lane == first, chosen_first, 0.0) + jnp.where(lane == second, chosen_second, 0.0)
    grad = total[:, :D]
    for index in range(EXPERTS):
        grad = grad + logits[:, index : index + 1] * gains_ref[2 + index : 3 + index, :]
    middle = middle_ref[...]
    factor = lax.rsqrt(jnp.mean(middle * middle, axis=-1, keepdims=True) + eps_norm)
    scaled = grad * gains_ref[1:2, :]
    mean = jnp.mean(scaled * middle, axis=-1, keepdims=True)
    result = cot_ref[...].astype(wide) + factor * scaled - middle * (factor * factor * factor * mean)
    grad_ref[...] = result
    block_ref[...] = result.astype(low)
    total_ref[...] = grad
    logits_ref[...] = logits


def back_two(*operands):
    return pl.pallas_call(
        back_two_kernel,
        out_shape=(
            jax.ShapeDtypeStruct((TOK, D), low),
            jax.ShapeDtypeStruct((TOK, D), wide),
            jax.ShapeDtypeStruct((TOK, D), wide),
            jax.ShapeDtypeStruct((TOK, 128), wide),
        ),
        in_specs=[vmem] * 8,
        out_specs=(vmem, vmem, vmem, vmem),
        compiler_params=params(32),
        cost_estimate=cost(1e7, 6e6),
        name="back_two",
    )(*operands)


def small_rows_kernel(total_ref, logits_ref, middle_ref, gains_ref, out_ref):
    middle = middle_ref[...]
    factor = lax.rsqrt(jnp.mean(middle * middle, axis=-1, keepdims=True) + eps_norm)
    gain_upper, gain_lower = halves(jnp.sum(total_ref[...] * middle * factor, axis=0, keepdims=True))
    normed = (middle * factor * gains_ref[1:2, :]).astype(low)
    logit_upper, logit_lower = halves(logits_ref[...].T[0:EXPERTS, :])
    router = mm(logit_upper, normed) + mm(logit_lower, normed)
    small = [gain_upper.astype(wide), gain_lower.astype(wide), router, jnp.zeros((6, D), wide)]
    out_ref[...] = jnp.concatenate(small, axis=0).astype(low)


def small_rows(*operands):
    return pl.pallas_call(
        small_rows_kernel,
        out_shape=jax.ShapeDtypeStruct((16, D), low),
        in_specs=[vmem] * 4,
        out_specs=vmem,
        compiler_params=params(32),
        cost_estimate=cost(1e7, 3e6),
        name="small_rows",
    )(*operands)


def norm_factor(values):
    return lax.rsqrt(jnp.mean(values * values, axis=-1, keepdims=True) + eps_norm)


def norm_back(values, factor, gain, grad):
    scaled = grad * gain
    inner = jnp.mean(scaled * values, axis=-1, keepdims=True)
    return factor * scaled - values * (factor * factor * factor * inner)


def per_device(
    hidden_in,
    cotangent,
    segments,
    routes,
    attn_gain,
    w_query,
    w_key,
    w_value,
    w_out,
    ffn_gain,
    w_router,
    shared_gate,
    shared_up,
    shared_down,
    expert_gate,
    expert_up,
    expert_down,
):
    expert = lax.axis_index("expert")
    z, core = expert // 2, expert % 2
    place = lax.axis_index("fsdp")

    misc = jnp.concatenate(
        [attn_gain[:, None], ffn_gain[:, None], w_router, jnp.zeros((TOK, 118), low)], axis=1
    )
    attn_pack = jnp.concatenate(
        [
            lax.dynamic_slice_in_dim(w_query, 256 * expert, 256, 1),
            lax.dynamic_slice_in_dim(w_key, HD * z, HD, 1),
            lax.dynamic_slice_in_dim(w_value, HD * z, HD, 1),
            lax.dynamic_slice_in_dim(w_out, 256 * expert, 256, 1),
            misc,
        ],
        axis=1,
    )
    attn_all = lax.all_gather(attn_pack, "fsdp", axis=0, tiled=True)
    half_in, half_out = SH // 2, SH_OWN // 2
    sel_column = jnp.arange(half_out)
    picked = SH_ROWS * (sel_column // SH_PAD) + SH_PART * expert + sel_column % SH_PAD
    picked = jnp.where(sel_column % SH_PAD < SH_PART, picked, -1)
    select = (jnp.arange(half_in)[:, None] == picked[None, :]).astype(low)
    own_shared = mm(
        jnp.concatenate(
            [shared_gate[:, :half_in], shared_gate[:, half_in:], shared_up[:, :half_in], shared_up[:, half_in:]],
            axis=0,
        ),
        select,
    ).astype(low)
    own_down = jnp.pad(
        lax.dynamic_slice_in_dim(shared_down, SH_PART * expert, SH_PART, 0),
        ((0, SH_PAD - SH_PART), (0, 0)),
    )
    ffn_pack = jnp.concatenate(
        [
            own_shared[:TOK],
            own_shared[TOK : 2 * TOK],
            own_shared[2 * TOK : 3 * TOK],
            own_shared[3 * TOK :],
            pack_tiles(own_down),
            expert_gate[:, 0],
            expert_up[:, 0],
            pack_tiles(expert_down[:, 0]),
        ],
        axis=1,
    )
    ffn_all = lax.all_gather(ffn_pack, "fsdp", axis=0, tiled=True)

    ids = jnp.concatenate(
        [
            segments.astype(low),
            jnp.pad(routes[0].reshape(1, TOK * TOPK), ((0, 0), (0, LENGTH - TOK * TOPK))).astype(low),
            jnp.zeros((14, LENGTH), low),
        ],
        axis=0,
    )
    hidden_pieces = gather_pieces(jnp.concatenate([hidden_in[0], ids], axis=0))
    cot_block, *hidden_pieces = together(cotangent[0], *hidden_pieces)
    cot_first = first_pieces(cot_block)

    inverse_freq = rope_base ** (-jnp.arange(HD // 2, dtype=wide) * 2.0 / HD)
    angles = jnp.arange(LENGTH).astype(wide)[:, None] * inverse_freq[None, :]
    cosine, sine = jnp.cos(angles), jnp.sin(angles)
    cos_all = jnp.concatenate([cosine, cosine], axis=1)
    sin_back = jnp.concatenate([sine, -sine], axis=1)
    cos_own = lax.dynamic_slice_in_dim(cos_all, place * TOK, TOK, 0)
    sin_own = -lax.dynamic_slice_in_dim(sin_back, place * TOK, TOK, 0)
    cos_two, sin_two = jnp.concatenate([cos_own, cos_own]), jnp.concatenate([sin_own, sin_own])
    put_row = jnp.arange(SH_PAD * EXPERTS * FSDP // 2)
    source, within = put_row // half_out, put_row % half_out
    target = SH_ROWS * (within // SH_PAD) + SH_PART * source + within % SH_PAD
    target = jnp.where(within % SH_PAD < SH_PART, target, -1)
    spread = (target[:, None] == jnp.arange(half_in)[None, :]).astype(low)
    put_row = jnp.arange(EXPERTS * SH_PAD)
    target = SH_PART * (put_row // SH_PAD) + put_row % SH_PAD
    target = jnp.where(put_row % SH_PAD < SH_PART, target, -1)
    spread_rows = (jnp.arange(SH_ROWS)[:, None] == target[None, :]).astype(low)
    attn_all, cos_two, sin_two, cos_all, sin_back = together(attn_all, cos_two, sin_two, cos_all, sin_back)
    normed_one, sent, factor_one, gains, ids_all = project(hidden_pieces, attn_all, cos_two, sin_two)

    sent, cot_block, *cot_first = together(sent, cot_block, *cot_first)
    cot_pieces = other_pieces(cot_block, *cot_first)
    qkv = lax.all_to_all(sent, "fsdp", split_axis=0, concat_axis=0, tiled=True)

    ids_all = ids_all.reshape(SEQS, 16, D)
    seg_row = lax.dynamic_slice_in_dim(ids_all[:, 0].astype(wide), place // 2, 1, 0)
    seg_blocks = jnp.pad(seg_row.reshape(FSDP, TOK), ((0, TOK - FSDP), (0, 0)))
    route_all = ids_all[:, 1, : TOK * TOPK].astype(jnp.int32).reshape(ALL, TOPK)
    hit = jnp.any(route_all == expert, axis=1).astype(wide)
    order = jnp.arange(ALL)
    rank = mm(hit.astype(low)[None, :], (order[:, None] < order[None, :]).astype(low))
    slot_bool = (rank.astype(jnp.int32) == jnp.arange(SLOTS)[:, None]) & (hit > 0.5)[None, :]
    slots = slot_bool.astype(low)
    slots_t = slot_bool.T.astype(low)
    out_columns = attn_all[:, 512:768].reshape(EXPERTS, 256, 256)
    owners = jnp.stack([relative_owner(expert, block) for block in range(EXPERTS)])
    out_blocks = [lax.dynamic_index_in_dim(out_columns, owners[block], 0) for block in range(EXPERTS)]
    out_mine, out_other = jnp.concatenate(out_blocks[:4]), jnp.concatenate(out_blocks[4:])
    out_mine, out_other, _ = together(out_mine, out_other, sent)
    w_out_own = out_rows(source_owners(expert), exchange(out_mine, swap_core(out_other)))
    router = attn_all[:, 768:896]
    is_first = core == 0
    kv_weight = attn_all[:, 256:512].reshape(D, 2, 2, HD // 2)
    kv_weight = jnp.where(is_first, kv_weight[:, :, 0], kv_weight[:, :, 1]).reshape(D, HD)
    qkv_weight = jnp.concatenate([attn_all[:, :256], kv_weight], axis=1)
    route_own = route_all[:TOK]
    qkv, seg_row, seg_blocks, route_all, slots, slots_t, w_out_own, router, qkv_weight, route_own, *cot_pieces = together(
        qkv, seg_row, seg_blocks, route_all, slots, slots_t, w_out_own, router, qkv_weight, route_own, *cot_pieces
    )
    mixed_head, log_total = attend(qkv, seg_row, seg_blocks)
    mixed = (
        lax.all_to_all(mixed_head, "fsdp", split_axis=0, concat_axis=0, tiled=True)
        .reshape(SEQS, 2, TOK, HD)
        .transpose(0, 2, 1, 3)
        .reshape(ALL, 2 * HD)
    )
    own_hidden = hidden_in[0].astype(wide)
    half = ALL // 2
    middle = own_hidden + scatter_rows(
        mm(mixed[:half], w_out_own).astype(low), mm(mixed[half:], w_out_own).astype(low)
    )
    factor_two = norm_factor(middle)
    gain_one, gain_two = gains[0:1], gains[1:2]
    normed_block = (middle * factor_two * gain_two).astype(low)

    base = 3 * SH_OWN
    normed_pieces = gather_pieces(normed_block)
    grad_mine, grad_other, gates, ffn_grads, hidden_shared, shared_down_w, gated_rows = ffn(
        expert[None], slots, slots_t, route_all, router, normed_pieces, cot_pieces, ffn_all
    )
    ffn_sums = lax.psum_scatter(ffn_grads, "fsdp", scatter_dimension=0, tiled=True)
    own_grad, to_above, to_below = scatter_start(grad_mine, swap_core(grad_other))
    from_below, from_above = move_z(to_above, 1), move_z(to_below, -1)
    back_block, grad_middle, grad_two, grad_logits = back_two(
        own_grad, from_below, from_above, middle, cotangent[0], gains, gates, route_own
    )
    back_block, hidden_shared, gated_rows = together(back_block, hidden_shared, gated_rows)
    below, above = first_pieces(back_block)
    small = small_rows(grad_two, grad_logits, middle, gains)
    result_other = (mm(hidden_shared[half:], shared_down_w) + mm(slots_t[half:], gated_rows)).astype(low)
    result_mine = (mm(hidden_shared[:half], shared_down_w) + mm(slots_t[:half], gated_rows)).astype(low)
    below, above, result_other, result_mine, small = together(below, above, result_other, result_mine, small)
    back_pieces = other_pieces(back_block, below, above)

    sent_back, grad_attn = mix_back(back_pieces, w_out_own, small)
    grad_head = lax.all_to_all(sent_back, "fsdp", split_axis=0, concat_axis=0, tiled=True)
    grads_head, small_sums = attend_back(qkv, grad_head, log_total, seg_row, seg_blocks, cos_all, sin_back)
    grads_qkv = lax.all_to_all(grads_head, "fsdp", split_axis=0, concat_axis=0, tiled=True)
    result_other, result_mine, _ = together(result_other, result_mine, sent_back)
    result_got = swap_core(result_other)
    result_got, grad_attn = together(result_got, grad_attn)
    out_mine, out_other = out_weights(owners, mixed, grad_attn)
    out_grads = gather_out(source_owners(expert), exchange(out_mine, swap_core(out_other)))
    result_own, to_above, to_below = scatter_start(result_mine, result_got)
    from_below, from_above = move_z(to_above, 1), move_z(to_below, -1)
    grads_qkv, from_below, from_above, out_grads = together(grads_qkv, from_below, from_above, out_grads)
    layer_out = (middle + scatter_end(result_own, from_below, from_above)).astype(low)
    out_parts = lax.all_to_all(out_grads, "fsdp", split_axis=0, concat_axis=0, tiled=True)

    grad_query, kv_mine, kv_other = collect(core[None], grads_qkv)
    attn_grads, grad_qkv = qkv_weights(normed_one, grad_query, kv_mine, swap_core(kv_other))
    grad_normed_other = mm_t(grad_qkv[half:], qkv_weight).astype(low)
    grad_normed_mine = mm_t(grad_qkv[:half], qkv_weight).astype(low)
    ffn_sums, _ = together(ffn_sums, grads_qkv)
    attn_grads, out_parts, grad_normed_other, grad_normed_mine, shared_sums = together(
        attn_grads, out_parts, grad_normed_other, grad_normed_mine, ffn_sums[:, :base]
    )
    attn_parts = lax.all_to_all(attn_grads, "fsdp", split_axis=0, concat_axis=0, tiled=True)

    own_grad_one, to_above, to_below = scatter_start(grad_normed_mine, swap_core(grad_normed_other))
    attn_parts, to_above, to_below = together(attn_parts, to_above, to_below)
    own_grad_one = scatter_end(own_grad_one, move_z(to_above, 1), move_z(to_below, -1))
    grad_input = (grad_middle + norm_back(own_hidden, factor_one[:TOK], gain_one, own_grad_one)).astype(low)
    shared_shards = lax.all_gather(shared_sums, "expert", axis=0)
    attn_parts, shared_shards = together(attn_parts, shared_shards)
    attn_sums = jnp.sum(attn_parts.reshape(FSDP, TOK, 3 * HD).astype(wide), axis=0)
    out_sums = jnp.sum(out_parts.reshape(FSDP, TOK, 256).astype(wide), axis=0)

    own_weight = lax.dynamic_slice_in_dim(qkv_weight, place * TOK, TOK, 0)
    gain_part = jnp.sum(attn_sums * own_weight.astype(wide), axis=1, keepdims=True)
    gain_upper, gain_lower = halves(gain_part / attn_gain.astype(wide)[:, None])
    small = [gain_upper, gain_lower, small_sums.T.astype(low), jnp.zeros((TOK, 110), low)]
    shards = jnp.concatenate([attn_sums.astype(low), out_sums.astype(low), *small], axis=1)

    attn_shards = lax.all_gather(shards, "expert", axis=0)
    grad_shared_gate, grad_shared_up, grad_shared_down = finish_dense(shared_shards, spread, spread_rows)
    grad_w_query, grad_w_key, grad_w_value, grad_w_out, small = finish(attn_shards)
    grad_expert_gate = ffn_sums[:, base : base + FF].astype(wide)[:, None]
    grad_expert_up = ffn_sums[:, base + FF : base + 2 * FF].astype(wide)[:, None]
    grad_expert_down = unpack_tiles(ffn_sums[:, base + 2 * FF :], 1).astype(wide)[:, None]
    return (
        layer_out[None],
        grad_input[None],
        small[:, 0] + small[:, 1],
        grad_w_query,
        grad_w_key,
        grad_w_value,
        grad_w_out,
        small[:, 2] + small[:, 3],
        small[:, 4 : 4 + EXPERTS],
        grad_shared_gate,
        grad_shared_up,
        grad_shared_down,
        grad_expert_gate,
        grad_expert_up,
        grad_expert_down,
    )


def solution(mesh):
    in_specs = (
        P("expert", "fsdp", None),
        P("expert", "fsdp", None),
        P("expert", None),
        P("expert", "fsdp", None),
        P("fsdp"),
        P("fsdp", None),
        P("fsdp", None),
        P("fsdp", None),
        P("fsdp", None),
        P("fsdp"),
        P("fsdp", None),
        P("fsdp", None),
        P("fsdp", None),
        P("fsdp", None),
        P("fsdp", "expert", None),
        P("fsdp", "expert", None),
        P("fsdp", "expert", None),
    )
    out_specs = (
        P("expert", "fsdp", None),
        P("expert", "fsdp", None),
        P("fsdp"),
        P("fsdp", None),
        P("fsdp", None),
        P("fsdp", None),
        P("fsdp", None),
        P("fsdp"),
        P("fsdp", None),
        P("fsdp", None),
        P("fsdp", None),
        P("fsdp", None),
        P("fsdp", "expert", None),
        P("fsdp", "expert", None),
        P("fsdp", "expert", None),
    )
    return jax.shard_map(
        per_device, mesh=mesh, in_specs=in_specs, out_specs=out_specs, check_vma=False
    )
```
